32 devices in a mesh: sec: 2 (over core), grp: 4 (over z), tp: 4 (over y, x).
Axes of the slice: x: 2, y: 2, z: 4, core: 2. Of those that a mesh axis runs over, the one named last changes fastest.
Arguments:
- inputs: bfloat16 [2, 64, 2880], P(None, 'grp'), may hold values from -12.5 to 12.5
- attention_gain: float32 [2880], replicated, may hold values from 0.25 to 1.75
- w_query: bfloat16 [2880, 4096], P(None, ('sec', 'tp')), may hold values from -0.109375 to 0.109375
- key_value_weight: bfloat16 [2880, 8, 128], P(None, ('sec', 'tp')), may hold values from -0.109375 to 0.109375
- head_sink_logits: float32 [64], P(('sec', 'tp')), may hold values from 0 to 6
- w_output: bfloat16 [4096, 2880], P(('sec', 'tp')), may hold values from -0.09375 to 0.09375
- cache_pairs: bfloat16 [64, 256, 8, 128], P('grp', None, ('sec', 'tp')), may hold values from -600 to 600
- lengths: int32 [64], P('grp'), may hold values from 1 to 256, 8192 in all
- expert_gain: float32 [2880], replicated, may hold values from 0.25 to 1.75
- w_gate: bfloat16 [4, 2880, 1440], P('grp', None, ('sec', 'tp')), may hold values from -0.109375 to 0.109375
- w_up: bfloat16 [4, 2880, 1440], P('grp', None, ('sec', 'tp')), may hold values from -0.109375 to 0.109375
- w_down: bfloat16 [4, 1440, 2880], P('grp', ('sec', 'tp')), may hold values from -0.15625 to 0.15625
- routes: int32 [2, 64, 4], P(None, 'grp'), may hold values from 0 to 3, as said below
- gate_weights: float32 [2, 64, 4], P(None, 'grp'), may hold values from 0.2 to 1
Outputs:
- outputs: bfloat16 [2, 64, 2880], P(None, 'grp', ('sec', 'tp'))
The draws below stay inside these ranges and needn't reach their ends.
Inputs may be any that keep to these rules, and one draw needn't show every extreme that they name: `routes`: A row names 4 different experts. In each step the 16 rows of one attention group (rows g * 16 to (g + 1) * 16 - 1) name each expert either 0 or 16 times in all, and in each step one expert is named 16 times by every group.
All inputs are finite; a program needn't handle non-finite values. No bound on the sum of `lengths` on one device may be relied on, other than what follows from the above.
Results may differ from the reference program's by a relative error of at most 0.012.
Values may be sent and summed in bfloat16 or wider, within the bound.
No kernel may reach another device: no remote copies, remote signals or barrier semaphores. Data moves between devices by JAX's collectives and lax.ppermute only.
A program may use at most 64 MiB of HBM per device.

```python
import math
import jax
import jax.numpy as jnp
import numpy as np
from jax import lax

MODEL_WIDTH = 2880
QUERY_HEADS = 64
KEY_VALUE_HEADS = 8
HEAD_SIZE = 64
TOP = 4
HID = 1440
STEPS = 2
GROUP_ROWS = 16
CONTEXT_SLOTS = 256
EXPERTS = 4
CAP = 16
TOTAL_ROWS = 64


def draw_inputs(key, part):
    key = jax.random.fold_in(key, 11)
    row_key, column_key, base_key = jax.random.split(key, 3)
    row_scale = jnp.exp(jax.random.uniform(row_key, (STEPS, TOTAL_ROWS, 1), jnp.float32, jnp.log(0.1), 0.0))
    column_scale = jnp.exp(jax.random.uniform(column_key, (1, 1, MODEL_WIDTH), jnp.float32, jnp.log(0.3), jnp.log(3.0)))
    base_values = jnp.clip(jax.random.normal(base_key, (STEPS, TOTAL_ROWS, MODEL_WIDTH), jnp.float32), -4.0, 4.0)
    return (base_values * row_scale * column_scale).astype(jnp.bfloat16)


def draw_cache_pairs(key, part):
    key = jax.random.fold_in(key, 23)
    key_key, value_key = jax.random.split(key, 2)
    half_rotary_shape = (TOTAL_ROWS, CONTEXT_SLOTS, KEY_VALUE_HEADS, HEAD_SIZE)
    key_part = jnp.clip(jax.random.normal(key_key, half_rotary_shape, jnp.float32), -4.0, 4.0)
    value_part = jnp.clip(jax.random.normal(value_key, half_rotary_shape, jnp.float32), -4.0, 4.0)
    return jnp.concatenate([key_part, value_part], axis=-1).astype(jnp.bfloat16)


def route_block(block_key, hot_expert):
    order_key, shuffle_key = jax.random.split(block_key)
    order = jax.random.permutation(order_key, EXPERTS).astype(jnp.int32)
    where_hot = jnp.argmax(order == hot_expert)
    order = order.at[where_hot].set(order[0]).at[0].set(hot_expert)
    chosen = max(TOP, EXPERTS // 2)
    per_round = chosen // TOP
    row_numbers = jnp.arange(GROUP_ROWS).astype(jnp.int32)
    round_index = row_numbers // per_round
    within = row_numbers % per_round
    picks = (TOP * within[:, None] + jnp.arange(TOP).astype(jnp.int32)[None, :] + TOP * round_index[:, None]) % chosen
    named = order[picks]
    shuffle = jax.random.permutation(shuffle_key, GROUP_ROWS)
    return named[shuffle]


def draw_routes(key, part):
    key = jax.random.fold_in(key, 37)
    hot_key, block_root = jax.random.split(key)
    blocks = TOTAL_ROWS // GROUP_ROWS
    hot_experts = jax.random.randint(hot_key, (STEPS,), 0, EXPERTS).astype(jnp.int32)
    step_keys = jax.random.split(block_root, STEPS)

    def one_step(step_key, hot_expert):
        block_keys = jax.random.split(step_key, blocks)
        return jax.vmap(route_block, in_axes=(0, None))(block_keys, hot_expert)
    named = jax.vmap(one_step)(step_keys, hot_experts)
    return named.reshape(STEPS, TOTAL_ROWS, TOP).astype(jnp.int32)


def block_levels(stream_key, dims, cuts, least, high):
    factor_of = 1.0
    for axis_at, shards_of in cuts:
        heights = jax.random.uniform(jax.random.fold_in(jax.random.fold_in(stream_key, 6), axis_at), (shards_of,), jnp.float32, least / len(cuts), high / len(cuts))
        factor_of = factor_of * jnp.repeat(jnp.exp(heights), dims[axis_at] // shards_of).reshape((-1,) + (1,) * (len(dims) - 1 - axis_at))
    return factor_of


def profile(count, total, most, slope):
    loads = [(1 << 20) // math.isqrt(standing ** slope) + 1 for standing in range(2, count + 1)]
    rest, holding = total - most - (count - 1), [1] * (count - 1)
    while rest > 0:
        free = [i for i in range(count - 1) if holding[i] < most]
        pool, budget = sum([loads[i] for i in free]), rest
        for i in free:
            addition = min(most - holding[i], max(1, budget * loads[i] // pool), rest)
            holding[i] = holding[i] + addition
            rest = rest - addition
    return np.array([most] + holding)


def uneven_parts(rng, count, total, reach, slope):
    if count == 2:
        one = jax.random.randint(rng, (), max(1, total - reach), min(reach, total - 1) + 1)
        return jnp.stack([one, total - one])
    sizes = jnp.asarray(profile(count, total, reach, slope), jnp.int32)
    pairs = (count - 1) // 2
    source_of, receiver = sizes[1:1 + 2 * pairs:2], sizes[2:2 + 2 * pairs:2]
    margin = jnp.minimum(source_of - 1, reach - receiver)
    moved = jax.random.randint(jax.random.fold_in(rng, 1), (pairs,), 0, 1 << 20) % (margin + 1)
    sizes = sizes.at[1:1 + 2 * pairs:2].set(source_of - moved).at[2:2 + 2 * pairs:2].set(receiver + moved)
    return sizes[jax.random.permutation(jax.random.fold_in(rng, 2), count)]


def centred(rng, shape, width, limit, cuts=(), held_as=jnp.bfloat16):
    values = width * jax.random.normal(rng, shape, jnp.float32)
    if cuts:
        values = values * block_levels(rng, shape, cuts, -0.22, 0.18)
    return jnp.clip(values, -limit, limit).astype(held_as)


def setup_inputs(seed: int = 0) -> dict:
    splits = jax.random.split(jax.random.key(seed), 15)
    inputs = draw_inputs(jax.random.fold_in(splits[14], 71), 0)
    attention_gain = jnp.clip(1.0 + 0.15 * jax.random.normal(splits[1], (MODEL_WIDTH,), jnp.float32), 0.25, 1.75)
    w_query = centred(splits[2], (MODEL_WIDTH, QUERY_HEADS * HEAD_SIZE), MODEL_WIDTH ** -0.5, 0.109375, ((1, 8),))
    key_value_weight = centred(splits[3], (MODEL_WIDTH, KEY_VALUE_HEADS, 2 * HEAD_SIZE), MODEL_WIDTH ** -0.5, 0.109375, ((1, 8),))
    head_sink_logits = jnp.clip(6.0 * jax.random.uniform(splits[4], (QUERY_HEADS,), jnp.float32) ** block_levels(splits[4], (QUERY_HEADS,), ((0, 8),), -0.2, 0.2), 0.0, 6.0)
    w_output = centred(splits[5], (QUERY_HEADS * HEAD_SIZE, MODEL_WIDTH), (QUERY_HEADS * HEAD_SIZE) ** -0.5, 0.09375, ((0, 8),))
    cache_pairs = draw_cache_pairs(jax.random.fold_in(splits[14], 71), 0)
    lengths = uneven_parts(splits[7], TOTAL_ROWS, TOTAL_ROWS * CONTEXT_SLOTS // 2, CONTEXT_SLOTS, 2).astype(jnp.int32)
    expert_gain = jnp.clip(1.0 + 0.15 * jax.random.normal(splits[8], (MODEL_WIDTH,), jnp.float32), 0.25, 1.75)
    w_gate = centred(splits[9], (EXPERTS, MODEL_WIDTH, HID), MODEL_WIDTH ** -0.5, 0.109375, ((0, 4), (2, 8)))
    w_up = centred(splits[10], (EXPERTS, MODEL_WIDTH, HID), MODEL_WIDTH ** -0.5, 0.109375, ((0, 4), (2, 8)))
    w_down = centred(splits[11], (EXPERTS, HID, MODEL_WIDTH), HID ** -0.5, 0.15625, ((0, 4), (1, 8)))
    routes = draw_routes(jax.random.fold_in(splits[14], 71), 0)
    gate_weights = jnp.clip(jnp.exp(math.log(1.0) - 1.609438 * jax.random.uniform(splits[13], (STEPS, TOTAL_ROWS, TOP), jnp.float32) ** block_levels(splits[13], (STEPS, TOTAL_ROWS, TOP), ((1, 4),), -0.2, 0.2)), 0.2, 1.0)
    return {"inputs": inputs, "attention_gain": attention_gain, "w_query": w_query, "key_value_weight": key_value_weight, "head_sink_logits": head_sink_logits, "w_output": w_output, "cache_pairs": cache_pairs, "lengths": lengths, "expert_gain": expert_gain, "w_gate": w_gate, "w_up": w_up, "w_down": w_down, "routes": routes, "gate_weights": gate_weights}


def rms_norm(values, scale_row):
    widened = values.astype(jnp.float32)
    scale_factor = lax.rsqrt(lax.optimization_barrier(jnp.mean(widened * widened, axis=-1, keepdims=True)) + 1e-05)
    return (widened * scale_factor * scale_row).astype(jnp.bfloat16)

def rotate(vectors, position):
    half_size = vectors.shape[-1] // 2
    counter = jnp.arange(half_size).astype(jnp.float32)
    frequency = jnp.power(jnp.float32(150000.0), counter * (-2.0 / vectors.shape[-1]))
    angle_table = position * frequency
    cosine = jnp.cos(angle_table)
    sine_table = jnp.sin(angle_table)
    first_half = vectors[..., :half_size]
    second_half = vectors[..., half_size:]
    return jnp.concatenate([first_half * cosine - second_half * sine_table, first_half * sine_table + second_half * cosine], axis=-1)

def head_attention(query_head, cached_keys, cached_values, fresh_keys, fresh_values, sink_row, valid):
    widened = query_head.astype(jnp.float32)
    cached = jnp.einsum('rgd,rjd->rgj', widened, cached_keys.astype(jnp.float32)) * 0.125
    cached = jnp.where(valid[:, None, :], cached, -jnp.inf)
    fresh = jnp.einsum('rgd,rid->rgi', widened, fresh_keys.astype(jnp.float32)) * 0.125
    largest = jnp.maximum(jnp.maximum(lax.optimization_barrier(jnp.max(cached, axis=-1)), lax.optimization_barrier(jnp.max(fresh, axis=-1))), sink_row[None, :])
    cached_exp = jnp.exp(cached - largest[..., None])
    fresh_exp = jnp.exp(fresh - largest[..., None])
    denominator = lax.optimization_barrier(jnp.sum(cached_exp, axis=-1)) + lax.optimization_barrier(jnp.sum(fresh_exp, axis=-1)) + jnp.exp(sink_row[None, :] - largest)
    cached_probs = (cached_exp / denominator[..., None]).astype(jnp.bfloat16)
    fresh_probs = (fresh_exp / denominator[..., None]).astype(jnp.bfloat16)
    mixed = jnp.einsum('rgj,rjd->rgd', cached_probs.astype(jnp.float32), cached_values.astype(jnp.float32))
    return mixed + jnp.einsum('rgi,rid->rgd', fresh_probs.astype(jnp.float32), fresh_values.astype(jnp.float32))

def expert_outputs(expert_in, route_step, w_gate, w_up, w_down):
    blocks = TOTAL_ROWS // GROUP_ROWS
    flat_routes = route_step.reshape(blocks, GROUP_ROWS * TOP)
    onehot = (flat_routes[..., None] == jnp.arange(EXPERTS).astype(jnp.int32)[None, None, :]).astype(jnp.int32)
    earlier = jnp.cumsum(onehot, axis=1) - onehot
    slot_index = lax.optimization_barrier(jnp.sum(earlier * onehot, axis=-1)).astype(jnp.int32)
    block_of = jnp.broadcast_to(jnp.arange(blocks).astype(jnp.int32)[:, None], flat_routes.shape)
    row_of = (block_of * GROUP_ROWS + jnp.arange(GROUP_ROWS * TOP).astype(jnp.int32)[None, :] // TOP).astype(jnp.int32)
    table = jnp.zeros((EXPERTS, blocks, CAP), jnp.int32).at[flat_routes, block_of, slot_index].set(row_of)

    def one_expert(pieces):
        rows_taken, gate_matrix, up_matrix, down_matrix = pieces
        taken = expert_in[rows_taken.reshape(-1)]
        gate_h = jnp.dot(taken, gate_matrix, preferred_element_type=jnp.float32)
        up_h = jnp.dot(taken, up_matrix, preferred_element_type=jnp.float32)
        act = ((up_h + 1.0) * gate_h * jax.nn.sigmoid(1.702 * gate_h)).astype(jnp.bfloat16)
        result = jnp.dot(act, down_matrix, preferred_element_type=jnp.float32).astype(jnp.bfloat16)
        return result.reshape(blocks, CAP, MODEL_WIDTH)
    buffers = lax.map(one_expert, (table, w_gate, w_up, w_down))
    return buffers[flat_routes, block_of, slot_index].reshape(TOTAL_ROWS, TOP, MODEL_WIDTH)

def reference(inputs, attention_gain, w_query, key_value_weight, head_sink_logits, w_output, cache_pairs, lengths, expert_gain, w_gate, w_up, w_down, routes, gate_weights):
    query_group_width = QUERY_HEADS // KEY_VALUE_HEADS
    head_cache = jnp.moveaxis(cache_pairs, 2, 0)
    valid = jnp.arange(CONTEXT_SLOTS).astype(jnp.int32)[None, :] < lengths[:, None]
    sinks_per_head = head_sink_logits.reshape(KEY_VALUE_HEADS, query_group_width)
    fresh_keys = []
    fresh_values = []
    results = []
    for step_index in range(STEPS):
        normalized_input = rms_norm(inputs[step_index], attention_gain)
        query = jnp.dot(normalized_input, w_query, preferred_element_type=jnp.float32).reshape(TOTAL_ROWS, QUERY_HEADS, HEAD_SIZE)
        cache_entry_pairs = jnp.dot(normalized_input, key_value_weight.reshape(MODEL_WIDTH, KEY_VALUE_HEADS * 2 * HEAD_SIZE), preferred_element_type=jnp.float32).reshape(TOTAL_ROWS, KEY_VALUE_HEADS, 2 * HEAD_SIZE)
        position = (lengths + step_index).astype(jnp.float32)[:, None, None]
        rotated_rows = rotate(query, position).astype(jnp.bfloat16)
        fresh_keys.append(rotate(cache_entry_pairs[..., :HEAD_SIZE], position).astype(jnp.bfloat16))
        fresh_values.append(cache_entry_pairs[..., HEAD_SIZE:].astype(jnp.bfloat16))
        stacked_keys = jnp.moveaxis(jnp.stack(fresh_keys, 2), 1, 0)
        stacked_values = jnp.moveaxis(jnp.stack(fresh_values, 2), 1, 0)
        grouped_queries = jnp.moveaxis(rotated_rows.reshape(TOTAL_ROWS, KEY_VALUE_HEADS, query_group_width, HEAD_SIZE), 1, 0)

        def one_head(pieces):
            query_head, cache_head, keys_head, values_head, sink_row = pieces
            return head_attention(query_head, cache_head[..., :HEAD_SIZE], cache_head[..., HEAD_SIZE:], keys_head, values_head, sink_row, valid)
        mixed = lax.map(one_head, (grouped_queries, head_cache, stacked_keys, stacked_values, sinks_per_head))
        attention_mix = jnp.moveaxis(mixed, 0, 1).reshape(TOTAL_ROWS, QUERY_HEADS * HEAD_SIZE).astype(jnp.bfloat16)
        projected = jnp.dot(attention_mix, w_output, preferred_element_type=jnp.float32)
        middle = (inputs[step_index].astype(jnp.float32) + projected).astype(jnp.bfloat16)
        expert_in = rms_norm(middle, expert_gain)
        expert_out = expert_outputs(expert_in, routes[step_index], w_gate, w_up, w_down)
        weighted = lax.optimization_barrier(jnp.sum(gate_weights[step_index][..., None] * expert_out.astype(jnp.float32), axis=1))
        results.append((middle.astype(jnp.float32) + weighted).astype(jnp.bfloat16))
    return jnp.stack(results, 0)
```

```python
import jax
import jax.numpy as jnp
from jax import lax
from jax.sharding import PartitionSpec as P

HEAD_SIZE = 64
TOP = 4


def rms_norm(values, scale_row):
    widened = values.astype(jnp.float32)
    scale_factor = lax.rsqrt(jnp.mean(widened * widened, axis=-1, keepdims=True) + 1e-05)
    return (widened * scale_factor * scale_row).astype(jnp.bfloat16)


def rotate(vectors, position):
    half_size = vectors.shape[-1] // 2
    counter = jnp.arange(half_size).astype(jnp.float32)
    frequency = jnp.power(jnp.float32(150000.0), counter * (-2.0 / vectors.shape[-1]))
    angle_table = position * frequency
    cosine = jnp.cos(angle_table)
    sine_table = jnp.sin(angle_table)
    first_half = vectors[..., :half_size]
    second_half = vectors[..., half_size:]
    return jnp.concatenate(
        [
            first_half * cosine - second_half * sine_table,
            first_half * sine_table + second_half * cosine,
        ],
        axis=-1,
    )


def attention_partial(normed, w_query, key_value_weight, head_sink_logits, w_output, cache_pairs, lengths, steps):
    rows = lengths.shape[0]
    query = jnp.dot(normed, w_query, preferred_element_type=jnp.float32)
    pairs = jnp.dot(normed, key_value_weight, preferred_element_type=jnp.float32)
    heads = query.shape[1] // HEAD_SIZE
    position = (lengths[None, :] + jnp.arange(steps)[:, None]).astype(jnp.float32)[..., None]
    turned = rotate(query.reshape(steps, rows, heads, HEAD_SIZE), position[..., None]).astype(jnp.bfloat16)
    pairs = pairs.reshape(steps, rows, 2 * HEAD_SIZE)
    new_key = rotate(pairs[..., :HEAD_SIZE], position).astype(jnp.bfloat16)
    new_value = pairs[..., HEAD_SIZE:].astype(jnp.bfloat16)
    cached = jnp.einsum("srgd,rjd->rsgj", turned, cache_pairs[..., :HEAD_SIZE], preferred_element_type=jnp.float32) * 0.125
    valid = (jnp.arange(cache_pairs.shape[1])[None, :] < lengths[:, None])[:, None, None, :]
    cached = jnp.where(valid, cached, -jnp.inf)
    fresh = jnp.einsum("srgd,ird->rsgi", turned, new_key, preferred_element_type=jnp.float32) * 0.125
    seen = (jnp.arange(steps)[None, :] <= jnp.arange(steps)[:, None])[None, :, None, :]
    fresh = jnp.where(seen, fresh, -jnp.inf)
    sink = head_sink_logits[None, None, :]
    largest = jnp.maximum(jnp.maximum(jnp.max(cached, -1), jnp.max(fresh, -1)), sink)
    cached_exp = jnp.exp(cached - largest[..., None])
    fresh_exp = jnp.exp(fresh - largest[..., None])
    total = jnp.sum(cached_exp, -1) + jnp.sum(fresh_exp, -1) + jnp.exp(sink - largest)
    cached_probs = (cached_exp / total[..., None]).astype(jnp.bfloat16)
    fresh_probs = (fresh_exp / total[..., None]).astype(jnp.bfloat16)
    mixed = jnp.einsum("rsgj,rjd->srgd", cached_probs, cache_pairs[..., HEAD_SIZE:], preferred_element_type=jnp.float32)
    mixed = mixed + jnp.einsum("rsgi,ird->srgd", fresh_probs, new_value, preferred_element_type=jnp.float32)
    mixed = mixed.reshape(steps * rows, heads * HEAD_SIZE).astype(jnp.bfloat16)
    return jnp.dot(mixed, w_output, preferred_element_type=jnp.float32)


def swap(value, axes, mask):
    size = lax.axis_size(axes)
    return lax.ppermute(value, axes, [(i, i ^ mask) for i in range(size)])


def every_expert_body(inputs, attention_gain, w_query, key_value_weight, head_sink_logits, w_output, cache_pairs, lengths,
                      expert_gain, w_gate, w_up, w_down, routes, gate_weights):
    shards = lax.axis_size(("sec", "tp"))
    mine = lax.axis_index(("sec", "tp"))
    sec, tp, grp = lax.axis_index("sec"), lax.axis_index("tp"), lax.axis_index("grp")
    secs, tps, groups = lax.axis_size("sec"), lax.axis_size("tp"), lax.axis_size("grp")
    steps, rows, width = inputs.shape
    part = width // shards
    flat = inputs.reshape(steps * rows, width)
    normed = rms_norm(flat, attention_gain)
    partial = attention_partial(normed, w_query, key_value_weight[:, 0], head_sink_logits, w_output,
                                cache_pairs[:, :, 0], lengths, steps)
    chunks = partial.reshape(steps * rows, shards, part).swapaxes(0, 1)
    own = lax.dynamic_index_in_dim(chunks, mine, 0, False)
    chunks = chunks.astype(jnp.bfloat16)
    arrived = [swap(lax.dynamic_index_in_dim(chunks, mine ^ m, 0, False), ("sec", "tp"), m) for m in range(1, shards)]
    own_input = lax.dynamic_slice_in_dim(flat, mine * part, part, 1).astype(jnp.float32)
    for piece in arrived:
        own = own + piece.astype(jnp.float32)
    middle = (own_input + own).astype(jnp.bfloat16)
    grouped = jnp.stack([middle] + [swap(middle, "grp", m) for m in range(1, groups)])
    grouped = jnp.stack([grouped] + [swap(grouped, "tp", m) for m in range(1, tps)])
    grouped = jnp.stack([grouped] + [swap(grouped, "sec", m) for m in range(1, secs)])
    grouped = jnp.take(grouped, jnp.arange(secs) ^ sec, axis=0)
    grouped = jnp.take(grouped, jnp.arange(tps) ^ tp, axis=1)
    everyone = grouped.transpose(2, 3, 0, 1, 4).reshape(groups * steps * rows, width)
    expert_in = rms_norm(everyone, expert_gain)
    gate_h = jnp.dot(expert_in, w_gate[0], preferred_element_type=jnp.float32)
    up_h = jnp.dot(expert_in, w_up[0], preferred_element_type=jnp.float32)
    act = ((up_h + 1.0) * gate_h * jax.nn.sigmoid(1.702 * gate_h)).astype(jnp.bfloat16)
    out = jnp.dot(act, w_down[0], preferred_element_type=jnp.float32)
    halves = out.reshape(-1, secs, tps * part).swapaxes(0, 1)
    held = lax.dynamic_index_in_dim(halves, sec, 0, False)
    for m in range(1, secs):
        held = held + swap(lax.dynamic_index_in_dim(halves, sec ^ m, 0, False).astype(jnp.bfloat16), "sec", m).astype(jnp.float32)
    quarters = held.reshape(-1, tps, part).swapaxes(0, 1)
    held = lax.dynamic_index_in_dim(quarters, tp, 0, False)
    quarters = quarters.astype(jnp.bfloat16)
    come = [swap(lax.dynamic_index_in_dim(quarters, tp ^ m, 0, False), "tp", m) for m in range(1, tps)]
    for piece in come:
        held = held + piece.astype(jnp.float32)
    held = held.astype(jnp.bfloat16).reshape(groups, steps * rows, part)
    back = [held[0]] + [swap(held[m], "grp", m) for m in range(1, groups)]
    weights = gate_weights.reshape(steps * rows, TOP)
    named = routes.reshape(steps * rows, TOP)
    result = middle.astype(jnp.float32)
    for m in range(groups):
        weight = jnp.sum(jnp.where(named == (grp ^ m), weights, 0.0), axis=1, keepdims=True)
        result = result + weight * back[m].astype(jnp.float32)
    return result.astype(jnp.bfloat16).reshape(steps, rows, part)


def body(*args):
    if lax.axis_size("grp") * args[9].shape[0] == TOP and args[9].shape[0] == 1:
        return every_expert_body(*args)
    return general_body(*args)


def attend(
    normalized_input,
    w_query,
    key_value_weight,
    head_sink_logits,
    w_output,
    cache_pairs,
    lengths,
    step_index,
    fresh_keys,
    fresh_values,
):
    row_count = normalized_input.shape[0]
    kv_heads = key_value_weight.shape[1]
    query = jnp.dot(normalized_input, w_query, preferred_element_type=jnp.float32).reshape(
        row_count, -1, HEAD_SIZE
    )
    cache_entry_pairs = jnp.dot(
        normalized_input,
        key_value_weight.reshape(key_value_weight.shape[0], -1),
        preferred_element_type=jnp.float32,
    ).reshape(row_count, kv_heads, 2 * HEAD_SIZE)
    position = (lengths + step_index).astype(jnp.float32)[:, None, None]
    rotated_rows = rotate(query, position).astype(jnp.bfloat16)
    fresh_keys = fresh_keys + [
        rotate(cache_entry_pairs[..., :HEAD_SIZE], position).astype(jnp.bfloat16)
    ]
    fresh_values = fresh_values + [cache_entry_pairs[..., HEAD_SIZE:].astype(jnp.bfloat16)]
    grouped_queries = rotated_rows.reshape(row_count, kv_heads, -1, HEAD_SIZE)
    new_keys = jnp.stack(fresh_keys, 1)
    new_values = jnp.stack(fresh_values, 1)
    cached = (
        jnp.einsum(
            "rkgd,rjkd->rkgj",
            grouped_queries,
            cache_pairs[..., :HEAD_SIZE],
            preferred_element_type=jnp.float32,
        )
        * 0.125
    )
    valid = (jnp.arange(cache_pairs.shape[1])[None, :] < lengths[:, None])[:, None, None, :]
    cached = jnp.where(valid, cached, -jnp.inf)
    fresh = (
        jnp.einsum("rkgd,rikd->rkgi", grouped_queries, new_keys, preferred_element_type=jnp.float32)
        * 0.125
    )
    sink_row = head_sink_logits.reshape(kv_heads, -1)[None]
    largest = jnp.maximum(jnp.maximum(jnp.max(cached, axis=-1), jnp.max(fresh, axis=-1)), sink_row)
    cached_exp = jnp.exp(cached - largest[..., None])
    fresh_exp = jnp.exp(fresh - largest[..., None])
    denominator = (
        jnp.sum(cached_exp, axis=-1) + jnp.sum(fresh_exp, axis=-1) + jnp.exp(sink_row - largest)
    )
    cached_probs = (cached_exp / denominator[..., None]).astype(jnp.bfloat16)
    fresh_probs = (fresh_exp / denominator[..., None]).astype(jnp.bfloat16)
    mixed = jnp.einsum(
        "rkgj,rjkd->rkgd",
        cached_probs,
        cache_pairs[..., HEAD_SIZE:],
        preferred_element_type=jnp.float32,
    )
    mixed = mixed + jnp.einsum(
        "rkgi,rikd->rkgd", fresh_probs, new_values, preferred_element_type=jnp.float32
    )
    attention_mix = mixed.reshape(row_count, -1).astype(jnp.bfloat16)
    partial_sum = jnp.dot(attention_mix, w_output, preferred_element_type=jnp.float32)
    return (partial_sum, fresh_keys, fresh_values)


def general_body(
    inputs,
    attention_gain,
    w_query,
    key_value_weight,
    head_sink_logits,
    w_output,
    cache_pairs,
    lengths,
    expert_gain,
    w_gate,
    w_up,
    w_down,
    routes,
    gate_weights,
):
    shards = lax.axis_size(("sec", "tp"))
    shard_index = lax.axis_index(("sec", "tp"))
    experts = lax.axis_size("grp") * w_gate.shape[0]
    group_rows = inputs.shape[1]
    width = inputs.shape[2]
    part_width = width // shards
    chosen = max(TOP, experts // 2)
    capacity = group_rows * TOP // chosen
    slot_total = experts * capacity
    gate_matrix = w_gate[0]
    up_matrix = w_up[0]
    down_matrix = w_down[0]
    fresh_keys = []
    fresh_values = []
    results = []
    for step_index in range(inputs.shape[0]):
        normalized_input = rms_norm(inputs[step_index], attention_gain)
        partial_sum, fresh_keys, fresh_values = attend(
            normalized_input,
            w_query,
            key_value_weight,
            head_sink_logits,
            w_output,
            cache_pairs,
            lengths,
            step_index,
            fresh_keys,
            fresh_values,
        )
        summed = lax.psum(partial_sum[None], ("sec", "tp"))
        middle = (inputs[step_index][None].astype(jnp.float32) + summed).astype(jnp.bfloat16)
        route_rows = routes[step_index][None]
        step_count = middle.shape[0]
        expert_in = rms_norm(middle, expert_gain)
        flat_routes = route_rows.reshape(step_count, group_rows * TOP)
        onehot = (flat_routes[..., None] == jnp.arange(experts)[None, None, :]).astype(jnp.int32)
        earlier = jnp.cumsum(onehot, axis=1) - onehot
        slot_index = jnp.sum(earlier * onehot, axis=-1).reshape(step_count, group_rows, TOP)
        target = route_rows * capacity + slot_index
        placed = target[..., None] == jnp.arange(slot_total)[None, None, None, :]
        dispatch_table = jnp.sum(placed.astype(jnp.int32), axis=2).astype(jnp.bfloat16)
        combine_table = jnp.sum(
            jnp.where(placed, gate_weights[step_index][None][..., None], 0.0), axis=2
        )
        outgoing = jnp.einsum(
            "crm,crd->cmd", dispatch_table, expert_in, preferred_element_type=jnp.float32
        )
        outgoing = outgoing.astype(jnp.bfloat16).reshape(step_count, experts, capacity, width)
        arrived = lax.all_to_all(outgoing, "grp", split_axis=1, concat_axis=1, tiled=True)
        gate_h = jnp.einsum(
            "snpd,dh->snph", arrived, gate_matrix, preferred_element_type=jnp.float32
        )
        up_h = jnp.einsum("snpd,dh->snph", arrived, up_matrix, preferred_element_type=jnp.float32)
        act = ((up_h + 1.0) * gate_h * jax.nn.sigmoid(1.702 * gate_h)).astype(jnp.bfloat16)
        partial_out = jnp.einsum(
            "snph,hd->snpd", act, down_matrix, preferred_element_type=jnp.float32
        )
        reduced = lax.psum_scatter(
            partial_out, ("sec", "tp"), scatter_dimension=3, tiled=True
        ).astype(jnp.bfloat16)
        returned = lax.all_to_all(reduced, "grp", split_axis=1, concat_axis=1, tiled=True)
        returned_rows = returned.reshape(step_count, slot_total, part_width).astype(jnp.float32)
        weighted = jnp.einsum(
            "srm,smd->srd", combine_table, returned_rows, precision=lax.Precision.HIGHEST
        )
        own_middle = lax.dynamic_slice_in_dim(
            middle, shard_index * part_width, part_width, 2
        ).astype(jnp.float32)
        results.append((own_middle + weighted).astype(jnp.bfloat16)[0])
    return jnp.stack(results, 0)


def solution(mesh):
    placed = (
        P(None, "grp", None),
        P(),
        P(None, ("sec", "tp")),
        P(None, ("sec", "tp"), None),
        P(("sec", "tp")),
        P(("sec", "tp"), None),
        P("grp", None, ("sec", "tp"), None),
        P("grp"),
        P(),
        P("grp", None, ("sec", "tp")),
        P("grp", None, ("sec", "tp")),
        P("grp", ("sec", "tp"), None),
        P(None, "grp", None),
        P(None, "grp", None),
    )
    return jax.shard_map(
        body, mesh=mesh, in_specs=placed, out_specs=P(None, "grp", ("sec", "tp")), check_vma=False
    )
```

```python
import functools

import jax
import jax.numpy as jnp
import numpy as np
from jax import lax
from jax.experimental import pallas as pl
from jax.experimental.pallas import tpu as pltpu
from jax.sharding import PartitionSpec as P

HEAD_SIZE = 64
TOP = 4


def rms_norm(values, scale_row):
    widened = values.astype(jnp.float32)
    scale_factor = lax.rsqrt(jnp.mean(widened * widened, axis=-1, keepdims=True) + 1e-05)
    return (widened * scale_factor * scale_row).astype(jnp.bfloat16)


def rotate(vectors, position):
    half_size = vectors.shape[-1] // 2
    counter = jnp.arange(half_size).astype(jnp.float32)
    frequency = jnp.power(jnp.float32(150000.0), counter * (-2.0 / vectors.shape[-1]))
    angle_table = position * frequency
    cosine = jnp.cos(angle_table)
    sine_table = jnp.sin(angle_table)
    first_half = vectors[..., :half_size]
    second_half = vectors[..., half_size:]
    return jnp.concatenate(
        [
            first_half * cosine - second_half * sine_table,
            first_half * sine_table + second_half * cosine,
        ],
        axis=-1,
    )


def attend(
    normalized_input,
    w_query,
    key_value_weight,
    head_sink_logits,
    w_output,
    cache_pairs,
    lengths,
    step_index,
    fresh_keys,
    fresh_values,
):
    row_count = normalized_input.shape[0]
    kv_heads = key_value_weight.shape[1]
    query = jnp.dot(normalized_input, w_query, preferred_element_type=jnp.float32).reshape(
        row_count, -1, HEAD_SIZE
    )
    cache_entry_pairs = jnp.dot(
        normalized_input,
        key_value_weight.reshape(key_value_weight.shape[0], -1),
        preferred_element_type=jnp.float32,
    ).reshape(row_count, kv_heads, 2 * HEAD_SIZE)
    position = (lengths + step_index).astype(jnp.float32)[:, None, None]
    rotated_rows = rotate(query, position).astype(jnp.bfloat16)
    fresh_keys = fresh_keys + [
        rotate(cache_entry_pairs[..., :HEAD_SIZE], position).astype(jnp.bfloat16)
    ]
    fresh_values = fresh_values + [cache_entry_pairs[..., HEAD_SIZE:].astype(jnp.bfloat16)]
    grouped_queries = rotated_rows.reshape(row_count, kv_heads, -1, HEAD_SIZE)
    new_keys = jnp.stack(fresh_keys, 1)
    new_values = jnp.stack(fresh_values, 1)
    cached = (
        jnp.einsum(
            "rkgd,rjkd->rkgj",
            grouped_queries,
            cache_pairs[..., :HEAD_SIZE],
            preferred_element_type=jnp.float32,
        )
        * 0.125
    )
    valid = (jnp.arange(cache_pairs.shape[1])[None, :] < lengths[:, None])[:, None, None, :]
    cached = jnp.where(valid, cached, -jnp.inf)
    fresh = (
        jnp.einsum("rkgd,rikd->rkgi", grouped_queries, new_keys, preferred_element_type=jnp.float32)
        * 0.125
    )
    sink_row = head_sink_logits.reshape(kv_heads, -1)[None]
    largest = jnp.maximum(jnp.maximum(jnp.max(cached, axis=-1), jnp.max(fresh, axis=-1)), sink_row)
    cached_exp = jnp.exp(cached - largest[..., None])
    fresh_exp = jnp.exp(fresh - largest[..., None])
    denominator = (
        jnp.sum(cached_exp, axis=-1) + jnp.sum(fresh_exp, axis=-1) + jnp.exp(sink_row - largest)
    )
    cached_probs = (cached_exp / denominator[..., None]).astype(jnp.bfloat16)
    fresh_probs = (fresh_exp / denominator[..., None]).astype(jnp.bfloat16)
    mixed = jnp.einsum(
        "rkgj,rjkd->rkgd",
        cached_probs,
        cache_pairs[..., HEAD_SIZE:],
        preferred_element_type=jnp.float32,
    )
    mixed = mixed + jnp.einsum(
        "rkgi,rikd->rkgd", fresh_probs, new_values, preferred_element_type=jnp.float32
    )
    attention_mix = mixed.reshape(row_count, -1).astype(jnp.bfloat16)
    partial_sum = jnp.dot(attention_mix, w_output, preferred_element_type=jnp.float32)
    return (partial_sum, fresh_keys, fresh_values)


def general_body(
    inputs,
    attention_gain,
    w_query,
    key_value_weight,
    head_sink_logits,
    w_output,
    cache_pairs,
    lengths,
    expert_gain,
    w_gate,
    w_up,
    w_down,
    routes,
    gate_weights,
):
    shards = lax.axis_size(("sec", "tp"))
    shard_index = lax.axis_index(("sec", "tp"))
    experts = lax.axis_size("grp") * w_gate.shape[0]
    group_rows = inputs.shape[1]
    width = inputs.shape[2]
    part_width = width // shards
    chosen = max(TOP, experts // 2)
    capacity = group_rows * TOP // chosen
    slot_total = experts * capacity
    gate_matrix = w_gate[0]
    up_matrix = w_up[0]
    down_matrix = w_down[0]
    fresh_keys = []
    fresh_values = []
    results = []
    for step_index in range(inputs.shape[0]):
        normalized_input = rms_norm(inputs[step_index], attention_gain)
        partial_sum, fresh_keys, fresh_values = attend(
            normalized_input,
            w_query,
            key_value_weight,
            head_sink_logits,
            w_output,
            cache_pairs,
            lengths,
            step_index,
            fresh_keys,
            fresh_values,
        )
        summed = lax.psum(partial_sum[None], ("sec", "tp"))
        middle = (inputs[step_index][None].astype(jnp.float32) + summed).astype(jnp.bfloat16)
        route_rows = routes[step_index][None]
        step_count = middle.shape[0]
        expert_in = rms_norm(middle, expert_gain)
        flat_routes = route_rows.reshape(step_count, group_rows * TOP)
        onehot = (flat_routes[..., None] == jnp.arange(experts)[None, None, :]).astype(jnp.int32)
        earlier = jnp.cumsum(onehot, axis=1) - onehot
        slot_index = jnp.sum(earlier * onehot, axis=-1).reshape(step_count, group_rows, TOP)
        target = route_rows * capacity + slot_index
        placed = target[..., None] == jnp.arange(slot_total)[None, None, None, :]
        dispatch_table = jnp.sum(placed.astype(jnp.int32), axis=2).astype(jnp.bfloat16)
        combine_table = jnp.sum(
            jnp.where(placed, gate_weights[step_index][None][..., None], 0.0), axis=2
        )
        outgoing = jnp.einsum(
            "crm,crd->cmd", dispatch_table, expert_in, preferred_element_type=jnp.float32
        )
        outgoing = outgoing.astype(jnp.bfloat16).reshape(step_count, experts, capacity, width)
        arrived = lax.all_to_all(outgoing, "grp", split_axis=1, concat_axis=1, tiled=True)
        gate_h = jnp.einsum(
            "snpd,dh->snph", arrived, gate_matrix, preferred_element_type=jnp.float32
        )
        up_h = jnp.einsum("snpd,dh->snph", arrived, up_matrix, preferred_element_type=jnp.float32)
        act = ((up_h + 1.0) * gate_h * jax.nn.sigmoid(1.702 * gate_h)).astype(jnp.bfloat16)
        partial_out = jnp.einsum(
            "snph,hd->snpd", act, down_matrix, preferred_element_type=jnp.float32
        )
        reduced = lax.psum_scatter(
            partial_out, ("sec", "tp"), scatter_dimension=3, tiled=True
        ).astype(jnp.bfloat16)
        returned = lax.all_to_all(reduced, "grp", split_axis=1, concat_axis=1, tiled=True)
        returned_rows = returned.reshape(step_count, slot_total, part_width).astype(jnp.float32)
        weighted = jnp.einsum(
            "srm,smd->srd", combine_table, returned_rows, precision=lax.Precision.HIGHEST
        )
        own_middle = lax.dynamic_slice_in_dim(
            middle, shard_index * part_width, part_width, 2
        ).astype(jnp.float32)
        results.append((own_middle + weighted).astype(jnp.bfloat16)[0])
    return jnp.stack(results, 0)


LANES = 384
BASE = 150000.0
MIB = 1 << 20


def shape_of(shape, dtype=jnp.bfloat16):
    return jax.ShapeDtypeStruct(shape, dtype)


def vmem():
    return pl.BlockSpec(memory_space=pltpu.VMEM)


def smem():
    return pl.BlockSpec(memory_space=pltpu.SMEM)


def outside():
    return pl.BlockSpec(memory_space=pltpu.HBM)


def dot_last(left, right):
    return lax.dot_general(left, right, (((1,), (1,)), ((), ())), preferred_element_type=jnp.float32)


def swap(value, axes, mask):
    size = lax.axis_size(axes)
    return lax.ppermute(value, axes, [(i, i ^ mask) for i in range(size)])


def split_width(width):
    cuts = list(range(0, width, 768)) + [width]
    return list(zip(cuts[:-1], cuts[1:]))


def attention_kernel(lengths_ref, sinks_ref, gain_ref, x_hbm, wq_hbm, wkv_hbm, cache_hbm, wo_hbm,
                     other_ref, mine_ref, own_x_ref,
                     x_ref, wq_ref, wkv_ref, cache_ref, wo_ref, xs_ref, turned_ref, mixed_ref, chunk_ref, sems):
    total_rows, width = x_ref.shape
    rows, slots, pair = cache_ref.shape
    steps = total_rows // rows
    heads = wq_ref.shape[1] // HEAD_SIZE
    per_row = heads * steps
    tps = mine_ref.shape[0]
    secs = chunk_ref.shape[0] // tps
    cuts = split_width(width)
    copies = [pltpu.make_async_copy(x_hbm, x_ref, sems.at[0]), pltpu.make_async_copy(wkv_hbm, wkv_ref, sems.at[1])]
    for n, (low, high) in enumerate(cuts):
        part = pl.ds(low, high - low)
        copies.append(pltpu.make_async_copy(wq_hbm.at[part], wq_ref.at[part], sems.at[4 + n]))
    copies.append(pltpu.make_async_copy(cache_hbm, cache_ref, sems.at[2]))
    copies.append(pltpu.make_async_copy(wo_hbm, wo_ref, sems.at[3]))
    for copy in copies:
        copy.start()

    lane = lax.broadcasted_iota(jnp.int32, (total_rows, pair), 1)
    line = lax.broadcasted_iota(jnp.int32, (total_rows, pair), 0)
    position = jnp.zeros((total_rows, pair), jnp.int32)
    for r in range(rows):
        for s in range(steps):
            position = jnp.where(line == s * rows + r, lengths_ref[r] + s, position)
    half = HEAD_SIZE // 2
    counter = jnp.bitwise_and(lane, half - 1).astype(jnp.float32)
    frequency = jnp.exp(counter * jnp.float32(-2.0 / HEAD_SIZE * np.log(BASE)))
    angle = position.astype(jnp.float32) * frequency
    cosine, sine = jnp.cos(angle), jnp.sin(angle)
    low_half = jnp.bitwise_and(lane, HEAD_SIZE - 1) < half
    sine = jnp.where(low_half, -sine, sine)

    def turn(two):
        return two * cosine + jnp.where(low_half, pltpu.roll(two, pair - half, 1), pltpu.roll(two, half, 1)) * sine

    copies[0].wait()
    x = x_ref[...].astype(jnp.float32)
    xs_ref[...] = jnp.concatenate([x, jnp.zeros((total_rows, xs_ref.shape[1] - width), jnp.float32)], axis=1)
    own = (lax.axis_index("sec") * tps + lax.axis_index("tp")) * LANES
    own_x_ref[...] = xs_ref[:, pl.ds(pl.multiple_of(own, LANES), LANES)]
    scale = lax.rsqrt(jnp.mean(x * x, axis=-1, keepdims=True) + 1e-05)
    normed = (x * scale * gain_ref[...]).astype(jnp.bfloat16)
    copies[1].wait()
    pairs = jnp.dot(normed, wkv_ref[...], preferred_element_type=jnp.float32)
    query = None
    for n, (low, high) in enumerate(cuts):
        copies[2 + n].wait()
        term = jnp.dot(normed[:, low:high], wq_ref[low:high, :], preferred_element_type=jnp.float32)
        query = term if query is None else query + term

    is_key = lane < HEAD_SIZE
    fresh = jnp.where(is_key, turn(pairs), pairs).astype(jnp.bfloat16)
    for m in range(heads // 2):
        two = turn(query[:, m * pair:(m + 1) * pair])
        for odd in range(2):
            one = two if odd == 0 else pltpu.roll(two, HEAD_SIZE, 1)
            one = jnp.where(is_key, one, 0.0)
            for s in range(steps):
                slot = (2 * m + odd) * steps + s
                turned_ref[pl.ds(slot, rows, stride=per_row), :] = one[s * rows:(s + 1) * rows]
    turned = turned_ref[...].astype(jnp.bfloat16)

    copies[-2].wait()
    place = lax.broadcasted_iota(jnp.int32, (per_row, slots), 1)
    scores = []
    for r in range(rows):
        score = dot_last(turned[r * per_row:(r + 1) * per_row], cache_ref[r]) * 0.125
        scores.append(jnp.where(place < lengths_ref[r], score, -jnp.inf))
    cached = jnp.concatenate(scores, axis=0)
    row_at = lax.broadcasted_iota(jnp.int32, (rows * per_row, total_rows), 0)
    fresh_at = lax.broadcasted_iota(jnp.int32, (rows * per_row, total_rows), 1)
    seen = (row_at // per_row == fresh_at % rows) & (fresh_at // rows <= row_at % steps)
    new = jnp.where(seen, dot_last(turned, fresh) * 0.125, -jnp.inf)
    head_at = lax.broadcasted_iota(jnp.int32, (rows * per_row, 1), 0) % per_row // steps
    sink = jnp.zeros((rows * per_row, 1), jnp.float32)
    for h in range(heads):
        sink = jnp.where(head_at == h, sinks_ref[h], sink)
    largest = jnp.maximum(jnp.maximum(jnp.max(cached, axis=-1, keepdims=True), jnp.max(new, axis=-1, keepdims=True)), sink)
    cached = jnp.exp(cached - largest)
    new = jnp.exp(new - largest)
    total = jnp.sum(cached, axis=-1, keepdims=True) + jnp.sum(new, axis=-1, keepdims=True) + jnp.exp(sink - largest)
    share = 1.0 / total
    cached = (cached * share).astype(jnp.bfloat16)
    new = (new * share).astype(jnp.bfloat16)
    mixed = []
    for r in range(rows):
        mixed.append(jnp.dot(cached[r * per_row:(r + 1) * per_row], cache_ref[r], preferred_element_type=jnp.float32))
    mixed_ref[...] = jnp.concatenate(mixed, axis=0) + jnp.dot(new, fresh, preferred_element_type=jnp.float32)

    def head(h):
        return jnp.concatenate([mixed_ref[pl.ds(h * steps + s, rows, stride=per_row), :] for s in range(steps)], axis=0)

    mix = jnp.concatenate(
        [jnp.where(is_key, pltpu.roll(head(2 * m), HEAD_SIZE, 1), head(2 * m + 1)) for m in range(heads // 2)], axis=1
    ).astype(jnp.bfloat16)
    copies[-1].wait()
    partial = dot_last(mix, wo_ref[...])
    for c in range(secs * tps):
        low, high = c * LANES, min((c + 1) * LANES, width)
        piece = partial[:, low:high]
        if high - low < LANES:
            piece = jnp.concatenate([piece, jnp.zeros((total_rows, LANES - (high - low)), jnp.float32)], axis=1)
        chunk_ref[c] = piece
    sec = lax.axis_index("sec")
    for t in range(tps):
        other_ref[t] = chunk_ref[(1 - sec) * tps + t].astype(jnp.bfloat16)
        mine_ref[t] = chunk_ref[sec * tps + t]


def attention_partial(flat, gain, w_query, key_value, sinks, w_output, cache, lengths, secs, tps):
    total_rows, width = flat.shape
    rows, slots, pair = cache.shape
    per_row = w_query.shape[1] // HEAD_SIZE * (total_rows // rows)
    shards = secs * tps
    return pl.pallas_call(
        attention_kernel,
        name="attention",
        out_shape=[shape_of((tps, total_rows, LANES)), shape_of((tps, total_rows, LANES), jnp.float32),
                   shape_of((total_rows, LANES), jnp.float32)],
        in_specs=[smem(), smem(), vmem(), outside(), outside(), outside(), outside(), outside()],
        out_specs=[vmem()] * 3,
        scratch_shapes=[
            pltpu.VMEM((total_rows, width), jnp.bfloat16),
            pltpu.VMEM(w_query.shape, jnp.bfloat16),
            pltpu.VMEM(key_value.shape, jnp.bfloat16),
            pltpu.VMEM(cache.shape, jnp.bfloat16),
            pltpu.VMEM((width, w_output.shape[0]), jnp.bfloat16),
            pltpu.VMEM((total_rows, shards * LANES), jnp.float32),
            pltpu.VMEM((rows * per_row, pair), jnp.float32),
            pltpu.VMEM((rows * per_row, pair), jnp.float32),
            pltpu.VMEM((shards, total_rows, LANES), jnp.float32),
            pltpu.SemaphoreType.DMA((4 + len(split_width(width)),)),
        ],
        compiler_params=pltpu.CompilerParams(vmem_limit_bytes=20 * MIB),
    )(lengths, sinks, gain.reshape(1, -1), flat, w_query, key_value, cache, w_output.swapaxes(0, 1))


def add_and_split_kernel(mine_ref, come_ref, *refs, with_extra):
    extra_ref, refs = (refs[0], refs[1:]) if with_extra else (None, refs)
    tp = lax.axis_index("tp")
    own = mine_ref[tp] + come_ref[tp].astype(jnp.float32)
    refs[0][...] = own if extra_ref is None else own + extra_ref[...]
    for m in range(1, mine_ref.shape[0]):
        to = jnp.bitwise_xor(tp, m)
        refs[m][...] = (mine_ref[to] + come_ref[to].astype(jnp.float32)).astype(jnp.bfloat16)


def add_and_split(mine, come, extra=None):
    tps = mine.shape[0]
    shape = mine.shape[1:]
    return pl.pallas_call(
        functools.partial(add_and_split_kernel, with_extra=extra is not None),
        name="add_and_split",
        out_shape=[shape_of(shape, jnp.float32)] + [shape_of(shape)] * (tps - 1),
        in_specs=[vmem()] * (2 if extra is None else 3),
        out_specs=[vmem()] * tps,
        compiler_params=pltpu.CompilerParams(vmem_limit_bytes=8 * MIB),
    )(*((mine, come) if extra is None else (mine, come, extra)))


def sum_kernel(own_ref, *refs):
    come, out = refs[:-1], refs[-1]
    total = own_ref[...]
    for ref in come:
        total = total + ref[...].astype(jnp.float32)
    out[...] = total.astype(jnp.bfloat16).reshape(out.shape)


def sum_pieces(own, come, shape):
    return pl.pallas_call(
        sum_kernel,
        name="sum_pieces",
        out_shape=shape_of(shape),
        in_specs=[vmem()] * (1 + len(come)),
        out_specs=vmem(),
        compiler_params=pltpu.CompilerParams(vmem_limit_bytes=4 * MIB),
    )(own, *come)


def expert_kernel(gain_ref, gate_ref, up_ref, down_ref, *refs, secs, tps):
    pieces, (other_ref, mine_ref, middle_ref, x_ref, chunk_ref, row_ref) = refs[:secs * tps], refs[secs * tps:]
    groups, total_rows, _ = pieces[0].shape
    width = gain_ref.shape[1]
    part = mine_ref.shape[2]
    sec, tp = lax.axis_index("sec"), lax.axis_index("tp")
    for n, piece in enumerate(pieces):
        at = jnp.bitwise_xor(sec, n // tps) * tps + jnp.bitwise_xor(tp, n % tps)
        x_ref[:, pl.ds(pl.multiple_of(at * LANES, LANES), LANES)] = piece[...].reshape(groups * total_rows, LANES)
    x = x_ref[:, :width].astype(jnp.float32)
    for c in range(secs * tps):
        row_ref[c] = x[:total_rows, c * part:(c + 1) * part]
    middle_ref[...] = row_ref[sec * tps + tp]
    scale = lax.rsqrt(jnp.mean(x * x, axis=-1, keepdims=True) + 1e-05)
    expert_in = (x * scale * gain_ref[...]).astype(jnp.bfloat16)
    gate_h = dot_last(expert_in, gate_ref[...])
    up_h = dot_last(expert_in, up_ref[...])
    act = ((up_h + 1.0) * gate_h * jax.nn.sigmoid(1.702 * gate_h)).astype(jnp.bfloat16)
    out = jnp.dot(act, down_ref[...], preferred_element_type=jnp.float32)
    for c in range(secs * tps):
        chunk_ref[c] = out[:, c * part:(c + 1) * part]
    for t in range(tps):
        other_ref[t] = chunk_ref[(1 - sec) * tps + t].astype(jnp.bfloat16)
        mine_ref[t] = chunk_ref[sec * tps + t]


def expert_partial(gain, w_gate, w_up, w_down, pieces, secs, tps):
    groups, total_rows, _ = pieces[0].shape
    width = gain.shape[0]
    shards = secs * tps
    part = width // shards
    lines = groups * total_rows
    return pl.pallas_call(
        functools.partial(expert_kernel, secs=secs, tps=tps),
        name="expert",
        out_shape=[shape_of((tps, lines, part)), shape_of((tps, lines, part), jnp.float32),
                   shape_of((total_rows, part), jnp.float32)],
        in_specs=[vmem()] * (4 + shards),
        out_specs=[vmem()] * 3,
        scratch_shapes=[
            pltpu.VMEM((lines, shards * LANES), jnp.bfloat16),
            pltpu.VMEM((shards, lines, part), jnp.float32),
            pltpu.VMEM((shards, total_rows, part), jnp.float32),
        ],
        compiler_params=pltpu.CompilerParams(vmem_limit_bytes=20 * MIB),
    )(gain.reshape(1, -1), w_gate.swapaxes(0, 1), w_up.swapaxes(0, 1), w_down, *pieces)


def combine_kernel(routes_ref, weights_ref, middle_ref, *refs):
    come, out_ref = refs[:-1], refs[-1]
    steps, rows, part = out_ref.shape
    grp = lax.axis_index("grp")
    corner = lax.broadcasted_iota(jnp.int32, (rows, rows), 0) == lax.broadcasted_iota(jnp.int32, (rows, rows), 1)
    for s in range(steps):
        at = pl.ds(s * rows, rows)
        total = middle_ref[at, :]
        for m, ref in enumerate(come):
            named = routes_ref[s] == jnp.bitwise_xor(grp, m)
            line = jnp.sum(jnp.where(named, weights_ref[s], 0.0), axis=0, keepdims=True)
            column = jnp.sum(jnp.where(corner, line, 0.0), axis=1, keepdims=True)
            total = total + column * ref[at, :].astype(jnp.float32)
        out_ref[s] = total.astype(jnp.bfloat16)


def combine(routes, weights, middle, come, steps):
    total_rows, part = middle.shape
    return pl.pallas_call(
        combine_kernel,
        name="combine",
        out_shape=shape_of((steps, total_rows // steps, part)),
        in_specs=[vmem()] * (3 + len(come)),
        out_specs=vmem(),
        compiler_params=pltpu.CompilerParams(vmem_limit_bytes=4 * MIB),
    )(routes.swapaxes(1, 2), weights.swapaxes(1, 2), middle, *come)


def unstack_kernel(own_ref, *refs, groups):
    come, outs = refs[:-groups], refs[-groups:]
    total = own_ref[...]
    for ref in come:
        total = total + ref[...].astype(jnp.float32)
    lines = outs[0].shape[0]
    for m, out in enumerate(outs):
        out[...] = total[m * lines:(m + 1) * lines].astype(jnp.bfloat16)


def sum_and_unstack(own, come, groups):
    lines, part = own.shape
    return pl.pallas_call(
        functools.partial(unstack_kernel, groups=groups),
        name="sum_and_unstack",
        out_shape=[shape_of((lines // groups, part))] * groups,
        in_specs=[vmem()] * (1 + len(come)),
        out_specs=[vmem()] * groups,
        compiler_params=pltpu.CompilerParams(vmem_limit_bytes=4 * MIB),
    )(own, *come)


def every_expert_body(inputs, attention_gain, w_query, key_value_weight, head_sink_logits, w_output, cache_pairs, lengths,
                      expert_gain, w_gate, w_up, w_down, routes, gate_weights):
    secs, tps, groups = lax.axis_size("sec"), lax.axis_size("tp"), lax.axis_size("grp")
    steps, rows, width = inputs.shape
    flat = inputs.reshape(steps * rows, width)
    other, mine, own_x = attention_partial(flat, attention_gain, w_query, key_value_weight[:, 0], head_sink_logits, w_output,
                                           cache_pairs[:, :, 0], lengths, secs, tps)
    own, *parts = add_and_split(mine, swap(other, "sec", 1), own_x)
    come = [swap(parts[m - 1], "tp", m) for m in reversed(range(1, tps))]
    middle = sum_pieces(own, come, own.shape)
    come = {m: swap(middle, "grp", m) for m in reversed(range(1, groups))}
    stacked = jnp.stack([middle] + [come[m] for m in range(1, groups)])
    come = {m: swap(stacked, "tp", m) for m in reversed(range(1, tps))}
    pieces = [stacked] + [come[m] for m in range(1, tps)]
    pieces = pieces + [swap(piece, "sec", 1) for piece in pieces]
    other, mine, own_middle = expert_partial(expert_gain, w_gate[0], w_up[0], w_down[0], pieces, secs, tps)
    own, *parts = add_and_split(mine, swap(other, "sec", 1))
    come = [swap(parts[m - 1], "tp", m) for m in reversed(range(1, tps))]
    held = sum_and_unstack(own, come, groups)
    come = {m: swap(held[m], "grp", m) for m in reversed(range(1, groups))}
    return combine(routes, gate_weights, own_middle, [held[0]] + [come[m] for m in range(1, groups)], steps)


def body(*args):
    if lax.axis_size("grp") * args[9].shape[0] == TOP and args[9].shape[0] == 1:
        return every_expert_body(*args)
    return general_body(*args)


def solution(mesh):
    placed = (
        P(None, "grp", None),
        P(),
        P(None, ("sec", "tp")),
        P(None, ("sec", "tp"), None),
        P(("sec", "tp")),
        P(("sec", "tp"), None),
        P("grp", None, ("sec", "tp"), None),
        P("grp"),
        P(),
        P("grp", None, ("sec", "tp")),
        P("grp", None, ("sec", "tp")),
        P("grp", ("sec", "tp"), None),
        P(None, "grp", None),
        P(None, "grp", None),
    )
    return jax.shard_map(
        body, mesh=mesh, in_specs=placed, out_specs=P(None, "grp", ("sec", "tp")), check_vma=False
    )
```

```python
import functools

import jax
import jax.numpy as jnp
import numpy as np
from jax import lax
from jax.experimental import pallas as pl
from jax.experimental.pallas import tpu as pltpu
from jax.sharding import PartitionSpec as P

HEAD_SIZE = 64
TOP = 4


def rms_norm(values, scale_row):
    widened = values.astype(jnp.float32)
    scale_factor = lax.rsqrt(jnp.mean(widened * widened, axis=-1, keepdims=True) + 1e-05)
    return (widened * scale_factor * scale_row).astype(jnp.bfloat16)


def rotate(vectors, position):
    half_size = vectors.shape[-1] // 2
    counter = jnp.arange(half_size).astype(jnp.float32)
    frequency = jnp.power(jnp.float32(150000.0), counter * (-2.0 / vectors.shape[-1]))
    angle_table = position * frequency
    cosine = jnp.cos(angle_table)
    sine_table = jnp.sin(angle_table)
    first_half = vectors[..., :half_size]
    second_half = vectors[..., half_size:]
    return jnp.concatenate(
        [
            first_half * cosine - second_half * sine_table,
            first_half * sine_table + second_half * cosine,
        ],
        axis=-1,
    )


def attend(
    normalized_input,
    w_query,
    key_value_weight,
    head_sink_logits,
    w_output,
    cache_pairs,
    lengths,
    step_index,
    fresh_keys,
    fresh_values,
):
    row_count = normalized_input.shape[0]
    kv_heads = key_value_weight.shape[1]
    query = jnp.dot(normalized_input, w_query, preferred_element_type=jnp.float32).reshape(
        row_count, -1, HEAD_SIZE
    )
    cache_entry_pairs = jnp.dot(
        normalized_input,
        key_value_weight.reshape(key_value_weight.shape[0], -1),
        preferred_element_type=jnp.float32,
    ).reshape(row_count, kv_heads, 2 * HEAD_SIZE)
    position = (lengths + step_index).astype(jnp.float32)[:, None, None]
    rotated_rows = rotate(query, position).astype(jnp.bfloat16)
    fresh_keys = fresh_keys + [
        rotate(cache_entry_pairs[..., :HEAD_SIZE], position).astype(jnp.bfloat16)
    ]
    fresh_values = fresh_values + [cache_entry_pairs[..., HEAD_SIZE:].astype(jnp.bfloat16)]
    grouped_queries = rotated_rows.reshape(row_count, kv_heads, -1, HEAD_SIZE)
    new_keys = jnp.stack(fresh_keys, 1)
    new_values = jnp.stack(fresh_values, 1)
    cached = (
        jnp.einsum(
            "rkgd,rjkd->rkgj",
            grouped_queries,
            cache_pairs[..., :HEAD_SIZE],
            preferred_element_type=jnp.float32,
        )
        * 0.125
    )
    valid = (jnp.arange(cache_pairs.shape[1])[None, :] < lengths[:, None])[:, None, None, :]
    cached = jnp.where(valid, cached, -jnp.inf)
    fresh = (
        jnp.einsum("rkgd,rikd->rkgi", grouped_queries, new_keys, preferred_element_type=jnp.float32)
        * 0.125
    )
    sink_row = head_sink_logits.reshape(kv_heads, -1)[None]
    largest = jnp.maximum(jnp.maximum(jnp.max(cached, axis=-1), jnp.max(fresh, axis=-1)), sink_row)
    cached_exp = jnp.exp(cached - largest[..., None])
    fresh_exp = jnp.exp(fresh - largest[..., None])
    denominator = (
        jnp.sum(cached_exp, axis=-1) + jnp.sum(fresh_exp, axis=-1) + jnp.exp(sink_row - largest)
    )
    cached_probs = (cached_exp / denominator[..., None]).astype(jnp.bfloat16)
    fresh_probs = (fresh_exp / denominator[..., None]).astype(jnp.bfloat16)
    mixed = jnp.einsum(
        "rkgj,rjkd->rkgd",
        cached_probs,
        cache_pairs[..., HEAD_SIZE:],
        preferred_element_type=jnp.float32,
    )
    mixed = mixed + jnp.einsum(
        "rkgi,rikd->rkgd", fresh_probs, new_values, preferred_element_type=jnp.float32
    )
    attention_mix = mixed.reshape(row_count, -1).astype(jnp.bfloat16)
    partial_sum = jnp.dot(attention_mix, w_output, preferred_element_type=jnp.float32)
    return (partial_sum, fresh_keys, fresh_values)


def general_body(
    inputs,
    attention_gain,
    w_query,
    key_value_weight,
    head_sink_logits,
    w_output,
    cache_pairs,
    lengths,
    expert_gain,
    w_gate,
    w_up,
    w_down,
    routes,
    gate_weights,
):
    shards = lax.axis_size(("sec", "tp"))
    shard_index = lax.axis_index(("sec", "tp"))
    experts = lax.axis_size("grp") * w_gate.shape[0]
    group_rows = inputs.shape[1]
    width = inputs.shape[2]
    part_width = width // shards
    chosen = max(TOP, experts // 2)
    capacity = group_rows * TOP // chosen
    slot_total = experts * capacity
    gate_matrix = w_gate[0]
    up_matrix = w_up[0]
    down_matrix = w_down[0]
    fresh_keys = []
    fresh_values = []
    results = []
    for step_index in range(inputs.shape[0]):
        normalized_input = rms_norm(inputs[step_index], attention_gain)
        partial_sum, fresh_keys, fresh_values = attend(
            normalized_input,
            w_query,
            key_value_weight,
            head_sink_logits,
            w_output,
            cache_pairs,
            lengths,
            step_index,
            fresh_keys,
            fresh_values,
        )
        summed = lax.psum(partial_sum[None], ("sec", "tp"))
        middle = (inputs[step_index][None].astype(jnp.float32) + summed).astype(jnp.bfloat16)
        route_rows = routes[step_index][None]
        step_count = middle.shape[0]
        expert_in = rms_norm(middle, expert_gain)
        flat_routes = route_rows.reshape(step_count, group_rows * TOP)
        onehot = (flat_routes[..., None] == jnp.arange(experts)[None, None, :]).astype(jnp.int32)
        earlier = jnp.cumsum(onehot, axis=1) - onehot
        slot_index = jnp.sum(earlier * onehot, axis=-1).reshape(step_count, group_rows, TOP)
        target = route_rows * capacity + slot_index
        placed = target[..., None] == jnp.arange(slot_total)[None, None, None, :]
        dispatch_table = jnp.sum(placed.astype(jnp.int32), axis=2).astype(jnp.bfloat16)
        combine_table = jnp.sum(
            jnp.where(placed, gate_weights[step_index][None][..., None], 0.0), axis=2
        )
        outgoing = jnp.einsum(
            "crm,crd->cmd", dispatch_table, expert_in, preferred_element_type=jnp.float32
        )
        outgoing = outgoing.astype(jnp.bfloat16).reshape(step_count, experts, capacity, width)
        arrived = lax.all_to_all(outgoing, "grp", split_axis=1, concat_axis=1, tiled=True)
        gate_h = jnp.einsum(
            "snpd,dh->snph", arrived, gate_matrix, preferred_element_type=jnp.float32
        )
        up_h = jnp.einsum("snpd,dh->snph", arrived, up_matrix, preferred_element_type=jnp.float32)
        act = ((up_h + 1.0) * gate_h * jax.nn.sigmoid(1.702 * gate_h)).astype(jnp.bfloat16)
        partial_out = jnp.einsum(
            "snph,hd->snpd", act, down_matrix, preferred_element_type=jnp.float32
        )
        reduced = lax.psum_scatter(
            partial_out, ("sec", "tp"), scatter_dimension=3, tiled=True
        ).astype(jnp.bfloat16)
        returned = lax.all_to_all(reduced, "grp", split_axis=1, concat_axis=1, tiled=True)
        returned_rows = returned.reshape(step_count, slot_total, part_width).astype(jnp.float32)
        weighted = jnp.einsum(
            "srm,smd->srd", combine_table, returned_rows, precision=lax.Precision.HIGHEST
        )
        own_middle = lax.dynamic_slice_in_dim(
            middle, shard_index * part_width, part_width, 2
        ).astype(jnp.float32)
        results.append((own_middle + weighted).astype(jnp.bfloat16)[0])
    return jnp.stack(results, 0)


LANES = 384
BASE = 150000.0
MIB = 1 << 20


def shape_of(shape, dtype=jnp.bfloat16):
    return jax.ShapeDtypeStruct(shape, dtype)


def vmem():
    return pl.BlockSpec(memory_space=pltpu.VMEM)


def smem():
    return pl.BlockSpec(memory_space=pltpu.SMEM)


def outside():
    return pl.BlockSpec(memory_space=pltpu.HBM)


def dot_last(left, right):
    return lax.dot_general(left, right, (((1,), (1,)), ((), ())), preferred_element_type=jnp.float32)


def swap(value, axes, mask):
    size = lax.axis_size(axes)
    return lax.ppermute(value, axes, [(i, i ^ mask) for i in range(size)])


def swap_by_core(value, axis, first):
    size = lax.axis_size(axis)
    masks = (1, 2) if first else (2, 1)
    pairs = [(s * size + i, s * size + (i ^ masks[s])) for s in range(2) for i in range(size)]
    return lax.ppermute(value, ("sec", axis), pairs)


def masks_by_core():
    sec = lax.axis_index("sec")
    return 1 + sec, 2 - sec


def split_width(width):
    cuts = list(range(0, width, 768)) + [width]
    return list(zip(cuts[:-1], cuts[1:]))


def attention_kernel(lengths_hbm, sinks_hbm, routes_hbm, weights_hbm, gain_hbm, x_hbm, wq_hbm, wkv_hbm, cache_hbm, wo_hbm,
                     other_ref, mine_ref, own_x_ref,
                     lengths_ref, sinks_ref, routes_ref, weights_ref, gain_ref, x_ref, wq_ref, wkv_ref, cache_ref, wo_ref,
                     xs_ref, turned_ref, mixed_ref, chunk_ref, sems):
    total_rows, width = x_ref.shape
    rows, slots, pair = cache_ref.shape
    steps = total_rows // rows
    heads = wq_ref.shape[1] // HEAD_SIZE
    per_row = heads * steps
    tps = mine_ref.shape[0]
    secs = chunk_ref.shape[0] // tps
    cuts = split_width(width)
    small = [(lengths_hbm, lengths_ref), (x_hbm, x_ref), (gain_hbm, gain_ref), (routes_hbm, routes_ref), (weights_hbm, weights_ref),
             (sinks_hbm, sinks_ref)]
    small = [pltpu.make_async_copy(source, target, sems.at[n]) for n, (source, target) in enumerate(small)]
    copies = [pltpu.make_async_copy(wkv_hbm, wkv_ref, sems.at[6])]
    for n, (low, high) in enumerate(cuts):
        part = pl.ds(low, high - low)
        copies.append(pltpu.make_async_copy(wq_hbm.at[part], wq_ref.at[part], sems.at[9 + n]))
    copies.append(pltpu.make_async_copy(cache_hbm, cache_ref, sems.at[7]))
    copies.append(pltpu.make_async_copy(wo_hbm, wo_ref, sems.at[8]))
    for copy in small + copies:
        copy.start()
    small[0].wait()

    lane = lax.broadcasted_iota(jnp.int32, (total_rows, pair), 1)
    line = lax.broadcasted_iota(jnp.int32, (total_rows, pair), 0)
    position = jnp.zeros((total_rows, pair), jnp.int32)
    for r in range(rows):
        for s in range(steps):
            position = jnp.where(line == s * rows + r, lengths_ref[r] + s, position)
    half = HEAD_SIZE // 2
    counter = jnp.bitwise_and(lane, half - 1).astype(jnp.float32)
    frequency = jnp.exp(counter * jnp.float32(-2.0 / HEAD_SIZE * np.log(BASE)))
    angle = position.astype(jnp.float32) * frequency
    cosine, sine = jnp.cos(angle), jnp.sin(angle)
    low_half = jnp.bitwise_and(lane, HEAD_SIZE - 1) < half
    sine = jnp.where(low_half, -sine, sine)

    def turn(two):
        return two * cosine + jnp.where(low_half, pltpu.roll(two, pair - half, 1), pltpu.roll(two, half, 1)) * sine

    for copy in small[1:]:
        copy.wait()
    spare = xs_ref.shape[1] - width
    spare_at = lax.broadcasted_iota(jnp.int32, (rows, spare), 1)
    corner = lax.broadcasted_iota(jnp.int32, (rows, rows), 0) == lax.broadcasted_iota(jnp.int32, (rows, rows), 1)
    tables = []
    for s in range(steps):
        table = jnp.zeros((rows, spare), jnp.float32)
        for e in range(TOP):
            across = jnp.sum(jnp.where(routes_ref[s] == e, weights_ref[s], 0.0), axis=0, keepdims=True)
            column = jnp.sum(jnp.where(corner, across, 0.0), axis=1, keepdims=True)
            high_part = column.astype(jnp.bfloat16).astype(jnp.float32)
            table = jnp.where(spare_at == 2 * e, high_part, jnp.where(spare_at == 2 * e + 1, column - high_part, table))
        tables.append(table)
    x = x_ref[...].astype(jnp.float32)
    xs_ref[...] = jnp.concatenate([x, jnp.concatenate(tables, axis=0)], axis=1)
    own = (lax.axis_index("sec") * tps + lax.axis_index("tp")) * LANES
    own_x_ref[...] = xs_ref[:, pl.ds(pl.multiple_of(own, LANES), LANES)]
    scale = lax.rsqrt(jnp.mean(x * x, axis=-1, keepdims=True) + 1e-05)
    normed = (x * scale * gain_ref[...].reshape(1, width)).astype(jnp.bfloat16)
    copies[0].wait()
    pairs = jnp.dot(normed, wkv_ref[...], preferred_element_type=jnp.float32)
    query = None
    for n, (low, high) in enumerate(cuts):
        copies[1 + n].wait()
        term = jnp.dot(normed[:, low:high], wq_ref[low:high, :], preferred_element_type=jnp.float32)
        query = term if query is None else query + term

    is_key = lane < HEAD_SIZE
    fresh = jnp.where(is_key, turn(pairs), pairs).astype(jnp.bfloat16)
    for m in range(heads // 2):
        two = turn(query[:, m * pair:(m + 1) * pair])
        for odd in range(2):
            one = two if odd == 0 else pltpu.roll(two, HEAD_SIZE, 1)
            one = jnp.where(is_key, one, 0.0)
            for s in range(steps):
                slot = (2 * m + odd) * steps + s
                turned_ref[pl.ds(slot, rows, stride=per_row), :] = one[s * rows:(s + 1) * rows]
    turned = turned_ref[...].astype(jnp.bfloat16)

    copies[-2].wait()
    place = lax.broadcasted_iota(jnp.int32, (per_row, slots), 1)
    scores = []
    for r in range(rows):
        score = dot_last(turned[r * per_row:(r + 1) * per_row], cache_ref[r]) * 0.125
        scores.append(jnp.where(place < lengths_ref[r], score, -jnp.inf))
    cached = jnp.concatenate(scores, axis=0)
    row_at = lax.broadcasted_iota(jnp.int32, (rows * per_row, total_rows), 0)
    fresh_at = lax.broadcasted_iota(jnp.int32, (rows * per_row, total_rows), 1)
    seen = (row_at // per_row == fresh_at % rows) & (fresh_at // rows <= row_at % steps)
    new = jnp.where(seen, dot_last(turned, fresh) * 0.125, -jnp.inf)
    head_at = lax.broadcasted_iota(jnp.int32, (rows * per_row, 1), 0) % per_row // steps
    sink = jnp.zeros((rows * per_row, 1), jnp.float32)
    for h in range(heads):
        sink = jnp.where(head_at == h, sinks_ref[h], sink)
    largest = jnp.maximum(jnp.maximum(jnp.max(cached, axis=-1, keepdims=True), jnp.max(new, axis=-1, keepdims=True)), sink)
    cached = jnp.exp(cached - largest)
    new = jnp.exp(new - largest)
    total = jnp.sum(cached, axis=-1, keepdims=True) + jnp.sum(new, axis=-1, keepdims=True) + jnp.exp(sink - largest)
    share = 1.0 / total
    cached = (cached * share).astype(jnp.bfloat16)
    new = (new * share).astype(jnp.bfloat16)
    mixed = []
    for r in range(rows):
        mixed.append(jnp.dot(cached[r * per_row:(r + 1) * per_row], cache_ref[r], preferred_element_type=jnp.float32))
    mixed_ref[...] = jnp.concatenate(mixed, axis=0) + jnp.dot(new, fresh, preferred_element_type=jnp.float32)

    def head(h):
        return jnp.concatenate([mixed_ref[pl.ds(h * steps + s, rows, stride=per_row), :] for s in range(steps)], axis=0)

    mix = jnp.concatenate(
        [jnp.where(is_key, pltpu.roll(head(2 * m), HEAD_SIZE, 1), head(2 * m + 1)) for m in range(heads // 2)], axis=1
    ).astype(jnp.bfloat16)
    copies[-1].wait()
    partial = dot_last(mix, wo_ref[...])
    for c in range(secs * tps):
        low, high = c * LANES, min((c + 1) * LANES, width)
        piece = partial[:, low:high]
        if high - low < LANES:
            piece = jnp.concatenate([piece, jnp.zeros((total_rows, LANES - (high - low)), jnp.float32)], axis=1)
        chunk_ref[c] = piece
    sec = lax.axis_index("sec")
    for t in range(tps):
        other_ref[t] = chunk_ref[(1 - sec) * tps + t].astype(jnp.bfloat16)
        mine_ref[t] = chunk_ref[sec * tps + t]


def attention_partial(flat, gain, w_query, key_value, sinks, w_output, cache, lengths, routes, weights, secs, tps):
    total_rows, width = flat.shape
    rows, slots, pair = cache.shape
    per_row = w_query.shape[1] // HEAD_SIZE * (total_rows // rows)
    shards = secs * tps
    operands = (lengths, sinks, routes, weights, gain, flat, w_query, key_value, cache, w_output.swapaxes(0, 1))
    return pl.pallas_call(
        attention_kernel,
        name="attention",
        out_shape=[shape_of((tps, total_rows, LANES)), shape_of((tps, total_rows, LANES), jnp.float32),
                   shape_of((total_rows, LANES), jnp.float32)],
        in_specs=[outside()] * len(operands),
        out_specs=[vmem()] * 3,
        scratch_shapes=[
            pltpu.SMEM(lengths.shape, jnp.int32),
            pltpu.SMEM(sinks.shape, jnp.float32),
            pltpu.VMEM(routes.shape, jnp.int32),
            pltpu.VMEM(weights.shape, jnp.float32),
            pltpu.VMEM(gain.shape, jnp.float32),
            pltpu.VMEM((total_rows, width), jnp.bfloat16),
            pltpu.VMEM(w_query.shape, jnp.bfloat16),
            pltpu.VMEM(key_value.shape, jnp.bfloat16),
            pltpu.VMEM(cache.shape, jnp.bfloat16),
            pltpu.VMEM((width, w_output.shape[0]), jnp.bfloat16),
            pltpu.VMEM((total_rows, shards * LANES), jnp.float32),
            pltpu.VMEM((rows * per_row, pair), jnp.float32),
            pltpu.VMEM((rows * per_row, pair), jnp.float32),
            pltpu.VMEM((shards, total_rows, LANES), jnp.float32),
            pltpu.SemaphoreType.DMA((9 + len(split_width(width)),)),
        ],
        compiler_params=pltpu.CompilerParams(vmem_limit_bytes=24 * MIB),
    )(*[pltpu.with_memory_space_constraint(operand, pltpu.HBM) for operand in operands])


def call(kernel, name, outs, *operands, limit=4):
    single = not isinstance(outs, list)
    return pl.pallas_call(
        kernel,
        name=name,
        out_shape=outs,
        in_specs=[vmem()] * len(operands),
        out_specs=vmem() if single else [vmem()] * len(outs),
        compiler_params=pltpu.CompilerParams(vmem_limit_bytes=limit * MIB),
    )(*operands)


def after_core_kernel(mine_ref, come_ref, keep_ref, send_ref):
    tp = lax.axis_index("tp")
    first, second = masks_by_core()
    for n, at in enumerate((tp, jnp.bitwise_xor(tp, second))):
        keep_ref[n] = mine_ref[at] + come_ref[at].astype(jnp.float32)
        at = jnp.bitwise_xor(at, first)
        send_ref[n] = (mine_ref[at] + come_ref[at].astype(jnp.float32)).astype(jnp.bfloat16)


def after_swap_kernel(keep_ref, come_ref, stay_ref, send_ref):
    stay_ref[...] = keep_ref[0] + come_ref[0].astype(jnp.float32)
    send_ref[...] = (keep_ref[1] + come_ref[1].astype(jnp.float32)).astype(jnp.bfloat16)


def sum_kernel(stay_ref, come_ref, extra_ref, out_ref):
    total = stay_ref[...] + come_ref[...].astype(jnp.float32) + extra_ref[...]
    out_ref[...] = total.astype(jnp.bfloat16).reshape(out_ref.shape)


def divide_rows_kernel(stay_ref, come_ref, keep_ref, send_ref):
    total = stay_ref[...] + come_ref[...].astype(jnp.float32)
    lines = keep_ref.shape[1]
    for n in range(2):
        keep_ref[n] = total[n * lines:(n + 1) * lines]
        send_ref[n] = total[(n + 2) * lines:(n + 3) * lines].astype(jnp.bfloat16)


def scatter_shards(mine, come):
    tps, lines, part = mine.shape
    keep, send = call(after_core_kernel, "after_core", [shape_of((2, lines, part), jnp.float32), shape_of((2, lines, part))],
                      mine, come)
    stay, send = call(after_swap_kernel, "after_swap", [shape_of((lines, part), jnp.float32), shape_of((lines, part))],
                      keep, swap_by_core(send, "tp", True))
    return stay, swap_by_core(send, "tp", False)


def expert_kernel(gain_ref, gate_ref, up_ref, down_ref, *refs):
    pieces, (other_ref, mine_ref, middle_ref, x_ref, chunk_ref, row_ref) = refs[:6], refs[6:]
    total_rows = middle_ref.shape[0]
    tps, lines, part = mine_ref.shape
    groups = lines // total_rows
    secs = chunk_ref.shape[0] // tps
    width = down_ref.shape[1]
    sec, tp, grp = lax.axis_index("sec"), lax.axis_index("tp"), lax.axis_index("grp")
    first, second = masks_by_core()

    def place(piece, at, by_other_core):
        at = pl.ds(pl.multiple_of(at * LANES, LANES), LANES)
        for n, m in enumerate((0, 2, 1, 3) if by_other_core else range(groups)):
            x_ref[n * total_rows:(n + 1) * total_rows, at] = piece[m]

    for other in range(secs):
        own, near, far = pieces[3 * other:3 * other + 3]
        base = jnp.bitwise_xor(sec, other) * tps
        one, two = (second, first) if other else (first, second)
        place(own, base + tp, other)
        place(near, base + jnp.bitwise_xor(tp, one), other)
        place(far.at[0], base + jnp.bitwise_xor(tp, two), other)
        place(far.at[1], base + jnp.bitwise_xor(tp, 3), other)
    x = x_ref[:, :width].astype(jnp.float32)
    for c in range(secs * tps):
        row_ref[c] = x[:total_rows, c * part:(c + 1) * part]
    middle_ref[...] = row_ref[sec * tps + tp]
    spare = x_ref[:, width:].astype(jnp.float32)
    spare_at = lax.broadcasted_iota(jnp.int32, spare.shape, 1)
    weight = jnp.sum(jnp.where((spare_at == 2 * grp) | (spare_at == 2 * grp + 1), spare, 0.0), axis=1, keepdims=True)
    scale = lax.rsqrt(jnp.mean(x * x, axis=-1, keepdims=True) + 1e-05)
    expert_in = (x * scale * gain_ref[...]).astype(jnp.bfloat16)
    gate_h = dot_last(expert_in, gate_ref[...])
    up_h = dot_last(expert_in, up_ref[...])
    act = ((up_h + 1.0) * gate_h * jax.nn.sigmoid(1.702 * gate_h)).astype(jnp.bfloat16)
    out = jnp.dot(act, down_ref[...], preferred_element_type=jnp.float32) * weight
    for c in range(secs * tps):
        chunk_ref[c] = out[:, c * part:(c + 1) * part]
    for t in range(tps):
        for n, m in enumerate((0, 2, 1, 3)):
            other_ref[t, n * total_rows:(n + 1) * total_rows] = chunk_ref[
                (1 - sec) * tps + t, m * total_rows:(m + 1) * total_rows].astype(jnp.bfloat16)
        mine_ref[t] = chunk_ref[sec * tps + t]


def expert_partial(gain, w_gate, w_up, w_down, pieces, secs, tps):
    groups, total_rows, _ = pieces[0].shape
    width = gain.shape[0]
    shards = secs * tps
    part = width // shards
    lines = groups * total_rows
    return pl.pallas_call(
        expert_kernel,
        name="expert",
        out_shape=[shape_of((tps, lines, part)), shape_of((tps, lines, part), jnp.float32),
                   shape_of((total_rows, part), jnp.float32)],
        in_specs=[vmem()] * (4 + len(pieces)),
        out_specs=[vmem()] * 3,
        scratch_shapes=[
            pltpu.VMEM((lines, shards * LANES), jnp.bfloat16),
            pltpu.VMEM((shards, lines, part), jnp.float32),
            pltpu.VMEM((shards, total_rows, part), jnp.float32),
        ],
        compiler_params=pltpu.CompilerParams(vmem_limit_bytes=20 * MIB),
    )(gain.reshape(1, -1), w_gate.swapaxes(0, 1), w_up.swapaxes(0, 1), w_down, *pieces)


def every_expert_body(inputs, attention_gain, w_query, key_value_weight, head_sink_logits, w_output, cache_pairs, lengths,
                      expert_gain, w_gate, w_up, w_down, routes, gate_weights):
    secs, tps, groups = lax.axis_size("sec"), lax.axis_size("tp"), lax.axis_size("grp")
    steps, rows, width = inputs.shape
    flat = inputs.reshape(steps * rows, width)
    other, mine, own_x = attention_partial(
        flat, attention_gain, w_query, key_value_weight[:, 0], head_sink_logits, w_output, cache_pairs[:, :, 0], lengths,
        routes.swapaxes(1, 2), gate_weights.swapaxes(1, 2), secs, tps)
    stay, come = scatter_shards(mine, swap(other, "sec", 1))
    middle = call(sum_kernel, "sum", shape_of((1, steps * rows, LANES)), stay, come, own_x)
    middle = jnp.concatenate([middle, swap_by_core(middle, "grp", True)], axis=0)
    own = jnp.concatenate([middle, swap_by_core(middle, "grp", False)], axis=0)
    near = swap_by_core(own, "tp", True)
    own_other = swap(own, "sec", 1)
    far = swap_by_core(jnp.stack([own, near]), "tp", False)
    near_other = swap(near, "sec", 1)
    far_other = swap(far, "sec", 1)
    pieces = [own, near, far, own_other, near_other, far_other]
    other, mine, own_middle = expert_partial(expert_gain, w_gate[0], w_up[0], w_down[0], pieces, secs, tps)
    stay, come = scatter_shards(mine, swap(other, "sec", 1))
    lines, part = steps * rows, stay.shape[1]
    keep, send = call(divide_rows_kernel, "divide_rows", [shape_of((2, lines, part), jnp.float32), shape_of((2, lines, part))],
                      stay, come)
    stay, send = call(after_swap_kernel, "after_swap", [shape_of((lines, part), jnp.float32), shape_of((lines, part))],
                      keep, swap_by_core(send, "grp", False))
    return call(sum_kernel, "combine", shape_of((steps, rows, part)), stay, swap_by_core(send, "grp", True), own_middle)


def body(*args):
    sizes = lax.axis_size("sec"), lax.axis_size("tp"), lax.axis_size("grp"), args[9].shape[0]
    if sizes == (2, 4, TOP, 1):
        return every_expert_body(*args)
    return general_body(*args)


def solution(mesh):
    placed = (
        P(None, "grp", None),
        P(),
        P(None, ("sec", "tp")),
        P(None, ("sec", "tp"), None),
        P(("sec", "tp")),
        P(("sec", "tp"), None),
        P("grp", None, ("sec", "tp"), None),
        P("grp"),
        P(),
        P("grp", None, ("sec", "tp")),
        P("grp", None, ("sec", "tp")),
        P("grp", ("sec", "tp"), None),
        P(None, "grp", None),
        P(None, "grp", None),
    )
    return jax.shard_map(
        body, mesh=mesh, in_specs=placed, out_specs=P(None, "grp", ("sec", "tp")), check_vma=False
    )
```

```python
import functools

import jax
import jax.numpy as jnp
import numpy as np
from jax import lax
from jax.experimental import pallas as pl
from jax.experimental.pallas import tpu as pltpu
from jax.sharding import PartitionSpec as P

HEAD_SIZE = 64
TOP = 4


def rms_norm(values, scale_row):
    widened = values.astype(jnp.float32)
    scale_factor = lax.rsqrt(jnp.mean(widened * widened, axis=-1, keepdims=True) + 1e-05)
    return (widened * scale_factor * scale_row).astype(jnp.bfloat16)


def rotate(vectors, position):
    half_size = vectors.shape[-1] // 2
    counter = jnp.arange(half_size).astype(jnp.float32)
    frequency = jnp.power(jnp.float32(150000.0), counter * (-2.0 / vectors.shape[-1]))
    angle_table = position * frequency
    cosine = jnp.cos(angle_table)
    sine_table = jnp.sin(angle_table)
    first_half = vectors[..., :half_size]
    second_half = vectors[..., half_size:]
    return jnp.concatenate(
        [
            first_half * cosine - second_half * sine_table,
            first_half * sine_table + second_half * cosine,
        ],
        axis=-1,
    )


def attend(
    normalized_input,
    w_query,
    key_value_weight,
    head_sink_logits,
    w_output,
    cache_pairs,
    lengths,
    step_index,
    fresh_keys,
    fresh_values,
):
    row_count = normalized_input.shape[0]
    kv_heads = key_value_weight.shape[1]
    query = jnp.dot(normalized_input, w_query, preferred_element_type=jnp.float32).reshape(
        row_count, -1, HEAD_SIZE
    )
    cache_entry_pairs = jnp.dot(
        normalized_input,
        key_value_weight.reshape(key_value_weight.shape[0], -1),
        preferred_element_type=jnp.float32,
    ).reshape(row_count, kv_heads, 2 * HEAD_SIZE)
    position = (lengths + step_index).astype(jnp.float32)[:, None, None]
    rotated_rows = rotate(query, position).astype(jnp.bfloat16)
    fresh_keys = fresh_keys + [
        rotate(cache_entry_pairs[..., :HEAD_SIZE], position).astype(jnp.bfloat16)
    ]
    fresh_values = fresh_values + [cache_entry_pairs[..., HEAD_SIZE:].astype(jnp.bfloat16)]
    grouped_queries = rotated_rows.reshape(row_count, kv_heads, -1, HEAD_SIZE)
    new_keys = jnp.stack(fresh_keys, 1)
    new_values = jnp.stack(fresh_values, 1)
    cached = (
        jnp.einsum(
            "rkgd,rjkd->rkgj",
            grouped_queries,
            cache_pairs[..., :HEAD_SIZE],
            preferred_element_type=jnp.float32,
        )
        * 0.125
    )
    valid = (jnp.arange(cache_pairs.shape[1])[None, :] < lengths[:, None])[:, None, None, :]
    cached = jnp.where(valid, cached, -jnp.inf)
    fresh = (
        jnp.einsum("rkgd,rikd->rkgi", grouped_queries, new_keys, preferred_element_type=jnp.float32)
        * 0.125
    )
    sink_row = head_sink_logits.reshape(kv_heads, -1)[None]
    largest = jnp.maximum(jnp.maximum(jnp.max(cached, axis=-1), jnp.max(fresh, axis=-1)), sink_row)
    cached_exp = jnp.exp(cached - largest[..., None])
    fresh_exp = jnp.exp(fresh - largest[..., None])
    denominator = (
        jnp.sum(cached_exp, axis=-1) + jnp.sum(fresh_exp, axis=-1) + jnp.exp(sink_row - largest)
    )
    cached_probs = (cached_exp / denominator[..., None]).astype(jnp.bfloat16)
    fresh_probs = (fresh_exp / denominator[..., None]).astype(jnp.bfloat16)
    mixed = jnp.einsum(
        "rkgj,rjkd->rkgd",
        cached_probs,
        cache_pairs[..., HEAD_SIZE:],
        preferred_element_type=jnp.float32,
    )
    mixed = mixed + jnp.einsum(
        "rkgi,rikd->rkgd", fresh_probs, new_values, preferred_element_type=jnp.float32
    )
    attention_mix = mixed.reshape(row_count, -1).astype(jnp.bfloat16)
    partial_sum = jnp.dot(attention_mix, w_output, preferred_element_type=jnp.float32)
    return (partial_sum, fresh_keys, fresh_values)


def general_body(
    inputs,
    attention_gain,
    w_query,
    key_value_weight,
    head_sink_logits,
    w_output,
    cache_pairs,
    lengths,
    expert_gain,
    w_gate,
    w_up,
    w_down,
    routes,
    gate_weights,
):
    shards = lax.axis_size(("sec", "tp"))
    shard_index = lax.axis_index(("sec", "tp"))
    experts = lax.axis_size("grp") * w_gate.shape[0]
    group_rows = inputs.shape[1]
    width = inputs.shape[2]
    part_width = width // shards
    chosen = max(TOP, experts // 2)
    capacity = group_rows * TOP // chosen
    slot_total = experts * capacity
    gate_matrix = w_gate[0]
    up_matrix = w_up[0]
    down_matrix = w_down[0]
    fresh_keys = []
    fresh_values = []
    results = []
    for step_index in range(inputs.shape[0]):
        normalized_input = rms_norm(inputs[step_index], attention_gain)
        partial_sum, fresh_keys, fresh_values = attend(
            normalized_input,
            w_query,
            key_value_weight,
            head_sink_logits,
            w_output,
            cache_pairs,
            lengths,
            step_index,
            fresh_keys,
            fresh_values,
        )
        summed = lax.psum(partial_sum[None], ("sec", "tp"))
        middle = (inputs[step_index][None].astype(jnp.float32) + summed).astype(jnp.bfloat16)
        route_rows = routes[step_index][None]
        step_count = middle.shape[0]
        expert_in = rms_norm(middle, expert_gain)
        flat_routes = route_rows.reshape(step_count, group_rows * TOP)
        onehot = (flat_routes[..., None] == jnp.arange(experts)[None, None, :]).astype(jnp.int32)
        earlier = jnp.cumsum(onehot, axis=1) - onehot
        slot_index = jnp.sum(earlier * onehot, axis=-1).reshape(step_count, group_rows, TOP)
        target = route_rows * capacity + slot_index
        placed = target[..., None] == jnp.arange(slot_total)[None, None, None, :]
        dispatch_table = jnp.sum(placed.astype(jnp.int32), axis=2).astype(jnp.bfloat16)
        combine_table = jnp.sum(
            jnp.where(placed, gate_weights[step_index][None][..., None], 0.0), axis=2
        )
        outgoing = jnp.einsum(
            "crm,crd->cmd", dispatch_table, expert_in, preferred_element_type=jnp.float32
        )
        outgoing = outgoing.astype(jnp.bfloat16).reshape(step_count, experts, capacity, width)
        arrived = lax.all_to_all(outgoing, "grp", split_axis=1, concat_axis=1, tiled=True)
        gate_h = jnp.einsum(
            "snpd,dh->snph", arrived, gate_matrix, preferred_element_type=jnp.float32
        )
        up_h = jnp.einsum("snpd,dh->snph", arrived, up_matrix, preferred_element_type=jnp.float32)
        act = ((up_h + 1.0) * gate_h * jax.nn.sigmoid(1.702 * gate_h)).astype(jnp.bfloat16)
        partial_out = jnp.einsum(
            "snph,hd->snpd", act, down_matrix, preferred_element_type=jnp.float32
        )
        reduced = lax.psum_scatter(
            partial_out, ("sec", "tp"), scatter_dimension=3, tiled=True
        ).astype(jnp.bfloat16)
        returned = lax.all_to_all(reduced, "grp", split_axis=1, concat_axis=1, tiled=True)
        returned_rows = returned.reshape(step_count, slot_total, part_width).astype(jnp.float32)
        weighted = jnp.einsum(
            "srm,smd->srd", combine_table, returned_rows, precision=lax.Precision.HIGHEST
        )
        own_middle = lax.dynamic_slice_in_dim(
            middle, shard_index * part_width, part_width, 2
        ).astype(jnp.float32)
        results.append((own_middle + weighted).astype(jnp.bfloat16)[0])
    return jnp.stack(results, 0)


LANES = 384
BASE = 150000.0
MIB = 1 << 20


def shape_of(shape, dtype=jnp.bfloat16):
    return jax.ShapeDtypeStruct(shape, dtype)


def vmem():
    return pl.BlockSpec(memory_space=pltpu.VMEM)


def smem():
    return pl.BlockSpec(memory_space=pltpu.SMEM)


def outside():
    return pl.BlockSpec(memory_space=pltpu.HBM)


def dot_last(left, right):
    return lax.dot_general(left, right, (((1,), (1,)), ((), ())), preferred_element_type=jnp.float32)


def swap(value, axes, mask):
    size = lax.axis_size(axes)
    return lax.ppermute(value, axes, [(i, i ^ mask) for i in range(size)])


def split_width(width):
    cuts = list(range(0, width, 768)) + [width]
    return list(zip(cuts[:-1], cuts[1:]))


def attention_kernel(lengths_hbm, sinks_hbm, routes_hbm, weights_hbm, gain_hbm, x_hbm, wq_hbm, wkv_hbm, cache_hbm, wo_hbm,
                     other_ref, mine_ref, own_x_ref,
                     lengths_ref, sinks_ref, routes_ref, weights_ref, gain_ref, x_ref, wq_ref, wkv_ref, cache_ref, wo_ref,
                     xs_ref, turned_ref, mixed_ref, chunk_ref, sems):
    total_rows, width = x_ref.shape
    rows, slots, pair = cache_ref.shape
    steps = total_rows // rows
    heads = wq_ref.shape[1] // HEAD_SIZE
    per_row = heads * steps
    tps = mine_ref.shape[0]
    secs = chunk_ref.shape[0] // tps
    cuts = split_width(width)
    small = [(lengths_hbm, lengths_ref), (x_hbm, x_ref), (gain_hbm, gain_ref), (routes_hbm, routes_ref), (weights_hbm, weights_ref),
             (sinks_hbm, sinks_ref)]
    small = [pltpu.make_async_copy(source, target, sems.at[n]) for n, (source, target) in enumerate(small)]
    copies = [pltpu.make_async_copy(wkv_hbm, wkv_ref, sems.at[6])]
    for n, (low, high) in enumerate(cuts):
        part = pl.ds(low, high - low)
        copies.append(pltpu.make_async_copy(wq_hbm.at[part], wq_ref.at[part], sems.at[9 + n]))
    copies.append(pltpu.make_async_copy(cache_hbm, cache_ref, sems.at[7]))
    copies.append(pltpu.make_async_copy(wo_hbm, wo_ref, sems.at[8]))
    for copy in small + copies:
        copy.start()
    small[0].wait()

    lane = lax.broadcasted_iota(jnp.int32, (total_rows, pair), 1)
    line = lax.broadcasted_iota(jnp.int32, (total_rows, pair), 0)
    position = jnp.zeros((total_rows, pair), jnp.int32)
    for r in range(rows):
        for s in range(steps):
            position = jnp.where(line == s * rows + r, lengths_ref[r] + s, position)
    half = HEAD_SIZE // 2
    counter = jnp.bitwise_and(lane, half - 1).astype(jnp.float32)
    frequency = jnp.exp(counter * jnp.float32(-2.0 / HEAD_SIZE * np.log(BASE)))
    angle = position.astype(jnp.float32) * frequency
    cosine, sine = jnp.cos(angle), jnp.sin(angle)
    low_half = jnp.bitwise_and(lane, HEAD_SIZE - 1) < half
    sine = jnp.where(low_half, -sine, sine)

    def turn(two):
        return two * cosine + jnp.where(low_half, pltpu.roll(two, pair - half, 1), pltpu.roll(two, half, 1)) * sine

    for copy in small[1:]:
        copy.wait()
    spare = xs_ref.shape[1] - width
    spare_at = lax.broadcasted_iota(jnp.int32, (rows, spare), 1)
    corner = lax.broadcasted_iota(jnp.int32, (rows, rows), 0) == lax.broadcasted_iota(jnp.int32, (rows, rows), 1)
    tables = []
    for s in range(steps):
        table = jnp.zeros((rows, spare), jnp.float32)
        for e in range(TOP):
            across = jnp.sum(jnp.where(routes_ref[s] == e, weights_ref[s], 0.0), axis=0, keepdims=True)
            column = jnp.sum(jnp.where(corner, across, 0.0), axis=1, keepdims=True)
            high_part = column.astype(jnp.bfloat16).astype(jnp.float32)
            table = jnp.where(spare_at == 2 * e, high_part, jnp.where(spare_at == 2 * e + 1, column - high_part, table))
        tables.append(table)
    x = x_ref[...].astype(jnp.float32)
    xs_ref[...] = jnp.concatenate([x, jnp.concatenate(tables, axis=0)], axis=1)
    own = (lax.axis_index("sec") * tps + lax.axis_index("tp")) * LANES
    own_x_ref[...] = xs_ref[:, pl.ds(pl.multiple_of(own, LANES), LANES)]
    scale = lax.rsqrt(jnp.mean(x * x, axis=-1, keepdims=True) + 1e-05)
    normed = (x * scale * gain_ref[...].reshape(1, width)).astype(jnp.bfloat16)
    copies[0].wait()
    pairs = jnp.dot(normed, wkv_ref[...], preferred_element_type=jnp.float32)
    query = None
    for n, (low, high) in enumerate(cuts):
        copies[1 + n].wait()
        term = jnp.dot(normed[:, low:high], wq_ref[low:high, :], preferred_element_type=jnp.float32)
        query = term if query is None else query + term

    is_key = lane < HEAD_SIZE
    fresh = jnp.where(is_key, turn(pairs), pairs).astype(jnp.bfloat16)
    for m in range(heads // 2):
        two = turn(query[:, m * pair:(m + 1) * pair])
        for odd in range(2):
            one = two if odd == 0 else pltpu.roll(two, HEAD_SIZE, 1)
            one = jnp.where(is_key, one, 0.0)
            for s in range(steps):
                slot = (2 * m + odd) * steps + s
                turned_ref[pl.ds(slot, rows, stride=per_row), :] = one[s * rows:(s + 1) * rows]
    turned = turned_ref[...].astype(jnp.bfloat16)

    copies[-2].wait()
    place = lax.broadcasted_iota(jnp.int32, (per_row, slots), 1)
    scores = []
    for r in range(rows):
        score = dot_last(turned[r * per_row:(r + 1) * per_row], cache_ref[r]) * 0.125
        scores.append(jnp.where(place < lengths_ref[r], score, -jnp.inf))
    cached = jnp.concatenate(scores, axis=0)
    row_at = lax.broadcasted_iota(jnp.int32, (rows * per_row, total_rows), 0)
    fresh_at = lax.broadcasted_iota(jnp.int32, (rows * per_row, total_rows), 1)
    seen = (row_at // per_row == fresh_at % rows) & (fresh_at // rows <= row_at % steps)
    new = jnp.where(seen, dot_last(turned, fresh) * 0.125, -jnp.inf)
    head_at = lax.broadcasted_iota(jnp.int32, (rows * per_row, 1), 0) % per_row // steps
    sink = jnp.zeros((rows * per_row, 1), jnp.float32)
    for h in range(heads):
        sink = jnp.where(head_at == h, sinks_ref[h], sink)
    largest = jnp.maximum(jnp.maximum(jnp.max(cached, axis=-1, keepdims=True), jnp.max(new, axis=-1, keepdims=True)), sink)
    cached = jnp.exp(cached - largest)
    new = jnp.exp(new - largest)
    total = jnp.sum(cached, axis=-1, keepdims=True) + jnp.sum(new, axis=-1, keepdims=True) + jnp.exp(sink - largest)
    share = 1.0 / total
    cached = (cached * share).astype(jnp.bfloat16)
    new = (new * share).astype(jnp.bfloat16)
    mixed = []
    for r in range(rows):
        mixed.append(jnp.dot(cached[r * per_row:(r + 1) * per_row], cache_ref[r], preferred_element_type=jnp.float32))
    mixed_ref[...] = jnp.concatenate(mixed, axis=0) + jnp.dot(new, fresh, preferred_element_type=jnp.float32)

    def head(h):
        return jnp.concatenate([mixed_ref[pl.ds(h * steps + s, rows, stride=per_row), :] for s in range(steps)], axis=0)

    mix = jnp.concatenate(
        [jnp.where(is_key, pltpu.roll(head(2 * m), HEAD_SIZE, 1), head(2 * m + 1)) for m in range(heads // 2)], axis=1
    ).astype(jnp.bfloat16)
    copies[-1].wait()
    partial = dot_last(mix, wo_ref[...])
    for c in range(secs * tps):
        low, high = c * LANES, min((c + 1) * LANES, width)
        piece = partial[:, low:high]
        if high - low < LANES:
            piece = jnp.concatenate([piece, jnp.zeros((total_rows, LANES - (high - low)), jnp.float32)], axis=1)
        chunk_ref[c] = piece
    sec = lax.axis_index("sec")
    for t in range(tps):
        other_ref[t] = chunk_ref[(1 - sec) * tps + t].astype(jnp.bfloat16)
        mine_ref[t] = chunk_ref[sec * tps + t]


def attention_partial(flat, gain, w_query, key_value, sinks, w_output, cache, lengths, routes, weights, secs, tps):
    total_rows, width = flat.shape
    rows, slots, pair = cache.shape
    per_row = w_query.shape[1] // HEAD_SIZE * (total_rows // rows)
    shards = secs * tps
    operands = (lengths, sinks, routes, weights, gain, flat, w_query, key_value, cache, w_output.swapaxes(0, 1))
    return pl.pallas_call(
        attention_kernel,
        name="attention",
        out_shape=[shape_of((tps, total_rows, LANES)), shape_of((tps, total_rows, LANES), jnp.float32),
                   shape_of((total_rows, LANES), jnp.float32)],
        in_specs=[outside()] * len(operands),
        out_specs=[vmem()] * 3,
        scratch_shapes=[
            pltpu.SMEM(lengths.shape, jnp.int32),
            pltpu.SMEM(sinks.shape, jnp.float32),
            pltpu.VMEM(routes.shape, jnp.int32),
            pltpu.VMEM(weights.shape, jnp.float32),
            pltpu.VMEM(gain.shape, jnp.float32),
            pltpu.VMEM((total_rows, width), jnp.bfloat16),
            pltpu.VMEM(w_query.shape, jnp.bfloat16),
            pltpu.VMEM(key_value.shape, jnp.bfloat16),
            pltpu.VMEM(cache.shape, jnp.bfloat16),
            pltpu.VMEM((width, w_output.shape[0]), jnp.bfloat16),
            pltpu.VMEM((total_rows, shards * LANES), jnp.float32),
            pltpu.VMEM((rows * per_row, pair), jnp.float32),
            pltpu.VMEM((rows * per_row, pair), jnp.float32),
            pltpu.VMEM((shards, total_rows, LANES), jnp.float32),
            pltpu.SemaphoreType.DMA((9 + len(split_width(width)),)),
        ],
        compiler_params=pltpu.CompilerParams(vmem_limit_bytes=24 * MIB),
    )(*[pltpu.with_memory_space_constraint(operand, pltpu.HBM) for operand in operands])


def call(kernel, name, outs, *operands, limit=4):
    single = not isinstance(outs, list)
    return pl.pallas_call(
        kernel,
        name=name,
        out_shape=outs,
        in_specs=[vmem()] * len(operands),
        out_specs=vmem() if single else [vmem()] * len(outs),
        compiler_params=pltpu.CompilerParams(vmem_limit_bytes=limit * MIB),
    )(*operands)


def after_core_kernel(mine_ref, come_ref, own_ref, *send_refs):
    tp = lax.axis_index("tp")
    own_ref[...] = mine_ref[tp] + come_ref[tp].astype(jnp.float32)
    for n, ref in enumerate(send_refs):
        to = jnp.bitwise_xor(tp, n + 1)
        ref[...] = (mine_ref[to] + come_ref[to].astype(jnp.float32)).astype(jnp.bfloat16)


def add_all(*refs):
    total = refs[0][...]
    for ref in refs[1:]:
        total = total + ref[...].astype(jnp.float32)
    return total


def sum_kernel(*refs):
    refs[-1][...] = add_all(*refs[:-1]).astype(jnp.bfloat16).reshape(refs[-1].shape)


def divide_rows_kernel(*refs, groups):
    total = add_all(*refs[:-groups])
    outs = refs[-groups:]
    lines = outs[0].shape[0]
    for n, out in enumerate(outs):
        out[...] = total[n * lines:(n + 1) * lines].astype(out.dtype)


def swap_all(parts, axis):
    count = len(parts)
    come = {m: swap(parts[m - 1], axis, m) for m in reversed(range(1, count + 1))}
    return [come[m] for m in range(1, count + 1)]


def scatter_shards(mine, come):
    tps, lines, part = mine.shape
    own, *parts = call(after_core_kernel, "after_core", [shape_of((lines, part), jnp.float32)] + [shape_of((lines, part))] * (tps - 1),
                       mine, come)
    return [own] + swap_all(parts, "tp")


def expert_kernel(gain_ref, gate_ref, up_ref, down_ref, *refs):
    pieces, (other_ref, mine_ref, middle_ref, x_ref, chunk_ref, row_ref) = refs[:-6], refs[-6:]
    total_rows = middle_ref.shape[0]
    tps, lines, part = mine_ref.shape
    secs = chunk_ref.shape[0] // tps
    width = down_ref.shape[1]
    sec, tp, grp = lax.axis_index("sec"), lax.axis_index("tp"), lax.axis_index("grp")
    for n, piece in enumerate(pieces):
        at = jnp.bitwise_xor(sec, n // tps) * tps + jnp.bitwise_xor(tp, n % tps)
        x_ref[:, pl.ds(pl.multiple_of(at * LANES, LANES), LANES)] = piece[...].reshape(lines, LANES)
    x = x_ref[:, :width].astype(jnp.float32)
    for c in range(secs * tps):
        row_ref[c] = x[:total_rows, c * part:(c + 1) * part]
    middle_ref[...] = row_ref[sec * tps + tp]
    spare = x_ref[:, width:].astype(jnp.float32)
    spare_at = lax.broadcasted_iota(jnp.int32, spare.shape, 1)
    weight = jnp.sum(jnp.where((spare_at == 2 * grp) | (spare_at == 2 * grp + 1), spare, 0.0), axis=1, keepdims=True)
    scale = lax.rsqrt(jnp.mean(x * x, axis=-1, keepdims=True) + 1e-05)
    expert_in = (x * scale * gain_ref[...]).astype(jnp.bfloat16)
    gate_h = dot_last(expert_in, gate_ref[...])
    up_h = dot_last(expert_in, up_ref[...])
    act = ((up_h + 1.0) * gate_h * jax.nn.sigmoid(1.702 * gate_h)).astype(jnp.bfloat16)
    out = jnp.dot(act, down_ref[...], preferred_element_type=jnp.float32) * weight
    for c in range(secs * tps):
        chunk_ref[c] = out[:, c * part:(c + 1) * part]
    for t in range(tps):
        other_ref[t] = chunk_ref[(1 - sec) * tps + t].astype(jnp.bfloat16)
        mine_ref[t] = chunk_ref[sec * tps + t]


def expert_partial(gain, w_gate, w_up, w_down, pieces, secs, tps):
    groups, total_rows, _ = pieces[0].shape
    width = gain.shape[0]
    shards = secs * tps
    part = width // shards
    lines = groups * total_rows
    return pl.pallas_call(
        expert_kernel,
        name="expert",
        out_shape=[shape_of((tps, lines, part)), shape_of((tps, lines, part), jnp.float32),
                   shape_of((total_rows, part), jnp.float32)],
        in_specs=[vmem()] * (4 + len(pieces)),
        out_specs=[vmem()] * 3,
        scratch_shapes=[
            pltpu.VMEM((lines, shards * LANES), jnp.bfloat16),
            pltpu.VMEM((shards, lines, part), jnp.float32),
            pltpu.VMEM((shards, total_rows, part), jnp.float32),
        ],
        compiler_params=pltpu.CompilerParams(vmem_limit_bytes=20 * MIB),
    )(gain.reshape(1, -1), w_gate.swapaxes(0, 1), w_up.swapaxes(0, 1), w_down, *pieces)


def every_expert_body(inputs, attention_gain, w_query, key_value_weight, head_sink_logits, w_output, cache_pairs, lengths,
                      expert_gain, w_gate, w_up, w_down, routes, gate_weights):
    secs, tps, groups = lax.axis_size("sec"), lax.axis_size("tp"), lax.axis_size("grp")
    steps, rows, width = inputs.shape
    flat = inputs.reshape(steps * rows, width)
    other, mine, own_x = attention_partial(
        flat, attention_gain, w_query, key_value_weight[:, 0], head_sink_logits, w_output, cache_pairs[:, :, 0], lengths,
        routes.swapaxes(1, 2), gate_weights.swapaxes(1, 2), secs, tps)
    terms = scatter_shards(mine, swap(other, "sec", 1))
    middle = call(sum_kernel, "sum", shape_of((steps * rows, LANES)), *terms, own_x)
    stacked = jnp.stack([middle] + swap_all([middle] * (groups - 1), "grp"))
    pieces = [stacked] + swap_all([stacked] * (tps - 1), "tp")
    pieces = pieces + [swap(piece, "sec", 1) for piece in pieces]
    other, mine, own_middle = expert_partial(expert_gain, w_gate[0], w_up[0], w_down[0], pieces, secs, tps)
    terms = scatter_shards(mine, swap(other, "sec", 1))
    lines, part = steps * rows, terms[0].shape[1]
    own, *parts = call(functools.partial(divide_rows_kernel, groups=groups), "divide_rows",
                       [shape_of((lines, part), jnp.float32)] + [shape_of((lines, part))] * (groups - 1), *terms)
    return call(sum_kernel, "combine", shape_of((steps, rows, part)), own, *swap_all(parts, "grp"), own_middle)


def body(*args):
    sizes = lax.axis_size("sec"), lax.axis_size("tp"), lax.axis_size("grp"), args[9].shape[0]
    if sizes == (2, 4, TOP, 1):
        return every_expert_body(*args)
    return general_body(*args)


def solution(mesh):
    placed = (
        P(None, "grp", None),
        P(),
        P(None, ("sec", "tp")),
        P(None, ("sec", "tp"), None),
        P(("sec", "tp")),
        P(("sec", "tp"), None),
        P("grp", None, ("sec", "tp"), None),
        P("grp"),
        P(),
        P("grp", None, ("sec", "tp")),
        P("grp", None, ("sec", "tp")),
        P("grp", ("sec", "tp"), None),
        P(None, "grp", None),
        P(None, "grp", None),
    )
    return jax.shard_map(
        body, mesh=mesh, in_specs=placed, out_specs=P(None, "grp", ("sec", "tp")), check_vma=False
    )
```

```python
import functools

import jax
import jax.numpy as jnp
import numpy as np
from jax import lax
from jax.experimental import pallas as pl
from jax.experimental.pallas import tpu as pltpu
from jax.sharding import PartitionSpec as P

HEAD_SIZE = 64
TOP = 4


def rms_norm(values, scale_row):
    widened = values.astype(jnp.float32)
    scale_factor = lax.rsqrt(jnp.mean(widened * widened, axis=-1, keepdims=True) + 1e-05)
    return (widened * scale_factor * scale_row).astype(jnp.bfloat16)


def rotate(vectors, position):
    half_size = vectors.shape[-1] // 2
    counter = jnp.arange(half_size).astype(jnp.float32)
    frequency = jnp.power(jnp.float32(150000.0), counter * (-2.0 / vectors.shape[-1]))
    angle_table = position * frequency
    cosine = jnp.cos(angle_table)
    sine_table = jnp.sin(angle_table)
    first_half = vectors[..., :half_size]
    second_half = vectors[..., half_size:]
    return jnp.concatenate(
        [
            first_half * cosine - second_half * sine_table,
            first_half * sine_table + second_half * cosine,
        ],
        axis=-1,
    )


def attend(
    normalized_input,
    w_query,
    key_value_weight,
    head_sink_logits,
    w_output,
    cache_pairs,
    lengths,
    step_index,
    fresh_keys,
    fresh_values,
):
    row_count = normalized_input.shape[0]
    kv_heads = key_value_weight.shape[1]
    query = jnp.dot(normalized_input, w_query, preferred_element_type=jnp.float32).reshape(
        row_count, -1, HEAD_SIZE
    )
    cache_entry_pairs = jnp.dot(
        normalized_input,
        key_value_weight.reshape(key_value_weight.shape[0], -1),
        preferred_element_type=jnp.float32,
    ).reshape(row_count, kv_heads, 2 * HEAD_SIZE)
    position = (lengths + step_index).astype(jnp.float32)[:, None, None]
    rotated_rows = rotate(query, position).astype(jnp.bfloat16)
    fresh_keys = fresh_keys + [
        rotate(cache_entry_pairs[..., :HEAD_SIZE], position).astype(jnp.bfloat16)
    ]
    fresh_values = fresh_values + [cache_entry_pairs[..., HEAD_SIZE:].astype(jnp.bfloat16)]
    grouped_queries = rotated_rows.reshape(row_count, kv_heads, -1, HEAD_SIZE)
    new_keys = jnp.stack(fresh_keys, 1)
    new_values = jnp.stack(fresh_values, 1)
    cached = (
        jnp.einsum(
            "rkgd,rjkd->rkgj",
            grouped_queries,
            cache_pairs[..., :HEAD_SIZE],
            preferred_element_type=jnp.float32,
        )
        * 0.125
    )
    valid = (jnp.arange(cache_pairs.shape[1])[None, :] < lengths[:, None])[:, None, None, :]
    cached = jnp.where(valid, cached, -jnp.inf)
    fresh = (
        jnp.einsum("rkgd,rikd->rkgi", grouped_queries, new_keys, preferred_element_type=jnp.float32)
        * 0.125
    )
    sink_row = head_sink_logits.reshape(kv_heads, -1)[None]
    largest = jnp.maximum(jnp.maximum(jnp.max(cached, axis=-1), jnp.max(fresh, axis=-1)), sink_row)
    cached_exp = jnp.exp(cached - largest[..., None])
    fresh_exp = jnp.exp(fresh - largest[..., None])
    denominator = (
        jnp.sum(cached_exp, axis=-1) + jnp.sum(fresh_exp, axis=-1) + jnp.exp(sink_row - largest)
    )
    cached_probs = (cached_exp / denominator[..., None]).astype(jnp.bfloat16)
    fresh_probs = (fresh_exp / denominator[..., None]).astype(jnp.bfloat16)
    mixed = jnp.einsum(
        "rkgj,rjkd->rkgd",
        cached_probs,
        cache_pairs[..., HEAD_SIZE:],
        preferred_element_type=jnp.float32,
    )
    mixed = mixed + jnp.einsum(
        "rkgi,rikd->rkgd", fresh_probs, new_values, preferred_element_type=jnp.float32
    )
    attention_mix = mixed.reshape(row_count, -1).astype(jnp.bfloat16)
    partial_sum = jnp.dot(attention_mix, w_output, preferred_element_type=jnp.float32)
    return (partial_sum, fresh_keys, fresh_values)


def general_body(
    inputs,
    attention_gain,
    w_query,
    key_value_weight,
    head_sink_logits,
    w_output,
    cache_pairs,
    lengths,
    expert_gain,
    w_gate,
    w_up,
    w_down,
    routes,
    gate_weights,
):
    shards = lax.axis_size(("sec", "tp"))
    shard_index = lax.axis_index(("sec", "tp"))
    experts = lax.axis_size("grp") * w_gate.shape[0]
    group_rows = inputs.shape[1]
    width = inputs.shape[2]
    part_width = width // shards
    chosen = max(TOP, experts // 2)
    capacity = group_rows * TOP // chosen
    slot_total = experts * capacity
    gate_matrix = w_gate[0]
    up_matrix = w_up[0]
    down_matrix = w_down[0]
    fresh_keys = []
    fresh_values = []
    results = []
    for step_index in range(inputs.shape[0]):
        normalized_input = rms_norm(inputs[step_index], attention_gain)
        partial_sum, fresh_keys, fresh_values = attend(
            normalized_input,
            w_query,
            key_value_weight,
            head_sink_logits,
            w_output,
            cache_pairs,
            lengths,
            step_index,
            fresh_keys,
            fresh_values,
        )
        summed = lax.psum(partial_sum[None], ("sec", "tp"))
        middle = (inputs[step_index][None].astype(jnp.float32) + summed).astype(jnp.bfloat16)
        route_rows = routes[step_index][None]
        step_count = middle.shape[0]
        expert_in = rms_norm(middle, expert_gain)
        flat_routes = route_rows.reshape(step_count, group_rows * TOP)
        onehot = (flat_routes[..., None] == jnp.arange(experts)[None, None, :]).astype(jnp.int32)
        earlier = jnp.cumsum(onehot, axis=1) - onehot
        slot_index = jnp.sum(earlier * onehot, axis=-1).reshape(step_count, group_rows, TOP)
        target = route_rows * capacity + slot_index
        placed = target[..., None] == jnp.arange(slot_total)[None, None, None, :]
        dispatch_table = jnp.sum(placed.astype(jnp.int32), axis=2).astype(jnp.bfloat16)
        combine_table = jnp.sum(
            jnp.where(placed, gate_weights[step_index][None][..., None], 0.0), axis=2
        )
        outgoing = jnp.einsum(
            "crm,crd->cmd", dispatch_table, expert_in, preferred_element_type=jnp.float32
        )
        outgoing = outgoing.astype(jnp.bfloat16).reshape(step_count, experts, capacity, width)
        arrived = lax.all_to_all(outgoing, "grp", split_axis=1, concat_axis=1, tiled=True)
        gate_h = jnp.einsum(
            "snpd,dh->snph", arrived, gate_matrix, preferred_element_type=jnp.float32
        )
        up_h = jnp.einsum("snpd,dh->snph", arrived, up_matrix, preferred_element_type=jnp.float32)
        act = ((up_h + 1.0) * gate_h * jax.nn.sigmoid(1.702 * gate_h)).astype(jnp.bfloat16)
        partial_out = jnp.einsum(
            "snph,hd->snpd", act, down_matrix, preferred_element_type=jnp.float32
        )
        reduced = lax.psum_scatter(
            partial_out, ("sec", "tp"), scatter_dimension=3, tiled=True
        ).astype(jnp.bfloat16)
        returned = lax.all_to_all(reduced, "grp", split_axis=1, concat_axis=1, tiled=True)
        returned_rows = returned.reshape(step_count, slot_total, part_width).astype(jnp.float32)
        weighted = jnp.einsum(
            "srm,smd->srd", combine_table, returned_rows, precision=lax.Precision.HIGHEST
        )
        own_middle = lax.dynamic_slice_in_dim(
            middle, shard_index * part_width, part_width, 2
        ).astype(jnp.float32)
        results.append((own_middle + weighted).astype(jnp.bfloat16)[0])
    return jnp.stack(results, 0)


LANES = 384
BASE = 150000.0
MIB = 1 << 20


def shape_of(shape, dtype=jnp.bfloat16):
    return jax.ShapeDtypeStruct(shape, dtype)


def vmem():
    return pl.BlockSpec(memory_space=pltpu.VMEM)


def smem():
    return pl.BlockSpec(memory_space=pltpu.SMEM)


def outside():
    return pl.BlockSpec(memory_space=pltpu.HBM)


def dot_last(left, right):
    return lax.dot_general(left, right, (((1,), (1,)), ((), ())), preferred_element_type=jnp.float32)


def swap(value, axes, mask):
    size = lax.axis_size(axes)
    return lax.ppermute(value, axes, [(i, i ^ mask) for i in range(size)])


def split_width(width):
    cuts = list(range(0, width, 768)) + [width]
    return list(zip(cuts[:-1], cuts[1:]))


def attention_kernel(lengths_hbm, sinks_hbm, routes_hbm, weights_hbm, gain_hbm, x_hbm, wq_hbm, wkv_hbm, cache_hbm, wo_hbm,
                     parts_ref, own_x_ref,
                     lengths_ref, sinks_ref, routes_ref, weights_ref, gain_ref, x_ref, wq_ref, wkv_ref, cache_ref, wo_ref,
                     xs_ref, turned_ref, mixed_ref, sems):
    total_rows, width = x_ref.shape
    rows, slots, pair = cache_ref.shape
    steps = total_rows // rows
    heads = wq_ref.shape[1] // HEAD_SIZE
    per_row = heads * steps
    shards = parts_ref.shape[0]
    tps = lax.axis_size("tp")
    cuts = split_width(width)
    small = [(lengths_hbm, lengths_ref), (x_hbm, x_ref), (gain_hbm, gain_ref), (routes_hbm, routes_ref), (weights_hbm, weights_ref),
             (sinks_hbm, sinks_ref)]
    small = [pltpu.make_async_copy(source, target, sems.at[n]) for n, (source, target) in enumerate(small)]
    copies = [pltpu.make_async_copy(wkv_hbm, wkv_ref, sems.at[6])]
    for n, (low, high) in enumerate(cuts):
        part = pl.ds(low, high - low)
        copies.append(pltpu.make_async_copy(wq_hbm.at[part], wq_ref.at[part], sems.at[9 + n]))
    copies.append(pltpu.make_async_copy(cache_hbm, cache_ref, sems.at[7]))
    copies.append(pltpu.make_async_copy(wo_hbm, wo_ref, sems.at[8]))
    for copy in small + copies:
        copy.start()
    small[0].wait()

    lane = lax.broadcasted_iota(jnp.int32, (total_rows, pair), 1)
    line = lax.broadcasted_iota(jnp.int32, (total_rows, pair), 0)
    position = jnp.zeros((total_rows, pair), jnp.int32)
    for r in range(rows):
        for s in range(steps):
            position = jnp.where(line == s * rows + r, lengths_ref[r] + s, position)
    half = HEAD_SIZE // 2
    counter = jnp.bitwise_and(lane, half - 1).astype(jnp.float32)
    frequency = jnp.exp(counter * jnp.float32(-2.0 / HEAD_SIZE * np.log(BASE)))
    angle = position.astype(jnp.float32) * frequency
    cosine, sine = jnp.cos(angle), jnp.sin(angle)
    low_half = jnp.bitwise_and(lane, HEAD_SIZE - 1) < half
    sine = jnp.where(low_half, -sine, sine)

    def turn(two):
        return two * cosine + jnp.where(low_half, pltpu.roll(two, pair - half, 1), pltpu.roll(two, half, 1)) * sine

    for copy in small[1:]:
        copy.wait()
    spare = xs_ref.shape[1] - width
    spare_at = lax.broadcasted_iota(jnp.int32, (rows, spare), 1)
    corner = lax.broadcasted_iota(jnp.int32, (rows, rows), 0) == lax.broadcasted_iota(jnp.int32, (rows, rows), 1)
    tables = []
    for s in range(steps):
        table = jnp.zeros((rows, spare), jnp.float32)
        for e in range(TOP):
            across = jnp.sum(jnp.where(routes_ref[s] == e, weights_ref[s], 0.0), axis=0, keepdims=True)
            column = jnp.sum(jnp.where(corner, across, 0.0), axis=1, keepdims=True)
            high_part = column.astype(jnp.bfloat16).astype(jnp.float32)
            table = jnp.where(spare_at == 2 * e, high_part, jnp.where(spare_at == 2 * e + 1, column - high_part, table))
        tables.append(table)
    x = x_ref[...].astype(jnp.float32)
    xs_ref[...] = jnp.concatenate([x, jnp.concatenate(tables, axis=0)], axis=1)
    own = (lax.axis_index("sec") * tps + lax.axis_index("tp")) * LANES
    own_x_ref[...] = xs_ref[:, pl.ds(pl.multiple_of(own, LANES), LANES)]
    scale = lax.rsqrt(jnp.mean(x * x, axis=-1, keepdims=True) + 1e-05)
    normed = (x * scale * gain_ref[...].reshape(1, width)).astype(jnp.bfloat16)
    copies[0].wait()
    pairs = jnp.dot(normed, wkv_ref[...], preferred_element_type=jnp.float32)
    query = None
    for n, (low, high) in enumerate(cuts):
        copies[1 + n].wait()
        term = jnp.dot(normed[:, low:high], wq_ref[low:high, :], preferred_element_type=jnp.float32)
        query = term if query is None else query + term

    is_key = lane < HEAD_SIZE
    fresh = jnp.where(is_key, turn(pairs), pairs).astype(jnp.bfloat16)
    for m in range(heads // 2):
        two = turn(query[:, m * pair:(m + 1) * pair])
        for odd in range(2):
            one = two if odd == 0 else pltpu.roll(two, HEAD_SIZE, 1)
            one = jnp.where(is_key, one, 0.0)
            for s in range(steps):
                slot = (2 * m + odd) * steps + s
                turned_ref[pl.ds(slot, rows, stride=per_row), :] = one[s * rows:(s + 1) * rows]
    turned = turned_ref[...].astype(jnp.bfloat16)

    copies[-2].wait()
    place = lax.broadcasted_iota(jnp.int32, (per_row, slots), 1)
    scores = []
    for r in range(rows):
        score = dot_last(turned[r * per_row:(r + 1) * per_row], cache_ref[r]) * 0.125
        scores.append(jnp.where(place < lengths_ref[r], score, -jnp.inf))
    cached = jnp.concatenate(scores, axis=0)
    row_at = lax.broadcasted_iota(jnp.int32, (rows * per_row, total_rows), 0)
    fresh_at = lax.broadcasted_iota(jnp.int32, (rows * per_row, total_rows), 1)
    seen = (row_at // per_row == fresh_at % rows) & (fresh_at // rows <= row_at % steps)
    new = jnp.where(seen, dot_last(turned, fresh) * 0.125, -jnp.inf)
    head_at = lax.broadcasted_iota(jnp.int32, (rows * per_row, 1), 0) % per_row // steps
    sink = jnp.zeros((rows * per_row, 1), jnp.float32)
    for h in range(heads):
        sink = jnp.where(head_at == h, sinks_ref[h], sink)
    largest = jnp.maximum(jnp.maximum(jnp.max(cached, axis=-1, keepdims=True), jnp.max(new, axis=-1, keepdims=True)), sink)
    cached = jnp.exp(cached - largest)
    new = jnp.exp(new - largest)
    total = jnp.sum(cached, axis=-1, keepdims=True) + jnp.sum(new, axis=-1, keepdims=True) + jnp.exp(sink - largest)
    share = 1.0 / total
    cached = (cached * share).astype(jnp.bfloat16)
    new = (new * share).astype(jnp.bfloat16)
    mixed = []
    for r in range(rows):
        mixed.append(jnp.dot(cached[r * per_row:(r + 1) * per_row], cache_ref[r], preferred_element_type=jnp.float32))
    mixed_ref[...] = jnp.concatenate(mixed, axis=0) + jnp.dot(new, fresh, preferred_element_type=jnp.float32)

    def head(h):
        return jnp.concatenate([mixed_ref[pl.ds(h * steps + s, rows, stride=per_row), :] for s in range(steps)], axis=0)

    mix = jnp.concatenate(
        [jnp.where(is_key, pltpu.roll(head(2 * m), HEAD_SIZE, 1), head(2 * m + 1)) for m in range(heads // 2)], axis=1
    ).astype(jnp.bfloat16)
    copies[-1].wait()
    partial = dot_last(mix, wo_ref[...])
    for c in range(shards):
        low, high = c * LANES, min((c + 1) * LANES, width)
        piece = partial[:, low:high]
        if high - low < LANES:
            piece = jnp.concatenate([piece, jnp.zeros((total_rows, LANES - (high - low)), jnp.float32)], axis=1)
        parts_ref[c] = piece.astype(jnp.bfloat16)


def attention_partial(flat, gain, w_query, key_value, sinks, w_output, cache, lengths, routes, weights, secs, tps):
    total_rows, width = flat.shape
    rows, slots, pair = cache.shape
    per_row = w_query.shape[1] // HEAD_SIZE * (total_rows // rows)
    shards = secs * tps
    operands = (lengths, sinks, routes, weights, gain, flat, w_query, key_value, cache, w_output.swapaxes(0, 1))
    return pl.pallas_call(
        attention_kernel,
        name="attention",
        out_shape=[shape_of((shards, total_rows, LANES)), shape_of((total_rows, LANES), jnp.float32)],
        in_specs=[outside()] * len(operands),
        out_specs=[vmem()] * 2,
        scratch_shapes=[
            pltpu.SMEM(lengths.shape, jnp.int32),
            pltpu.SMEM(sinks.shape, jnp.float32),
            pltpu.VMEM(routes.shape, jnp.int32),
            pltpu.VMEM(weights.shape, jnp.float32),
            pltpu.VMEM(gain.shape, jnp.float32),
            pltpu.VMEM((total_rows, width), jnp.bfloat16),
            pltpu.VMEM(w_query.shape, jnp.bfloat16),
            pltpu.VMEM(key_value.shape, jnp.bfloat16),
            pltpu.VMEM(cache.shape, jnp.bfloat16),
            pltpu.VMEM((width, w_output.shape[0]), jnp.bfloat16),
            pltpu.VMEM((total_rows, shards * LANES), jnp.float32),
            pltpu.VMEM((rows * per_row, pair), jnp.float32),
            pltpu.VMEM((rows * per_row, pair), jnp.float32),
            pltpu.SemaphoreType.DMA((9 + len(split_width(width)),)),
        ],
        compiler_params=pltpu.CompilerParams(vmem_limit_bytes=24 * MIB),
    )(*[pltpu.with_memory_space_constraint(operand, pltpu.HBM) for operand in operands])


def call(kernel, name, outs, *operands, limit=4):
    single = not isinstance(outs, list)
    return pl.pallas_call(
        kernel,
        name=name,
        out_shape=outs,
        in_specs=[vmem()] * len(operands),
        out_specs=vmem() if single else [vmem()] * len(outs),
        compiler_params=pltpu.CompilerParams(vmem_limit_bytes=limit * MIB),
    )(*operands)


def after_core_kernel(mine_ref, come_ref, own_ref, *send_refs):
    tp = lax.axis_index("tp")
    own_ref[...] = mine_ref[tp] + come_ref[tp].astype(jnp.float32)
    for n, ref in enumerate(send_refs):
        to = jnp.bitwise_xor(tp, n + 1)
        ref[...] = (mine_ref[to] + come_ref[to].astype(jnp.float32)).astype(jnp.bfloat16)


def add_all(*refs):
    total = refs[0][...]
    for ref in refs[1:]:
        total = total + ref[...].astype(jnp.float32)
    return total


def sum_parts_kernel(parts_ref, own_ref, out_ref):
    total = own_ref[...]
    for n in range(parts_ref.shape[0]):
        total = total + parts_ref[n].astype(jnp.float32)
    out_ref[...] = total.astype(jnp.bfloat16)


def sum_kernel(*refs):
    refs[-1][...] = add_all(*refs[:-1]).astype(jnp.bfloat16).reshape(refs[-1].shape)


def divide_rows_kernel(*refs, groups):
    total = add_all(*refs[:-groups])
    outs = refs[-groups:]
    lines = outs[0].shape[0]
    for n, out in enumerate(outs):
        out[...] = total[n * lines:(n + 1) * lines].astype(out.dtype)


def swap_all(parts, axis):
    count = len(parts)
    come = {m: swap(parts[m - 1], axis, m) for m in reversed(range(1, count + 1))}
    return [come[m] for m in range(1, count + 1)]


def scatter_shards(mine, come):
    tps, lines, part = mine.shape
    own, *parts = call(after_core_kernel, "after_core", [shape_of((lines, part), jnp.float32)] + [shape_of((lines, part))] * (tps - 1),
                       mine, come)
    return [own] + swap_all(parts, "tp")


def expert_kernel(gain_ref, gate_ref, up_ref, down_ref, *refs):
    pieces, (other_ref, mine_ref, middle_ref, x_ref, chunk_ref, row_ref) = refs[:-6], refs[-6:]
    total_rows = middle_ref.shape[0]
    tps, lines, part = mine_ref.shape
    secs = chunk_ref.shape[0] // tps
    width = down_ref.shape[1]
    sec, tp, grp = lax.axis_index("sec"), lax.axis_index("tp"), lax.axis_index("grp")
    for n, piece in enumerate(pieces):
        at = jnp.bitwise_xor(sec, n // tps) * tps + jnp.bitwise_xor(tp, n % tps)
        x_ref[:, pl.ds(pl.multiple_of(at * LANES, LANES), LANES)] = piece[...].reshape(lines, LANES)
    x = x_ref[:, :width].astype(jnp.float32)
    for c in range(secs * tps):
        row_ref[c] = x[:total_rows, c * part:(c + 1) * part]
    middle_ref[...] = row_ref[sec * tps + tp]
    spare = x_ref[:, width:].astype(jnp.float32)
    spare_at = lax.broadcasted_iota(jnp.int32, spare.shape, 1)
    weight = jnp.sum(jnp.where((spare_at == 2 * grp) | (spare_at == 2 * grp + 1), spare, 0.0), axis=1, keepdims=True)
    scale = lax.rsqrt(jnp.mean(x * x, axis=-1, keepdims=True) + 1e-05)
    expert_in = (x * scale * gain_ref[...]).astype(jnp.bfloat16)
    gate_h = dot_last(expert_in, gate_ref[...])
    up_h = dot_last(expert_in, up_ref[...])
    act = ((up_h + 1.0) * gate_h * jax.nn.sigmoid(1.702 * gate_h)).astype(jnp.bfloat16)
    out = jnp.dot(act, down_ref[...], preferred_element_type=jnp.float32) * weight
    for c in range(secs * tps):
        chunk_ref[c] = out[:, c * part:(c + 1) * part]
    for t in range(tps):
        other_ref[t] = chunk_ref[(1 - sec) * tps + t].astype(jnp.bfloat16)
        mine_ref[t] = chunk_ref[sec * tps + t]


def expert_partial(gain, w_gate, w_up, w_down, pieces, secs, tps):
    groups, total_rows, _ = pieces[0].shape
    width = gain.shape[0]
    shards = secs * tps
    part = width // shards
    lines = groups * total_rows
    return pl.pallas_call(
        expert_kernel,
        name="expert",
        out_shape=[shape_of((tps, lines, part)), shape_of((tps, lines, part), jnp.float32),
                   shape_of((total_rows, part), jnp.float32)],
        in_specs=[vmem()] * (4 + len(pieces)),
        out_specs=[vmem()] * 3,
        scratch_shapes=[
            pltpu.VMEM((lines, shards * LANES), jnp.bfloat16),
            pltpu.VMEM((shards, lines, part), jnp.float32),
            pltpu.VMEM((shards, total_rows, part), jnp.float32),
        ],
        compiler_params=pltpu.CompilerParams(vmem_limit_bytes=20 * MIB),
    )(gain.reshape(1, -1), w_gate.swapaxes(0, 1), w_up.swapaxes(0, 1), w_down, *pieces)


def every_expert_body(inputs, attention_gain, w_query, key_value_weight, head_sink_logits, w_output, cache_pairs, lengths,
                      expert_gain, w_gate, w_up, w_down, routes, gate_weights):
    secs, tps, groups = lax.axis_size("sec"), lax.axis_size("tp"), lax.axis_size("grp")
    steps, rows, width = inputs.shape
    flat = inputs.reshape(steps * rows, width)
    parts, own_x = attention_partial(
        flat, attention_gain, w_query, key_value_weight[:, 0], head_sink_logits, w_output, cache_pairs[:, :, 0], lengths,
        routes.swapaxes(1, 2), gate_weights.swapaxes(1, 2), secs, tps)
    parts = lax.all_to_all(parts, ("sec", "tp"), 0, 0, tiled=True)
    middle = call(sum_parts_kernel, "sum_parts", shape_of((steps * rows, LANES)), parts, own_x)
    stacked = jnp.stack([middle] + swap_all([middle] * (groups - 1), "grp"))
    pieces = [stacked] + swap_all([stacked] * (tps - 1), "tp")
    pieces = pieces + [swap(piece, "sec", 1) for piece in pieces]
    other, mine, own_middle = expert_partial(expert_gain, w_gate[0], w_up[0], w_down[0], pieces, secs, tps)
    terms = scatter_shards(mine, swap(other, "sec", 1))
    lines, part = steps * rows, terms[0].shape[1]
    own, *parts = call(functools.partial(divide_rows_kernel, groups=groups), "divide_rows",
                       [shape_of((lines, part), jnp.float32)] + [shape_of((lines, part))] * (groups - 1), *terms)
    return call(sum_kernel, "combine", shape_of((steps, rows, part)), own, *swap_all(parts, "grp"), own_middle)


def body(*args):
    sizes = lax.axis_size("sec"), lax.axis_size("tp"), lax.axis_size("grp"), args[9].shape[0]
    if sizes == (2, 4, TOP, 1):
        return every_expert_body(*args)
    return general_body(*args)


def solution(mesh):
    placed = (
        P(None, "grp", None),
        P(),
        P(None, ("sec", "tp")),
        P(None, ("sec", "tp"), None),
        P(("sec", "tp")),
        P(("sec", "tp"), None),
        P("grp", None, ("sec", "tp"), None),
        P("grp"),
        P(),
        P("grp", None, ("sec", "tp")),
        P("grp", None, ("sec", "tp")),
        P("grp", ("sec", "tp"), None),
        P(None, "grp", None),
        P(None, "grp", None),
    )
    return jax.shard_map(
        body, mesh=mesh, in_specs=placed, out_specs=P(None, "grp", ("sec", "tp")), check_vma=False
    )
```

```python
import functools
import math

import jax
import jax.numpy as jnp
import numpy as np
from jax import lax
from jax.experimental import pallas as pl
from jax.experimental.pallas import tpu as pltpu
from jax.sharding import PartitionSpec as P

HEAD_SIZE = 64
TOP = 4


def rms_norm(values, scale_row):
    widened = values.astype(jnp.float32)
    scale_factor = lax.rsqrt(jnp.mean(widened * widened, axis=-1, keepdims=True) + 1e-05)
    return (widened * scale_factor * scale_row).astype(jnp.bfloat16)


def rotate(vectors, position):
    half_size = vectors.shape[-1] // 2
    counter = jnp.arange(half_size).astype(jnp.float32)
    frequency = jnp.power(jnp.float32(150000.0), counter * (-2.0 / vectors.shape[-1]))
    angle_table = position * frequency
    cosine = jnp.cos(angle_table)
    sine_table = jnp.sin(angle_table)
    first_half = vectors[..., :half_size]
    second_half = vectors[..., half_size:]
    return jnp.concatenate(
        [
            first_half * cosine - second_half * sine_table,
            first_half * sine_table + second_half * cosine,
        ],
        axis=-1,
    )


def attend(
    normalized_input,
    w_query,
    key_value_weight,
    head_sink_logits,
    w_output,
    cache_pairs,
    lengths,
    step_index,
    fresh_keys,
    fresh_values,
):
    row_count = normalized_input.shape[0]
    kv_heads = key_value_weight.shape[1]
    query = jnp.dot(normalized_input, w_query, preferred_element_type=jnp.float32).reshape(
        row_count, -1, HEAD_SIZE
    )
    cache_entry_pairs = jnp.dot(
        normalized_input,
        key_value_weight.reshape(key_value_weight.shape[0], -1),
        preferred_element_type=jnp.float32,
    ).reshape(row_count, kv_heads, 2 * HEAD_SIZE)
    position = (lengths + step_index).astype(jnp.float32)[:, None, None]
    rotated_rows = rotate(query, position).astype(jnp.bfloat16)
    fresh_keys = fresh_keys + [
        rotate(cache_entry_pairs[..., :HEAD_SIZE], position).astype(jnp.bfloat16)
    ]
    fresh_values = fresh_values + [cache_entry_pairs[..., HEAD_SIZE:].astype(jnp.bfloat16)]
    grouped_queries = rotated_rows.reshape(row_count, kv_heads, -1, HEAD_SIZE)
    new_keys = jnp.stack(fresh_keys, 1)
    new_values = jnp.stack(fresh_values, 1)
    cached = (
        jnp.einsum(
            "rkgd,rjkd->rkgj",
            grouped_queries,
            cache_pairs[..., :HEAD_SIZE],
            preferred_element_type=jnp.float32,
        )
        * 0.125
    )
    valid = (jnp.arange(cache_pairs.shape[1])[None, :] < lengths[:, None])[:, None, None, :]
    cached = jnp.where(valid, cached, -jnp.inf)
    fresh = (
        jnp.einsum("rkgd,rikd->rkgi", grouped_queries, new_keys, preferred_element_type=jnp.float32)
        * 0.125
    )
    sink_row = head_sink_logits.reshape(kv_heads, -1)[None]
    largest = jnp.maximum(jnp.maximum(jnp.max(cached, axis=-1), jnp.max(fresh, axis=-1)), sink_row)
    cached_exp = jnp.exp(cached - largest[..., None])
    fresh_exp = jnp.exp(fresh - largest[..., None])
    denominator = (
        jnp.sum(cached_exp, axis=-1) + jnp.sum(fresh_exp, axis=-1) + jnp.exp(sink_row - largest)
    )
    cached_probs = (cached_exp / denominator[..., None]).astype(jnp.bfloat16)
    fresh_probs = (fresh_exp / denominator[..., None]).astype(jnp.bfloat16)
    mixed = jnp.einsum(
        "rkgj,rjkd->rkgd",
        cached_probs,
        cache_pairs[..., HEAD_SIZE:],
        preferred_element_type=jnp.float32,
    )
    mixed = mixed + jnp.einsum(
        "rkgi,rikd->rkgd", fresh_probs, new_values, preferred_element_type=jnp.float32
    )
    attention_mix = mixed.reshape(row_count, -1).astype(jnp.bfloat16)
    partial_sum = jnp.dot(attention_mix, w_output, preferred_element_type=jnp.float32)
    return (partial_sum, fresh_keys, fresh_values)


def general_body(
    inputs,
    attention_gain,
    w_query,
    key_value_weight,
    head_sink_logits,
    w_output,
    cache_pairs,
    lengths,
    expert_gain,
    w_gate,
    w_up,
    w_down,
    routes,
    gate_weights,
):
    shards = lax.axis_size(("sec", "tp"))
    shard_index = lax.axis_index(("sec", "tp"))
    experts = lax.axis_size("grp") * w_gate.shape[0]
    group_rows = inputs.shape[1]
    width = inputs.shape[2]
    part_width = width // shards
    chosen = max(TOP, experts // 2)
    capacity = group_rows * TOP // chosen
    slot_total = experts * capacity
    gate_matrix = w_gate[0]
    up_matrix = w_up[0]
    down_matrix = w_down[0]
    fresh_keys = []
    fresh_values = []
    results = []
    for step_index in range(inputs.shape[0]):
        normalized_input = rms_norm(inputs[step_index], attention_gain)
        partial_sum, fresh_keys, fresh_values = attend(
            normalized_input,
            w_query,
            key_value_weight,
            head_sink_logits,
            w_output,
            cache_pairs,
            lengths,
            step_index,
            fresh_keys,
            fresh_values,
        )
        summed = lax.psum(partial_sum[None], ("sec", "tp"))
        middle = (inputs[step_index][None].astype(jnp.float32) + summed).astype(jnp.bfloat16)
        route_rows = routes[step_index][None]
        step_count = middle.shape[0]
        expert_in = rms_norm(middle, expert_gain)
        flat_routes = route_rows.reshape(step_count, group_rows * TOP)
        onehot = (flat_routes[..., None] == jnp.arange(experts)[None, None, :]).astype(jnp.int32)
        earlier = jnp.cumsum(onehot, axis=1) - onehot
        slot_index = jnp.sum(earlier * onehot, axis=-1).reshape(step_count, group_rows, TOP)
        target = route_rows * capacity + slot_index
        placed = target[..., None] == jnp.arange(slot_total)[None, None, None, :]
        dispatch_table = jnp.sum(placed.astype(jnp.int32), axis=2).astype(jnp.bfloat16)
        combine_table = jnp.sum(
            jnp.where(placed, gate_weights[step_index][None][..., None], 0.0), axis=2
        )
        outgoing = jnp.einsum(
            "crm,crd->cmd", dispatch_table, expert_in, preferred_element_type=jnp.float32
        )
        outgoing = outgoing.astype(jnp.bfloat16).reshape(step_count, experts, capacity, width)
        arrived = lax.all_to_all(outgoing, "grp", split_axis=1, concat_axis=1, tiled=True)
        gate_h = jnp.einsum(
            "snpd,dh->snph", arrived, gate_matrix, preferred_element_type=jnp.float32
        )
        up_h = jnp.einsum("snpd,dh->snph", arrived, up_matrix, preferred_element_type=jnp.float32)
        act = ((up_h + 1.0) * gate_h * jax.nn.sigmoid(1.702 * gate_h)).astype(jnp.bfloat16)
        partial_out = jnp.einsum(
            "snph,hd->snpd", act, down_matrix, preferred_element_type=jnp.float32
        )
        reduced = lax.psum_scatter(
            partial_out, ("sec", "tp"), scatter_dimension=3, tiled=True
        ).astype(jnp.bfloat16)
        returned = lax.all_to_all(reduced, "grp", split_axis=1, concat_axis=1, tiled=True)
        returned_rows = returned.reshape(step_count, slot_total, part_width).astype(jnp.float32)
        weighted = jnp.einsum(
            "srm,smd->srd", combine_table, returned_rows, precision=lax.Precision.HIGHEST
        )
        own_middle = lax.dynamic_slice_in_dim(
            middle, shard_index * part_width, part_width, 2
        ).astype(jnp.float32)
        results.append((own_middle + weighted).astype(jnp.bfloat16)[0])
    return jnp.stack(results, 0)


LANES = 384
BASE = 150000.0
MIB = 1 << 20


def shape_of(shape, dtype=jnp.bfloat16):
    return jax.ShapeDtypeStruct(shape, dtype)


def vmem():
    return pl.BlockSpec(memory_space=pltpu.VMEM)


def smem():
    return pl.BlockSpec(memory_space=pltpu.SMEM)


def outside():
    return pl.BlockSpec(memory_space=pltpu.HBM)


def dot_last(left, right):
    return lax.dot_general(left, right, (((1,), (1,)), ((), ())), preferred_element_type=jnp.float32)


def swap(value, axes, mask):
    size = lax.axis_size(axes)
    return lax.ppermute(value, axes, [(i, i ^ mask) for i in range(size)])


def swap_by_core(value, axis, masks):
    size = lax.axis_size(axis)
    pairs = [(s * size + i, s * size + (i ^ masks[s])) for s in range(2) for i in range(size)]
    return lax.ppermute(value, ("sec", axis), pairs)


def shard_swaps(parts):
    return [swap_by_core(part, "tp", masks) for part, masks in zip(parts, ((3, 3), (1, 2), (2, 1)))]


def shard_masks():
    sec = lax.axis_index("sec")
    return 3, 1 + sec, 2 - sec


def split_width(width):
    cuts = list(range(0, width, 768)) + [width]
    return list(zip(cuts[:-1], cuts[1:]))


def attention_kernel(lengths_hbm, sinks_hbm, routes_hbm, weights_hbm, gain_hbm, x_hbm, wq_hbm, wkv_hbm, cache_hbm, wo_hbm,
                     other_ref, own_x_ref, mix_ref, wo_ref,
                     lengths_ref, sinks_ref, routes_ref, weights_ref, gain_ref, x_ref, wq_ref, wkv_ref, cache_ref,
                     xs_ref, turned_ref, mixed_ref, sems):
    total_rows, width = x_ref.shape
    rows, slots, pair = cache_ref.shape
    steps = total_rows // rows
    heads = wq_ref.shape[1] // HEAD_SIZE
    per_row = heads * steps
    tps = other_ref.shape[0]
    cuts = split_width(width)
    small = [(lengths_hbm, lengths_ref), (x_hbm, x_ref), (gain_hbm, gain_ref), (routes_hbm, routes_ref), (weights_hbm, weights_ref),
             (sinks_hbm, sinks_ref)]
    small = [pltpu.make_async_copy(source, target, sems.at[n]) for n, (source, target) in enumerate(small)]
    copies = [pltpu.make_async_copy(wkv_hbm, wkv_ref, sems.at[6])]
    for n, (low, high) in enumerate(cuts):
        part = pl.ds(low, high - low)
        copies.append(pltpu.make_async_copy(wq_hbm.at[part], wq_ref.at[part], sems.at[9 + n]))
    copies.append(pltpu.make_async_copy(cache_hbm, cache_ref, sems.at[7]))
    copies.append(pltpu.make_async_copy(wo_hbm, wo_ref, sems.at[8]))
    for copy in small + copies:
        copy.start()
    small[0].wait()

    lane = lax.broadcasted_iota(jnp.int32, (total_rows, pair), 1)
    line = lax.broadcasted_iota(jnp.int32, (total_rows, pair), 0)
    position = jnp.zeros((total_rows, pair), jnp.int32)
    for r in range(rows):
        for s in range(steps):
            position = jnp.where(line == s * rows + r, lengths_ref[r] + s, position)
    half = HEAD_SIZE // 2
    counter = jnp.bitwise_and(lane, half - 1).astype(jnp.float32)
    frequency = jnp.exp(counter * jnp.float32(-2.0 / HEAD_SIZE * np.log(BASE)))
    angle = position.astype(jnp.float32) * frequency
    cosine, sine = jnp.cos(angle), jnp.sin(angle)
    low_half = jnp.bitwise_and(lane, HEAD_SIZE - 1) < half
    sine = jnp.where(low_half, -sine, sine)

    def turn(two):
        return two * cosine + jnp.where(low_half, pltpu.roll(two, pair - half, 1), pltpu.roll(two, half, 1)) * sine

    for copy in small[1:]:
        copy.wait()
    spare = xs_ref.shape[1] - width
    spare_at = lax.broadcasted_iota(jnp.int32, (rows, spare), 1)
    corner = lax.broadcasted_iota(jnp.int32, (rows, rows), 0) == lax.broadcasted_iota(jnp.int32, (rows, rows), 1)
    tables = []
    for s in range(steps):
        table = jnp.zeros((rows, spare), jnp.float32)
        for e in range(TOP):
            across = jnp.sum(jnp.where(routes_ref[s] == e, weights_ref[s], 0.0), axis=0, keepdims=True)
            column = jnp.sum(jnp.where(corner, across, 0.0), axis=1, keepdims=True)
            high_part = column.astype(jnp.bfloat16).astype(jnp.float32)
            table = jnp.where(spare_at == 2 * e, high_part, jnp.where(spare_at == 2 * e + 1, column - high_part, table))
        tables.append(table)
    x = x_ref[...].astype(jnp.float32)
    xs_ref[...] = jnp.concatenate([x, jnp.concatenate(tables, axis=0)], axis=1)
    own = (lax.axis_index("sec") * tps + lax.axis_index("tp")) * LANES
    own_x_ref[...] = xs_ref[:, pl.ds(pl.multiple_of(own, LANES), LANES)]
    scale = lax.rsqrt(jnp.mean(x * x, axis=-1, keepdims=True) + 1e-05)
    normed = (x * scale * gain_ref[...].reshape(1, width)).astype(jnp.bfloat16)
    copies[0].wait()
    pairs = jnp.dot(normed, wkv_ref[...], preferred_element_type=jnp.float32)
    query = None
    for n, (low, high) in enumerate(cuts):
        copies[1 + n].wait()
        term = jnp.dot(normed[:, low:high], wq_ref[low:high, :], preferred_element_type=jnp.float32)
        query = term if query is None else query + term

    is_key = lane < HEAD_SIZE
    fresh = jnp.where(is_key, turn(pairs), pairs).astype(jnp.bfloat16)
    for m in range(heads // 2):
        two = turn(query[:, m * pair:(m + 1) * pair])
        for odd in range(2):
            one = two if odd == 0 else pltpu.roll(two, HEAD_SIZE, 1)
            one = jnp.where(is_key, one, 0.0)
            for s in range(steps):
                slot = (2 * m + odd) * steps + s
                turned_ref[pl.ds(slot, rows, stride=per_row), :] = one[s * rows:(s + 1) * rows]
    turned = turned_ref[...].astype(jnp.bfloat16)

    copies[-2].wait()
    place = lax.broadcasted_iota(jnp.int32, (per_row, slots), 1)
    scores = []
    for r in range(rows):
        score = dot_last(turned[r * per_row:(r + 1) * per_row], cache_ref[r]) * 0.125
        scores.append(jnp.where(place < lengths_ref[r], score, -jnp.inf))
    cached = jnp.concatenate(scores, axis=0)
    row_at = lax.broadcasted_iota(jnp.int32, (rows * per_row, total_rows), 0)
    fresh_at = lax.broadcasted_iota(jnp.int32, (rows * per_row, total_rows), 1)
    seen = (row_at // per_row == fresh_at % rows) & (fresh_at // rows <= row_at % steps)
    new = jnp.where(seen, dot_last(turned, fresh) * 0.125, -jnp.inf)
    head_at = lax.broadcasted_iota(jnp.int32, (rows * per_row, 1), 0) % per_row // steps
    sink = jnp.zeros((rows * per_row, 1), jnp.float32)
    for h in range(heads):
        sink = jnp.where(head_at == h, sinks_ref[h], sink)
    largest = jnp.maximum(jnp.maximum(jnp.max(cached, axis=-1, keepdims=True), jnp.max(new, axis=-1, keepdims=True)), sink)
    cached = jnp.exp(cached - largest)
    new = jnp.exp(new - largest)
    total = jnp.sum(cached, axis=-1, keepdims=True) + jnp.sum(new, axis=-1, keepdims=True) + jnp.exp(sink - largest)
    share = 1.0 / total
    cached = (cached * share).astype(jnp.bfloat16)
    new = (new * share).astype(jnp.bfloat16)
    mixed = []
    for r in range(rows):
        mixed.append(jnp.dot(cached[r * per_row:(r + 1) * per_row], cache_ref[r], preferred_element_type=jnp.float32))
    mixed_ref[...] = jnp.concatenate(mixed, axis=0) + jnp.dot(new, fresh, preferred_element_type=jnp.float32)

    def head(h):
        return jnp.concatenate([mixed_ref[pl.ds(h * steps + s, rows, stride=per_row), :] for s in range(steps)], axis=0)

    mix_ref[...] = jnp.concatenate(
        [jnp.where(is_key, pltpu.roll(head(2 * m), HEAD_SIZE, 1), head(2 * m + 1)) for m in range(heads // 2)], axis=1
    ).astype(jnp.bfloat16)
    copies[-1].wait()
    project(mix_ref, wo_ref, other_ref, 1 - lax.axis_index("sec"))


def project(mix_ref, wo_ref, out_ref, side):
    width, (tps, total_rows, _) = wo_ref.shape[0], out_ref.shape
    for at in range(2):
        start, stop = at * tps * LANES, min((at + 1) * tps * LANES, width)

        @pl.when(side == at)
        def _(start=start, stop=stop):
            partial = dot_last(mix_ref[...], wo_ref[start:stop, :])
            for t in range(tps):
                low, high = t * LANES, min((t + 1) * LANES, stop - start)
                piece = partial[:, low:high]
                if high - low < LANES:
                    piece = jnp.concatenate([piece, jnp.zeros((total_rows, LANES - (high - low)), jnp.float32)], axis=1)
                out_ref[t] = piece.astype(out_ref.dtype)


def own_projection_kernel(mix_ref, wo_ref, mine_ref):
    project(mix_ref, wo_ref, mine_ref, lax.axis_index("sec"))


def attention_partial(flat, gain, w_query, key_value, sinks, w_output, cache, lengths, routes, weights, secs, tps):
    total_rows, width = flat.shape
    rows, slots, pair = cache.shape
    per_row = w_query.shape[1] // HEAD_SIZE * (total_rows // rows)
    shards = secs * tps
    operands = (lengths, sinks, routes, weights, gain, flat, w_query, key_value, cache, w_output.swapaxes(0, 1))
    return pl.pallas_call(
        attention_kernel,
        name="attention",
        out_shape=[shape_of((tps, total_rows, LANES)), shape_of((total_rows, LANES), jnp.float32),
                   shape_of((total_rows, w_output.shape[0])), shape_of((width, w_output.shape[0]))],
        in_specs=[outside()] * len(operands),
        out_specs=[vmem()] * 4,
        scratch_shapes=[
            pltpu.SMEM(lengths.shape, jnp.int32),
            pltpu.SMEM(sinks.shape, jnp.float32),
            pltpu.VMEM(routes.shape, jnp.int32),
            pltpu.VMEM(weights.shape, jnp.float32),
            pltpu.VMEM(gain.shape, jnp.float32),
            pltpu.VMEM((total_rows, width), jnp.bfloat16),
            pltpu.VMEM(w_query.shape, jnp.bfloat16),
            pltpu.VMEM(key_value.shape, jnp.bfloat16),
            pltpu.VMEM(cache.shape, jnp.bfloat16),
            pltpu.VMEM((total_rows, shards * LANES), jnp.float32),
            pltpu.VMEM((rows * per_row, pair), jnp.float32),
            pltpu.VMEM((rows * per_row, pair), jnp.float32),
            pltpu.SemaphoreType.DMA((9 + len(split_width(width)),)),
        ],
        compiler_params=pltpu.CompilerParams(vmem_limit_bytes=24 * MIB),
    )(*[pltpu.with_memory_space_constraint(operand, pltpu.HBM) for operand in operands])


def call(kernel, name, outs, *operands, limit=4, flops=0):
    single = not isinstance(outs, list)
    held = [*operands, *([outs] if single else outs)]
    return pl.pallas_call(
        kernel,
        name=name,
        out_shape=outs,
        in_specs=[vmem()] * len(operands),
        out_specs=vmem() if single else [vmem()] * len(outs),
        compiler_params=pltpu.CompilerParams(vmem_limit_bytes=limit * MIB),
        cost_estimate=pl.CostEstimate(flops=flops, transcendentals=0,
                                      bytes_accessed=sum(math.prod(a.shape) * a.dtype.itemsize for a in held)),
    )(*operands)


def after_core_kernel(mine_ref, come_ref, own_ref, *send_refs):
    tp = lax.axis_index("tp")
    own_ref[...] = mine_ref[tp] + come_ref[tp].astype(jnp.float32)
    for mask, ref in zip(shard_masks(), send_refs):
        to = jnp.bitwise_xor(tp, mask)
        ref[...] = (mine_ref[to] + come_ref[to].astype(jnp.float32)).astype(jnp.bfloat16)


def add_all(*refs):
    total = refs[0][...]
    for ref in refs[1:]:
        total = total + ref[...].astype(jnp.float32)
    return total


def sum_kernel(*refs):
    refs[-1][...] = add_all(*refs[:-1]).astype(jnp.bfloat16).reshape(refs[-1].shape)


def divide_rows_kernel(*refs, groups):
    total = add_all(*refs[:-groups])
    outs = refs[-groups:]
    lines = outs[0].shape[0]
    for n, out in enumerate(outs):
        out[...] = total[n * lines:(n + 1) * lines].astype(out.dtype)


def swap_all(parts, axis):
    count = len(parts)
    come = {m: swap(parts[m - 1], axis, m) for m in reversed(range(1, count + 1))}
    return [come[m] for m in range(1, count + 1)]


def scatter_shards(mine, come):
    tps, lines, part = mine.shape
    own, *parts = call(after_core_kernel, "after_core", [shape_of((lines, part), jnp.float32)] + [shape_of((lines, part))] * (tps - 1),
                       mine, come)
    return [own] + shard_swaps(parts)


def first_products(pieces, masks, side, x_ref, gain_ref, gate_ref, up_ref, gate_out, up_out, square_out):
    width, lines = gate_ref.shape[1], x_ref.shape[0]
    tp = lax.axis_index("tp")
    for mask, piece in zip(masks, pieces):
        at = pl.multiple_of(jnp.bitwise_xor(tp, mask) * LANES, LANES)
        x_ref[:, pl.ds(at, LANES)] = piece[...].reshape(lines, LANES)
    for at in range(2):
        start, stop = at * x_ref.shape[1], min((at + 1) * x_ref.shape[1], width)

        @pl.when(side == at)
        def _(start=start, stop=stop):
            x = x_ref[:, :stop - start].astype(jnp.float32)
            square_out[...] = jnp.broadcast_to(jnp.sum(x * x, axis=-1, keepdims=True), square_out.shape)
            scaled = (x * gain_ref[:, start:stop]).astype(jnp.bfloat16)
            gate_out[...] = dot_last(scaled, gate_ref[:, start:stop])
            up_out[...] = dot_last(scaled, up_ref[:, start:stop])


def near_kernel(gain_ref, gate_ref, up_ref, *refs):
    pieces, (x_ref, gate_out, up_out, square_out) = refs[:-4], refs[-4:]
    first_products(pieces, (0, *shard_masks()), lax.axis_index("sec"), x_ref, gain_ref, gate_ref, up_ref, gate_out, up_out,
                   square_out)


def second_product(act_ref, down_ref, out_ref, side):
    width, (tps, lines, part) = down_ref.shape[1], out_ref.shape
    for at in range(2):
        start, stop = at * tps * part, (at + 1) * tps * part
        shift = start % 128

        @pl.when(side == at)
        def _(start=start, stop=stop, shift=shift):
            out = jnp.dot(act_ref[...], down_ref[:, start - shift:stop], preferred_element_type=jnp.float32)
            for t in range(tps):
                out_ref[t] = out[:, shift + t * part:shift + (t + 1) * part].astype(out_ref.dtype)


def far_kernel(gain_ref, gate_ref, up_ref, down_ref, near_x_ref, near_gate_ref, near_up_ref, near_square_ref, *refs):
    pieces, (other_ref, act_ref, far_x_ref, gate_out, up_out, square_out) = refs[:-6], refs[-6:]
    sec, grp = lax.axis_index("sec"), lax.axis_index("grp")
    masks = shard_masks()
    first_products(pieces, (0, masks[0], masks[2], masks[1]), 1 - sec, far_x_ref, gain_ref, gate_ref, up_ref, gate_out, up_out,
                   square_out)
    width, half = gate_ref.shape[1], near_x_ref.shape[1]
    spare = jnp.where(sec == 1, near_x_ref[:, width - half:], far_x_ref[:, width - half:]).astype(jnp.float32)
    spare_at = lax.broadcasted_iota(jnp.int32, spare.shape, 1)
    weight = jnp.sum(jnp.where((spare_at == 2 * grp) | (spare_at == 2 * grp + 1), spare, 0.0), axis=1, keepdims=True)
    square = (near_square_ref[...] + square_out[...])[:, :1]
    scale = lax.rsqrt(square / width + 1e-05)
    gate_h = (near_gate_ref[...] + gate_out[...]) * scale
    up_h = (near_up_ref[...] + up_out[...]) * scale
    act_ref[...] = ((up_h + 1.0) * gate_h * jax.nn.sigmoid(1.702 * gate_h) * weight).astype(jnp.bfloat16)
    second_product(act_ref, down_ref, other_ref, 1 - sec)


def last_kernel(act_ref, down_ref, near_x_ref, far_x_ref, mine_ref, middle_ref, row_ref):
    sec, tp = lax.axis_index("sec"), lax.axis_index("tp")
    second_product(act_ref, down_ref, mine_ref, sec)
    total_rows, part = middle_ref.shape
    near, far = near_x_ref[:total_rows].astype(jnp.float32), far_x_ref[:total_rows].astype(jnp.float32)
    first = sec == 0
    x = jnp.concatenate([jnp.where(first, near, far), jnp.where(first, far, near)], axis=1)
    for c in range(row_ref.shape[0]):
        row_ref[c] = x[:, c * part:(c + 1) * part]
    middle_ref[...] = row_ref[sec * mine_ref.shape[0] + tp]


def experts(gain, w_gate, w_up, w_down, pieces, far_pieces, part):
    groups, total_rows, _ = pieces[0].shape
    tps, lines, (width, hidden) = len(pieces), groups * total_rows, w_gate.shape
    gain, w_gate, w_up = gain.reshape(1, -1), w_gate.swapaxes(0, 1), w_up.swapaxes(0, 1)
    halves = [shape_of((lines, tps * LANES)), shape_of((lines, hidden), jnp.float32), shape_of((lines, hidden), jnp.float32),
              shape_of((lines, 128), jnp.float32)]
    near = call(near_kernel, "near_columns", halves, gain, w_gate, w_up, *pieces, limit=12, flops=2 * lines * width * hidden)
    other, act, far_x = pl.pallas_call(
        far_kernel,
        name="far_columns",
        out_shape=[shape_of((tps, lines, part)), shape_of((lines, hidden)), halves[0]],
        in_specs=[vmem()] * (8 + tps),
        out_specs=[vmem()] * 3,
        scratch_shapes=[pltpu.VMEM(half.shape, half.dtype) for half in halves[1:]],
        compiler_params=pltpu.CompilerParams(vmem_limit_bytes=16 * MIB),
    )(gain, w_gate, w_up, w_down, *near, *far_pieces)
    come = swap(other, "sec", 1)
    mine, middle = pl.pallas_call(
        last_kernel,
        name="own_columns",
        out_shape=[shape_of((tps, lines, part), jnp.float32), shape_of((total_rows, part), jnp.float32)],
        in_specs=[vmem()] * 4,
        out_specs=[vmem()] * 2,
        scratch_shapes=[pltpu.VMEM((2 * tps, total_rows, part), jnp.float32)],
        compiler_params=pltpu.CompilerParams(vmem_limit_bytes=12 * MIB),
        cost_estimate=pl.CostEstimate(flops=lines * width * hidden, transcendentals=0, bytes_accessed=2 * lines * width),
    )(act, w_down, near[0], far_x)
    return mine, come, middle


def every_expert_body(inputs, attention_gain, w_query, key_value_weight, head_sink_logits, w_output, cache_pairs, lengths,
                      expert_gain, w_gate, w_up, w_down, routes, gate_weights):
    secs, tps, groups = lax.axis_size("sec"), lax.axis_size("tp"), lax.axis_size("grp")
    steps, rows, width = inputs.shape
    flat = inputs.reshape(steps * rows, width)
    other, own_x, mix, held = attention_partial(
        flat, attention_gain, w_query, key_value_weight[:, 0], head_sink_logits, w_output, cache_pairs[:, :, 0], lengths,
        routes.swapaxes(1, 2), gate_weights.swapaxes(1, 2), secs, tps)
    come = swap(other, "sec", 1)
    mine = call(own_projection_kernel, "own_projection", shape_of(other.shape, jnp.float32), mix, held, limit=12,
                flops=mix.size * width)
    middle = call(sum_kernel, "sum", shape_of((steps * rows, LANES)), *scatter_shards(mine, come), own_x)
    stacked = jnp.stack([middle] + swap_all([middle] * (groups - 1), "grp"))
    pieces = [stacked] + shard_swaps([stacked] * (tps - 1))
    far_pieces = [swap(piece, "sec", 1) for piece in pieces]
    mine, come, own_middle = experts(expert_gain, w_gate[0], w_up[0], w_down[0], pieces, far_pieces, width // (secs * tps))
    terms = scatter_shards(mine, come)
    lines, part = steps * rows, terms[0].shape[1]
    own, *parts = call(functools.partial(divide_rows_kernel, groups=groups), "divide_rows",
                       [shape_of((lines, part), jnp.float32)] + [shape_of((lines, part))] * (groups - 1), *terms)
    return call(sum_kernel, "combine", shape_of((steps, rows, part)), own, *swap_all(parts, "grp"), own_middle)


def body(*args):
    sizes = lax.axis_size("sec"), lax.axis_size("tp"), lax.axis_size("grp"), args[9].shape[0]
    if sizes == (2, 4, TOP, 1):
        return every_expert_body(*args)
    return general_body(*args)


def solution(mesh):
    placed = (
        P(None, "grp", None),
        P(),
        P(None, ("sec", "tp")),
        P(None, ("sec", "tp"), None),
        P(("sec", "tp")),
        P(("sec", "tp"), None),
        P("grp", None, ("sec", "tp"), None),
        P("grp"),
        P(),
        P("grp", None, ("sec", "tp")),
        P("grp", None, ("sec", "tp")),
        P("grp", ("sec", "tp"), None),
        P(None, "grp", None),
        P(None, "grp", None),
    )
    return jax.shard_map(
        body, mesh=mesh, in_specs=placed, out_specs=P(None, "grp", ("sec", "tp")), check_vma=False
    )
```

```python
import functools
import math

import jax
import jax.numpy as jnp
import numpy as np
from jax import lax
from jax.experimental import pallas as pl
from jax.experimental.pallas import tpu as pltpu
from jax.sharding import PartitionSpec as P

HEAD_SIZE = 64
TOP = 4


def rms_norm(values, scale_row):
    widened = values.astype(jnp.float32)
    scale_factor = lax.rsqrt(jnp.mean(widened * widened, axis=-1, keepdims=True) + 1e-05)
    return (widened * scale_factor * scale_row).astype(jnp.bfloat16)


def rotate(vectors, position):
    half_size = vectors.shape[-1] // 2
    counter = jnp.arange(half_size).astype(jnp.float32)
    frequency = jnp.power(jnp.float32(150000.0), counter * (-2.0 / vectors.shape[-1]))
    angle_table = position * frequency
    cosine = jnp.cos(angle_table)
    sine_table = jnp.sin(angle_table)
    first_half = vectors[..., :half_size]
    second_half = vectors[..., half_size:]
    return jnp.concatenate(
        [
            first_half * cosine - second_half * sine_table,
            first_half * sine_table + second_half * cosine,
        ],
        axis=-1,
    )


def attend(
    normalized_input,
    w_query,
    key_value_weight,
    head_sink_logits,
    w_output,
    cache_pairs,
    lengths,
    step_index,
    fresh_keys,
    fresh_values,
):
    row_count = normalized_input.shape[0]
    kv_heads = key_value_weight.shape[1]
    query = jnp.dot(normalized_input, w_query, preferred_element_type=jnp.float32).reshape(
        row_count, -1, HEAD_SIZE
    )
    cache_entry_pairs = jnp.dot(
        normalized_input,
        key_value_weight.reshape(key_value_weight.shape[0], -1),
        preferred_element_type=jnp.float32,
    ).reshape(row_count, kv_heads, 2 * HEAD_SIZE)
    position = (lengths + step_index).astype(jnp.float32)[:, None, None]
    rotated_rows = rotate(query, position).astype(jnp.bfloat16)
    fresh_keys = fresh_keys + [
        rotate(cache_entry_pairs[..., :HEAD_SIZE], position).astype(jnp.bfloat16)
    ]
    fresh_values = fresh_values + [cache_entry_pairs[..., HEAD_SIZE:].astype(jnp.bfloat16)]
    grouped_queries = rotated_rows.reshape(row_count, kv_heads, -1, HEAD_SIZE)
    new_keys = jnp.stack(fresh_keys, 1)
    new_values = jnp.stack(fresh_values, 1)
    cached = (
        jnp.einsum(
            "rkgd,rjkd->rkgj",
            grouped_queries,
            cache_pairs[..., :HEAD_SIZE],
            preferred_element_type=jnp.float32,
        )
        * 0.125
    )
    valid = (jnp.arange(cache_pairs.shape[1])[None, :] < lengths[:, None])[:, None, None, :]
    cached = jnp.where(valid, cached, -jnp.inf)
    fresh = (
        jnp.einsum("rkgd,rikd->rkgi", grouped_queries, new_keys, preferred_element_type=jnp.float32)
        * 0.125
    )
    sink_row = head_sink_logits.reshape(kv_heads, -1)[None]
    largest = jnp.maximum(jnp.maximum(jnp.max(cached, axis=-1), jnp.max(fresh, axis=-1)), sink_row)
    cached_exp = jnp.exp(cached - largest[..., None])
    fresh_exp = jnp.exp(fresh - largest[..., None])
    denominator = (
        jnp.sum(cached_exp, axis=-1) + jnp.sum(fresh_exp, axis=-1) + jnp.exp(sink_row - largest)
    )
    cached_probs = (cached_exp / denominator[..., None]).astype(jnp.bfloat16)
    fresh_probs = (fresh_exp / denominator[..., None]).astype(jnp.bfloat16)
    mixed = jnp.einsum(
        "rkgj,rjkd->rkgd",
        cached_probs,
        cache_pairs[..., HEAD_SIZE:],
        preferred_element_type=jnp.float32,
    )
    mixed = mixed + jnp.einsum(
        "rkgi,rikd->rkgd", fresh_probs, new_values, preferred_element_type=jnp.float32
    )
    attention_mix = mixed.reshape(row_count, -1).astype(jnp.bfloat16)
    partial_sum = jnp.dot(attention_mix, w_output, preferred_element_type=jnp.float32)
    return (partial_sum, fresh_keys, fresh_values)


def general_body(
    inputs,
    attention_gain,
    w_query,
    key_value_weight,
    head_sink_logits,
    w_output,
    cache_pairs,
    lengths,
    expert_gain,
    w_gate,
    w_up,
    w_down,
    routes,
    gate_weights,
):
    shards = lax.axis_size(("sec", "tp"))
    shard_index = lax.axis_index(("sec", "tp"))
    experts = lax.axis_size("grp") * w_gate.shape[0]
    group_rows = inputs.shape[1]
    width = inputs.shape[2]
    part_width = width // shards
    chosen = max(TOP, experts // 2)
    capacity = group_rows * TOP // chosen
    slot_total = experts * capacity
    gate_matrix = w_gate[0]
    up_matrix = w_up[0]
    down_matrix = w_down[0]
    fresh_keys = []
    fresh_values = []
    results = []
    for step_index in range(inputs.shape[0]):
        normalized_input = rms_norm(inputs[step_index], attention_gain)
        partial_sum, fresh_keys, fresh_values = attend(
            normalized_input,
            w_query,
            key_value_weight,
            head_sink_logits,
            w_output,
            cache_pairs,
            lengths,
            step_index,
            fresh_keys,
            fresh_values,
        )
        summed = lax.psum(partial_sum[None], ("sec", "tp"))
        middle = (inputs[step_index][None].astype(jnp.float32) + summed).astype(jnp.bfloat16)
        route_rows = routes[step_index][None]
        step_count = middle.shape[0]
        expert_in = rms_norm(middle, expert_gain)
        flat_routes = route_rows.reshape(step_count, group_rows * TOP)
        onehot = (flat_routes[..., None] == jnp.arange(experts)[None, None, :]).astype(jnp.int32)
        earlier = jnp.cumsum(onehot, axis=1) - onehot
        slot_index = jnp.sum(earlier * onehot, axis=-1).reshape(step_count, group_rows, TOP)
        target = route_rows * capacity + slot_index
        placed = target[..., None] == jnp.arange(slot_total)[None, None, None, :]
        dispatch_table = jnp.sum(placed.astype(jnp.int32), axis=2).astype(jnp.bfloat16)
        combine_table = jnp.sum(
            jnp.where(placed, gate_weights[step_index][None][..., None], 0.0), axis=2
        )
        outgoing = jnp.einsum(
            "crm,crd->cmd", dispatch_table, expert_in, preferred_element_type=jnp.float32
        )
        outgoing = outgoing.astype(jnp.bfloat16).reshape(step_count, experts, capacity, width)
        arrived = lax.all_to_all(outgoing, "grp", split_axis=1, concat_axis=1, tiled=True)
        gate_h = jnp.einsum(
            "snpd,dh->snph", arrived, gate_matrix, preferred_element_type=jnp.float32
        )
        up_h = jnp.einsum("snpd,dh->snph", arrived, up_matrix, preferred_element_type=jnp.float32)
        act = ((up_h + 1.0) * gate_h * jax.nn.sigmoid(1.702 * gate_h)).astype(jnp.bfloat16)
        partial_out = jnp.einsum(
            "snph,hd->snpd", act, down_matrix, preferred_element_type=jnp.float32
        )
        reduced = lax.psum_scatter(
            partial_out, ("sec", "tp"), scatter_dimension=3, tiled=True
        ).astype(jnp.bfloat16)
        returned = lax.all_to_all(reduced, "grp", split_axis=1, concat_axis=1, tiled=True)
        returned_rows = returned.reshape(step_count, slot_total, part_width).astype(jnp.float32)
        weighted = jnp.einsum(
            "srm,smd->srd", combine_table, returned_rows, precision=lax.Precision.HIGHEST
        )
        own_middle = lax.dynamic_slice_in_dim(
            middle, shard_index * part_width, part_width, 2
        ).astype(jnp.float32)
        results.append((own_middle + weighted).astype(jnp.bfloat16)[0])
    return jnp.stack(results, 0)


LANES = 384
BASE = 150000.0
MIB = 1 << 20


def shape_of(shape, dtype=jnp.bfloat16):
    return jax.ShapeDtypeStruct(shape, dtype)


def vmem():
    return pl.BlockSpec(memory_space=pltpu.VMEM)


def smem():
    return pl.BlockSpec(memory_space=pltpu.SMEM)


def outside():
    return pl.BlockSpec(memory_space=pltpu.HBM)


def dot_last(left, right):
    return lax.dot_general(left, right, (((1,), (1,)), ((), ())), preferred_element_type=jnp.float32)


def swap(value, axes, mask):
    size = lax.axis_size(axes)
    return lax.ppermute(value, axes, [(i, i ^ mask) for i in range(size)])


def swap_by_core(value, axis, masks):
    size = lax.axis_size(axis)
    pairs = [(s * size + i, s * size + (i ^ masks[s])) for s in range(2) for i in range(size)]
    return lax.ppermute(value, ("sec", axis), pairs)


def shard_swaps(parts):
    return [swap_by_core(part, "tp", masks) for part, masks in zip(parts, ((3, 3), (1, 2), (2, 1)))]


def shard_masks():
    sec = lax.axis_index("sec")
    return 3, 1 + sec, 2 - sec


def split_width(width):
    cuts = list(range(0, width, 768)) + [width]
    return list(zip(cuts[:-1], cuts[1:]))


def attention_kernel(lengths_hbm, sinks_hbm, routes_hbm, weights_hbm, gain_hbm, x_hbm, wq_hbm, wkv_hbm, cache_hbm, wo_hbm,
                     other_ref, own_x_ref, mix_ref, wo_ref,
                     lengths_ref, sinks_ref, routes_ref, weights_ref, gain_ref, x_ref, wq_ref, wkv_ref, cache_ref,
                     xs_ref, turned_ref, mixed_ref, sems):
    total_rows, width = x_ref.shape
    rows, slots, pair = cache_ref.shape
    steps = total_rows // rows
    heads = wq_ref.shape[1] // HEAD_SIZE
    per_row = heads * steps
    tps = other_ref.shape[0]
    cuts = split_width(width)
    small = [(lengths_hbm, lengths_ref), (x_hbm, x_ref), (gain_hbm, gain_ref), (routes_hbm, routes_ref), (weights_hbm, weights_ref),
             (sinks_hbm, sinks_ref)]
    small = [pltpu.make_async_copy(source, target, sems.at[n]) for n, (source, target) in enumerate(small)]
    copies = [pltpu.make_async_copy(wkv_hbm, wkv_ref, sems.at[6])]
    for n, (low, high) in enumerate(cuts):
        part = pl.ds(low, high - low)
        copies.append(pltpu.make_async_copy(wq_hbm.at[part], wq_ref.at[part], sems.at[9 + n]))
    copies.append(pltpu.make_async_copy(cache_hbm, cache_ref, sems.at[7]))
    copies.append(pltpu.make_async_copy(wo_hbm, wo_ref, sems.at[8]))
    for copy in small + copies:
        copy.start()
    small[0].wait()

    lane = lax.broadcasted_iota(jnp.int32, (total_rows, pair), 1)
    line = lax.broadcasted_iota(jnp.int32, (total_rows, pair), 0)
    position = jnp.zeros((total_rows, pair), jnp.int32)
    for r in range(rows):
        for s in range(steps):
            position = jnp.where(line == s * rows + r, lengths_ref[r] + s, position)
    half = HEAD_SIZE // 2
    counter = jnp.bitwise_and(lane, half - 1).astype(jnp.float32)
    frequency = jnp.exp(counter * jnp.float32(-2.0 / HEAD_SIZE * np.log(BASE)))
    angle = position.astype(jnp.float32) * frequency
    cosine, sine = jnp.cos(angle), jnp.sin(angle)
    low_half = jnp.bitwise_and(lane, HEAD_SIZE - 1) < half
    sine = jnp.where(low_half, -sine, sine)

    def turn(two):
        return two * cosine + jnp.where(low_half, pltpu.roll(two, pair - half, 1), pltpu.roll(two, half, 1)) * sine

    for copy in small[1:]:
        copy.wait()
    spare = xs_ref.shape[1] - width
    spare_at = lax.broadcasted_iota(jnp.int32, (rows, spare), 1)
    corner = lax.broadcasted_iota(jnp.int32, (rows, rows), 0) == lax.broadcasted_iota(jnp.int32, (rows, rows), 1)
    tables = []
    for s in range(steps):
        table = jnp.zeros((rows, spare), jnp.float32)
        for e in range(TOP):
            across = jnp.sum(jnp.where(routes_ref[s] == e, weights_ref[s], 0.0), axis=0, keepdims=True)
            column = jnp.sum(jnp.where(corner, across, 0.0), axis=1, keepdims=True)
            high_part = column.astype(jnp.bfloat16).astype(jnp.float32)
            table = jnp.where(spare_at == 2 * e, high_part, jnp.where(spare_at == 2 * e + 1, column - high_part, table))
        tables.append(table)
    x = x_ref[...].astype(jnp.float32)
    xs_ref[...] = jnp.concatenate([x, jnp.concatenate(tables, axis=0)], axis=1)
    own = (lax.axis_index("sec") * tps + lax.axis_index("tp")) * LANES
    own_x_ref[...] = xs_ref[:, pl.ds(pl.multiple_of(own, LANES), LANES)]
    scale = lax.rsqrt(jnp.mean(x * x, axis=-1, keepdims=True) + 1e-05)
    normed = (x * scale * gain_ref[...].reshape(1, width)).astype(jnp.bfloat16)
    copies[0].wait()
    pairs = jnp.dot(normed, wkv_ref[...], preferred_element_type=jnp.float32)
    query = None
    for n, (low, high) in enumerate(cuts):
        copies[1 + n].wait()
        term = jnp.dot(normed[:, low:high], wq_ref[low:high, :], preferred_element_type=jnp.float32)
        query = term if query is None else query + term

    is_key = lane < HEAD_SIZE
    fresh = jnp.where(is_key, turn(pairs), pairs).astype(jnp.bfloat16)
    for m in range(heads // 2):
        two = turn(query[:, m * pair:(m + 1) * pair])
        for odd in range(2):
            one = two if odd == 0 else pltpu.roll(two, HEAD_SIZE, 1)
            one = jnp.where(is_key, one, 0.0)
            for s in range(steps):
                slot = (2 * m + odd) * steps + s
                turned_ref[pl.ds(slot, rows, stride=per_row), :] = one[s * rows:(s + 1) * rows]
    turned = turned_ref[...].astype(jnp.bfloat16)

    copies[-2].wait()
    place = lax.broadcasted_iota(jnp.int32, (per_row, slots), 1)
    scores = []
    for r in range(rows):
        score = dot_last(turned[r * per_row:(r + 1) * per_row], cache_ref[r]) * 0.125
        scores.append(jnp.where(place < lengths_ref[r], score, -jnp.inf))
    cached = jnp.concatenate(scores, axis=0)
    row_at = lax.broadcasted_iota(jnp.int32, (rows * per_row, total_rows), 0)
    fresh_at = lax.broadcasted_iota(jnp.int32, (rows * per_row, total_rows), 1)
    seen = (row_at // per_row == fresh_at % rows) & (fresh_at // rows <= row_at % steps)
    new = jnp.where(seen, dot_last(turned, fresh) * 0.125, -jnp.inf)
    head_at = lax.broadcasted_iota(jnp.int32, (rows * per_row, 1), 0) % per_row // steps
    sink = jnp.zeros((rows * per_row, 1), jnp.float32)
    for h in range(heads):
        sink = jnp.where(head_at == h, sinks_ref[h], sink)
    largest = jnp.maximum(jnp.maximum(jnp.max(cached, axis=-1, keepdims=True), jnp.max(new, axis=-1, keepdims=True)), sink)
    cached = jnp.exp(cached - largest)
    new = jnp.exp(new - largest)
    total = jnp.sum(cached, axis=-1, keepdims=True) + jnp.sum(new, axis=-1, keepdims=True) + jnp.exp(sink - largest)
    share = 1.0 / total
    cached = (cached * share).astype(jnp.bfloat16)
    new = (new * share).astype(jnp.bfloat16)
    mixed = []
    for r in range(rows):
        mixed.append(jnp.dot(cached[r * per_row:(r + 1) * per_row], cache_ref[r], preferred_element_type=jnp.float32))
    mixed_ref[...] = jnp.concatenate(mixed, axis=0) + jnp.dot(new, fresh, preferred_element_type=jnp.float32)

    def head(h):
        return jnp.concatenate([mixed_ref[pl.ds(h * steps + s, rows, stride=per_row), :] for s in range(steps)], axis=0)

    mix_ref[...] = jnp.concatenate(
        [jnp.where(is_key, pltpu.roll(head(2 * m), HEAD_SIZE, 1), head(2 * m + 1)) for m in range(heads // 2)], axis=1
    ).astype(jnp.bfloat16)
    copies[-1].wait()
    project(mix_ref, wo_ref, other_ref, 1 - lax.axis_index("sec"))


def project(mix_ref, wo_ref, out_ref, side):
    width, (tps, total_rows, _) = wo_ref.shape[0], out_ref.shape
    for at in range(2):
        start, stop = at * tps * LANES, min((at + 1) * tps * LANES, width)

        @pl.when(side == at)
        def _(start=start, stop=stop):
            partial = dot_last(mix_ref[...], wo_ref[start:stop, :])
            for t in range(tps):
                low, high = t * LANES, min((t + 1) * LANES, stop - start)
                piece = partial[:, low:high]
                if high - low < LANES:
                    piece = jnp.concatenate([piece, jnp.zeros((total_rows, LANES - (high - low)), jnp.float32)], axis=1)
                out_ref[t] = piece.astype(out_ref.dtype)


def own_projection_kernel(mix_ref, wo_ref, mine_ref):
    project(mix_ref, wo_ref, mine_ref, lax.axis_index("sec"))


def attention_partial(flat, gain, w_query, key_value, sinks, w_output, cache, lengths, routes, weights, secs, tps):
    total_rows, width = flat.shape
    rows, slots, pair = cache.shape
    per_row = w_query.shape[1] // HEAD_SIZE * (total_rows // rows)
    shards = secs * tps
    operands = (lengths, sinks, routes, weights, gain, flat, w_query, key_value, cache, w_output.swapaxes(0, 1))
    return pl.pallas_call(
        attention_kernel,
        name="attention",
        out_shape=[shape_of((tps, total_rows, LANES)), shape_of((total_rows, LANES), jnp.float32),
                   shape_of((total_rows, w_output.shape[0])), shape_of((width, w_output.shape[0]))],
        in_specs=[outside()] * len(operands),
        out_specs=[vmem()] * 4,
        scratch_shapes=[
            pltpu.SMEM(lengths.shape, jnp.int32),
            pltpu.SMEM(sinks.shape, jnp.float32),
            pltpu.VMEM(routes.shape, jnp.int32),
            pltpu.VMEM(weights.shape, jnp.float32),
            pltpu.VMEM(gain.shape, jnp.float32),
            pltpu.VMEM((total_rows, width), jnp.bfloat16),
            pltpu.VMEM(w_query.shape, jnp.bfloat16),
            pltpu.VMEM(key_value.shape, jnp.bfloat16),
            pltpu.VMEM(cache.shape, jnp.bfloat16),
            pltpu.VMEM((total_rows, shards * LANES), jnp.float32),
            pltpu.VMEM((rows * per_row, pair), jnp.float32),
            pltpu.VMEM((rows * per_row, pair), jnp.float32),
            pltpu.SemaphoreType.DMA((9 + len(split_width(width)),)),
        ],
        compiler_params=pltpu.CompilerParams(vmem_limit_bytes=24 * MIB),
    )(*[pltpu.with_memory_space_constraint(operand, pltpu.HBM) for operand in operands])


def call(kernel, name, outs, *operands, limit=4, flops=0):
    single = not isinstance(outs, list)
    held = [*operands, *([outs] if single else outs)]
    return pl.pallas_call(
        kernel,
        name=name,
        out_shape=outs,
        in_specs=[vmem()] * len(operands),
        out_specs=vmem() if single else [vmem()] * len(outs),
        compiler_params=pltpu.CompilerParams(vmem_limit_bytes=limit * MIB),
        cost_estimate=pl.CostEstimate(flops=flops, transcendentals=0,
                                      bytes_accessed=sum(math.prod(a.shape) * a.dtype.itemsize for a in held)),
    )(*operands)


def after_core_kernel(mine_ref, come_ref, own_ref, *send_refs):
    tp = lax.axis_index("tp")
    own_ref[...] = mine_ref[tp] + come_ref[tp].astype(jnp.float32)
    for mask, ref in zip(shard_masks(), send_refs):
        to = jnp.bitwise_xor(tp, mask)
        ref[...] = (mine_ref[to] + come_ref[to].astype(jnp.float32)).astype(jnp.bfloat16)


def after_core_halves_kernel(mine_ref, come_ref, own_ref, *send_refs):
    tp, half = lax.axis_index("tp"), mine_ref.shape[1] // 2
    own_ref[...] = mine_ref[tp] + come_ref[tp].astype(jnp.float32)
    for mask, second, first in zip(shard_masks(), send_refs[:3], send_refs[3:]):
        to = jnp.bitwise_xor(tp, mask)
        part = (mine_ref[to] + come_ref[to].astype(jnp.float32)).astype(jnp.bfloat16)
        second[...] = part[half:]
        first[...] = part[:half]


def add_all(*refs):
    total = refs[0][...]
    for ref in refs[1:]:
        total = total + ref[...].astype(jnp.float32)
    return total


def sum_kernel(*refs):
    refs[-1][...] = add_all(*refs[:-1]).astype(jnp.bfloat16).reshape(refs[-1].shape)


def sum_rows_kernel(own_ref, *refs, line):
    come, outs = refs[:3], refs[3:]
    lines = outs[0].shape[0]
    total = own_ref[line:line + len(outs) * lines]
    for ref in come:
        total = total + ref[...].astype(jnp.float32)
    for n, out in enumerate(outs):
        out[...] = total[n * lines:(n + 1) * lines].astype(out.dtype)


def scatter_shards(mine, come):
    tps, lines, part = mine.shape
    own, *parts = call(after_core_kernel, "after_core", [shape_of((lines, part), jnp.float32)] + [shape_of((lines, part))] * (tps - 1),
                       mine, come)
    return [own] + shard_swaps(parts)


def first_products(pieces, masks, side, x_ref, gain_ref, gate_ref, up_ref, gate_out, up_out, square_out):
    width, lines = gate_ref.shape[1], x_ref.shape[0] // 2
    tp = lax.axis_index("tp")
    for n, piece in enumerate(pieces):
        half, mask = 1 - n // len(masks), masks[n % len(masks)]
        at = pl.multiple_of(jnp.bitwise_xor(tp, mask) * LANES, LANES)
        x_ref[half * lines:(half + 1) * lines, pl.ds(at, LANES)] = piece[...].reshape(lines, LANES)
    for at in range(2):
        start, stop = at * x_ref.shape[1], min((at + 1) * x_ref.shape[1], width)

        @pl.when(side == at)
        def _(start=start, stop=stop):
            x = x_ref[:, :stop - start].astype(jnp.float32)
            square_out[...] = jnp.broadcast_to(jnp.sum(x * x, axis=-1, keepdims=True), square_out.shape)
            scaled = (x * gain_ref[:, start:stop]).astype(jnp.bfloat16)
            gate_out[...] = dot_last(scaled, gate_ref[:, start:stop])
            up_out[...] = dot_last(scaled, up_ref[:, start:stop])


def near_kernel(gain_ref, gate_ref, up_ref, *refs):
    pieces, (x_ref, gate_out, up_out, square_out) = refs[:-4], refs[-4:]
    first_products(pieces, (0, *shard_masks()), lax.axis_index("sec"), x_ref, gain_ref, gate_ref, up_ref, gate_out, up_out,
                   square_out)


def second_product(act_ref, down_ref, out_ref, side):
    width, (tps, lines, part) = down_ref.shape[1], out_ref.shape
    for at in range(2):
        start, stop = at * tps * part, (at + 1) * tps * part
        shift = start % 128

        @pl.when(side == at)
        def _(start=start, stop=stop, shift=shift):
            out = jnp.dot(act_ref[...], down_ref[:, start - shift:stop], preferred_element_type=jnp.float32)
            for t in range(tps):
                out_ref[t] = out[:, shift + t * part:shift + (t + 1) * part].astype(out_ref.dtype)


def far_kernel(gain_ref, gate_ref, up_ref, down_ref, near_x_ref, near_gate_ref, near_up_ref, near_square_ref, *refs):
    pieces, (other_ref, act_ref, far_x_ref, gate_out, up_out, square_out) = refs[:-6], refs[-6:]
    sec, grp = lax.axis_index("sec"), lax.axis_index("grp")
    masks = shard_masks()
    first_products(pieces, (0, masks[0], masks[2], masks[1]), 1 - sec, far_x_ref, gain_ref, gate_ref, up_ref, gate_out, up_out,
                   square_out)
    width, half = gate_ref.shape[1], near_x_ref.shape[1]
    spare = jnp.where(sec == 1, near_x_ref[:, width - half:], far_x_ref[:, width - half:]).astype(jnp.float32)
    spare_at = lax.broadcasted_iota(jnp.int32, spare.shape, 1)
    weight = jnp.sum(jnp.where((spare_at == 2 * grp) | (spare_at == 2 * grp + 1), spare, 0.0), axis=1, keepdims=True)
    square = (near_square_ref[...] + square_out[...])[:, :1]
    scale = lax.rsqrt(square / width + 1e-05)
    gate_h = (near_gate_ref[...] + gate_out[...]) * scale
    up_h = (near_up_ref[...] + up_out[...]) * scale
    act_ref[...] = ((up_h + 1.0) * gate_h * jax.nn.sigmoid(1.702 * gate_h) * weight).astype(jnp.bfloat16)
    second_product(act_ref, down_ref, other_ref, 1 - sec)


def last_kernel(act_ref, down_ref, near_x_ref, far_x_ref, mine_ref, middle_ref, row_ref):
    sec, tp = lax.axis_index("sec"), lax.axis_index("tp")
    second_product(act_ref, down_ref, mine_ref, sec)
    total_rows, part = middle_ref.shape
    near, far = near_x_ref[:total_rows].astype(jnp.float32), far_x_ref[:total_rows].astype(jnp.float32)
    first = sec == 0
    x = jnp.concatenate([jnp.where(first, near, far), jnp.where(first, far, near)], axis=1)
    for c in range(row_ref.shape[0]):
        row_ref[c] = x[:, c * part:(c + 1) * part]
    middle_ref[...] = row_ref[sec * mine_ref.shape[0] + tp]


def experts(gain, w_gate, w_up, w_down, pieces, part):
    gain, w_gate, w_up = gain.reshape(1, -1), w_gate.swapaxes(0, 1), w_up.swapaxes(0, 1)
    (hidden, width), tps, (groups, total_rows, _) = w_gate.shape, len(pieces) // 2, pieces[0].shape
    lines = 2 * groups * total_rows
    far_pieces = [swap(piece, "sec", 1) for piece in pieces]
    halves = [shape_of((lines, tps * LANES)), shape_of((lines, hidden), jnp.float32), shape_of((lines, hidden), jnp.float32),
              shape_of((lines, 128), jnp.float32)]
    near = call(near_kernel, "near_columns", halves, gain, w_gate, w_up, *pieces, limit=12, flops=2 * lines * width * hidden)
    other, act, far_x = pl.pallas_call(
        far_kernel,
        name="far_columns",
        out_shape=[shape_of((tps, lines, part)), shape_of((lines, hidden)), halves[0]],
        in_specs=[vmem()] * (8 + len(far_pieces)),
        out_specs=[vmem()] * 3,
        scratch_shapes=[pltpu.VMEM(half.shape, half.dtype) for half in halves[1:]],
        compiler_params=pltpu.CompilerParams(vmem_limit_bytes=16 * MIB),
    )(gain, w_gate, w_up, w_down, *near, *far_pieces)
    come = swap(other, "sec", 1)
    mine, middle = pl.pallas_call(
        last_kernel,
        name="own_columns",
        out_shape=[shape_of((tps, lines, part), jnp.float32), shape_of((total_rows, part), jnp.float32)],
        in_specs=[vmem()] * 4,
        out_specs=[vmem()] * 2,
        scratch_shapes=[pltpu.VMEM((2 * tps, total_rows, part), jnp.float32)],
        compiler_params=pltpu.CompilerParams(vmem_limit_bytes=12 * MIB),
        cost_estimate=pl.CostEstimate(flops=lines * width * hidden, transcendentals=0, bytes_accessed=2 * lines * width),
    )(act, w_down, near[0], far_x)
    return mine, come, middle


def every_expert_body(inputs, attention_gain, w_query, key_value_weight, head_sink_logits, w_output, cache_pairs, lengths,
                      expert_gain, w_gate, w_up, w_down, routes, gate_weights):
    secs, tps, groups = lax.axis_size("sec"), lax.axis_size("tp"), lax.axis_size("grp")
    steps, rows, width = inputs.shape
    flat = inputs.reshape(steps * rows, width)
    other, own_x, mix, held = attention_partial(
        flat, attention_gain, w_query, key_value_weight[:, 0], head_sink_logits, w_output, cache_pairs[:, :, 0], lengths,
        routes.swapaxes(1, 2), gate_weights.swapaxes(1, 2), secs, tps)
    come = swap(other, "sec", 1)
    mine = call(own_projection_kernel, "own_projection", shape_of(other.shape, jnp.float32), mix, held, limit=12,
                flops=mix.size * width)
    middle = call(sum_kernel, "sum", shape_of((steps * rows, LANES)), *scatter_shards(mine, come), own_x)
    nearest, second, third = [swap(middle, "grp", m) for m in (1, 2, 3)]
    near_rows = jnp.stack([middle, nearest])
    first_pieces = [near_rows] + shard_swaps([near_rows] * (tps - 1))
    far_rows = jnp.stack([second, third])
    second_pieces = [far_rows] + shard_swaps([far_rows] * (tps - 1))
    part = width // (secs * tps)
    mine, come, own_middle = experts(expert_gain, w_gate[0], w_up[0], w_down[0], second_pieces + first_pieces, part)
    lines = steps * rows
    own, *parts = call(after_core_halves_kernel, "after_core_halves",
                       [shape_of((groups * lines, part), jnp.float32)] + [shape_of((groups // 2 * lines, part))] * 6, mine, come)
    second_come, first_come = shard_swaps(parts[:3]), shard_swaps(parts[3:])
    second, third = call(functools.partial(sum_rows_kernel, line=2 * lines), "sum_far_rows", [shape_of((lines, part))] * 2,
                         own, *second_come)
    third, second = swap(third, "grp", 3), swap(second, "grp", 2)
    own, nearest = call(functools.partial(sum_rows_kernel, line=0), "sum_near_rows",
                        [shape_of((lines, part), jnp.float32), shape_of((lines, part))], own, *first_come)
    return call(sum_kernel, "combine", shape_of((steps, rows, part)), own, third, second, swap(nearest, "grp", 1), own_middle)


def body(*args):
    sizes = lax.axis_size("sec"), lax.axis_size("tp"), lax.axis_size("grp"), args[9].shape[0]
    if sizes == (2, 4, TOP, 1):
        return every_expert_body(*args)
    return general_body(*args)


def solution(mesh):
    placed = (
        P(None, "grp", None),
        P(),
        P(None, ("sec", "tp")),
        P(None, ("sec", "tp"), None),
        P(("sec", "tp")),
        P(("sec", "tp"), None),
        P("grp", None, ("sec", "tp"), None),
        P("grp"),
        P(),
        P("grp", None, ("sec", "tp")),
        P("grp", None, ("sec", "tp")),
        P("grp", ("sec", "tp"), None),
        P(None, "grp", None),
        P(None, "grp", None),
    )
    return jax.shard_map(
        body, mesh=mesh, in_specs=placed, out_specs=P(None, "grp", ("sec", "tp")), check_vma=False
    )
```

```python
import functools
import math

import jax
import jax.numpy as jnp
import numpy as np
from jax import lax
from jax.experimental import pallas as pl
from jax.experimental.pallas import tpu as pltpu
from jax.sharding import PartitionSpec as P

HEAD_SIZE = 64
TOP = 4


def rms_norm(values, scale_row):
    widened = values.astype(jnp.float32)
    scale_factor = lax.rsqrt(jnp.mean(widened * widened, axis=-1, keepdims=True) + 1e-05)
    return (widened * scale_factor * scale_row).astype(jnp.bfloat16)


def rotate(vectors, position):
    half_size = vectors.shape[-1] // 2
    counter = jnp.arange(half_size).astype(jnp.float32)
    frequency = jnp.power(jnp.float32(150000.0), counter * (-2.0 / vectors.shape[-1]))
    angle_table = position * frequency
    cosine = jnp.cos(angle_table)
    sine_table = jnp.sin(angle_table)
    first_half = vectors[..., :half_size]
    second_half = vectors[..., half_size:]
    return jnp.concatenate(
        [
            first_half * cosine - second_half * sine_table,
            first_half * sine_table + second_half * cosine,
        ],
        axis=-1,
    )


def attend(
    normalized_input,
    w_query,
    key_value_weight,
    head_sink_logits,
    w_output,
    cache_pairs,
    lengths,
    step_index,
    fresh_keys,
    fresh_values,
):
    row_count = normalized_input.shape[0]
    kv_heads = key_value_weight.shape[1]
    query = jnp.dot(normalized_input, w_query, preferred_element_type=jnp.float32).reshape(
        row_count, -1, HEAD_SIZE
    )
    cache_entry_pairs = jnp.dot(
        normalized_input,
        key_value_weight.reshape(key_value_weight.shape[0], -1),
        preferred_element_type=jnp.float32,
    ).reshape(row_count, kv_heads, 2 * HEAD_SIZE)
    position = (lengths + step_index).astype(jnp.float32)[:, None, None]
    rotated_rows = rotate(query, position).astype(jnp.bfloat16)
    fresh_keys = fresh_keys + [
        rotate(cache_entry_pairs[..., :HEAD_SIZE], position).astype(jnp.bfloat16)
    ]
    fresh_values = fresh_values + [cache_entry_pairs[..., HEAD_SIZE:].astype(jnp.bfloat16)]
    grouped_queries = rotated_rows.reshape(row_count, kv_heads, -1, HEAD_SIZE)
    new_keys = jnp.stack(fresh_keys, 1)
    new_values = jnp.stack(fresh_values, 1)
    cached = (
        jnp.einsum(
            "rkgd,rjkd->rkgj",
            grouped_queries,
            cache_pairs[..., :HEAD_SIZE],
            preferred_element_type=jnp.float32,
        )
        * 0.125
    )
    valid = (jnp.arange(cache_pairs.shape[1])[None, :] < lengths[:, None])[:, None, None, :]
    cached = jnp.where(valid, cached, -jnp.inf)
    fresh = (
        jnp.einsum("rkgd,rikd->rkgi", grouped_queries, new_keys, preferred_element_type=jnp.float32)
        * 0.125
    )
    sink_row = head_sink_logits.reshape(kv_heads, -1)[None]
    largest = jnp.maximum(jnp.maximum(jnp.max(cached, axis=-1), jnp.max(fresh, axis=-1)), sink_row)
    cached_exp = jnp.exp(cached - largest[..., None])
    fresh_exp = jnp.exp(fresh - largest[..., None])
    denominator = (
        jnp.sum(cached_exp, axis=-1) + jnp.sum(fresh_exp, axis=-1) + jnp.exp(sink_row - largest)
    )
    cached_probs = (cached_exp / denominator[..., None]).astype(jnp.bfloat16)
    fresh_probs = (fresh_exp / denominator[..., None]).astype(jnp.bfloat16)
    mixed = jnp.einsum(
        "rkgj,rjkd->rkgd",
        cached_probs,
        cache_pairs[..., HEAD_SIZE:],
        preferred_element_type=jnp.float32,
    )
    mixed = mixed + jnp.einsum(
        "rkgi,rikd->rkgd", fresh_probs, new_values, preferred_element_type=jnp.float32
    )
    attention_mix = mixed.reshape(row_count, -1).astype(jnp.bfloat16)
    partial_sum = jnp.dot(attention_mix, w_output, preferred_element_type=jnp.float32)
    return (partial_sum, fresh_keys, fresh_values)


def general_body(
    inputs,
    attention_gain,
    w_query,
    key_value_weight,
    head_sink_logits,
    w_output,
    cache_pairs,
    lengths,
    expert_gain,
    w_gate,
    w_up,
    w_down,
    routes,
    gate_weights,
):
    shards = lax.axis_size(("sec", "tp"))
    shard_index = lax.axis_index(("sec", "tp"))
    experts = lax.axis_size("grp") * w_gate.shape[0]
    group_rows = inputs.shape[1]
    width = inputs.shape[2]
    part_width = width // shards
    chosen = max(TOP, experts // 2)
    capacity = group_rows * TOP // chosen
    slot_total = experts * capacity
    gate_matrix = w_gate[0]
    up_matrix = w_up[0]
    down_matrix = w_down[0]
    fresh_keys = []
    fresh_values = []
    results = []
    for step_index in range(inputs.shape[0]):
        normalized_input = rms_norm(inputs[step_index], attention_gain)
        partial_sum, fresh_keys, fresh_values = attend(
            normalized_input,
            w_query,
            key_value_weight,
            head_sink_logits,
            w_output,
            cache_pairs,
            lengths,
            step_index,
            fresh_keys,
            fresh_values,
        )
        summed = lax.psum(partial_sum[None], ("sec", "tp"))
        middle = (inputs[step_index][None].astype(jnp.float32) + summed).astype(jnp.bfloat16)
        route_rows = routes[step_index][None]
        step_count = middle.shape[0]
        expert_in = rms_norm(middle, expert_gain)
        flat_routes = route_rows.reshape(step_count, group_rows * TOP)
        onehot = (flat_routes[..., None] == jnp.arange(experts)[None, None, :]).astype(jnp.int32)
        earlier = jnp.cumsum(onehot, axis=1) - onehot
        slot_index = jnp.sum(earlier * onehot, axis=-1).reshape(step_count, group_rows, TOP)
        target = route_rows * capacity + slot_index
        placed = target[..., None] == jnp.arange(slot_total)[None, None, None, :]
        dispatch_table = jnp.sum(placed.astype(jnp.int32), axis=2).astype(jnp.bfloat16)
        combine_table = jnp.sum(
            jnp.where(placed, gate_weights[step_index][None][..., None], 0.0), axis=2
        )
        outgoing = jnp.einsum(
            "crm,crd->cmd", dispatch_table, expert_in, preferred_element_type=jnp.float32
        )
        outgoing = outgoing.astype(jnp.bfloat16).reshape(step_count, experts, capacity, width)
        arrived = lax.all_to_all(outgoing, "grp", split_axis=1, concat_axis=1, tiled=True)
        gate_h = jnp.einsum(
            "snpd,dh->snph", arrived, gate_matrix, preferred_element_type=jnp.float32
        )
        up_h = jnp.einsum("snpd,dh->snph", arrived, up_matrix, preferred_element_type=jnp.float32)
        act = ((up_h + 1.0) * gate_h * jax.nn.sigmoid(1.702 * gate_h)).astype(jnp.bfloat16)
        partial_out = jnp.einsum(
            "snph,hd->snpd", act, down_matrix, preferred_element_type=jnp.float32
        )
        reduced = lax.psum_scatter(
            partial_out, ("sec", "tp"), scatter_dimension=3, tiled=True
        ).astype(jnp.bfloat16)
        returned = lax.all_to_all(reduced, "grp", split_axis=1, concat_axis=1, tiled=True)
        returned_rows = returned.reshape(step_count, slot_total, part_width).astype(jnp.float32)
        weighted = jnp.einsum(
            "srm,smd->srd", combine_table, returned_rows, precision=lax.Precision.HIGHEST
        )
        own_middle = lax.dynamic_slice_in_dim(
            middle, shard_index * part_width, part_width, 2
        ).astype(jnp.float32)
        results.append((own_middle + weighted).astype(jnp.bfloat16)[0])
    return jnp.stack(results, 0)


LANES = 384
BASE = 150000.0
MIB = 1 << 20


def shape_of(shape, dtype=jnp.bfloat16):
    return jax.ShapeDtypeStruct(shape, dtype)


def vmem():
    return pl.BlockSpec(memory_space=pltpu.VMEM)


def smem():
    return pl.BlockSpec(memory_space=pltpu.SMEM)


def outside():
    return pl.BlockSpec(memory_space=pltpu.HBM)


def dot_last(left, right):
    return lax.dot_general(left, right, (((1,), (1,)), ((), ())), preferred_element_type=jnp.float32)


def swap(value, axes, mask):
    size = lax.axis_size(axes)
    return lax.ppermute(value, axes, [(i, i ^ mask) for i in range(size)])


def swap_by_core(value, axis, masks):
    size = lax.axis_size(axis)
    pairs = [(s * size + i, s * size + (i ^ masks[s])) for s in range(2) for i in range(size)]
    return lax.ppermute(value, ("sec", axis), pairs)


def shard_swaps(parts):
    return [swap_by_core(part, "tp", masks) for part, masks in zip(parts, ((3, 3), (1, 2), (2, 1)))]


def shard_masks():
    sec = lax.axis_index("sec")
    return 3, 1 + sec, 2 - sec


def split_width(width):
    cuts = list(range(0, width, 768)) + [width]
    return list(zip(cuts[:-1], cuts[1:]))


def attention_kernel(lengths_hbm, sinks_hbm, routes_hbm, weights_hbm, gain_hbm, x_hbm, wq_hbm, wkv_hbm, cache_hbm, wo_hbm,
                     other_ref, own_x_ref, mix_ref, wo_ref,
                     lengths_ref, sinks_ref, routes_ref, weights_ref, gain_ref, x_ref, wq_ref, wkv_ref, cache_ref,
                     xs_ref, turned_ref, mixed_ref, sems):
    total_rows, width = x_ref.shape
    rows, slots, pair = cache_ref.shape
    steps = total_rows // rows
    heads = wq_ref.shape[1] // HEAD_SIZE
    per_row = heads * steps
    tps = other_ref.shape[0]
    cuts = split_width(width)
    small = [(lengths_hbm, lengths_ref), (x_hbm, x_ref), (gain_hbm, gain_ref), (routes_hbm, routes_ref), (weights_hbm, weights_ref),
             (sinks_hbm, sinks_ref)]
    small = [pltpu.make_async_copy(source, target, sems.at[n]) for n, (source, target) in enumerate(small)]
    copies = [pltpu.make_async_copy(wkv_hbm, wkv_ref, sems.at[6])]
    for n, (low, high) in enumerate(cuts):
        part = pl.ds(low, high - low)
        copies.append(pltpu.make_async_copy(wq_hbm.at[part], wq_ref.at[part], sems.at[9 + n]))
    copies.append(pltpu.make_async_copy(cache_hbm, cache_ref, sems.at[7]))
    copies.append(pltpu.make_async_copy(wo_hbm, wo_ref, sems.at[8]))
    for copy in small + copies:
        copy.start()
    small[0].wait()

    lane = lax.broadcasted_iota(jnp.int32, (total_rows, pair), 1)
    line = lax.broadcasted_iota(jnp.int32, (total_rows, pair), 0)
    position = jnp.zeros((total_rows, pair), jnp.int32)
    for r in range(rows):
        for s in range(steps):
            position = jnp.where(line == s * rows + r, lengths_ref[r] + s, position)
    half = HEAD_SIZE // 2
    counter = jnp.bitwise_and(lane, half - 1).astype(jnp.float32)
    frequency = jnp.exp(counter * jnp.float32(-2.0 / HEAD_SIZE * np.log(BASE)))
    angle = position.astype(jnp.float32) * frequency
    cosine, sine = jnp.cos(angle), jnp.sin(angle)
    low_half = jnp.bitwise_and(lane, HEAD_SIZE - 1) < half
    sine = jnp.where(low_half, -sine, sine)

    def turn(two):
        return two * cosine + jnp.where(low_half, pltpu.roll(two, pair - half, 1), pltpu.roll(two, half, 1)) * sine

    for copy in small[1:]:
        copy.wait()
    spare = xs_ref.shape[1] - width
    spare_at = lax.broadcasted_iota(jnp.int32, (rows, spare), 1)
    corner = lax.broadcasted_iota(jnp.int32, (rows, rows), 0) == lax.broadcasted_iota(jnp.int32, (rows, rows), 1)
    tables = []
    for s in range(steps):
        table = jnp.zeros((rows, spare), jnp.float32)
        for e in range(TOP):
            across = jnp.sum(jnp.where(routes_ref[s] == e, weights_ref[s], 0.0), axis=0, keepdims=True)
            column = jnp.sum(jnp.where(corner, across, 0.0), axis=1, keepdims=True)
            high_part = column.astype(jnp.bfloat16).astype(jnp.float32)
            table = jnp.where(spare_at == 2 * e, high_part, jnp.where(spare_at == 2 * e + 1, column - high_part, table))
        tables.append(table)
    x = x_ref[...].astype(jnp.float32)
    xs_ref[...] = jnp.concatenate([x, jnp.concatenate(tables, axis=0)], axis=1)
    own = (lax.axis_index("sec") * tps + lax.axis_index("tp")) * LANES
    own_x_ref[...] = xs_ref[:, pl.ds(pl.multiple_of(own, LANES), LANES)]
    scale = lax.rsqrt(jnp.mean(x * x, axis=-1, keepdims=True) + 1e-05)
    normed = (x * scale * gain_ref[...].reshape(1, width)).astype(jnp.bfloat16)
    copies[0].wait()
    pairs = jnp.dot(normed, wkv_ref[...], preferred_element_type=jnp.float32)
    query = None
    for n, (low, high) in enumerate(cuts):
        copies[1 + n].wait()
        term = jnp.dot(normed[:, low:high], wq_ref[low:high, :], preferred_element_type=jnp.float32)
        query = term if query is None else query + term

    is_key = lane < HEAD_SIZE
    fresh = jnp.where(is_key, turn(pairs), pairs).astype(jnp.bfloat16)
    for m in range(heads // 2):
        two = turn(query[:, m * pair:(m + 1) * pair])
        for odd in range(2):
            one = two if odd == 0 else pltpu.roll(two, HEAD_SIZE, 1)
            one = jnp.where(is_key, one, 0.0)
            for s in range(steps):
                slot = (2 * m + odd) * steps + s
                turned_ref[pl.ds(slot, rows, stride=per_row), :] = one[s * rows:(s + 1) * rows]
    turned = turned_ref[...].astype(jnp.bfloat16)

    copies[-2].wait()
    place = lax.broadcasted_iota(jnp.int32, (per_row, slots), 1)
    scores = []
    for r in range(rows):
        score = dot_last(turned[r * per_row:(r + 1) * per_row], cache_ref[r]) * 0.125
        scores.append(jnp.where(place < lengths_ref[r], score, -jnp.inf))
    cached = jnp.concatenate(scores, axis=0)
    row_at = lax.broadcasted_iota(jnp.int32, (rows * per_row, total_rows), 0)
    fresh_at = lax.broadcasted_iota(jnp.int32, (rows * per_row, total_rows), 1)
    seen = (row_at // per_row == fresh_at % rows) & (fresh_at // rows <= row_at % steps)
    new = jnp.where(seen, dot_last(turned, fresh) * 0.125, -jnp.inf)
    head_at = lax.broadcasted_iota(jnp.int32, (rows * per_row, 1), 0) % per_row // steps
    sink = jnp.zeros((rows * per_row, 1), jnp.float32)
    for h in range(heads):
        sink = jnp.where(head_at == h, sinks_ref[h], sink)
    largest = jnp.maximum(jnp.maximum(jnp.max(cached, axis=-1, keepdims=True), jnp.max(new, axis=-1, keepdims=True)), sink)
    cached = jnp.exp(cached - largest)
    new = jnp.exp(new - largest)
    total = jnp.sum(cached, axis=-1, keepdims=True) + jnp.sum(new, axis=-1, keepdims=True) + jnp.exp(sink - largest)
    share = 1.0 / total
    cached = (cached * share).astype(jnp.bfloat16)
    new = (new * share).astype(jnp.bfloat16)
    mixed = []
    for r in range(rows):
        mixed.append(jnp.dot(cached[r * per_row:(r + 1) * per_row], cache_ref[r], preferred_element_type=jnp.float32))
    mixed_ref[...] = jnp.concatenate(mixed, axis=0) + jnp.dot(new, fresh, preferred_element_type=jnp.float32)

    def head(h):
        return jnp.concatenate([mixed_ref[pl.ds(h * steps + s, rows, stride=per_row), :] for s in range(steps)], axis=0)

    mix_ref[...] = jnp.concatenate(
        [jnp.where(is_key, pltpu.roll(head(2 * m), HEAD_SIZE, 1), head(2 * m + 1)) for m in range(heads // 2)], axis=1
    ).astype(jnp.bfloat16)
    copies[-1].wait()
    project(mix_ref, wo_ref, other_ref, 1 - lax.axis_index("sec"))


def project(mix_ref, wo_ref, out_ref, side):
    width, (tps, total_rows, _) = wo_ref.shape[0], out_ref.shape
    for at in range(2):
        start, stop = at * tps * LANES, min((at + 1) * tps * LANES, width)

        @pl.when(side == at)
        def _(start=start, stop=stop):
            partial = dot_last(mix_ref[...], wo_ref[start:stop, :])
            for t in range(tps):
                low, high = t * LANES, min((t + 1) * LANES, stop - start)
                piece = partial[:, low:high]
                if high - low < LANES:
                    piece = jnp.concatenate([piece, jnp.zeros((total_rows, LANES - (high - low)), jnp.float32)], axis=1)
                out_ref[t] = piece.astype(out_ref.dtype)


def own_projection_kernel(mix_ref, wo_ref, mine_ref):
    project(mix_ref, wo_ref, mine_ref, lax.axis_index("sec"))


def attention_partial(flat, gain, w_query, key_value, sinks, w_output, cache, lengths, routes, weights, secs, tps):
    total_rows, width = flat.shape
    rows, slots, pair = cache.shape
    per_row = w_query.shape[1] // HEAD_SIZE * (total_rows // rows)
    shards = secs * tps
    operands = (lengths, sinks, routes, weights, gain, flat, w_query, key_value, cache, w_output.swapaxes(0, 1))
    return pl.pallas_call(
        attention_kernel,
        name="attention",
        out_shape=[shape_of((tps, total_rows, LANES)), shape_of((total_rows, LANES), jnp.float32),
                   shape_of((total_rows, w_output.shape[0])), shape_of((width, w_output.shape[0]))],
        in_specs=[outside()] * len(operands),
        out_specs=[vmem()] * 4,
        scratch_shapes=[
            pltpu.SMEM(lengths.shape, jnp.int32),
            pltpu.SMEM(sinks.shape, jnp.float32),
            pltpu.VMEM(routes.shape, jnp.int32),
            pltpu.VMEM(weights.shape, jnp.float32),
            pltpu.VMEM(gain.shape, jnp.float32),
            pltpu.VMEM((total_rows, width), jnp.bfloat16),
            pltpu.VMEM(w_query.shape, jnp.bfloat16),
            pltpu.VMEM(key_value.shape, jnp.bfloat16),
            pltpu.VMEM(cache.shape, jnp.bfloat16),
            pltpu.VMEM((total_rows, shards * LANES), jnp.float32),
            pltpu.VMEM((rows * per_row, pair), jnp.float32),
            pltpu.VMEM((rows * per_row, pair), jnp.float32),
            pltpu.SemaphoreType.DMA((9 + len(split_width(width)),)),
        ],
        compiler_params=pltpu.CompilerParams(vmem_limit_bytes=24 * MIB),
    )(*[pltpu.with_memory_space_constraint(operand, pltpu.HBM) for operand in operands])


def call(kernel, name, outs, *operands, limit=4, flops=0):
    single = not isinstance(outs, list)
    held = [*operands, *([outs] if single else outs)]
    return pl.pallas_call(
        kernel,
        name=name,
        out_shape=outs,
        in_specs=[vmem()] * len(operands),
        out_specs=vmem() if single else [vmem()] * len(outs),
        compiler_params=pltpu.CompilerParams(vmem_limit_bytes=limit * MIB),
        cost_estimate=pl.CostEstimate(flops=flops, transcendentals=0,
                                      bytes_accessed=sum(math.prod(a.shape) * a.dtype.itemsize for a in held)),
    )(*operands)


def after_core_kernel(mine_ref, come_ref, own_ref, *send_refs):
    tp = lax.axis_index("tp")
    own_ref[...] = mine_ref[tp] + come_ref[tp].astype(jnp.float32)
    for mask, ref in zip(shard_masks(), send_refs):
        to = jnp.bitwise_xor(tp, mask)
        ref[...] = (mine_ref[to] + come_ref[to].astype(jnp.float32)).astype(jnp.bfloat16)


def after_core_halves_kernel(mine_ref, come_ref, own_ref, *send_refs):
    tp, half = lax.axis_index("tp"), mine_ref.shape[1] // 2
    own_ref[...] = mine_ref[tp] + come_ref[tp].astype(jnp.float32)
    for mask, second, first in zip(shard_masks(), send_refs[:3], send_refs[3:]):
        to = jnp.bitwise_xor(tp, mask)
        part = (mine_ref[to] + come_ref[to].astype(jnp.float32)).astype(jnp.bfloat16)
        second[...] = part[half:]
        first[...] = part[:half]


def add_all(*refs):
    total = refs[0][...]
    for ref in refs[1:]:
        total = total + ref[...].astype(jnp.float32)
    return total


def sum_kernel(*refs):
    refs[-1][...] = add_all(*refs[:-1]).astype(jnp.bfloat16).reshape(refs[-1].shape)


def sum_rows_kernel(own_ref, *refs, line):
    come, outs = refs[:3], refs[3:]
    lines = outs[0].shape[0]
    total = own_ref[line:line + len(outs) * lines]
    for ref in come:
        total = total + ref[...].astype(jnp.float32)
    for n, out in enumerate(outs):
        out[...] = total[n * lines:(n + 1) * lines].astype(out.dtype)


def scatter_shards(mine, come):
    tps, lines, part = mine.shape
    own, *parts = call(after_core_kernel, "after_core", [shape_of((lines, part), jnp.float32)] + [shape_of((lines, part))] * (tps - 1),
                       mine, come)
    return [own] + shard_swaps(parts)


def first_products(pieces, masks, side, x_ref, gain_ref, gate_ref, up_ref, gate_out, up_out, square_out):
    width, lines = gate_ref.shape[1], x_ref.shape[0]
    tp = lax.axis_index("tp")
    for mask, piece in zip(masks, pieces):
        at = pl.multiple_of(jnp.bitwise_xor(tp, mask) * LANES, LANES)
        x_ref[:, pl.ds(at, LANES)] = piece[...].reshape(lines, LANES)
    for at in range(2):
        start, stop = at * x_ref.shape[1], min((at + 1) * x_ref.shape[1], width)

        @pl.when(side == at)
        def _(start=start, stop=stop):
            x = x_ref[:, :stop - start].astype(jnp.float32)
            square_out[...] = jnp.broadcast_to(jnp.sum(x * x, axis=-1, keepdims=True), square_out.shape)
            scaled = (x * gain_ref[:, start:stop]).astype(jnp.bfloat16)
            gate_out[...] = dot_last(scaled, gate_ref[:, start:stop])
            up_out[...] = dot_last(scaled, up_ref[:, start:stop])


def near_kernel(gain_ref, gate_ref, up_ref, *refs):
    pieces, (x_ref, gate_out, up_out, square_out) = refs[:-4], refs[-4:]
    first_products(pieces, (0, *shard_masks()), lax.axis_index("sec"), x_ref, gain_ref, gate_ref, up_ref, gate_out, up_out,
                   square_out)


def second_product(act_ref, down_ref, out_ref, side):
    width, (tps, lines, part) = down_ref.shape[1], out_ref.shape
    for at in range(2):
        start, stop = at * tps * part, (at + 1) * tps * part
        shift = start % 128

        @pl.when(side == at)
        def _(start=start, stop=stop, shift=shift):
            out = jnp.dot(act_ref[...], down_ref[:, start - shift:stop], preferred_element_type=jnp.float32)
            for t in range(tps):
                out_ref[t] = out[:, shift + t * part:shift + (t + 1) * part].astype(out_ref.dtype)


def far_kernel(gain_ref, gate_ref, up_ref, down_ref, near_x_ref, near_gate_ref, near_up_ref, near_square_ref, *refs):
    pieces, (other_ref, act_ref, far_x_ref, gate_out, up_out, square_out) = refs[:-6], refs[-6:]
    sec, grp = lax.axis_index("sec"), lax.axis_index("grp")
    masks = shard_masks()
    first_products(pieces, (0, masks[0], masks[2], masks[1]), 1 - sec, far_x_ref, gain_ref, gate_ref, up_ref, gate_out, up_out,
                   square_out)
    width, half = gate_ref.shape[1], near_x_ref.shape[1]
    spare = jnp.where(sec == 1, near_x_ref[:, width - half:], far_x_ref[:, width - half:]).astype(jnp.float32)
    spare_at = lax.broadcasted_iota(jnp.int32, spare.shape, 1)
    weight = jnp.sum(jnp.where((spare_at == 2 * grp) | (spare_at == 2 * grp + 1), spare, 0.0), axis=1, keepdims=True)
    square = (near_square_ref[...] + square_out[...])[:, :1]
    scale = lax.rsqrt(square / width + 1e-05)
    gate_h = (near_gate_ref[...] + gate_out[...]) * scale
    up_h = (near_up_ref[...] + up_out[...]) * scale
    act_ref[...] = ((up_h + 1.0) * gate_h * jax.nn.sigmoid(1.702 * gate_h) * weight).astype(jnp.bfloat16)
    second_product(act_ref, down_ref, other_ref, 1 - sec)


def last_kernel(act_ref, down_ref, near_x_ref, far_x_ref, mine_ref, middle_ref, row_ref):
    sec, tp = lax.axis_index("sec"), lax.axis_index("tp")
    second_product(act_ref, down_ref, mine_ref, sec)
    total_rows, part = middle_ref.shape
    near, far = near_x_ref[:total_rows].astype(jnp.float32), far_x_ref[:total_rows].astype(jnp.float32)
    first = sec == 0
    x = jnp.concatenate([jnp.where(first, near, far), jnp.where(first, far, near)], axis=1)
    for c in range(row_ref.shape[0]):
        row_ref[c] = x[:, c * part:(c + 1) * part]
    middle_ref[...] = row_ref[sec * mine_ref.shape[0] + tp]


def experts(gain, w_gate, w_up, w_down, pieces, part):
    gain, w_gate, w_up = gain.reshape(1, -1), w_gate.swapaxes(0, 1), w_up.swapaxes(0, 1)
    (hidden, width), tps, (groups, total_rows, _) = w_gate.shape, len(pieces), pieces[0].shape
    lines = groups * total_rows
    far_pieces = [swap(piece, "sec", 1) for piece in pieces]
    halves = [shape_of((lines, tps * LANES)), shape_of((lines, hidden), jnp.float32), shape_of((lines, hidden), jnp.float32),
              shape_of((lines, 128), jnp.float32)]
    near = call(near_kernel, "near_columns", halves, gain, w_gate, w_up, *pieces, limit=12, flops=2 * lines * width * hidden)
    other, act, far_x = pl.pallas_call(
        far_kernel,
        name="far_columns",
        out_shape=[shape_of((tps, lines, part)), shape_of((lines, hidden)), halves[0]],
        in_specs=[vmem()] * (8 + len(far_pieces)),
        out_specs=[vmem()] * 3,
        scratch_shapes=[pltpu.VMEM(half.shape, half.dtype) for half in halves[1:]],
        compiler_params=pltpu.CompilerParams(vmem_limit_bytes=16 * MIB),
    )(gain, w_gate, w_up, w_down, *near, *far_pieces)
    come = swap(other, "sec", 1)
    mine, middle = pl.pallas_call(
        last_kernel,
        name="own_columns",
        out_shape=[shape_of((tps, lines, part), jnp.float32), shape_of((total_rows, part), jnp.float32)],
        in_specs=[vmem()] * 4,
        out_specs=[vmem()] * 2,
        scratch_shapes=[pltpu.VMEM((2 * tps, total_rows, part), jnp.float32)],
        compiler_params=pltpu.CompilerParams(vmem_limit_bytes=12 * MIB),
        cost_estimate=pl.CostEstimate(flops=lines * width * hidden, transcendentals=0, bytes_accessed=2 * lines * width),
    )(act, w_down, near[0], far_x)
    return mine, come, middle


def every_expert_body(inputs, attention_gain, w_query, key_value_weight, head_sink_logits, w_output, cache_pairs, lengths,
                      expert_gain, w_gate, w_up, w_down, routes, gate_weights):
    secs, tps, groups = lax.axis_size("sec"), lax.axis_size("tp"), lax.axis_size("grp")
    steps, rows, width = inputs.shape
    flat = inputs.reshape(steps * rows, width)
    other, own_x, mix, held = attention_partial(
        flat, attention_gain, w_query, key_value_weight[:, 0], head_sink_logits, w_output, cache_pairs[:, :, 0], lengths,
        routes.swapaxes(1, 2), gate_weights.swapaxes(1, 2), secs, tps)
    come = swap(other, "sec", 1)
    mine = call(own_projection_kernel, "own_projection", shape_of(other.shape, jnp.float32), mix, held, limit=12,
                flops=mix.size * width)
    middle = call(sum_kernel, "sum", shape_of((steps * rows, LANES)), *scatter_shards(mine, come), own_x)
    stacked = jnp.stack([middle] + [swap(middle, "grp", m) for m in range(1, groups)])
    pieces = [stacked] + shard_swaps([stacked] * (tps - 1))
    part = width // (secs * tps)
    mine, come, own_middle = experts(expert_gain, w_gate[0], w_up[0], w_down[0], pieces, part)
    lines = steps * rows
    own, *parts = call(after_core_halves_kernel, "after_core_halves",
                       [shape_of((groups * lines, part), jnp.float32)] + [shape_of((groups // 2 * lines, part))] * 6, mine, come)
    second_come, first_come = shard_swaps(parts[:3]), shard_swaps(parts[3:])
    second, third = call(functools.partial(sum_rows_kernel, line=2 * lines), "sum_far_rows", [shape_of((lines, part))] * 2,
                         own, *second_come)
    third, second = swap(third, "grp", 3), swap(second, "grp", 2)
    own, nearest = call(functools.partial(sum_rows_kernel, line=0), "sum_near_rows",
                        [shape_of((lines, part), jnp.float32), shape_of((lines, part))], own, *first_come)
    return call(sum_kernel, "combine", shape_of((steps, rows, part)), own, third, second, swap(nearest, "grp", 1), own_middle)


def body(*args):
    sizes = lax.axis_size("sec"), lax.axis_size("tp"), lax.axis_size("grp"), args[9].shape[0]
    if sizes == (2, 4, TOP, 1):
        return every_expert_body(*args)
    return general_body(*args)


def solution(mesh):
    placed = (
        P(None, "grp", None),
        P(),
        P(None, ("sec", "tp")),
        P(None, ("sec", "tp"), None),
        P(("sec", "tp")),
        P(("sec", "tp"), None),
        P("grp", None, ("sec", "tp"), None),
        P("grp"),
        P(),
        P("grp", None, ("sec", "tp")),
        P("grp", None, ("sec", "tp")),
        P("grp", ("sec", "tp"), None),
        P(None, "grp", None),
        P(None, "grp", None),
    )
    return jax.shard_map(
        body, mesh=mesh, in_specs=placed, out_specs=P(None, "grp", ("sec", "tp")), check_vma=False
    )
```

```python
import functools
import math

import jax
import jax.numpy as jnp
import numpy as np
from jax import lax
from jax.experimental import pallas as pl
from jax.experimental.pallas import tpu as pltpu
from jax.sharding import PartitionSpec as P

HEAD_SIZE = 64
TOP = 4


def rms_norm(values, scale_row):
    widened = values.astype(jnp.float32)
    scale_factor = lax.rsqrt(jnp.mean(widened * widened, axis=-1, keepdims=True) + 1e-05)
    return (widened * scale_factor * scale_row).astype(jnp.bfloat16)


def rotate(vectors, position):
    half_size = vectors.shape[-1] // 2
    counter = jnp.arange(half_size).astype(jnp.float32)
    frequency = jnp.power(jnp.float32(150000.0), counter * (-2.0 / vectors.shape[-1]))
    angle_table = position * frequency
    cosine = jnp.cos(angle_table)
    sine_table = jnp.sin(angle_table)
    first_half = vectors[..., :half_size]
    second_half = vectors[..., half_size:]
    return jnp.concatenate(
        [
            first_half * cosine - second_half * sine_table,
            first_half * sine_table + second_half * cosine,
        ],
        axis=-1,
    )


def attend(
    normalized_input,
    w_query,
    key_value_weight,
    head_sink_logits,
    w_output,
    cache_pairs,
    lengths,
    step_index,
    fresh_keys,
    fresh_values,
):
    row_count = normalized_input.shape[0]
    kv_heads = key_value_weight.shape[1]
    query = jnp.dot(normalized_input, w_query, preferred_element_type=jnp.float32).reshape(
        row_count, -1, HEAD_SIZE
    )
    cache_entry_pairs = jnp.dot(
        normalized_input,
        key_value_weight.reshape(key_value_weight.shape[0], -1),
        preferred_element_type=jnp.float32,
    ).reshape(row_count, kv_heads, 2 * HEAD_SIZE)
    position = (lengths + step_index).astype(jnp.float32)[:, None, None]
    rotated_rows = rotate(query, position).astype(jnp.bfloat16)
    fresh_keys = fresh_keys + [
        rotate(cache_entry_pairs[..., :HEAD_SIZE], position).astype(jnp.bfloat16)
    ]
    fresh_values = fresh_values + [cache_entry_pairs[..., HEAD_SIZE:].astype(jnp.bfloat16)]
    grouped_queries = rotated_rows.reshape(row_count, kv_heads, -1, HEAD_SIZE)
    new_keys = jnp.stack(fresh_keys, 1)
    new_values = jnp.stack(fresh_values, 1)
    cached = (
        jnp.einsum(
            "rkgd,rjkd->rkgj",
            grouped_queries,
            cache_pairs[..., :HEAD_SIZE],
            preferred_element_type=jnp.float32,
        )
        * 0.125
    )
    valid = (jnp.arange(cache_pairs.shape[1])[None, :] < lengths[:, None])[:, None, None, :]
    cached = jnp.where(valid, cached, -jnp.inf)
    fresh = (
        jnp.einsum("rkgd,rikd->rkgi", grouped_queries, new_keys, preferred_element_type=jnp.float32)
        * 0.125
    )
    sink_row = head_sink_logits.reshape(kv_heads, -1)[None]
    largest = jnp.maximum(jnp.maximum(jnp.max(cached, axis=-1), jnp.max(fresh, axis=-1)), sink_row)
    cached_exp = jnp.exp(cached - largest[..., None])
    fresh_exp = jnp.exp(fresh - largest[..., None])
    denominator = (
        jnp.sum(cached_exp, axis=-1) + jnp.sum(fresh_exp, axis=-1) + jnp.exp(sink_row - largest)
    )
    cached_probs = (cached_exp / denominator[..., None]).astype(jnp.bfloat16)
    fresh_probs = (fresh_exp / denominator[..., None]).astype(jnp.bfloat16)
    mixed = jnp.einsum(
        "rkgj,rjkd->rkgd",
        cached_probs,
        cache_pairs[..., HEAD_SIZE:],
        preferred_element_type=jnp.float32,
    )
    mixed = mixed + jnp.einsum(
        "rkgi,rikd->rkgd", fresh_probs, new_values, preferred_element_type=jnp.float32
    )
    attention_mix = mixed.reshape(row_count, -1).astype(jnp.bfloat16)
    partial_sum = jnp.dot(attention_mix, w_output, preferred_element_type=jnp.float32)
    return (partial_sum, fresh_keys, fresh_values)


def general_body(
    inputs,
    attention_gain,
    w_query,
    key_value_weight,
    head_sink_logits,
    w_output,
    cache_pairs,
    lengths,
    expert_gain,
    w_gate,
    w_up,
    w_down,
    routes,
    gate_weights,
):
    shards = lax.axis_size(("sec", "tp"))
    shard_index = lax.axis_index(("sec", "tp"))
    experts = lax.axis_size("grp") * w_gate.shape[0]
    group_rows = inputs.shape[1]
    width = inputs.shape[2]
    part_width = width // shards
    chosen = max(TOP, experts // 2)
    capacity = group_rows * TOP // chosen
    slot_total = experts * capacity
    gate_matrix = w_gate[0]
    up_matrix = w_up[0]
    down_matrix = w_down[0]
    fresh_keys = []
    fresh_values = []
    results = []
    for step_index in range(inputs.shape[0]):
        normalized_input = rms_norm(inputs[step_index], attention_gain)
        partial_sum, fresh_keys, fresh_values = attend(
            normalized_input,
            w_query,
            key_value_weight,
            head_sink_logits,
            w_output,
            cache_pairs,
            lengths,
            step_index,
            fresh_keys,
            fresh_values,
        )
        summed = lax.psum(partial_sum[None], ("sec", "tp"))
        middle = (inputs[step_index][None].astype(jnp.float32) + summed).astype(jnp.bfloat16)
        route_rows = routes[step_index][None]
        step_count = middle.shape[0]
        expert_in = rms_norm(middle, expert_gain)
        flat_routes = route_rows.reshape(step_count, group_rows * TOP)
        onehot = (flat_routes[..., None] == jnp.arange(experts)[None, None, :]).astype(jnp.int32)
        earlier = jnp.cumsum(onehot, axis=1) - onehot
        slot_index = jnp.sum(earlier * onehot, axis=-1).reshape(step_count, group_rows, TOP)
        target = route_rows * capacity + slot_index
        placed = target[..., None] == jnp.arange(slot_total)[None, None, None, :]
        dispatch_table = jnp.sum(placed.astype(jnp.int32), axis=2).astype(jnp.bfloat16)
        combine_table = jnp.sum(
            jnp.where(placed, gate_weights[step_index][None][..., None], 0.0), axis=2
        )
        outgoing = jnp.einsum(
            "crm,crd->cmd", dispatch_table, expert_in, preferred_element_type=jnp.float32
        )
        outgoing = outgoing.astype(jnp.bfloat16).reshape(step_count, experts, capacity, width)
        arrived = lax.all_to_all(outgoing, "grp", split_axis=1, concat_axis=1, tiled=True)
        gate_h = jnp.einsum(
            "snpd,dh->snph", arrived, gate_matrix, preferred_element_type=jnp.float32
        )
        up_h = jnp.einsum("snpd,dh->snph", arrived, up_matrix, preferred_element_type=jnp.float32)
        act = ((up_h + 1.0) * gate_h * jax.nn.sigmoid(1.702 * gate_h)).astype(jnp.bfloat16)
        partial_out = jnp.einsum(
            "snph,hd->snpd", act, down_matrix, preferred_element_type=jnp.float32
        )
        reduced = lax.psum_scatter(
            partial_out, ("sec", "tp"), scatter_dimension=3, tiled=True
        ).astype(jnp.bfloat16)
        returned = lax.all_to_all(reduced, "grp", split_axis=1, concat_axis=1, tiled=True)
        returned_rows = returned.reshape(step_count, slot_total, part_width).astype(jnp.float32)
        weighted = jnp.einsum(
            "srm,smd->srd", combine_table, returned_rows, precision=lax.Precision.HIGHEST
        )
        own_middle = lax.dynamic_slice_in_dim(
            middle, shard_index * part_width, part_width, 2
        ).astype(jnp.float32)
        results.append((own_middle + weighted).astype(jnp.bfloat16)[0])
    return jnp.stack(results, 0)


LANES = 768
BASE = 150000.0
MIB = 1 << 20
SHARD_MASKS = (3, 1, 2)


def shape_of(shape, dtype=jnp.bfloat16):
    return jax.ShapeDtypeStruct(shape, dtype)


def vmem():
    return pl.BlockSpec(memory_space=pltpu.VMEM)


def smem():
    return pl.BlockSpec(memory_space=pltpu.SMEM)


def outside():
    return pl.BlockSpec(memory_space=pltpu.HBM)


def dot_last(left, right):
    return lax.dot_general(left, right, (((1,), (1,)), ((), ())), preferred_element_type=jnp.float32)


def swap(value, axis, mask):
    size = lax.axis_size(axis)
    return lax.ppermute(value, ("sec", axis), [(size + i, size + (i ^ mask)) for i in range(size)])


def shard_swaps(parts):
    return [swap(part, "tp", mask) for part, mask in zip(parts, SHARD_MASKS)]


def hand_over(value, to):
    return lax.ppermute(value, "sec", [(1 - to, to)])


def split_width(width):
    cuts = list(range(0, width, 768)) + [width]
    return list(zip(cuts[:-1], cuts[1:]))


def attention_kernel(lengths_hbm, sinks_hbm, routes_hbm, weights_hbm, gain_hbm, x_hbm, wq_hbm, wkv_hbm, cache_hbm, wo_hbm,
                     keep_ref, send_ref, own_x_ref,
                     lengths_ref, sinks_ref, routes_ref, weights_ref, gain_ref, x_ref, wq_ref, wkv_ref, cache_ref, wo_ref,
                     xs_ref, turned_ref, mixed_ref, sems):
    total_rows, width = x_ref.shape
    rows, slots, pair = cache_ref.shape
    steps = total_rows // rows
    heads = wq_ref.shape[1] // HEAD_SIZE
    per_row = heads * steps
    tps = keep_ref.shape[0]
    cuts = split_width(width)
    small = [(lengths_hbm, lengths_ref), (x_hbm, x_ref), (gain_hbm, gain_ref), (routes_hbm, routes_ref), (weights_hbm, weights_ref),
             (sinks_hbm, sinks_ref)]
    small = [pltpu.make_async_copy(source, target, sems.at[n]) for n, (source, target) in enumerate(small)]
    copies = [pltpu.make_async_copy(wkv_hbm, wkv_ref, sems.at[6])]
    for n, (low, high) in enumerate(cuts):
        part = pl.ds(low, high - low)
        copies.append(pltpu.make_async_copy(wq_hbm.at[part], wq_ref.at[part], sems.at[9 + n]))
    copies.append(pltpu.make_async_copy(cache_hbm, cache_ref, sems.at[7]))
    copies.append(pltpu.make_async_copy(wo_hbm, wo_ref, sems.at[8]))
    for copy in small + copies:
        copy.start()
    small[0].wait()

    lane = lax.broadcasted_iota(jnp.int32, (total_rows, pair), 1)
    line = lax.broadcasted_iota(jnp.int32, (total_rows, pair), 0)
    position = jnp.zeros((total_rows, pair), jnp.int32)
    for r in range(rows):
        for s in range(steps):
            position = jnp.where(line == s * rows + r, lengths_ref[r] + s, position)
    half = HEAD_SIZE // 2
    counter = jnp.bitwise_and(lane, half - 1).astype(jnp.float32)
    frequency = jnp.exp(counter * jnp.float32(-2.0 / HEAD_SIZE * np.log(BASE)))
    angle = position.astype(jnp.float32) * frequency
    cosine, sine = jnp.cos(angle), jnp.sin(angle)
    low_half = jnp.bitwise_and(lane, HEAD_SIZE - 1) < half
    sine = jnp.where(low_half, -sine, sine)

    def turn(two):
        return two * cosine + jnp.where(low_half, pltpu.roll(two, pair - half, 1), pltpu.roll(two, half, 1)) * sine

    for copy in small[1:]:
        copy.wait()
    spare = xs_ref.shape[1] - width
    spare_at = lax.broadcasted_iota(jnp.int32, (rows, spare), 1)
    corner = lax.broadcasted_iota(jnp.int32, (rows, rows), 0) == lax.broadcasted_iota(jnp.int32, (rows, rows), 1)
    tables = []
    for s in range(steps):
        table = jnp.zeros((rows, spare), jnp.float32)
        for e in range(TOP):
            across = jnp.sum(jnp.where(routes_ref[s] == e, weights_ref[s], 0.0), axis=0, keepdims=True)
            column = jnp.sum(jnp.where(corner, across, 0.0), axis=1, keepdims=True)
            high_part = column.astype(jnp.bfloat16).astype(jnp.float32)
            table = jnp.where(spare_at == 2 * e, high_part, jnp.where(spare_at == 2 * e + 1, column - high_part, table))
        tables.append(table)
    x = x_ref[...].astype(jnp.float32)
    xs_ref[...] = jnp.concatenate([x, jnp.concatenate(tables, axis=0)], axis=1)
    own = lax.axis_index("tp") * LANES
    own_x_ref[...] = xs_ref[:, pl.ds(pl.multiple_of(own, LANES), LANES)]
    scale = lax.rsqrt(jnp.mean(x * x, axis=-1, keepdims=True) + 1e-05)
    normed = (x * scale * gain_ref[...].reshape(1, width)).astype(jnp.bfloat16)
    copies[0].wait()
    pairs = jnp.dot(normed, wkv_ref[...], preferred_element_type=jnp.float32)
    query = None
    for n, (low, high) in enumerate(cuts):
        copies[1 + n].wait()
        term = jnp.dot(normed[:, low:high], wq_ref[low:high, :], preferred_element_type=jnp.float32)
        query = term if query is None else query + term

    is_key = lane < HEAD_SIZE
    fresh = jnp.where(is_key, turn(pairs), pairs).astype(jnp.bfloat16)
    for m in range(heads // 2):
        two = turn(query[:, m * pair:(m + 1) * pair])
        for odd in range(2):
            one = two if odd == 0 else pltpu.roll(two, HEAD_SIZE, 1)
            one = jnp.where(is_key, one, 0.0)
            for s in range(steps):
                slot = (2 * m + odd) * steps + s
                turned_ref[pl.ds(slot, rows, stride=per_row), :] = one[s * rows:(s + 1) * rows]
    turned = turned_ref[...].astype(jnp.bfloat16)

    copies[-2].wait()
    place = lax.broadcasted_iota(jnp.int32, (per_row, slots), 1)
    scores = []
    for r in range(rows):
        score = dot_last(turned[r * per_row:(r + 1) * per_row], cache_ref[r]) * 0.125
        scores.append(jnp.where(place < lengths_ref[r], score, -jnp.inf))
    cached = jnp.concatenate(scores, axis=0)
    row_at = lax.broadcasted_iota(jnp.int32, (rows * per_row, total_rows), 0)
    fresh_at = lax.broadcasted_iota(jnp.int32, (rows * per_row, total_rows), 1)
    seen = (row_at // per_row == fresh_at % rows) & (fresh_at // rows <= row_at % steps)
    new = jnp.where(seen, dot_last(turned, fresh) * 0.125, -jnp.inf)
    head_at = lax.broadcasted_iota(jnp.int32, (rows * per_row, 1), 0) % per_row // steps
    sink = jnp.zeros((rows * per_row, 1), jnp.float32)
    for h in range(heads):
        sink = jnp.where(head_at == h, sinks_ref[h], sink)
    largest = jnp.maximum(jnp.maximum(jnp.max(cached, axis=-1, keepdims=True), jnp.max(new, axis=-1, keepdims=True)), sink)
    cached = jnp.exp(cached - largest)
    new = jnp.exp(new - largest)
    total = jnp.sum(cached, axis=-1, keepdims=True) + jnp.sum(new, axis=-1, keepdims=True) + jnp.exp(sink - largest)
    share = 1.0 / total
    cached = (cached * share).astype(jnp.bfloat16)
    new = (new * share).astype(jnp.bfloat16)
    mixed = []
    for r in range(rows):
        mixed.append(jnp.dot(cached[r * per_row:(r + 1) * per_row], cache_ref[r], preferred_element_type=jnp.float32))
    mixed_ref[...] = jnp.concatenate(mixed, axis=0) + jnp.dot(new, fresh, preferred_element_type=jnp.float32)

    def head(h):
        return jnp.concatenate([mixed_ref[pl.ds(h * steps + s, rows, stride=per_row), :] for s in range(steps)], axis=0)

    mix = jnp.concatenate(
        [jnp.where(is_key, pltpu.roll(head(2 * m), HEAD_SIZE, 1), head(2 * m + 1)) for m in range(heads // 2)], axis=1
    ).astype(jnp.bfloat16)
    copies[-1].wait()
    for t in range(tps):
        low, high = t * LANES, min((t + 1) * LANES, width)
        piece = dot_last(mix, wo_ref[low:high, :])
        if high - low < LANES:
            piece = jnp.concatenate([piece, jnp.zeros((total_rows, LANES - (high - low)), jnp.float32)], axis=1)
        keep_ref[t] = piece
        send_ref[t] = piece.astype(jnp.bfloat16)


def attention_partial(flat, gain, w_query, key_value, sinks, w_output, cache, lengths, routes, weights, tps):
    total_rows, width = flat.shape
    rows, slots, pair = cache.shape
    per_row = w_query.shape[1] // HEAD_SIZE * (total_rows // rows)
    operands = (lengths, sinks, routes, weights, gain, flat, w_query, key_value, cache, w_output.swapaxes(0, 1))
    return pl.pallas_call(
        attention_kernel,
        name="attention",
        out_shape=[shape_of((tps, total_rows, LANES), jnp.float32), shape_of((tps, total_rows, LANES)),
                   shape_of((total_rows, LANES), jnp.float32)],
        in_specs=[outside()] * len(operands),
        out_specs=[vmem()] * 3,
        scratch_shapes=[
            pltpu.SMEM(lengths.shape, jnp.int32),
            pltpu.SMEM(sinks.shape, jnp.float32),
            pltpu.VMEM(routes.shape, jnp.int32),
            pltpu.VMEM(weights.shape, jnp.float32),
            pltpu.VMEM(gain.shape, jnp.float32),
            pltpu.VMEM((total_rows, width), jnp.bfloat16),
            pltpu.VMEM(w_query.shape, jnp.bfloat16),
            pltpu.VMEM(key_value.shape, jnp.bfloat16),
            pltpu.VMEM(cache.shape, jnp.bfloat16),
            pltpu.VMEM((width, w_output.shape[0]), jnp.bfloat16),
            pltpu.VMEM((total_rows, tps * LANES), jnp.float32),
            pltpu.VMEM((rows * per_row, pair), jnp.float32),
            pltpu.VMEM((rows * per_row, pair), jnp.float32),
            pltpu.SemaphoreType.DMA((9 + len(split_width(width)),)),
        ],
        compiler_params=pltpu.CompilerParams(vmem_limit_bytes=24 * MIB),
    )(*[pltpu.with_memory_space_constraint(operand, pltpu.HBM) for operand in operands])


def call(kernel, name, outs, *operands, limit=4, flops=0):
    single = not isinstance(outs, list)
    held = [*operands, *([outs] if single else outs)]
    return pl.pallas_call(
        kernel,
        name=name,
        out_shape=outs,
        in_specs=[vmem()] * len(operands),
        out_specs=vmem() if single else [vmem()] * len(outs),
        compiler_params=pltpu.CompilerParams(vmem_limit_bytes=limit * MIB),
        cost_estimate=pl.CostEstimate(flops=flops, transcendentals=0,
                                      bytes_accessed=sum(math.prod(a.shape) * a.dtype.itemsize for a in held)),
    )(*operands)


def after_core_kernel(keep_ref, come_ref, own_x_ref, own_ref, *send_refs):
    tp = lax.axis_index("tp")
    own_ref[...] = keep_ref[tp] + come_ref[tp].astype(jnp.float32) + own_x_ref[...]
    for mask, ref in zip(SHARD_MASKS, send_refs):
        to = jnp.bitwise_xor(tp, mask)
        ref[...] = (keep_ref[to] + come_ref[to].astype(jnp.float32)).astype(jnp.bfloat16)


def after_core_halves_kernel(low_ref, high_ref, low_come_ref, high_come_ref, own_ref, *send_refs):
    tp, half = lax.axis_index("tp"), low_ref.shape[2] // 2

    def part(to):
        at = jnp.bitwise_and(to, 1)
        low = low_ref[at] + low_come_ref[at].astype(jnp.float32)
        return jnp.where(to < 2, low, high_ref[at] + high_come_ref[at].astype(jnp.float32))

    own_ref[...] = part(tp)
    for mask, second, first in zip(SHARD_MASKS, send_refs[:3], send_refs[3:]):
        whole = part(jnp.bitwise_xor(tp, mask)).astype(jnp.bfloat16)
        second[...] = whole[:, half:]
        first[...] = whole[:, :half]


def add_all(*refs):
    total = refs[0][...]
    for ref in refs[1:]:
        total = total + ref[...].astype(jnp.float32)
    return total


def sum_kernel(*refs):
    refs[-1][...] = add_all(*refs[:-1]).astype(jnp.bfloat16).reshape(refs[-1].shape)


def sum_rows_kernel(own_ref, *refs, line):
    come, outs = refs[:3], refs[3:]
    lines = outs[0].shape[1]
    total = own_ref[:, line:line + len(outs) * lines]
    for ref in come:
        total = total + ref[...].astype(jnp.float32)
    for n, out in enumerate(outs):
        out[...] = total[:, n * lines:(n + 1) * lines].astype(out.dtype)


def combine_kernel(*refs):
    terms, outs = refs[:-2], refs[-2:]
    total = add_all(*terms).astype(jnp.bfloat16)
    for n, out in enumerate(outs):
        out[...] = total[n]


def choose_kernel(own_ref, come_ref, out_ref):
    out_ref[...] = jnp.where(lax.axis_index("sec") == 1, own_ref[...].astype(jnp.float32),
                             come_ref[...].astype(jnp.float32)).astype(jnp.bfloat16).reshape(out_ref.shape)


def first_products(pieces, masks, outer, x_ref, gain_ref, gate_ref, up_ref, outs):
    width, lines = gate_ref.shape[1], x_ref.shape[0]
    sec, tp = lax.axis_index("sec"), lax.axis_index("tp")
    for mask, at_second, at_first in zip(masks, pieces[::2], pieces[1::2]):
        at = pl.ds(pl.multiple_of(jnp.bitwise_xor(tp, mask) * LANES, LANES), LANES)

        @pl.when(sec == 1)
        def _(at=at, piece=at_second):
            x_ref[:, at] = piece[...].reshape(lines, LANES)

        @pl.when(sec == 0)
        def _(at=at, piece=at_first):
            x_ref[:, at] = piece[...].reshape(lines, LANES)

    for where, cuts in ((outer, ((0, LANES), (3 * LANES, width))), (jnp.logical_not(outer), ((LANES, 3 * LANES),))):
        @pl.when(where)
        def _(cuts=cuts):
            sums = None
            for start, stop in cuts:
                x = x_ref[:, start:stop].astype(jnp.float32)
                scaled = (x * gain_ref[:, start:stop]).astype(jnp.bfloat16)
                terms = (dot_last(scaled, gate_ref[:, start:stop]), dot_last(scaled, up_ref[:, start:stop]),
                         jnp.sum(x * x, axis=-1, keepdims=True))
                sums = terms if sums is None else [a + b for a, b in zip(sums, terms)]
            for out, total in zip(outs, sums):
                out[...] = jnp.broadcast_to(total, out.shape)


def outer_chip():
    tp = lax.axis_index("tp")
    return (tp == 0) | (tp == 3)


def near_kernel(gain_ref, gate_ref, up_ref, *refs):
    pieces, (x_ref, *outs) = refs[:-4], refs[-4:]
    first_products(pieces, (0, SHARD_MASKS[0]), outer_chip(), x_ref, gain_ref, gate_ref, up_ref, outs)


def second_product(act_ref, down_ref, keep_ref, send_ref, first):
    chips, secs, _, part = keep_ref.shape
    for n in range(secs):
        start = (n * 4 + first) * part
        shift = start % 128
        out = jnp.dot(act_ref[...], down_ref[:, start - shift:start + chips * part], preferred_element_type=jnp.float32)
        for t in range(chips):
            piece = out[:, shift + t * part:shift + (t + 1) * part]
            keep_ref[t, n] = piece
            send_ref[t, n] = piece.astype(jnp.bfloat16)


def far_kernel(gain_ref, gate_ref, up_ref, down_ref, near_x_ref, near_gate_ref, near_up_ref, near_square_ref, *refs):
    pieces, (keep_ref, send_ref, act_ref, far_x_ref, *outs) = refs[:4], refs[4:]
    grp, outer = lax.axis_index("grp"), outer_chip()
    first_products(pieces, SHARD_MASKS[1:], jnp.logical_not(outer), far_x_ref, gain_ref, gate_ref, up_ref, outs)
    gate_out, up_out, square_out = outs
    width = gate_ref.shape[1]
    spare = jnp.where(outer, near_x_ref[:, width:].astype(jnp.float32), far_x_ref[:, width:].astype(jnp.float32))
    spare_at = lax.broadcasted_iota(jnp.int32, spare.shape, 1)
    weight = jnp.sum(jnp.where((spare_at == 2 * grp) | (spare_at == 2 * grp + 1), spare, 0.0), axis=1, keepdims=True)
    square = (near_square_ref[...] + square_out[...])[:, :1]
    scale = lax.rsqrt(square / width + 1e-05)
    gate_h = (near_gate_ref[...] + gate_out[...]) * scale
    up_h = (near_up_ref[...] + up_out[...]) * scale
    act_ref[...] = ((up_h + 1.0) * gate_h * jax.nn.sigmoid(1.702 * gate_h) * weight).astype(jnp.bfloat16)
    second_product(act_ref, down_ref, keep_ref, send_ref, 0)


def last_kernel(act_ref, down_ref, near_x_ref, far_x_ref, keep_ref, send_ref, middle_ref, row_ref):
    second_product(act_ref, down_ref, keep_ref, send_ref, 2)
    secs, total_rows, part = middle_ref.shape
    outer, tp = outer_chip(), lax.axis_index("tp")
    columns = []
    for t in range(4):
        at = slice(t * LANES, (t + 1) * LANES)
        near, far = near_x_ref[:total_rows, at].astype(jnp.float32), far_x_ref[:total_rows, at].astype(jnp.float32)
        columns.append(jnp.where(outer if t in (0, 3) else jnp.logical_not(outer), near, far))
    x = jnp.concatenate(columns, axis=1)
    for c in range(row_ref.shape[0]):
        row_ref[c] = x[:, c * part:(c + 1) * part]
    for n in range(secs):
        middle_ref[n] = row_ref[n * 4 + tp]


def experts(gain, w_gate, w_up, w_down, pieces, part):
    gain, w_gate, w_up = gain.reshape(1, -1), w_gate.swapaxes(0, 1), w_up.swapaxes(0, 1)
    (hidden, width), tps, (groups, total_rows, _) = w_gate.shape, len(pieces), pieces[0].shape
    lines = groups * total_rows
    both = [copy for piece in pieces for copy in (piece, hand_over(piece, 0))]
    halves = [shape_of((lines, tps * LANES)), shape_of((lines, hidden), jnp.float32), shape_of((lines, hidden), jnp.float32),
              shape_of((lines, 128), jnp.float32)]
    near = call(near_kernel, "near_columns", halves, gain, w_gate, w_up, *both[:4], limit=16, flops=2 * lines * width * hidden)
    outs = [shape_of((2, 2, lines, part), jnp.float32), shape_of((2, 2, lines, part))]
    low, low_send, act, far_x = pl.pallas_call(
        far_kernel,
        name="far_columns",
        out_shape=outs + [shape_of((lines, hidden)), halves[0]],
        in_specs=[vmem()] * 12,
        out_specs=[vmem()] * 4,
        scratch_shapes=[pltpu.VMEM(half.shape, half.dtype) for half in halves[1:]],
        compiler_params=pltpu.CompilerParams(vmem_limit_bytes=20 * MIB),
    )(gain, w_gate, w_up, w_down, *near, *both[4:])
    low_come = hand_over(low_send, 1)
    high, high_send, middle = pl.pallas_call(
        last_kernel,
        name="last_columns",
        out_shape=outs + [shape_of((2, total_rows, part), jnp.float32)],
        in_specs=[vmem()] * 4,
        out_specs=[vmem()] * 3,
        scratch_shapes=[pltpu.VMEM((2 * tps, total_rows, part), jnp.float32)],
        compiler_params=pltpu.CompilerParams(vmem_limit_bytes=16 * MIB),
        cost_estimate=pl.CostEstimate(flops=lines * width * hidden, transcendentals=0, bytes_accessed=2 * lines * width),
    )(act, w_down, near[0], far_x)
    return low, high, low_come, hand_over(high_send, 1), middle


def every_expert_body(inputs, attention_gain, w_query, key_value_weight, head_sink_logits, w_output, cache_pairs, lengths,
                      expert_gain, w_gate, w_up, w_down, routes, gate_weights):
    tps, groups = lax.axis_size("tp"), lax.axis_size("grp")
    steps, rows, width = inputs.shape
    lines = steps * rows
    keep, send, own_x = attention_partial(
        inputs.reshape(lines, width), attention_gain, w_query, key_value_weight[:, 0], head_sink_logits, w_output,
        cache_pairs[:, :, 0], lengths, routes.swapaxes(1, 2), gate_weights.swapaxes(1, 2), tps)
    own, *parts = call(after_core_kernel, "after_core", [shape_of((lines, LANES), jnp.float32)] + [shape_of((lines, LANES))] * 3,
                       keep, hand_over(send, 1), own_x)
    middle = call(sum_kernel, "sum", shape_of((lines, LANES)), own, *shard_swaps(parts))
    stacked = jnp.stack([middle] + [swap(middle, "grp", m) for m in range(1, groups)])
    pieces = [stacked] + shard_swaps([stacked] * 3)
    part = width // (2 * tps)
    *terms, own_middle = experts(expert_gain, w_gate[0], w_up[0], w_down[0], pieces, part)
    own, *parts = call(after_core_halves_kernel, "after_core_halves",
                       [shape_of((2, groups * lines, part), jnp.float32)] + [shape_of((2, groups // 2 * lines, part))] * 6, *terms,
                       limit=12)
    second_come, first_come = shard_swaps(parts[:3]), shard_swaps(parts[3:])
    second, third = call(functools.partial(sum_rows_kernel, line=2 * lines), "sum_far_rows", [shape_of((2, lines, part))] * 2,
                         own, *second_come)
    third, second = swap(third, "grp", 3), swap(second, "grp", 2)
    own, nearest = call(functools.partial(sum_rows_kernel, line=0), "sum_near_rows",
                        [shape_of((2, lines, part), jnp.float32), shape_of((2, lines, part))], own, *first_come)
    first_core, second_core = call(combine_kernel, "combine", [shape_of((lines, part))] * 2, own, third, second,
                                   swap(nearest, "grp", 1), own_middle)
    return call(choose_kernel, "choose", shape_of((steps, rows, part)), second_core, hand_over(first_core, 0))


def body(*args):
    sizes = lax.axis_size("sec"), lax.axis_size("tp"), lax.axis_size("grp"), args[9].shape[0]
    if sizes == (2, 4, TOP, 1):
        return every_expert_body(*args)
    return general_body(*args)


def solution(mesh):
    placed = (
        P(None, "grp", None),
        P(),
        P(None, ("sec", "tp")),
        P(None, ("sec", "tp"), None),
        P(("sec", "tp")),
        P(("sec", "tp"), None),
        P("grp", None, ("sec", "tp"), None),
        P("grp"),
        P(),
        P("grp", None, ("sec", "tp")),
        P("grp", None, ("sec", "tp")),
        P("grp", ("sec", "tp"), None),
        P(None, "grp", None),
        P(None, "grp", None),
    )
    return jax.shard_map(
        body, mesh=mesh, in_specs=placed, out_specs=P(None, "grp", ("sec", "tp")), check_vma=False
    )
```

```python
import functools
import math

import jax
import jax.numpy as jnp
import numpy as np
from jax import lax
from jax.experimental import pallas as pl
from jax.experimental.pallas import tpu as pltpu
from jax.sharding import PartitionSpec as P

HEAD_SIZE = 64
TOP = 4


def rms_norm(values, scale_row):
    widened = values.astype(jnp.float32)
    scale_factor = lax.rsqrt(jnp.mean(widened * widened, axis=-1, keepdims=True) + 1e-05)
    return (widened * scale_factor * scale_row).astype(jnp.bfloat16)


def rotate(vectors, position):
    half_size = vectors.shape[-1] // 2
    counter = jnp.arange(half_size).astype(jnp.float32)
    frequency = jnp.power(jnp.float32(150000.0), counter * (-2.0 / vectors.shape[-1]))
    angle_table = position * frequency
    cosine = jnp.cos(angle_table)
    sine_table = jnp.sin(angle_table)
    first_half = vectors[..., :half_size]
    second_half = vectors[..., half_size:]
    return jnp.concatenate(
        [
            first_half * cosine - second_half * sine_table,
            first_half * sine_table + second_half * cosine,
        ],
        axis=-1,
    )


def attend(
    normalized_input,
    w_query,
    key_value_weight,
    head_sink_logits,
    w_output,
    cache_pairs,
    lengths,
    step_index,
    fresh_keys,
    fresh_values,
):
    row_count = normalized_input.shape[0]
    kv_heads = key_value_weight.shape[1]
    query = jnp.dot(normalized_input, w_query, preferred_element_type=jnp.float32).reshape(
        row_count, -1, HEAD_SIZE
    )
    cache_entry_pairs = jnp.dot(
        normalized_input,
        key_value_weight.reshape(key_value_weight.shape[0], -1),
        preferred_element_type=jnp.float32,
    ).reshape(row_count, kv_heads, 2 * HEAD_SIZE)
    position = (lengths + step_index).astype(jnp.float32)[:, None, None]
    rotated_rows = rotate(query, position).astype(jnp.bfloat16)
    fresh_keys = fresh_keys + [
        rotate(cache_entry_pairs[..., :HEAD_SIZE], position).astype(jnp.bfloat16)
    ]
    fresh_values = fresh_values + [cache_entry_pairs[..., HEAD_SIZE:].astype(jnp.bfloat16)]
    grouped_queries = rotated_rows.reshape(row_count, kv_heads, -1, HEAD_SIZE)
    new_keys = jnp.stack(fresh_keys, 1)
    new_values = jnp.stack(fresh_values, 1)
    cached = (
        jnp.einsum(
            "rkgd,rjkd->rkgj",
            grouped_queries,
            cache_pairs[..., :HEAD_SIZE],
            preferred_element_type=jnp.float32,
        )
        * 0.125
    )
    valid = (jnp.arange(cache_pairs.shape[1])[None, :] < lengths[:, None])[:, None, None, :]
    cached = jnp.where(valid, cached, -jnp.inf)
    fresh = (
        jnp.einsum("rkgd,rikd->rkgi", grouped_queries, new_keys, preferred_element_type=jnp.float32)
        * 0.125
    )
    sink_row = head_sink_logits.reshape(kv_heads, -1)[None]
    largest = jnp.maximum(jnp.maximum(jnp.max(cached, axis=-1), jnp.max(fresh, axis=-1)), sink_row)
    cached_exp = jnp.exp(cached - largest[..., None])
    fresh_exp = jnp.exp(fresh - largest[..., None])
    denominator = (
        jnp.sum(cached_exp, axis=-1) + jnp.sum(fresh_exp, axis=-1) + jnp.exp(sink_row - largest)
    )
    cached_probs = (cached_exp / denominator[..., None]).astype(jnp.bfloat16)
    fresh_probs = (fresh_exp / denominator[..., None]).astype(jnp.bfloat16)
    mixed = jnp.einsum(
        "rkgj,rjkd->rkgd",
        cached_probs,
        cache_pairs[..., HEAD_SIZE:],
        preferred_element_type=jnp.float32,
    )
    mixed = mixed + jnp.einsum(
        "rkgi,rikd->rkgd", fresh_probs, new_values, preferred_element_type=jnp.float32
    )
    attention_mix = mixed.reshape(row_count, -1).astype(jnp.bfloat16)
    partial_sum = jnp.dot(attention_mix, w_output, preferred_element_type=jnp.float32)
    return (partial_sum, fresh_keys, fresh_values)


def general_body(
    inputs,
    attention_gain,
    w_query,
    key_value_weight,
    head_sink_logits,
    w_output,
    cache_pairs,
    lengths,
    expert_gain,
    w_gate,
    w_up,
    w_down,
    routes,
    gate_weights,
):
    shards = lax.axis_size(("sec", "tp"))
    shard_index = lax.axis_index(("sec", "tp"))
    experts = lax.axis_size("grp") * w_gate.shape[0]
    group_rows = inputs.shape[1]
    width = inputs.shape[2]
    part_width = width // shards
    chosen = max(TOP, experts // 2)
    capacity = group_rows * TOP // chosen
    slot_total = experts * capacity
    gate_matrix = w_gate[0]
    up_matrix = w_up[0]
    down_matrix = w_down[0]
    fresh_keys = []
    fresh_values = []
    results = []
    for step_index in range(inputs.shape[0]):
        normalized_input = rms_norm(inputs[step_index], attention_gain)
        partial_sum, fresh_keys, fresh_values = attend(
            normalized_input,
            w_query,
            key_value_weight,
            head_sink_logits,
            w_output,
            cache_pairs,
            lengths,
            step_index,
            fresh_keys,
            fresh_values,
        )
        summed = lax.psum(partial_sum[None], ("sec", "tp"))
        middle = (inputs[step_index][None].astype(jnp.float32) + summed).astype(jnp.bfloat16)
        route_rows = routes[step_index][None]
        step_count = middle.shape[0]
        expert_in = rms_norm(middle, expert_gain)
        flat_routes = route_rows.reshape(step_count, group_rows * TOP)
        onehot = (flat_routes[..., None] == jnp.arange(experts)[None, None, :]).astype(jnp.int32)
        earlier = jnp.cumsum(onehot, axis=1) - onehot
        slot_index = jnp.sum(earlier * onehot, axis=-1).reshape(step_count, group_rows, TOP)
        target = route_rows * capacity + slot_index
        placed = target[..., None] == jnp.arange(slot_total)[None, None, None, :]
        dispatch_table = jnp.sum(placed.astype(jnp.int32), axis=2).astype(jnp.bfloat16)
        combine_table = jnp.sum(
            jnp.where(placed, gate_weights[step_index][None][..., None], 0.0), axis=2
        )
        outgoing = jnp.einsum(
            "crm,crd->cmd", dispatch_table, expert_in, preferred_element_type=jnp.float32
        )
        outgoing = outgoing.astype(jnp.bfloat16).reshape(step_count, experts, capacity, width)
        arrived = lax.all_to_all(outgoing, "grp", split_axis=1, concat_axis=1, tiled=True)
        gate_h = jnp.einsum(
            "snpd,dh->snph", arrived, gate_matrix, preferred_element_type=jnp.float32
        )
        up_h = jnp.einsum("snpd,dh->snph", arrived, up_matrix, preferred_element_type=jnp.float32)
        act = ((up_h + 1.0) * gate_h * jax.nn.sigmoid(1.702 * gate_h)).astype(jnp.bfloat16)
        partial_out = jnp.einsum(
            "snph,hd->snpd", act, down_matrix, preferred_element_type=jnp.float32
        )
        reduced = lax.psum_scatter(
            partial_out, ("sec", "tp"), scatter_dimension=3, tiled=True
        ).astype(jnp.bfloat16)
        returned = lax.all_to_all(reduced, "grp", split_axis=1, concat_axis=1, tiled=True)
        returned_rows = returned.reshape(step_count, slot_total, part_width).astype(jnp.float32)
        weighted = jnp.einsum(
            "srm,smd->srd", combine_table, returned_rows, precision=lax.Precision.HIGHEST
        )
        own_middle = lax.dynamic_slice_in_dim(
            middle, shard_index * part_width, part_width, 2
        ).astype(jnp.float32)
        results.append((own_middle + weighted).astype(jnp.bfloat16)[0])
    return jnp.stack(results, 0)


LANES = 768
BASE = 150000.0
MIB = 1 << 20
SHARD_MASKS = (3, 1, 2)


def shape_of(shape, dtype=jnp.bfloat16):
    return jax.ShapeDtypeStruct(shape, dtype)


def vmem():
    return pl.BlockSpec(memory_space=pltpu.VMEM)


def smem():
    return pl.BlockSpec(memory_space=pltpu.SMEM)


def outside():
    return pl.BlockSpec(memory_space=pltpu.HBM)


def dot_last(left, right):
    return lax.dot_general(left, right, (((1,), (1,)), ((), ())), preferred_element_type=jnp.float32)


def swap(value, axis, mask):
    size = lax.axis_size(axis)
    return lax.ppermute(value, ("sec", axis), [(i, i if i < size else size + (i - size ^ mask)) for i in range(2 * size)])


def shard_swaps(parts):
    return [swap(part, "tp", mask) for part, mask in zip(parts, SHARD_MASKS)]


def hand_over(value):
    return lax.ppermute(value, "sec", [(0, 1), (1, 0)])


def split_width(width):
    cuts = list(range(0, width, 768)) + [width]
    return list(zip(cuts[:-1], cuts[1:]))


def attention_kernel(lengths_hbm, sinks_hbm, routes_hbm, weights_hbm, gain_hbm, x_hbm, wq_hbm, wkv_hbm, cache_hbm, wo_hbm,
                     keep_ref, send_ref, own_x_ref,
                     lengths_ref, sinks_ref, routes_ref, weights_ref, gain_ref, x_ref, wq_ref, wkv_ref, cache_ref, wo_ref,
                     xs_ref, turned_ref, mixed_ref, sems):
    total_rows, width = x_ref.shape
    rows, slots, pair = cache_ref.shape
    steps = total_rows // rows
    heads = wq_ref.shape[1] // HEAD_SIZE
    per_row = heads * steps
    tps = keep_ref.shape[0]
    cuts = split_width(width)
    small = [(lengths_hbm, lengths_ref), (x_hbm, x_ref), (gain_hbm, gain_ref), (routes_hbm, routes_ref), (weights_hbm, weights_ref),
             (sinks_hbm, sinks_ref)]
    small = [pltpu.make_async_copy(source, target, sems.at[n]) for n, (source, target) in enumerate(small)]
    copies = [pltpu.make_async_copy(wkv_hbm, wkv_ref, sems.at[6])]
    for n, (low, high) in enumerate(cuts):
        part = pl.ds(low, high - low)
        copies.append(pltpu.make_async_copy(wq_hbm.at[part], wq_ref.at[part], sems.at[9 + n]))
    copies.append(pltpu.make_async_copy(cache_hbm, cache_ref, sems.at[7]))
    copies.append(pltpu.make_async_copy(wo_hbm, wo_ref, sems.at[8]))
    for copy in small + copies:
        copy.start()
    small[0].wait()

    lane = lax.broadcasted_iota(jnp.int32, (total_rows, pair), 1)
    line = lax.broadcasted_iota(jnp.int32, (total_rows, pair), 0)
    position = jnp.zeros((total_rows, pair), jnp.int32)
    for r in range(rows):
        for s in range(steps):
            position = jnp.where(line == s * rows + r, lengths_ref[r] + s, position)
    half = HEAD_SIZE // 2
    counter = jnp.bitwise_and(lane, half - 1).astype(jnp.float32)
    frequency = jnp.exp(counter * jnp.float32(-2.0 / HEAD_SIZE * np.log(BASE)))
    angle = position.astype(jnp.float32) * frequency
    cosine, sine = jnp.cos(angle), jnp.sin(angle)
    low_half = jnp.bitwise_and(lane, HEAD_SIZE - 1) < half
    sine = jnp.where(low_half, -sine, sine)

    def turn(two):
        return two * cosine + jnp.where(low_half, pltpu.roll(two, pair - half, 1), pltpu.roll(two, half, 1)) * sine

    for copy in small[1:]:
        copy.wait()
    spare = xs_ref.shape[1] - width
    spare_at = lax.broadcasted_iota(jnp.int32, (rows, spare), 1)
    corner = lax.broadcasted_iota(jnp.int32, (rows, rows), 0) == lax.broadcasted_iota(jnp.int32, (rows, rows), 1)
    tables = []
    for s in range(steps):
        table = jnp.zeros((rows, spare), jnp.float32)
        for e in range(TOP):
            across = jnp.sum(jnp.where(routes_ref[s] == e, weights_ref[s], 0.0), axis=0, keepdims=True)
            column = jnp.sum(jnp.where(corner, across, 0.0), axis=1, keepdims=True)
            high_part = column.astype(jnp.bfloat16).astype(jnp.float32)
            table = jnp.where(spare_at == 2 * e, high_part, jnp.where(spare_at == 2 * e + 1, column - high_part, table))
        tables.append(table)
    x = x_ref[...].astype(jnp.float32)
    xs_ref[...] = jnp.concatenate([x, jnp.concatenate(tables, axis=0)], axis=1)
    own = lax.axis_index("tp") * LANES
    own_x_ref[...] = xs_ref[:, pl.ds(pl.multiple_of(own, LANES), LANES)]
    scale = lax.rsqrt(jnp.mean(x * x, axis=-1, keepdims=True) + 1e-05)
    normed = (x * scale * gain_ref[...].reshape(1, width)).astype(jnp.bfloat16)
    copies[0].wait()
    pairs = jnp.dot(normed, wkv_ref[...], preferred_element_type=jnp.float32)
    query = None
    for n, (low, high) in enumerate(cuts):
        copies[1 + n].wait()
        term = jnp.dot(normed[:, low:high], wq_ref[low:high, :], preferred_element_type=jnp.float32)
        query = term if query is None else query + term

    is_key = lane < HEAD_SIZE
    fresh = jnp.where(is_key, turn(pairs), pairs).astype(jnp.bfloat16)
    for m in range(heads // 2):
        two = turn(query[:, m * pair:(m + 1) * pair])
        for odd in range(2):
            one = two if odd == 0 else pltpu.roll(two, HEAD_SIZE, 1)
            one = jnp.where(is_key, one, 0.0)
            for s in range(steps):
                slot = (2 * m + odd) * steps + s
                turned_ref[pl.ds(slot, rows, stride=per_row), :] = one[s * rows:(s + 1) * rows]
    turned = turned_ref[...].astype(jnp.bfloat16)

    copies[-2].wait()
    place = lax.broadcasted_iota(jnp.int32, (per_row, slots), 1)
    scores = []
    for r in range(rows):
        score = dot_last(turned[r * per_row:(r + 1) * per_row], cache_ref[r]) * 0.125
        scores.append(jnp.where(place < lengths_ref[r], score, -jnp.inf))
    cached = jnp.concatenate(scores, axis=0)
    row_at = lax.broadcasted_iota(jnp.int32, (rows * per_row, total_rows), 0)
    fresh_at = lax.broadcasted_iota(jnp.int32, (rows * per_row, total_rows), 1)
    seen = (row_at // per_row == fresh_at % rows) & (fresh_at // rows <= row_at % steps)
    new = jnp.where(seen, dot_last(turned, fresh) * 0.125, -jnp.inf)
    head_at = lax.broadcasted_iota(jnp.int32, (rows * per_row, 1), 0) % per_row // steps
    sink = jnp.zeros((rows * per_row, 1), jnp.float32)
    for h in range(heads):
        sink = jnp.where(head_at == h, sinks_ref[h], sink)
    largest = jnp.maximum(jnp.maximum(jnp.max(cached, axis=-1, keepdims=True), jnp.max(new, axis=-1, keepdims=True)), sink)
    cached = jnp.exp(cached - largest)
    new = jnp.exp(new - largest)
    total = jnp.sum(cached, axis=-1, keepdims=True) + jnp.sum(new, axis=-1, keepdims=True) + jnp.exp(sink - largest)
    share = 1.0 / total
    cached = (cached * share).astype(jnp.bfloat16)
    new = (new * share).astype(jnp.bfloat16)
    mixed = []
    for r in range(rows):
        mixed.append(jnp.dot(cached[r * per_row:(r + 1) * per_row], cache_ref[r], preferred_element_type=jnp.float32))
    mixed_ref[...] = jnp.concatenate(mixed, axis=0) + jnp.dot(new, fresh, preferred_element_type=jnp.float32)

    def head(h):
        return jnp.concatenate([mixed_ref[pl.ds(h * steps + s, rows, stride=per_row), :] for s in range(steps)], axis=0)

    mix = jnp.concatenate(
        [jnp.where(is_key, pltpu.roll(head(2 * m), HEAD_SIZE, 1), head(2 * m + 1)) for m in range(heads // 2)], axis=1
    ).astype(jnp.bfloat16)
    copies[-1].wait()
    for t in range(tps):
        low, high = t * LANES, min((t + 1) * LANES, width)
        piece = dot_last(mix, wo_ref[low:high, :])
        if high - low < LANES:
            piece = jnp.concatenate([piece, jnp.zeros((total_rows, LANES - (high - low)), jnp.float32)], axis=1)
        keep_ref[t] = piece
        send_ref[t] = piece.astype(jnp.bfloat16)


def attention_partial(flat, gain, w_query, key_value, sinks, w_output, cache, lengths, routes, weights, tps):
    total_rows, width = flat.shape
    rows, slots, pair = cache.shape
    per_row = w_query.shape[1] // HEAD_SIZE * (total_rows // rows)
    operands = (lengths, sinks, routes, weights, gain, flat, w_query, key_value, cache, w_output.swapaxes(0, 1))
    return pl.pallas_call(
        attention_kernel,
        name="attention",
        out_shape=[shape_of((tps, total_rows, LANES), jnp.float32), shape_of((tps, total_rows, LANES)),
                   shape_of((total_rows, LANES), jnp.float32)],
        in_specs=[outside()] * len(operands),
        out_specs=[vmem()] * 3,
        scratch_shapes=[
            pltpu.SMEM(lengths.shape, jnp.int32),
            pltpu.SMEM(sinks.shape, jnp.float32),
            pltpu.VMEM(routes.shape, jnp.int32),
            pltpu.VMEM(weights.shape, jnp.float32),
            pltpu.VMEM(gain.shape, jnp.float32),
            pltpu.VMEM((total_rows, width), jnp.bfloat16),
            pltpu.VMEM(w_query.shape, jnp.bfloat16),
            pltpu.VMEM(key_value.shape, jnp.bfloat16),
            pltpu.VMEM(cache.shape, jnp.bfloat16),
            pltpu.VMEM((width, w_output.shape[0]), jnp.bfloat16),
            pltpu.VMEM((total_rows, tps * LANES), jnp.float32),
            pltpu.VMEM((rows * per_row, pair), jnp.float32),
            pltpu.VMEM((rows * per_row, pair), jnp.float32),
            pltpu.SemaphoreType.DMA((9 + len(split_width(width)),)),
        ],
        compiler_params=pltpu.CompilerParams(vmem_limit_bytes=24 * MIB),
    )(*[pltpu.with_memory_space_constraint(operand, pltpu.HBM) for operand in operands])


def call(kernel, name, outs, *operands, limit=4, flops=0):
    single = not isinstance(outs, list)
    held = [*operands, *([outs] if single else outs)]
    return pl.pallas_call(
        kernel,
        name=name,
        out_shape=outs,
        in_specs=[vmem()] * len(operands),
        out_specs=vmem() if single else [vmem()] * len(outs),
        compiler_params=pltpu.CompilerParams(vmem_limit_bytes=limit * MIB),
        cost_estimate=pl.CostEstimate(flops=flops, transcendentals=0,
                                      bytes_accessed=sum(math.prod(a.shape) * a.dtype.itemsize for a in held)),
    )(*operands)


def after_core_kernel(keep_ref, come_ref, own_x_ref, own_ref, *send_refs):
    tp = lax.axis_index("tp")
    own_ref[...] = keep_ref[tp] + come_ref[tp].astype(jnp.float32) + own_x_ref[...]
    for mask, ref in zip(SHARD_MASKS, send_refs):
        to = jnp.bitwise_xor(tp, mask)
        ref[...] = (keep_ref[to] + come_ref[to].astype(jnp.float32)).astype(jnp.bfloat16)


def after_core_halves_kernel(low_ref, high_ref, low_come_ref, high_come_ref, own_ref, *send_refs):
    tp, half = lax.axis_index("tp"), low_ref.shape[2] // 2

    def part(to):
        at = jnp.bitwise_and(to, 1)
        low = low_ref[at] + low_come_ref[at].astype(jnp.float32)
        return jnp.where(to < 2, low, high_ref[at] + high_come_ref[at].astype(jnp.float32))

    own_ref[...] = part(tp)
    for mask, second, first in zip(SHARD_MASKS, send_refs[:3], send_refs[3:]):
        whole = part(jnp.bitwise_xor(tp, mask)).astype(jnp.bfloat16)
        second[...] = whole[:, half:]
        first[...] = whole[:, :half]


def add_all(*refs):
    total = refs[0][...]
    for ref in refs[1:]:
        total = total + ref[...].astype(jnp.float32)
    return total


def sum_kernel(*refs):
    refs[-1][...] = add_all(*refs[:-1]).astype(jnp.bfloat16).reshape(refs[-1].shape)


def sum_rows_kernel(own_ref, *refs, line):
    come, outs = refs[:3], refs[3:]
    lines = outs[0].shape[1]
    total = own_ref[:, line:line + len(outs) * lines]
    for ref in come:
        total = total + ref[...].astype(jnp.float32)
    for n, out in enumerate(outs):
        out[...] = total[:, n * lines:(n + 1) * lines].astype(out.dtype)


def combine_kernel(*refs):
    terms, outs = refs[:-2], refs[-2:]
    total = add_all(*terms).astype(jnp.bfloat16)
    for n, out in enumerate(outs):
        out[...] = total[n]


def choose_kernel(own_ref, come_ref, out_ref):
    out_ref[...] = jnp.where(lax.axis_index("sec") == 1, own_ref[...].astype(jnp.float32),
                             come_ref[...].astype(jnp.float32)).astype(jnp.bfloat16).reshape(out_ref.shape)


def first_products(pieces, masks, outer, x_ref, gain_ref, gate_ref, up_ref, outs):
    width, lines = gate_ref.shape[1], x_ref.shape[0]
    sec, tp = lax.axis_index("sec"), lax.axis_index("tp")
    for mask, at_second, at_first in zip(masks, pieces[::2], pieces[1::2]):
        at = pl.ds(pl.multiple_of(jnp.bitwise_xor(tp, mask) * LANES, LANES), LANES)

        @pl.when(sec == 1)
        def _(at=at, piece=at_second):
            x_ref[:, at] = piece[...].reshape(lines, LANES)

        @pl.when(sec == 0)
        def _(at=at, piece=at_first):
            x_ref[:, at] = piece[...].reshape(lines, LANES)

    for where, cuts in ((outer, ((0, LANES), (3 * LANES, width))), (jnp.logical_not(outer), ((LANES, 3 * LANES),))):
        @pl.when(where)
        def _(cuts=cuts):
            sums = None
            for start, stop in cuts:
                x = x_ref[:, start:stop].astype(jnp.float32)
                scaled = (x * gain_ref[:, start:stop]).astype(jnp.bfloat16)
                terms = (dot_last(scaled, gate_ref[:, start:stop]), dot_last(scaled, up_ref[:, start:stop]),
                         jnp.sum(x * x, axis=-1, keepdims=True))
                sums = terms if sums is None else [a + b for a, b in zip(sums, terms)]
            for out, total in zip(outs, sums):
                out[...] = jnp.broadcast_to(total, out.shape)


def outer_chip():
    tp = lax.axis_index("tp")
    return (tp == 0) | (tp == 3)


def near_kernel(gain_ref, gate_ref, up_ref, *refs):
    pieces, (x_ref, *outs) = refs[:-4], refs[-4:]
    first_products(pieces, (0, SHARD_MASKS[0]), outer_chip(), x_ref, gain_ref, gate_ref, up_ref, outs)


def second_product(act_ref, down_ref, keep_ref, send_ref, first):
    chips, secs, _, part = keep_ref.shape
    for n in range(secs):
        start = (n * 4 + first) * part
        shift = start % 128
        out = jnp.dot(act_ref[...], down_ref[:, start - shift:start + chips * part], preferred_element_type=jnp.float32)
        for t in range(chips):
            piece = out[:, shift + t * part:shift + (t + 1) * part]
            keep_ref[t, n] = piece
            send_ref[t, n] = piece.astype(jnp.bfloat16)


def far_kernel(gain_ref, gate_ref, up_ref, down_ref, near_x_ref, near_gate_ref, near_up_ref, near_square_ref, *refs):
    pieces, (keep_ref, send_ref, act_ref, far_x_ref, *outs) = refs[:4], refs[4:]
    grp, outer = lax.axis_index("grp"), outer_chip()
    first_products(pieces, SHARD_MASKS[1:], jnp.logical_not(outer), far_x_ref, gain_ref, gate_ref, up_ref, outs)
    gate_out, up_out, square_out = outs
    width = gate_ref.shape[1]
    spare = jnp.where(outer, near_x_ref[:, width:].astype(jnp.float32), far_x_ref[:, width:].astype(jnp.float32))
    spare_at = lax.broadcasted_iota(jnp.int32, spare.shape, 1)
    weight = jnp.sum(jnp.where((spare_at == 2 * grp) | (spare_at == 2 * grp + 1), spare, 0.0), axis=1, keepdims=True)
    square = (near_square_ref[...] + square_out[...])[:, :1]
    scale = lax.rsqrt(square / width + 1e-05)
    gate_h = (near_gate_ref[...] + gate_out[...]) * scale
    up_h = (near_up_ref[...] + up_out[...]) * scale
    act_ref[...] = ((up_h + 1.0) * gate_h * jax.nn.sigmoid(1.702 * gate_h) * weight).astype(jnp.bfloat16)
    second_product(act_ref, down_ref, keep_ref, send_ref, 0)


def last_kernel(act_ref, down_ref, near_x_ref, far_x_ref, keep_ref, send_ref, middle_ref, row_ref):
    second_product(act_ref, down_ref, keep_ref, send_ref, 2)
    secs, total_rows, part = middle_ref.shape
    outer, tp = outer_chip(), lax.axis_index("tp")
    columns = []
    for t in range(4):
        at = slice(t * LANES, (t + 1) * LANES)
        near, far = near_x_ref[:total_rows, at].astype(jnp.float32), far_x_ref[:total_rows, at].astype(jnp.float32)
        columns.append(jnp.where(outer if t in (0, 3) else jnp.logical_not(outer), near, far))
    x = jnp.concatenate(columns, axis=1)
    for c in range(row_ref.shape[0]):
        row_ref[c] = x[:, c * part:(c + 1) * part]
    for n in range(secs):
        middle_ref[n] = row_ref[n * 4 + tp]


def experts(gain, w_gate, w_up, w_down, pieces, part):
    gain, w_gate, w_up = gain.reshape(1, -1), w_gate.swapaxes(0, 1), w_up.swapaxes(0, 1)
    (hidden, width), tps, (groups, total_rows, _) = w_gate.shape, len(pieces), pieces[0].shape
    lines = groups * total_rows
    both = [copy for piece in pieces for copy in (piece, hand_over(piece))]
    halves = [shape_of((lines, tps * LANES)), shape_of((lines, hidden), jnp.float32), shape_of((lines, hidden), jnp.float32),
              shape_of((lines, 128), jnp.float32)]
    near = call(near_kernel, "near_columns", halves, gain, w_gate, w_up, *both[:4], limit=16, flops=2 * lines * width * hidden)
    outs = [shape_of((2, 2, lines, part), jnp.float32), shape_of((2, 2, lines, part))]
    low, low_send, act, far_x = pl.pallas_call(
        far_kernel,
        name="far_columns",
        out_shape=outs + [shape_of((lines, hidden)), halves[0]],
        in_specs=[vmem()] * 12,
        out_specs=[vmem()] * 4,
        scratch_shapes=[pltpu.VMEM(half.shape, half.dtype) for half in halves[1:]],
        compiler_params=pltpu.CompilerParams(vmem_limit_bytes=20 * MIB),
    )(gain, w_gate, w_up, w_down, *near, *both[4:])
    low_come = hand_over(low_send)
    high, high_send, middle = pl.pallas_call(
        last_kernel,
        name="last_columns",
        out_shape=outs + [shape_of((2, total_rows, part), jnp.float32)],
        in_specs=[vmem()] * 4,
        out_specs=[vmem()] * 3,
        scratch_shapes=[pltpu.VMEM((2 * tps, total_rows, part), jnp.float32)],
        compiler_params=pltpu.CompilerParams(vmem_limit_bytes=16 * MIB),
        cost_estimate=pl.CostEstimate(flops=lines * width * hidden, transcendentals=0, bytes_accessed=2 * lines * width),
    )(act, w_down, near[0], far_x)
    return low, high, low_come, hand_over(high_send), middle


def every_expert_body(inputs, attention_gain, w_query, key_value_weight, head_sink_logits, w_output, cache_pairs, lengths,
                      expert_gain, w_gate, w_up, w_down, routes, gate_weights):
    tps, groups = lax.axis_size("tp"), lax.axis_size("grp")
    steps, rows, width = inputs.shape
    lines = steps * rows
    keep, send, own_x = attention_partial(
        inputs.reshape(lines, width), attention_gain, w_query, key_value_weight[:, 0], head_sink_logits, w_output,
        cache_pairs[:, :, 0], lengths, routes.swapaxes(1, 2), gate_weights.swapaxes(1, 2), tps)
    own, *parts = call(after_core_kernel, "after_core", [shape_of((lines, LANES), jnp.float32)] + [shape_of((lines, LANES))] * 3,
                       keep, hand_over(send), own_x)
    middle = call(sum_kernel, "sum", shape_of((lines, LANES)), own, *shard_swaps(parts))
    stacked = jnp.stack([middle] + [swap(middle, "grp", m) for m in range(1, groups)])
    pieces = [stacked] + shard_swaps([stacked] * 3)
    part = width // (2 * tps)
    *terms, own_middle = experts(expert_gain, w_gate[0], w_up[0], w_down[0], pieces, part)
    own, *parts = call(after_core_halves_kernel, "after_core_halves",
                       [shape_of((2, groups * lines, part), jnp.float32)] + [shape_of((2, groups // 2 * lines, part))] * 6, *terms,
                       limit=12)
    second_come, first_come = shard_swaps(parts[:3]), shard_swaps(parts[3:])
    second, third = call(functools.partial(sum_rows_kernel, line=2 * lines), "sum_far_rows", [shape_of((2, lines, part))] * 2,
                         own, *second_come)
    third, second = swap(third, "grp", 3), swap(second, "grp", 2)
    own, nearest = call(functools.partial(sum_rows_kernel, line=0), "sum_near_rows",
                        [shape_of((2, lines, part), jnp.float32), shape_of((2, lines, part))], own, *first_come)
    first_core, second_core = call(combine_kernel, "combine", [shape_of((lines, part))] * 2, own, third, second,
                                   swap(nearest, "grp", 1), own_middle)
    return call(choose_kernel, "choose", shape_of((steps, rows, part)), second_core, hand_over(first_core))


def body(*args):
    sizes = lax.axis_size("sec"), lax.axis_size("tp"), lax.axis_size("grp"), args[9].shape[0]
    if sizes == (2, 4, TOP, 1):
        return every_expert_body(*args)
    return general_body(*args)


def solution(mesh):
    placed = (
        P(None, "grp", None),
        P(),
        P(None, ("sec", "tp")),
        P(None, ("sec", "tp"), None),
        P(("sec", "tp")),
        P(("sec", "tp"), None),
        P("grp", None, ("sec", "tp"), None),
        P("grp"),
        P(),
        P("grp", None, ("sec", "tp")),
        P("grp", None, ("sec", "tp")),
        P("grp", ("sec", "tp"), None),
        P(None, "grp", None),
        P(None, "grp", None),
    )
    return jax.shard_map(
        body, mesh=mesh, in_specs=placed, out_specs=P(None, "grp", ("sec", "tp")), check_vma=False
    )
```

```python
import functools
import math

import jax
import jax.numpy as jnp
import numpy as np
from jax import lax
from jax.experimental import pallas as pl
from jax.experimental.pallas import tpu as pltpu
from jax.sharding import PartitionSpec as P

HEAD_SIZE = 64
TOP = 4


def rms_norm(values, scale_row):
    widened = values.astype(jnp.float32)
    scale_factor = lax.rsqrt(jnp.mean(widened * widened, axis=-1, keepdims=True) + 1e-05)
    return (widened * scale_factor * scale_row).astype(jnp.bfloat16)


def rotate(vectors, position):
    half_size = vectors.shape[-1] // 2
    counter = jnp.arange(half_size).astype(jnp.float32)
    frequency = jnp.power(jnp.float32(150000.0), counter * (-2.0 / vectors.shape[-1]))
    angle_table = position * frequency
    cosine = jnp.cos(angle_table)
    sine_table = jnp.sin(angle_table)
    first_half = vectors[..., :half_size]
    second_half = vectors[..., half_size:]
    return jnp.concatenate(
        [
            first_half * cosine - second_half * sine_table,
            first_half * sine_table + second_half * cosine,
        ],
        axis=-1,
    )


def attend(
    normalized_input,
    w_query,
    key_value_weight,
    head_sink_logits,
    w_output,
    cache_pairs,
    lengths,
    step_index,
    fresh_keys,
    fresh_values,
):
    row_count = normalized_input.shape[0]
    kv_heads = key_value_weight.shape[1]
    query = jnp.dot(normalized_input, w_query, preferred_element_type=jnp.float32).reshape(
        row_count, -1, HEAD_SIZE
    )
    cache_entry_pairs = jnp.dot(
        normalized_input,
        key_value_weight.reshape(key_value_weight.shape[0], -1),
        preferred_element_type=jnp.float32,
    ).reshape(row_count, kv_heads, 2 * HEAD_SIZE)
    position = (lengths + step_index).astype(jnp.float32)[:, None, None]
    rotated_rows = rotate(query, position).astype(jnp.bfloat16)
    fresh_keys = fresh_keys + [
        rotate(cache_entry_pairs[..., :HEAD_SIZE], position).astype(jnp.bfloat16)
    ]
    fresh_values = fresh_values + [cache_entry_pairs[..., HEAD_SIZE:].astype(jnp.bfloat16)]
    grouped_queries = rotated_rows.reshape(row_count, kv_heads, -1, HEAD_SIZE)
    new_keys = jnp.stack(fresh_keys, 1)
    new_values = jnp.stack(fresh_values, 1)
    cached = (
        jnp.einsum(
            "rkgd,rjkd->rkgj",
            grouped_queries,
            cache_pairs[..., :HEAD_SIZE],
            preferred_element_type=jnp.float32,
        )
        * 0.125
    )
    valid = (jnp.arange(cache_pairs.shape[1])[None, :] < lengths[:, None])[:, None, None, :]
    cached = jnp.where(valid, cached, -jnp.inf)
    fresh = (
        jnp.einsum("rkgd,rikd->rkgi", grouped_queries, new_keys, preferred_element_type=jnp.float32)
        * 0.125
    )
    sink_row = head_sink_logits.reshape(kv_heads, -1)[None]
    largest = jnp.maximum(jnp.maximum(jnp.max(cached, axis=-1), jnp.max(fresh, axis=-1)), sink_row)
    cached_exp = jnp.exp(cached - largest[..., None])
    fresh_exp = jnp.exp(fresh - largest[..., None])
    denominator = (
        jnp.sum(cached_exp, axis=-1) + jnp.sum(fresh_exp, axis=-1) + jnp.exp(sink_row - largest)
    )
    cached_probs = (cached_exp / denominator[..., None]).astype(jnp.bfloat16)
    fresh_probs = (fresh_exp / denominator[..., None]).astype(jnp.bfloat16)
    mixed = jnp.einsum(
        "rkgj,rjkd->rkgd",
        cached_probs,
        cache_pairs[..., HEAD_SIZE:],
        preferred_element_type=jnp.float32,
    )
    mixed = mixed + jnp.einsum(
        "rkgi,rikd->rkgd", fresh_probs, new_values, preferred_element_type=jnp.float32
    )
    attention_mix = mixed.reshape(row_count, -1).astype(jnp.bfloat16)
    partial_sum = jnp.dot(attention_mix, w_output, preferred_element_type=jnp.float32)
    return (partial_sum, fresh_keys, fresh_values)


def general_body(
    inputs,
    attention_gain,
    w_query,
    key_value_weight,
    head_sink_logits,
    w_output,
    cache_pairs,
    lengths,
    expert_gain,
    w_gate,
    w_up,
    w_down,
    routes,
    gate_weights,
):
    shards = lax.axis_size(("sec", "tp"))
    shard_index = lax.axis_index(("sec", "tp"))
    experts = lax.axis_size("grp") * w_gate.shape[0]
    group_rows = inputs.shape[1]
    width = inputs.shape[2]
    part_width = width // shards
    chosen = max(TOP, experts // 2)
    capacity = group_rows * TOP // chosen
    slot_total = experts * capacity
    gate_matrix = w_gate[0]
    up_matrix = w_up[0]
    down_matrix = w_down[0]
    fresh_keys = []
    fresh_values = []
    results = []
    for step_index in range(inputs.shape[0]):
        normalized_input = rms_norm(inputs[step_index], attention_gain)
        partial_sum, fresh_keys, fresh_values = attend(
            normalized_input,
            w_query,
            key_value_weight,
            head_sink_logits,
            w_output,
            cache_pairs,
            lengths,
            step_index,
            fresh_keys,
            fresh_values,
        )
        summed = lax.psum(partial_sum[None], ("sec", "tp"))
        middle = (inputs[step_index][None].astype(jnp.float32) + summed).astype(jnp.bfloat16)
        route_rows = routes[step_index][None]
        step_count = middle.shape[0]
        expert_in = rms_norm(middle, expert_gain)
        flat_routes = route_rows.reshape(step_count, group_rows * TOP)
        onehot = (flat_routes[..., None] == jnp.arange(experts)[None, None, :]).astype(jnp.int32)
        earlier = jnp.cumsum(onehot, axis=1) - onehot
        slot_index = jnp.sum(earlier * onehot, axis=-1).reshape(step_count, group_rows, TOP)
        target = route_rows * capacity + slot_index
        placed = target[..., None] == jnp.arange(slot_total)[None, None, None, :]
        dispatch_table = jnp.sum(placed.astype(jnp.int32), axis=2).astype(jnp.bfloat16)
        combine_table = jnp.sum(
            jnp.where(placed, gate_weights[step_index][None][..., None], 0.0), axis=2
        )
        outgoing = jnp.einsum(
            "crm,crd->cmd", dispatch_table, expert_in, preferred_element_type=jnp.float32
        )
        outgoing = outgoing.astype(jnp.bfloat16).reshape(step_count, experts, capacity, width)
        arrived = lax.all_to_all(outgoing, "grp", split_axis=1, concat_axis=1, tiled=True)
        gate_h = jnp.einsum(
            "snpd,dh->snph", arrived, gate_matrix, preferred_element_type=jnp.float32
        )
        up_h = jnp.einsum("snpd,dh->snph", arrived, up_matrix, preferred_element_type=jnp.float32)
        act = ((up_h + 1.0) * gate_h * jax.nn.sigmoid(1.702 * gate_h)).astype(jnp.bfloat16)
        partial_out = jnp.einsum(
            "snph,hd->snpd", act, down_matrix, preferred_element_type=jnp.float32
        )
        reduced = lax.psum_scatter(
            partial_out, ("sec", "tp"), scatter_dimension=3, tiled=True
        ).astype(jnp.bfloat16)
        returned = lax.all_to_all(reduced, "grp", split_axis=1, concat_axis=1, tiled=True)
        returned_rows = returned.reshape(step_count, slot_total, part_width).astype(jnp.float32)
        weighted = jnp.einsum(
            "srm,smd->srd", combine_table, returned_rows, precision=lax.Precision.HIGHEST
        )
        own_middle = lax.dynamic_slice_in_dim(
            middle, shard_index * part_width, part_width, 2
        ).astype(jnp.float32)
        results.append((own_middle + weighted).astype(jnp.bfloat16)[0])
    return jnp.stack(results, 0)


LANES = 384
BASE = 150000.0
MIB = 1 << 20


def shape_of(shape, dtype=jnp.bfloat16):
    return jax.ShapeDtypeStruct(shape, dtype)


def vmem():
    return pl.BlockSpec(memory_space=pltpu.VMEM)


def smem():
    return pl.BlockSpec(memory_space=pltpu.SMEM)


def outside():
    return pl.BlockSpec(memory_space=pltpu.HBM)


def dot_last(left, right):
    return lax.dot_general(left, right, (((1,), (1,)), ((), ())), preferred_element_type=jnp.float32)


def swap(value, axes, mask):
    size = lax.axis_size(axes)
    return lax.ppermute(value, axes, [(i, i ^ mask) for i in range(size)])


def swap_by_core(value, axis, masks):
    size = lax.axis_size(axis)
    pairs = [(s * size + i, s * size + (i ^ masks[s])) for s in range(2) for i in range(size)]
    return lax.ppermute(value, ("sec", axis), pairs)


def shard_swaps(parts):
    return [swap_by_core(part, "tp", masks) for part, masks in zip(parts, ((3, 3), (1, 2), (2, 1)))]


def shard_masks():
    sec = lax.axis_index("sec")
    return 3, 1 + sec, 2 - sec


def split_width(width):
    cuts = list(range(0, width, 768)) + [width]
    return list(zip(cuts[:-1], cuts[1:]))


def attention_kernel(lengths_hbm, sinks_hbm, routes_hbm, weights_hbm, gain_hbm, x_hbm, wq_hbm, wkv_hbm, cache_hbm, wo_hbm,
                     other_ref, own_x_ref, mix_ref, wo_ref,
                     lengths_ref, sinks_ref, routes_ref, weights_ref, gain_ref, x_ref, wq_ref, wkv_ref, cache_ref,
                     xs_ref, turned_ref, mixed_ref, sems):
    total_rows, width = x_ref.shape
    rows, slots, pair = cache_ref.shape
    steps = total_rows // rows
    heads = wq_ref.shape[1] // HEAD_SIZE
    per_row = heads * steps
    tps = other_ref.shape[0]
    cuts = split_width(width)
    small = [(lengths_hbm, lengths_ref), (x_hbm, x_ref), (gain_hbm, gain_ref), (routes_hbm, routes_ref), (weights_hbm, weights_ref),
             (sinks_hbm, sinks_ref)]
    small = [pltpu.make_async_copy(source, target, sems.at[n]) for n, (source, target) in enumerate(small)]
    copies = [pltpu.make_async_copy(wkv_hbm, wkv_ref, sems.at[6])]
    for n, (low, high) in enumerate(cuts):
        part = pl.ds(low, high - low)
        copies.append(pltpu.make_async_copy(wq_hbm.at[part], wq_ref.at[part], sems.at[9 + n]))
    copies.append(pltpu.make_async_copy(cache_hbm, cache_ref, sems.at[7]))
    copies.append(pltpu.make_async_copy(wo_hbm, wo_ref, sems.at[8]))
    for copy in small + copies:
        copy.start()
    small[1].wait()
    small[2].wait()
    x = x_ref[...].astype(jnp.float32)
    scale = lax.rsqrt(jnp.mean(x * x, axis=-1, keepdims=True) + 1e-05)
    normed = (x * scale * gain_ref[...].reshape(1, width)).astype(jnp.bfloat16)
    copies[0].wait()
    pairs = jnp.dot(normed, wkv_ref[...], preferred_element_type=jnp.float32)
    query = jnp.zeros((total_rows, wq_ref.shape[1]), jnp.float32)
    for n, (low, high) in enumerate(cuts[:-1]):
        copies[1 + n].wait()
        query = query + jnp.dot(normed[:, low:high], wq_ref[low:high, :], preferred_element_type=jnp.float32)
    for copy in (small[0], *small[3:], copies[len(cuts)]):
        copy.wait()
    query = query + jnp.dot(normed[:, cuts[-1][0]:], wq_ref[cuts[-1][0]:, :], preferred_element_type=jnp.float32)

    lane = lax.broadcasted_iota(jnp.int32, (total_rows, pair), 1)
    line = lax.broadcasted_iota(jnp.int32, (total_rows, pair), 0)
    position = jnp.zeros((total_rows, pair), jnp.int32)
    for r in range(rows):
        for s in range(steps):
            position = jnp.where(line == s * rows + r, lengths_ref[r] + s, position)
    half = HEAD_SIZE // 2
    counter = jnp.bitwise_and(lane, half - 1).astype(jnp.float32)
    frequency = jnp.exp(counter * jnp.float32(-2.0 / HEAD_SIZE * np.log(BASE)))
    angle = position.astype(jnp.float32) * frequency
    cosine, sine = jnp.cos(angle), jnp.sin(angle)
    low_half = jnp.bitwise_and(lane, HEAD_SIZE - 1) < half
    sine = jnp.where(low_half, -sine, sine)

    def turn(two):
        return two * cosine + jnp.where(low_half, pltpu.roll(two, pair - half, 1), pltpu.roll(two, half, 1)) * sine

    spare = xs_ref.shape[1] - width
    spare_at = lax.broadcasted_iota(jnp.int32, (rows, spare), 1)
    corner = lax.broadcasted_iota(jnp.int32, (rows, rows), 0) == lax.broadcasted_iota(jnp.int32, (rows, rows), 1)
    tables = []
    for s in range(steps):
        table = jnp.zeros((rows, spare), jnp.float32)
        for e in range(TOP):
            across = jnp.sum(jnp.where(routes_ref[s] == e, weights_ref[s], 0.0), axis=0, keepdims=True)
            column = jnp.sum(jnp.where(corner, across, 0.0), axis=1, keepdims=True)
            high_part = column.astype(jnp.bfloat16).astype(jnp.float32)
            table = jnp.where(spare_at == 2 * e, high_part, jnp.where(spare_at == 2 * e + 1, column - high_part, table))
        tables.append(table)
    xs_ref[...] = jnp.concatenate([x, jnp.concatenate(tables, axis=0)], axis=1)
    own = (lax.axis_index("sec") * tps + lax.axis_index("tp")) * LANES
    own_x_ref[...] = xs_ref[:, pl.ds(pl.multiple_of(own, LANES), LANES)]
    is_key = lane < HEAD_SIZE
    fresh = jnp.where(is_key, turn(pairs), pairs).astype(jnp.bfloat16)
    for m in range(heads // 2):
        two = turn(query[:, m * pair:(m + 1) * pair])
        for odd in range(2):
            one = two if odd == 0 else pltpu.roll(two, HEAD_SIZE, 1)
            one = jnp.where(is_key, one, 0.0)
            for s in range(steps):
                slot = (2 * m + odd) * steps + s
                turned_ref[pl.ds(slot, rows, stride=per_row), :] = one[s * rows:(s + 1) * rows]
    turned = turned_ref[...].astype(jnp.bfloat16)

    copies[-2].wait()
    place = lax.broadcasted_iota(jnp.int32, (per_row, slots), 1)
    scores = []
    for r in range(rows):
        score = dot_last(turned[r * per_row:(r + 1) * per_row], cache_ref[r]) * 0.125
        scores.append(jnp.where(place < lengths_ref[r], score, -jnp.inf))
    cached = jnp.concatenate(scores, axis=0)
    row_at = lax.broadcasted_iota(jnp.int32, (rows * per_row, total_rows), 0)
    fresh_at = lax.broadcasted_iota(jnp.int32, (rows * per_row, total_rows), 1)
    seen = (row_at // per_row == fresh_at % rows) & (fresh_at // rows <= row_at % steps)
    new = jnp.where(seen, dot_last(turned, fresh) * 0.125, -jnp.inf)
    head_at = lax.broadcasted_iota(jnp.int32, (rows * per_row, 1), 0) % per_row // steps
    sink = jnp.zeros((rows * per_row, 1), jnp.float32)
    for h in range(heads):
        sink = jnp.where(head_at == h, sinks_ref[h], sink)
    largest = jnp.maximum(jnp.maximum(jnp.max(cached, axis=-1, keepdims=True), jnp.max(new, axis=-1, keepdims=True)), sink)
    cached = jnp.exp(cached - largest)
    new = jnp.exp(new - largest)
    total = jnp.sum(cached, axis=-1, keepdims=True) + jnp.sum(new, axis=-1, keepdims=True) + jnp.exp(sink - largest)
    share = 1.0 / total
    cached = (cached * share).astype(jnp.bfloat16)
    new = (new * share).astype(jnp.bfloat16)
    mixed = []
    for r in range(rows):
        mixed.append(jnp.dot(cached[r * per_row:(r + 1) * per_row], cache_ref[r], preferred_element_type=jnp.float32))
    mixed_ref[...] = jnp.concatenate(mixed, axis=0) + jnp.dot(new, fresh, preferred_element_type=jnp.float32)

    def head(h):
        return jnp.concatenate([mixed_ref[pl.ds(h * steps + s, rows, stride=per_row), :] for s in range(steps)], axis=0)

    mix_ref[...] = jnp.concatenate(
        [jnp.where(is_key, pltpu.roll(head(2 * m), HEAD_SIZE, 1), head(2 * m + 1)) for m in range(heads // 2)], axis=1
    ).astype(jnp.bfloat16)
    copies[-1].wait()
    project(mix_ref, wo_ref, other_ref, 1 - lax.axis_index("sec"))


def project(mix_ref, wo_ref, out_ref, side):
    width, (tps, total_rows, _) = wo_ref.shape[0], out_ref.shape
    for at in range(2):
        start, stop = at * tps * LANES, min((at + 1) * tps * LANES, width)

        @pl.when(side == at)
        def _(start=start, stop=stop):
            partial = dot_last(mix_ref[...], wo_ref[start:stop, :])
            for t in range(tps):
                low, high = t * LANES, min((t + 1) * LANES, stop - start)
                piece = partial[:, low:high]
                if high - low < LANES:
                    piece = jnp.concatenate([piece, jnp.zeros((total_rows, LANES - (high - low)), jnp.float32)], axis=1)
                out_ref[t] = piece.astype(out_ref.dtype)


def own_projection_kernel(mix_ref, wo_ref, mine_ref):
    project(mix_ref, wo_ref, mine_ref, lax.axis_index("sec"))


def attention_partial(flat, gain, w_query, key_value, sinks, w_output, cache, lengths, routes, weights, secs, tps):
    total_rows, width = flat.shape
    rows, slots, pair = cache.shape
    per_row = w_query.shape[1] // HEAD_SIZE * (total_rows // rows)
    shards = secs * tps
    operands = (lengths, sinks, routes, weights, gain, flat, w_query, key_value, cache, w_output.swapaxes(0, 1))
    return pl.pallas_call(
        attention_kernel,
        name="attention",
        out_shape=[shape_of((tps, total_rows, LANES)), shape_of((total_rows, LANES), jnp.float32),
                   shape_of((total_rows, w_output.shape[0])), shape_of((width, w_output.shape[0]))],
        in_specs=[outside()] * len(operands),
        out_specs=[vmem()] * 4,
        scratch_shapes=[
            pltpu.SMEM(lengths.shape, jnp.int32),
            pltpu.SMEM(sinks.shape, jnp.float32),
            pltpu.VMEM(routes.shape, jnp.int32),
            pltpu.VMEM(weights.shape, jnp.float32),
            pltpu.VMEM(gain.shape, jnp.float32),
            pltpu.VMEM((total_rows, width), jnp.bfloat16),
            pltpu.VMEM(w_query.shape, jnp.bfloat16),
            pltpu.VMEM(key_value.shape, jnp.bfloat16),
            pltpu.VMEM(cache.shape, jnp.bfloat16),
            pltpu.VMEM((total_rows, shards * LANES), jnp.float32),
            pltpu.VMEM((rows * per_row, pair), jnp.float32),
            pltpu.VMEM((rows * per_row, pair), jnp.float32),
            pltpu.SemaphoreType.DMA((9 + len(split_width(width)),)),
        ],
        compiler_params=pltpu.CompilerParams(vmem_limit_bytes=24 * MIB),
    )(*[pltpu.with_memory_space_constraint(operand, pltpu.HBM) for operand in operands])


def call(kernel, name, outs, *operands, limit=4, flops=0):
    single = not isinstance(outs, list)
    held = [*operands, *([outs] if single else outs)]
    return pl.pallas_call(
        kernel,
        name=name,
        out_shape=outs,
        in_specs=[vmem()] * len(operands),
        out_specs=vmem() if single else [vmem()] * len(outs),
        compiler_params=pltpu.CompilerParams(vmem_limit_bytes=limit * MIB),
        cost_estimate=pl.CostEstimate(flops=flops, transcendentals=0,
                                      bytes_accessed=sum(math.prod(a.shape) * a.dtype.itemsize for a in held)),
    )(*operands)


def after_core_kernel(mine_ref, come_ref, own_ref, *send_refs):
    tp = lax.axis_index("tp")
    own_ref[...] = mine_ref[tp] + come_ref[tp].astype(jnp.float32)
    for mask, ref in zip(shard_masks(), send_refs):
        to = jnp.bitwise_xor(tp, mask)
        ref[...] = (mine_ref[to] + come_ref[to].astype(jnp.float32)).astype(jnp.bfloat16)


def after_core_halves_kernel(mine_ref, come_ref, own_ref, *send_refs):
    tp, half = lax.axis_index("tp"), mine_ref.shape[1] // 2
    own_ref[...] = mine_ref[tp] + come_ref[tp].astype(jnp.float32)
    for mask, second, first in zip(shard_masks(), send_refs[:3], send_refs[3:]):
        to = jnp.bitwise_xor(tp, mask)
        part = (mine_ref[to] + come_ref[to].astype(jnp.float32)).astype(jnp.bfloat16)
        second[...] = part[half:]
        first[...] = part[:half]


def add_all(*refs):
    total = refs[0][...]
    for ref in refs[1:]:
        total = total + ref[...].astype(jnp.float32)
    return total


def sum_kernel(*refs):
    refs[-1][...] = add_all(*refs[:-1]).astype(jnp.bfloat16).reshape(refs[-1].shape)


def sum_rows_kernel(own_ref, *refs, line):
    come, outs = refs[:3], refs[3:]
    lines = outs[0].shape[0]
    total = own_ref[line:line + len(outs) * lines]
    for ref in come:
        total = total + ref[...].astype(jnp.float32)
    for n, out in enumerate(outs):
        out[...] = total[n * lines:(n + 1) * lines].astype(out.dtype)


def scatter_shards(mine, come):
    tps, lines, part = mine.shape
    own, *parts = call(after_core_kernel, "after_core", [shape_of((lines, part), jnp.float32)] + [shape_of((lines, part))] * (tps - 1),
                       mine, come)
    return [own] + shard_swaps(parts)


def first_products(pieces, masks, side, x_ref, gain_ref, gate_ref, up_ref, gate_out, up_out, square_out):
    width, lines = gate_ref.shape[1], x_ref.shape[0]
    tp = lax.axis_index("tp")
    for mask, piece in zip(masks, pieces):
        at = pl.multiple_of(jnp.bitwise_xor(tp, mask) * LANES, LANES)
        x_ref[:, pl.ds(at, LANES)] = piece[...].reshape(lines, LANES)
    for at in range(2):
        start, stop = at * x_ref.shape[1], min((at + 1) * x_ref.shape[1], width)

        @pl.when(side == at)
        def _(start=start, stop=stop):
            x = x_ref[:, :stop - start].astype(jnp.float32)
            square_out[...] = jnp.broadcast_to(jnp.sum(x * x, axis=-1, keepdims=True), square_out.shape)
            scaled = (x * gain_ref[:, start:stop]).astype(jnp.bfloat16)
            gate_out[...] = dot_last(scaled, gate_ref[:, start:stop])
            up_out[...] = dot_last(scaled, up_ref[:, start:stop])


def near_kernel(gain_ref, gate_ref, up_ref, *refs):
    pieces, (x_ref, gate_out, up_out, square_out) = refs[:-4], refs[-4:]
    first_products(pieces, (0, *shard_masks()), lax.axis_index("sec"), x_ref, gain_ref, gate_ref, up_ref, gate_out, up_out,
                   square_out)


def second_product(act_ref, down_ref, out_ref, side):
    width, (tps, lines, part) = down_ref.shape[1], out_ref.shape
    for at in range(2):
        start, stop = at * tps * part, (at + 1) * tps * part
        shift = start % 128

        @pl.when(side == at)
        def _(start=start, stop=stop, shift=shift):
            out = jnp.dot(act_ref[...], down_ref[:, start - shift:stop], preferred_element_type=jnp.float32)
            for t in range(tps):
                out_ref[t] = out[:, shift + t * part:shift + (t + 1) * part].astype(out_ref.dtype)


def far_kernel(gain_ref, gate_ref, up_ref, down_ref, near_x_ref, near_gate_ref, near_up_ref, near_square_ref, *refs):
    pieces, (other_ref, act_ref, far_x_ref, gate_out, up_out, square_out) = refs[:-6], refs[-6:]
    sec, grp = lax.axis_index("sec"), lax.axis_index("grp")
    masks = shard_masks()
    first_products(pieces, (0, masks[0], masks[2], masks[1]), 1 - sec, far_x_ref, gain_ref, gate_ref, up_ref, gate_out, up_out,
                   square_out)
    width, half = gate_ref.shape[1], near_x_ref.shape[1]
    spare = jnp.where(sec == 1, near_x_ref[:, width - half:], far_x_ref[:, width - half:]).astype(jnp.float32)
    spare_at = lax.broadcasted_iota(jnp.int32, spare.shape, 1)
    weight = jnp.sum(jnp.where((spare_at == 2 * grp) | (spare_at == 2 * grp + 1), spare, 0.0), axis=1, keepdims=True)
    square = (near_square_ref[...] + square_out[...])[:, :1]
    scale = lax.rsqrt(square / width + 1e-05)
    gate_h = (near_gate_ref[...] + gate_out[...]) * scale
    up_h = (near_up_ref[...] + up_out[...]) * scale
    act_ref[...] = ((up_h + 1.0) * gate_h * jax.nn.sigmoid(1.702 * gate_h) * weight).astype(jnp.bfloat16)
    second_product(act_ref, down_ref, other_ref, 1 - sec)


def last_kernel(act_ref, down_ref, near_x_ref, far_x_ref, mine_ref, middle_ref, row_ref):
    sec, tp = lax.axis_index("sec"), lax.axis_index("tp")
    second_product(act_ref, down_ref, mine_ref, sec)
    total_rows, part = middle_ref.shape
    near, far = near_x_ref[:total_rows].astype(jnp.float32), far_x_ref[:total_rows].astype(jnp.float32)
    first = sec == 0
    x = jnp.concatenate([jnp.where(first, near, far), jnp.where(first, far, near)], axis=1)
    for c in range(row_ref.shape[0]):
        row_ref[c] = x[:, c * part:(c + 1) * part]
    middle_ref[...] = row_ref[sec * mine_ref.shape[0] + tp]


def experts(gain, w_gate, w_up, w_down, pieces, part):
    gain, w_gate, w_up = gain.reshape(1, -1), w_gate.swapaxes(0, 1), w_up.swapaxes(0, 1)
    (hidden, width), tps, (groups, total_rows, _) = w_gate.shape, len(pieces), pieces[0].shape
    lines = groups * total_rows
    far_pieces = [swap(piece, "sec", 1) for piece in pieces]
    halves = [shape_of((lines, tps * LANES)), shape_of((lines, hidden), jnp.float32), shape_of((lines, hidden), jnp.float32),
              shape_of((lines, 128), jnp.float32)]
    near = call(near_kernel, "near_columns", halves, gain, w_gate, w_up, *pieces, limit=12, flops=2 * lines * width * hidden)
    other, act, far_x = pl.pallas_call(
        far_kernel,
        name="far_columns",
        out_shape=[shape_of((tps, lines, part)), shape_of((lines, hidden)), halves[0]],
        in_specs=[vmem()] * (8 + len(far_pieces)),
        out_specs=[vmem()] * 3,
        scratch_shapes=[pltpu.VMEM(half.shape, half.dtype) for half in halves[1:]],
        compiler_params=pltpu.CompilerParams(vmem_limit_bytes=16 * MIB),
    )(gain, w_gate, w_up, w_down, *near, *far_pieces)
    come = swap(other, "sec", 1)
    mine, middle = pl.pallas_call(
        last_kernel,
        name="own_columns",
        out_shape=[shape_of((tps, lines, part), jnp.float32), shape_of((total_rows, part), jnp.float32)],
        in_specs=[vmem()] * 4,
        out_specs=[vmem()] * 2,
        scratch_shapes=[pltpu.VMEM((2 * tps, total_rows, part), jnp.float32)],
        compiler_params=pltpu.CompilerParams(vmem_limit_bytes=12 * MIB),
        cost_estimate=pl.CostEstimate(flops=lines * width * hidden, transcendentals=0, bytes_accessed=2 * lines * width),
    )(act, w_down, near[0], far_x)
    return mine, come, middle


def every_expert_body(inputs, attention_gain, w_query, key_value_weight, head_sink_logits, w_output, cache_pairs, lengths,
                      expert_gain, w_gate, w_up, w_down, routes, gate_weights):
    secs, tps, groups = lax.axis_size("sec"), lax.axis_size("tp"), lax.axis_size("grp")
    steps, rows, width = inputs.shape
    flat = inputs.reshape(steps * rows, width)
    other, own_x, mix, held = attention_partial(
        flat, attention_gain, w_query, key_value_weight[:, 0], head_sink_logits, w_output, cache_pairs[:, :, 0], lengths,
        routes.swapaxes(1, 2), gate_weights.swapaxes(1, 2), secs, tps)
    come = swap(other, "sec", 1)
    mine = call(own_projection_kernel, "own_projection", shape_of(other.shape, jnp.float32), mix, held, limit=12,
                flops=mix.size * width)
    middle = call(sum_kernel, "sum", shape_of((steps * rows, LANES)), *scatter_shards(mine, come), own_x)
    stacked = jnp.stack([middle] + [swap(middle, "grp", m) for m in range(1, groups)])
    pieces = [stacked] + shard_swaps([stacked] * (tps - 1))
    part = width // (secs * tps)
    mine, come, own_middle = experts(expert_gain, w_gate[0], w_up[0], w_down[0], pieces, part)
    lines = steps * rows
    own, *parts = call(after_core_halves_kernel, "after_core_halves",
                       [shape_of((groups * lines, part), jnp.float32)] + [shape_of((groups // 2 * lines, part))] * 6, mine, come)
    second_come, first_come = shard_swaps(parts[:3]), shard_swaps(parts[3:])
    second, third = call(functools.partial(sum_rows_kernel, line=2 * lines), "sum_far_rows", [shape_of((lines, part))] * 2,
                         own, *second_come)
    third, second = swap(third, "grp", 3), swap(second, "grp", 2)
    own, nearest = call(functools.partial(sum_rows_kernel, line=0), "sum_near_rows",
                        [shape_of((lines, part), jnp.float32), shape_of((lines, part))], own, *first_come)
    return call(sum_kernel, "combine", shape_of((steps, rows, part)), own, third, second, swap(nearest, "grp", 1), own_middle)


def body(*args):
    sizes = lax.axis_size("sec"), lax.axis_size("tp"), lax.axis_size("grp"), args[9].shape[0]
    if sizes == (2, 4, TOP, 1):
        return every_expert_body(*args)
    return general_body(*args)


def solution(mesh):
    placed = (
        P(None, "grp", None),
        P(),
        P(None, ("sec", "tp")),
        P(None, ("sec", "tp"), None),
        P(("sec", "tp")),
        P(("sec", "tp"), None),
        P("grp", None, ("sec", "tp"), None),
        P("grp"),
        P(),
        P("grp", None, ("sec", "tp")),
        P("grp", None, ("sec", "tp")),
        P("grp", ("sec", "tp"), None),
        P(None, "grp", None),
        P(None, "grp", None),
    )
    return jax.shard_map(
        body, mesh=mesh, in_specs=placed, out_specs=P(None, "grp", ("sec", "tp")), check_vma=False
    )
```

```python
import functools
import math

import jax
import jax.numpy as jnp
import numpy as np
from jax import lax
from jax.experimental import pallas as pl
from jax.experimental.pallas import tpu as pltpu
from jax.sharding import PartitionSpec as P

HEAD_SIZE = 64
TOP = 4


def rms_norm(values, scale_row):
    widened = values.astype(jnp.float32)
    scale_factor = lax.rsqrt(jnp.mean(widened * widened, axis=-1, keepdims=True) + 1e-05)
    return (widened * scale_factor * scale_row).astype(jnp.bfloat16)


def rotate(vectors, position):
    half_size = vectors.shape[-1] // 2
    counter = jnp.arange(half_size).astype(jnp.float32)
    frequency = jnp.power(jnp.float32(150000.0), counter * (-2.0 / vectors.shape[-1]))
    angle_table = position * frequency
    cosine = jnp.cos(angle_table)
    sine_table = jnp.sin(angle_table)
    first_half = vectors[..., :half_size]
    second_half = vectors[..., half_size:]
    return jnp.concatenate(
        [
            first_half * cosine - second_half * sine_table,
            first_half * sine_table + second_half * cosine,
        ],
        axis=-1,
    )


def attend(
    normalized_input,
    w_query,
    key_value_weight,
    head_sink_logits,
    w_output,
    cache_pairs,
    lengths,
    step_index,
    fresh_keys,
    fresh_values,
):
    row_count = normalized_input.shape[0]
    kv_heads = key_value_weight.shape[1]
    query = jnp.dot(normalized_input, w_query, preferred_element_type=jnp.float32).reshape(
        row_count, -1, HEAD_SIZE
    )
    cache_entry_pairs = jnp.dot(
        normalized_input,
        key_value_weight.reshape(key_value_weight.shape[0], -1),
        preferred_element_type=jnp.float32,
    ).reshape(row_count, kv_heads, 2 * HEAD_SIZE)
    position = (lengths + step_index).astype(jnp.float32)[:, None, None]
    rotated_rows = rotate(query, position).astype(jnp.bfloat16)
    fresh_keys = fresh_keys + [
        rotate(cache_entry_pairs[..., :HEAD_SIZE], position).astype(jnp.bfloat16)
    ]
    fresh_values = fresh_values + [cache_entry_pairs[..., HEAD_SIZE:].astype(jnp.bfloat16)]
    grouped_queries = rotated_rows.reshape(row_count, kv_heads, -1, HEAD_SIZE)
    new_keys = jnp.stack(fresh_keys, 1)
    new_values = jnp.stack(fresh_values, 1)
    cached = (
        jnp.einsum(
            "rkgd,rjkd->rkgj",
            grouped_queries,
            cache_pairs[..., :HEAD_SIZE],
            preferred_element_type=jnp.float32,
        )
        * 0.125
    )
    valid = (jnp.arange(cache_pairs.shape[1])[None, :] < lengths[:, None])[:, None, None, :]
    cached = jnp.where(valid, cached, -jnp.inf)
    fresh = (
        jnp.einsum("rkgd,rikd->rkgi", grouped_queries, new_keys, preferred_element_type=jnp.float32)
        * 0.125
    )
    sink_row = head_sink_logits.reshape(kv_heads, -1)[None]
    largest = jnp.maximum(jnp.maximum(jnp.max(cached, axis=-1), jnp.max(fresh, axis=-1)), sink_row)
    cached_exp = jnp.exp(cached - largest[..., None])
    fresh_exp = jnp.exp(fresh - largest[..., None])
    denominator = (
        jnp.sum(cached_exp, axis=-1) + jnp.sum(fresh_exp, axis=-1) + jnp.exp(sink_row - largest)
    )
    cached_probs = (cached_exp / denominator[..., None]).astype(jnp.bfloat16)
    fresh_probs = (fresh_exp / denominator[..., None]).astype(jnp.bfloat16)
    mixed = jnp.einsum(
        "rkgj,rjkd->rkgd",
        cached_probs,
        cache_pairs[..., HEAD_SIZE:],
        preferred_element_type=jnp.float32,
    )
    mixed = mixed + jnp.einsum(
        "rkgi,rikd->rkgd", fresh_probs, new_values, preferred_element_type=jnp.float32
    )
    attention_mix = mixed.reshape(row_count, -1).astype(jnp.bfloat16)
    partial_sum = jnp.dot(attention_mix, w_output, preferred_element_type=jnp.float32)
    return (partial_sum, fresh_keys, fresh_values)


def general_body(
    inputs,
    attention_gain,
    w_query,
    key_value_weight,
    head_sink_logits,
    w_output,
    cache_pairs,
    lengths,
    expert_gain,
    w_gate,
    w_up,
    w_down,
    routes,
    gate_weights,
):
    shards = lax.axis_size(("sec", "tp"))
    shard_index = lax.axis_index(("sec", "tp"))
    experts = lax.axis_size("grp") * w_gate.shape[0]
    group_rows = inputs.shape[1]
    width = inputs.shape[2]
    part_width = width // shards
    chosen = max(TOP, experts // 2)
    capacity = group_rows * TOP // chosen
    slot_total = experts * capacity
    gate_matrix = w_gate[0]
    up_matrix = w_up[0]
    down_matrix = w_down[0]
    fresh_keys = []
    fresh_values = []
    results = []
    for step_index in range(inputs.shape[0]):
        normalized_input = rms_norm(inputs[step_index], attention_gain)
        partial_sum, fresh_keys, fresh_values = attend(
            normalized_input,
            w_query,
            key_value_weight,
            head_sink_logits,
            w_output,
            cache_pairs,
            lengths,
            step_index,
            fresh_keys,
            fresh_values,
        )
        summed = lax.psum(partial_sum[None], ("sec", "tp"))
        middle = (inputs[step_index][None].astype(jnp.float32) + summed).astype(jnp.bfloat16)
        route_rows = routes[step_index][None]
        step_count = middle.shape[0]
        expert_in = rms_norm(middle, expert_gain)
        flat_routes = route_rows.reshape(step_count, group_rows * TOP)
        onehot = (flat_routes[..., None] == jnp.arange(experts)[None, None, :]).astype(jnp.int32)
        earlier = jnp.cumsum(onehot, axis=1) - onehot
        slot_index = jnp.sum(earlier * onehot, axis=-1).reshape(step_count, group_rows, TOP)
        target = route_rows * capacity + slot_index
        placed = target[..., None] == jnp.arange(slot_total)[None, None, None, :]
        dispatch_table = jnp.sum(placed.astype(jnp.int32), axis=2).astype(jnp.bfloat16)
        combine_table = jnp.sum(
            jnp.where(placed, gate_weights[step_index][None][..., None], 0.0), axis=2
        )
        outgoing = jnp.einsum(
            "crm,crd->cmd", dispatch_table, expert_in, preferred_element_type=jnp.float32
        )
        outgoing = outgoing.astype(jnp.bfloat16).reshape(step_count, experts, capacity, width)
        arrived = lax.all_to_all(outgoing, "grp", split_axis=1, concat_axis=1, tiled=True)
        gate_h = jnp.einsum(
            "snpd,dh->snph", arrived, gate_matrix, preferred_element_type=jnp.float32
        )
        up_h = jnp.einsum("snpd,dh->snph", arrived, up_matrix, preferred_element_type=jnp.float32)
        act = ((up_h + 1.0) * gate_h * jax.nn.sigmoid(1.702 * gate_h)).astype(jnp.bfloat16)
        partial_out = jnp.einsum(
            "snph,hd->snpd", act, down_matrix, preferred_element_type=jnp.float32
        )
        reduced = lax.psum_scatter(
            partial_out, ("sec", "tp"), scatter_dimension=3, tiled=True
        ).astype(jnp.bfloat16)
        returned = lax.all_to_all(reduced, "grp", split_axis=1, concat_axis=1, tiled=True)
        returned_rows = returned.reshape(step_count, slot_total, part_width).astype(jnp.float32)
        weighted = jnp.einsum(
            "srm,smd->srd", combine_table, returned_rows, precision=lax.Precision.HIGHEST
        )
        own_middle = lax.dynamic_slice_in_dim(
            middle, shard_index * part_width, part_width, 2
        ).astype(jnp.float32)
        results.append((own_middle + weighted).astype(jnp.bfloat16)[0])
    return jnp.stack(results, 0)


LANES = 384
BASE = 150000.0
MIB = 1 << 20


def shape_of(shape, dtype=jnp.bfloat16):
    return jax.ShapeDtypeStruct(shape, dtype)


def vmem():
    return pl.BlockSpec(memory_space=pltpu.VMEM)


def smem():
    return pl.BlockSpec(memory_space=pltpu.SMEM)


def outside():
    return pl.BlockSpec(memory_space=pltpu.HBM)


def dot_last(left, right):
    return lax.dot_general(left, right, (((1,), (1,)), ((), ())), preferred_element_type=jnp.float32)


def swap(value, axes, mask):
    size = lax.axis_size(axes)
    return lax.ppermute(value, axes, [(i, i ^ mask) for i in range(size)])


def lane_of(by_group):
    tp = lax.axis_index("tp")
    number = lax.axis_index("sec") ^ (tp & 1) ^ (tp >> 1)
    return number ^ (lax.axis_index("grp") & 1) if by_group else number


def lane_swap(value, mask, shard_masks_by_lane, by_group):
    groups, tps = lax.axis_size("grp"), lax.axis_size("tp")

    def parity(group, shard):
        return (shard & 1) ^ (shard >> 1) ^ (group & 1 if by_group else 0)

    pairs = []
    for core in range(2):
        for group in range(groups):
            for shard in range(tps):
                number = core ^ parity(group, shard)
                to_group, to_shard = group ^ mask, shard ^ shard_masks_by_lane[number]
                to_core = number ^ parity(to_group, to_shard)
                pairs.append(((core * groups + group) * tps + shard, (to_core * groups + to_group) * tps + to_shard))
    return lax.ppermute(value, ("sec", "grp", "tp"), pairs)


def shard_swaps(parts, by_group):
    return [lane_swap(part, 0, masks, by_group) for part, masks in zip(parts, ((3, 3), (1, 2), (2, 1)))]


def shard_masks(by_group):
    number = lane_of(by_group)
    return 3, 1 + number, 2 - number


def split_width(width):
    cuts = list(range(0, width, 768)) + [width]
    return list(zip(cuts[:-1], cuts[1:]))


def attention_kernel(lengths_hbm, sinks_hbm, routes_hbm, weights_hbm, gain_hbm, x_hbm, wq_hbm, wkv_hbm, cache_hbm, wo_hbm,
                     other_ref, own_x_ref, mix_ref, wo_ref,
                     lengths_ref, sinks_ref, routes_ref, weights_ref, gain_ref, x_ref, wq_ref, wkv_ref, cache_ref,
                     xs_ref, turned_ref, mixed_ref, sems):
    total_rows, width = x_ref.shape
    rows, slots, pair = cache_ref.shape
    steps = total_rows // rows
    heads = wq_ref.shape[1] // HEAD_SIZE
    per_row = heads * steps
    tps = other_ref.shape[0]
    cuts = split_width(width)
    small = [(lengths_hbm, lengths_ref), (x_hbm, x_ref), (gain_hbm, gain_ref), (routes_hbm, routes_ref), (weights_hbm, weights_ref),
             (sinks_hbm, sinks_ref)]
    small = [pltpu.make_async_copy(source, target, sems.at[n]) for n, (source, target) in enumerate(small)]
    copies = [pltpu.make_async_copy(wkv_hbm, wkv_ref, sems.at[6])]
    for n, (low, high) in enumerate(cuts):
        part = pl.ds(low, high - low)
        copies.append(pltpu.make_async_copy(wq_hbm.at[part], wq_ref.at[part], sems.at[9 + n]))
    copies.append(pltpu.make_async_copy(cache_hbm, cache_ref, sems.at[7]))
    copies.append(pltpu.make_async_copy(wo_hbm, wo_ref, sems.at[8]))
    for copy in small + copies:
        copy.start()
    small[1].wait()
    small[2].wait()
    x = x_ref[...].astype(jnp.float32)
    scale = lax.rsqrt(jnp.mean(x * x, axis=-1, keepdims=True) + 1e-05)
    normed = (x * scale * gain_ref[...].reshape(1, width)).astype(jnp.bfloat16)
    copies[0].wait()
    pairs = jnp.dot(normed, wkv_ref[...], preferred_element_type=jnp.float32)
    query = jnp.zeros((total_rows, wq_ref.shape[1]), jnp.float32)
    for n, (low, high) in enumerate(cuts[:-1]):
        copies[1 + n].wait()
        query = query + jnp.dot(normed[:, low:high], wq_ref[low:high, :], preferred_element_type=jnp.float32)
    for copy in (small[0], *small[3:], copies[len(cuts)]):
        copy.wait()
    query = query + jnp.dot(normed[:, cuts[-1][0]:], wq_ref[cuts[-1][0]:, :], preferred_element_type=jnp.float32)

    lane = lax.broadcasted_iota(jnp.int32, (total_rows, pair), 1)
    line = lax.broadcasted_iota(jnp.int32, (total_rows, pair), 0)
    position = jnp.zeros((total_rows, pair), jnp.int32)
    for r in range(rows):
        for s in range(steps):
            position = jnp.where(line == s * rows + r, lengths_ref[r] + s, position)
    half = HEAD_SIZE // 2
    counter = jnp.bitwise_and(lane, half - 1).astype(jnp.float32)
    frequency = jnp.exp(counter * jnp.float32(-2.0 / HEAD_SIZE * np.log(BASE)))
    angle = position.astype(jnp.float32) * frequency
    cosine, sine = jnp.cos(angle), jnp.sin(angle)
    low_half = jnp.bitwise_and(lane, HEAD_SIZE - 1) < half
    sine = jnp.where(low_half, -sine, sine)

    def turn(two):
        return two * cosine + jnp.where(low_half, pltpu.roll(two, pair - half, 1), pltpu.roll(two, half, 1)) * sine

    spare = xs_ref.shape[1] - width
    spare_at = lax.broadcasted_iota(jnp.int32, (rows, spare), 1)
    corner = lax.broadcasted_iota(jnp.int32, (rows, rows), 0) == lax.broadcasted_iota(jnp.int32, (rows, rows), 1)
    tables = []
    for s in range(steps):
        table = jnp.zeros((rows, spare), jnp.float32)
        for e in range(TOP):
            across = jnp.sum(jnp.where(routes_ref[s] == e, weights_ref[s], 0.0), axis=0, keepdims=True)
            column = jnp.sum(jnp.where(corner, across, 0.0), axis=1, keepdims=True)
            high_part = column.astype(jnp.bfloat16).astype(jnp.float32)
            table = jnp.where(spare_at == 2 * e, high_part, jnp.where(spare_at == 2 * e + 1, column - high_part, table))
        tables.append(table)
    xs_ref[...] = jnp.concatenate([x, jnp.concatenate(tables, axis=0)], axis=1)
    own = (lane_of(True) * tps + lax.axis_index("tp")) * LANES
    own_x_ref[...] = xs_ref[:, pl.ds(pl.multiple_of(own, LANES), LANES)]
    is_key = lane < HEAD_SIZE
    fresh = jnp.where(is_key, turn(pairs), pairs).astype(jnp.bfloat16)
    for m in range(heads // 2):
        two = turn(query[:, m * pair:(m + 1) * pair])
        for odd in range(2):
            one = two if odd == 0 else pltpu.roll(two, HEAD_SIZE, 1)
            one = jnp.where(is_key, one, 0.0)
            for s in range(steps):
                slot = (2 * m + odd) * steps + s
                turned_ref[pl.ds(slot, rows, stride=per_row), :] = one[s * rows:(s + 1) * rows]
    turned = turned_ref[...].astype(jnp.bfloat16)

    copies[-2].wait()
    place = lax.broadcasted_iota(jnp.int32, (per_row, slots), 1)
    scores = []
    for r in range(rows):
        score = dot_last(turned[r * per_row:(r + 1) * per_row], cache_ref[r]) * 0.125
        scores.append(jnp.where(place < lengths_ref[r], score, -jnp.inf))
    cached = jnp.concatenate(scores, axis=0)
    row_at = lax.broadcasted_iota(jnp.int32, (rows * per_row, total_rows), 0)
    fresh_at = lax.broadcasted_iota(jnp.int32, (rows * per_row, total_rows), 1)
    seen = (row_at // per_row == fresh_at % rows) & (fresh_at // rows <= row_at % steps)
    new = jnp.where(seen, dot_last(turned, fresh) * 0.125, -jnp.inf)
    head_at = lax.broadcasted_iota(jnp.int32, (rows * per_row, 1), 0) % per_row // steps
    sink = jnp.zeros((rows * per_row, 1), jnp.float32)
    for h in range(heads):
        sink = jnp.where(head_at == h, sinks_ref[h], sink)
    largest = jnp.maximum(jnp.maximum(jnp.max(cached, axis=-1, keepdims=True), jnp.max(new, axis=-1, keepdims=True)), sink)
    cached = jnp.exp(cached - largest)
    new = jnp.exp(new - largest)
    total = jnp.sum(cached, axis=-1, keepdims=True) + jnp.sum(new, axis=-1, keepdims=True) + jnp.exp(sink - largest)
    share = 1.0 / total
    cached = (cached * share).astype(jnp.bfloat16)
    new = (new * share).astype(jnp.bfloat16)
    mixed = []
    for r in range(rows):
        mixed.append(jnp.dot(cached[r * per_row:(r + 1) * per_row], cache_ref[r], preferred_element_type=jnp.float32))
    mixed_ref[...] = jnp.concatenate(mixed, axis=0) + jnp.dot(new, fresh, preferred_element_type=jnp.float32)

    def head(h):
        return jnp.concatenate([mixed_ref[pl.ds(h * steps + s, rows, stride=per_row), :] for s in range(steps)], axis=0)

    mix_ref[...] = jnp.concatenate(
        [jnp.where(is_key, pltpu.roll(head(2 * m), HEAD_SIZE, 1), head(2 * m + 1)) for m in range(heads // 2)], axis=1
    ).astype(jnp.bfloat16)
    copies[-1].wait()
    project(mix_ref, wo_ref, other_ref, 1 - lane_of(True))


def project(mix_ref, wo_ref, out_ref, side):
    width, (tps, total_rows, _) = wo_ref.shape[0], out_ref.shape
    for at in range(2):
        start, stop = at * tps * LANES, min((at + 1) * tps * LANES, width)

        @pl.when(side == at)
        def _(start=start, stop=stop):
            partial = dot_last(mix_ref[...], wo_ref[start:stop, :])
            for t in range(tps):
                low, high = t * LANES, min((t + 1) * LANES, stop - start)
                piece = partial[:, low:high]
                if high - low < LANES:
                    piece = jnp.concatenate([piece, jnp.zeros((total_rows, LANES - (high - low)), jnp.float32)], axis=1)
                out_ref[t] = piece.astype(out_ref.dtype)


def own_projection_kernel(mix_ref, wo_ref, mine_ref):
    project(mix_ref, wo_ref, mine_ref, lane_of(True))


def attention_partial(flat, gain, w_query, key_value, sinks, w_output, cache, lengths, routes, weights, secs, tps):
    total_rows, width = flat.shape
    rows, slots, pair = cache.shape
    per_row = w_query.shape[1] // HEAD_SIZE * (total_rows // rows)
    shards = secs * tps
    operands = (lengths, sinks, routes, weights, gain, flat, w_query, key_value, cache, w_output.swapaxes(0, 1))
    return pl.pallas_call(
        attention_kernel,
        name="attention",
        out_shape=[shape_of((tps, total_rows, LANES)), shape_of((total_rows, LANES), jnp.float32),
                   shape_of((total_rows, w_output.shape[0])), shape_of((width, w_output.shape[0]))],
        in_specs=[outside()] * len(operands),
        out_specs=[vmem()] * 4,
        scratch_shapes=[
            pltpu.SMEM(lengths.shape, jnp.int32),
            pltpu.SMEM(sinks.shape, jnp.float32),
            pltpu.VMEM(routes.shape, jnp.int32),
            pltpu.VMEM(weights.shape, jnp.float32),
            pltpu.VMEM(gain.shape, jnp.float32),
            pltpu.VMEM((total_rows, width), jnp.bfloat16),
            pltpu.VMEM(w_query.shape, jnp.bfloat16),
            pltpu.VMEM(key_value.shape, jnp.bfloat16),
            pltpu.VMEM(cache.shape, jnp.bfloat16),
            pltpu.VMEM((total_rows, shards * LANES), jnp.float32),
            pltpu.VMEM((rows * per_row, pair), jnp.float32),
            pltpu.VMEM((rows * per_row, pair), jnp.float32),
            pltpu.SemaphoreType.DMA((9 + len(split_width(width)),)),
        ],
        compiler_params=pltpu.CompilerParams(vmem_limit_bytes=24 * MIB),
    )(*[pltpu.with_memory_space_constraint(operand, pltpu.HBM) for operand in operands])


def call(kernel, name, outs, *operands, limit=4, flops=0):
    single = not isinstance(outs, list)
    held = [*operands, *([outs] if single else outs)]
    return pl.pallas_call(
        kernel,
        name=name,
        out_shape=outs,
        in_specs=[vmem()] * len(operands),
        out_specs=vmem() if single else [vmem()] * len(outs),
        compiler_params=pltpu.CompilerParams(vmem_limit_bytes=limit * MIB),
        cost_estimate=pl.CostEstimate(flops=flops, transcendentals=0,
                                      bytes_accessed=sum(math.prod(a.shape) * a.dtype.itemsize for a in held)),
    )(*operands)


def after_core_kernel(mine_ref, come_ref, own_ref, *send_refs):
    tp = lax.axis_index("tp")
    own_ref[...] = mine_ref[tp] + come_ref[tp].astype(jnp.float32)
    for mask, ref in zip(shard_masks(True), send_refs):
        to = jnp.bitwise_xor(tp, mask)
        ref[...] = (mine_ref[to] + come_ref[to].astype(jnp.float32)).astype(jnp.bfloat16)


def after_core_halves_kernel(mine_ref, come_ref, own_ref, *send_refs):
    tp, half = lax.axis_index("tp"), mine_ref.shape[1] // 2
    own_ref[...] = mine_ref[tp] + come_ref[tp].astype(jnp.float32)
    for mask, second, first in zip(shard_masks(False), send_refs[:3], send_refs[3:]):
        to = jnp.bitwise_xor(tp, mask)
        part = (mine_ref[to] + come_ref[to].astype(jnp.float32)).astype(jnp.bfloat16)
        second[...] = part[half:]
        first[...] = part[:half]


def add_all(*refs):
    total = refs[0][...]
    for ref in refs[1:]:
        total = total + ref[...].astype(jnp.float32)
    return total


def sum_kernel(*refs):
    refs[-1][...] = add_all(*refs[:-1]).astype(jnp.bfloat16).reshape(refs[-1].shape)


def sum_rows_kernel(own_ref, *refs, line):
    come, outs = refs[:3], refs[3:]
    lines = outs[0].shape[0]
    total = own_ref[line:line + len(outs) * lines]
    for ref in come:
        total = total + ref[...].astype(jnp.float32)
    for n, out in enumerate(outs):
        out[...] = total[n * lines:(n + 1) * lines].astype(out.dtype)


def scatter_shards(mine, come):
    tps, lines, part = mine.shape
    own, *parts = call(after_core_kernel, "after_core", [shape_of((lines, part), jnp.float32)] + [shape_of((lines, part))] * (tps - 1),
                       mine, come)
    return [own] + shard_swaps(parts, True)


def first_products(pieces, masks, side, x_ref, gain_ref, gate_ref, up_ref, gate_out, up_out, square_out):
    width, lines = gate_ref.shape[1], x_ref.shape[0]
    tp = lax.axis_index("tp")
    for mask, piece in zip(masks, pieces):
        at = pl.multiple_of(jnp.bitwise_xor(tp, mask) * LANES, LANES)
        x_ref[:, pl.ds(at, LANES)] = piece[...].reshape(lines, LANES)
    for at in range(2):
        start, stop = at * x_ref.shape[1], min((at + 1) * x_ref.shape[1], width)

        @pl.when(side == at)
        def _(start=start, stop=stop):
            x = x_ref[:, :stop - start].astype(jnp.float32)
            square_out[...] = jnp.broadcast_to(jnp.sum(x * x, axis=-1, keepdims=True), square_out.shape)
            scaled = (x * gain_ref[:, start:stop]).astype(jnp.bfloat16)
            gate_out[...] = dot_last(scaled, gate_ref[:, start:stop])
            up_out[...] = dot_last(scaled, up_ref[:, start:stop])


def near_kernel(gain_ref, gate_ref, up_ref, *refs):
    pieces, (x_ref, gate_out, up_out, square_out) = refs[:-4], refs[-4:]
    first_products(pieces, (0, *shard_masks(True)), lane_of(True), x_ref, gain_ref, gate_ref, up_ref, gate_out, up_out,
                   square_out)


def second_product(act_ref, down_ref, out_ref, number):
    tps, _, part = out_ref.shape

    for at in range(2):
        starts = [((at ^ (t & 1) ^ (t >> 1)) * tps + t) * part for t in range(tps)]

        @pl.when(number == at)
        def _(starts=starts):
            for first, last in ((0, 0), (1, 2), (3, 3)):
                shift = starts[first] % 128
                out = jnp.dot(act_ref[...], down_ref[:, starts[first] - shift:starts[last] + part],
                              preferred_element_type=jnp.float32)
                for n, t in enumerate(range(first, last + 1)):
                    out_ref[t] = out[:, shift + n * part:shift + (n + 1) * part].astype(out_ref.dtype)


def far_kernel(gain_ref, gate_ref, up_ref, down_ref, near_x_ref, near_gate_ref, near_up_ref, near_square_ref, *refs):
    pieces, (other_ref, act_ref, far_x_ref, gate_out, up_out, square_out) = refs[:-6], refs[-6:]
    side, grp = lane_of(True), lax.axis_index("grp")
    masks = shard_masks(True)
    first_products(pieces, (0, masks[0], masks[2], masks[1]), 1 - side, far_x_ref, gain_ref, gate_ref, up_ref, gate_out, up_out,
                   square_out)
    width, half = gate_ref.shape[1], near_x_ref.shape[1]
    spare = jnp.where(side == 1, near_x_ref[:, width - half:], far_x_ref[:, width - half:]).astype(jnp.float32)
    spare_at = lax.broadcasted_iota(jnp.int32, spare.shape, 1)
    weight = jnp.sum(jnp.where((spare_at == 2 * grp) | (spare_at == 2 * grp + 1), spare, 0.0), axis=1, keepdims=True)
    square = (near_square_ref[...] + square_out[...])[:, :1]
    scale = lax.rsqrt(square / width + 1e-05)
    gate_h = (near_gate_ref[...] + gate_out[...]) * scale
    up_h = (near_up_ref[...] + up_out[...]) * scale
    act_ref[...] = ((up_h + 1.0) * gate_h * jax.nn.sigmoid(1.702 * gate_h) * weight).astype(jnp.bfloat16)
    second_product(act_ref, down_ref, other_ref, 1 - lane_of(False))


def last_kernel(act_ref, down_ref, near_x_ref, far_x_ref, mine_ref, middle_ref, row_ref):
    sec, tp = lax.axis_index("sec"), lax.axis_index("tp")
    second_product(act_ref, down_ref, mine_ref, lane_of(False))
    total_rows, part = middle_ref.shape
    near, far = near_x_ref[:total_rows].astype(jnp.float32), far_x_ref[:total_rows].astype(jnp.float32)
    first = lane_of(True) == 0
    x = jnp.concatenate([jnp.where(first, near, far), jnp.where(first, far, near)], axis=1)
    for c in range(row_ref.shape[0]):
        row_ref[c] = x[:, c * part:(c + 1) * part]
    middle_ref[...] = row_ref[sec * mine_ref.shape[0] + tp]


def experts(gain, w_gate, w_up, w_down, pieces, part):
    gain, w_gate, w_up = gain.reshape(1, -1), w_gate.swapaxes(0, 1), w_up.swapaxes(0, 1)
    (hidden, width), tps, (groups, total_rows, _) = w_gate.shape, len(pieces), pieces[0].shape
    lines = groups * total_rows
    far_pieces = [swap(piece, "sec", 1) for piece in pieces]
    halves = [shape_of((lines, tps * LANES)), shape_of((lines, hidden), jnp.float32), shape_of((lines, hidden), jnp.float32),
              shape_of((lines, 128), jnp.float32)]
    near = call(near_kernel, "near_columns", halves, gain, w_gate, w_up, *pieces, limit=12, flops=2 * lines * width * hidden)
    other, act, far_x = pl.pallas_call(
        far_kernel,
        name="far_columns",
        out_shape=[shape_of((tps, lines, part)), shape_of((lines, hidden)), halves[0]],
        in_specs=[vmem()] * (8 + len(far_pieces)),
        out_specs=[vmem()] * 3,
        scratch_shapes=[pltpu.VMEM(half.shape, half.dtype) for half in halves[1:]],
        compiler_params=pltpu.CompilerParams(vmem_limit_bytes=16 * MIB),
    )(gain, w_gate, w_up, w_down, *near, *far_pieces)
    come = swap(other, "sec", 1)
    mine, middle = pl.pallas_call(
        last_kernel,
        name="own_columns",
        out_shape=[shape_of((tps, lines, part), jnp.float32), shape_of((total_rows, part), jnp.float32)],
        in_specs=[vmem()] * 4,
        out_specs=[vmem()] * 2,
        scratch_shapes=[pltpu.VMEM((2 * tps, total_rows, part), jnp.float32)],
        compiler_params=pltpu.CompilerParams(vmem_limit_bytes=12 * MIB),
        cost_estimate=pl.CostEstimate(flops=lines * width * hidden, transcendentals=0, bytes_accessed=2 * lines * width),
    )(act, w_down, near[0], far_x)
    return mine, come, middle


def every_expert_body(inputs, attention_gain, w_query, key_value_weight, head_sink_logits, w_output, cache_pairs, lengths,
                      expert_gain, w_gate, w_up, w_down, routes, gate_weights):
    secs, tps, groups = lax.axis_size("sec"), lax.axis_size("tp"), lax.axis_size("grp")
    steps, rows, width = inputs.shape
    flat = inputs.reshape(steps * rows, width)
    other, own_x, mix, held = attention_partial(
        flat, attention_gain, w_query, key_value_weight[:, 0], head_sink_logits, w_output, cache_pairs[:, :, 0], lengths,
        routes.swapaxes(1, 2), gate_weights.swapaxes(1, 2), secs, tps)
    come = swap(other, "sec", 1)
    mine = call(own_projection_kernel, "own_projection", shape_of(other.shape, jnp.float32), mix, held, limit=12,
                flops=mix.size * width)
    middle = call(sum_kernel, "sum", shape_of((steps * rows, LANES)), *scatter_shards(mine, come), own_x)
    stacked = jnp.stack([middle] + [lane_swap(middle, m, (0, 0), True) for m in range(1, groups)])
    pieces = [stacked] + shard_swaps([stacked] * (tps - 1), True)
    part = width // (secs * tps)
    mine, come, own_middle = experts(expert_gain, w_gate[0], w_up[0], w_down[0], pieces, part)
    lines = steps * rows
    own, *parts = call(after_core_halves_kernel, "after_core_halves",
                       [shape_of((groups * lines, part), jnp.float32)] + [shape_of((groups // 2 * lines, part))] * 6, mine, come)
    second_come, first_come = shard_swaps(parts[:3], False), shard_swaps(parts[3:], False)
    second, third = call(functools.partial(sum_rows_kernel, line=2 * lines), "sum_far_rows", [shape_of((lines, part))] * 2,
                         own, *second_come)
    third, second = swap(third, "grp", 3), swap(second, "grp", 2)
    own, nearest = call(functools.partial(sum_rows_kernel, line=0), "sum_near_rows",
                        [shape_of((lines, part), jnp.float32), shape_of((lines, part))], own, *first_come)
    return call(sum_kernel, "combine", shape_of((steps, rows, part)), own, third, second, swap(nearest, "grp", 1), own_middle)


def body(*args):
    sizes = lax.axis_size("sec"), lax.axis_size("tp"), lax.axis_size("grp"), args[9].shape[0]
    if sizes == (2, 4, TOP, 1):
        return every_expert_body(*args)
    return general_body(*args)


def solution(mesh):
    placed = (
        P(None, "grp", None),
        P(),
        P(None, ("sec", "tp")),
        P(None, ("sec", "tp"), None),
        P(("sec", "tp")),
        P(("sec", "tp"), None),
        P("grp", None, ("sec", "tp"), None),
        P("grp"),
        P(),
        P("grp", None, ("sec", "tp")),
        P("grp", None, ("sec", "tp")),
        P("grp", ("sec", "tp"), None),
        P(None, "grp", None),
        P(None, "grp", None),
    )
    return jax.shard_map(
        body, mesh=mesh, in_specs=placed, out_specs=P(None, "grp", ("sec", "tp")), check_vma=False
    )
```

```python
import functools
import math

import jax
import jax.numpy as jnp
import numpy as np
from jax import lax
from jax.experimental import pallas as pl
from jax.experimental.pallas import tpu as pltpu
from jax.sharding import PartitionSpec as P

HEAD_SIZE = 64
TOP = 4


def rms_norm(values, scale_row):
    widened = values.astype(jnp.float32)
    scale_factor = lax.rsqrt(jnp.mean(widened * widened, axis=-1, keepdims=True) + 1e-05)
    return (widened * scale_factor * scale_row).astype(jnp.bfloat16)


def rotate(vectors, position):
    half_size = vectors.shape[-1] // 2
    counter = jnp.arange(half_size).astype(jnp.float32)
    frequency = jnp.power(jnp.float32(150000.0), counter * (-2.0 / vectors.shape[-1]))
    angle_table = position * frequency
    cosine = jnp.cos(angle_table)
    sine_table = jnp.sin(angle_table)
    first_half = vectors[..., :half_size]
    second_half = vectors[..., half_size:]
    return jnp.concatenate(
        [
            first_half * cosine - second_half * sine_table,
            first_half * sine_table + second_half * cosine,
        ],
        axis=-1,
    )


def attend(
    normalized_input,
    w_query,
    key_value_weight,
    head_sink_logits,
    w_output,
    cache_pairs,
    lengths,
    step_index,
    fresh_keys,
    fresh_values,
):
    row_count = normalized_input.shape[0]
    kv_heads = key_value_weight.shape[1]
    query = jnp.dot(normalized_input, w_query, preferred_element_type=jnp.float32).reshape(
        row_count, -1, HEAD_SIZE
    )
    cache_entry_pairs = jnp.dot(
        normalized_input,
        key_value_weight.reshape(key_value_weight.shape[0], -1),
        preferred_element_type=jnp.float32,
    ).reshape(row_count, kv_heads, 2 * HEAD_SIZE)
    position = (lengths + step_index).astype(jnp.float32)[:, None, None]
    rotated_rows = rotate(query, position).astype(jnp.bfloat16)
    fresh_keys = fresh_keys + [
        rotate(cache_entry_pairs[..., :HEAD_SIZE], position).astype(jnp.bfloat16)
    ]
    fresh_values = fresh_values + [cache_entry_pairs[..., HEAD_SIZE:].astype(jnp.bfloat16)]
    grouped_queries = rotated_rows.reshape(row_count, kv_heads, -1, HEAD_SIZE)
    new_keys = jnp.stack(fresh_keys, 1)
    new_values = jnp.stack(fresh_values, 1)
    cached = (
        jnp.einsum(
            "rkgd,rjkd->rkgj",
            grouped_queries,
            cache_pairs[..., :HEAD_SIZE],
            preferred_element_type=jnp.float32,
        )
        * 0.125
    )
    valid = (jnp.arange(cache_pairs.shape[1])[None, :] < lengths[:, None])[:, None, None, :]
    cached = jnp.where(valid, cached, -jnp.inf)
    fresh = (
        jnp.einsum("rkgd,rikd->rkgi", grouped_queries, new_keys, preferred_element_type=jnp.float32)
        * 0.125
    )
    sink_row = head_sink_logits.reshape(kv_heads, -1)[None]
    largest = jnp.maximum(jnp.maximum(jnp.max(cached, axis=-1), jnp.max(fresh, axis=-1)), sink_row)
    cached_exp = jnp.exp(cached - largest[..., None])
    fresh_exp = jnp.exp(fresh - largest[..., None])
    denominator = (
        jnp.sum(cached_exp, axis=-1) + jnp.sum(fresh_exp, axis=-1) + jnp.exp(sink_row - largest)
    )
    cached_probs = (cached_exp / denominator[..., None]).astype(jnp.bfloat16)
    fresh_probs = (fresh_exp / denominator[..., None]).astype(jnp.bfloat16)
    mixed = jnp.einsum(
        "rkgj,rjkd->rkgd",
        cached_probs,
        cache_pairs[..., HEAD_SIZE:],
        preferred_element_type=jnp.float32,
    )
    mixed = mixed + jnp.einsum(
        "rkgi,rikd->rkgd", fresh_probs, new_values, preferred_element_type=jnp.float32
    )
    attention_mix = mixed.reshape(row_count, -1).astype(jnp.bfloat16)
    partial_sum = jnp.dot(attention_mix, w_output, preferred_element_type=jnp.float32)
    return (partial_sum, fresh_keys, fresh_values)


def general_body(
    inputs,
    attention_gain,
    w_query,
    key_value_weight,
    head_sink_logits,
    w_output,
    cache_pairs,
    lengths,
    expert_gain,
    w_gate,
    w_up,
    w_down,
    routes,
    gate_weights,
):
    shards = lax.axis_size(("sec", "tp"))
    shard_index = lax.axis_index(("sec", "tp"))
    experts = lax.axis_size("grp") * w_gate.shape[0]
    group_rows = inputs.shape[1]
    width = inputs.shape[2]
    part_width = width // shards
    chosen = max(TOP, experts // 2)
    capacity = group_rows * TOP // chosen
    slot_total = experts * capacity
    gate_matrix = w_gate[0]
    up_matrix = w_up[0]
    down_matrix = w_down[0]
    fresh_keys = []
    fresh_values = []
    results = []
    for step_index in range(inputs.shape[0]):
        normalized_input = rms_norm(inputs[step_index], attention_gain)
        partial_sum, fresh_keys, fresh_values = attend(
            normalized_input,
            w_query,
            key_value_weight,
            head_sink_logits,
            w_output,
            cache_pairs,
            lengths,
            step_index,
            fresh_keys,
            fresh_values,
        )
        summed = lax.psum(partial_sum[None], ("sec", "tp"))
        middle = (inputs[step_index][None].astype(jnp.float32) + summed).astype(jnp.bfloat16)
        route_rows = routes[step_index][None]
        step_count = middle.shape[0]
        expert_in = rms_norm(middle, expert_gain)
        flat_routes = route_rows.reshape(step_count, group_rows * TOP)
        onehot = (flat_routes[..., None] == jnp.arange(experts)[None, None, :]).astype(jnp.int32)
        earlier = jnp.cumsum(onehot, axis=1) - onehot
        slot_index = jnp.sum(earlier * onehot, axis=-1).reshape(step_count, group_rows, TOP)
        target = route_rows * capacity + slot_index
        placed = target[..., None] == jnp.arange(slot_total)[None, None, None, :]
        dispatch_table = jnp.sum(placed.astype(jnp.int32), axis=2).astype(jnp.bfloat16)
        combine_table = jnp.sum(
            jnp.where(placed, gate_weights[step_index][None][..., None], 0.0), axis=2
        )
        outgoing = jnp.einsum(
            "crm,crd->cmd", dispatch_table, expert_in, preferred_element_type=jnp.float32
        )
        outgoing = outgoing.astype(jnp.bfloat16).reshape(step_count, experts, capacity, width)
        arrived = lax.all_to_all(outgoing, "grp", split_axis=1, concat_axis=1, tiled=True)
        gate_h = jnp.einsum(
            "snpd,dh->snph", arrived, gate_matrix, preferred_element_type=jnp.float32
        )
        up_h = jnp.einsum("snpd,dh->snph", arrived, up_matrix, preferred_element_type=jnp.float32)
        act = ((up_h + 1.0) * gate_h * jax.nn.sigmoid(1.702 * gate_h)).astype(jnp.bfloat16)
        partial_out = jnp.einsum(
            "snph,hd->snpd", act, down_matrix, preferred_element_type=jnp.float32
        )
        reduced = lax.psum_scatter(
            partial_out, ("sec", "tp"), scatter_dimension=3, tiled=True
        ).astype(jnp.bfloat16)
        returned = lax.all_to_all(reduced, "grp", split_axis=1, concat_axis=1, tiled=True)
        returned_rows = returned.reshape(step_count, slot_total, part_width).astype(jnp.float32)
        weighted = jnp.einsum(
            "srm,smd->srd", combine_table, returned_rows, precision=lax.Precision.HIGHEST
        )
        own_middle = lax.dynamic_slice_in_dim(
            middle, shard_index * part_width, part_width, 2
        ).astype(jnp.float32)
        results.append((own_middle + weighted).astype(jnp.bfloat16)[0])
    return jnp.stack(results, 0)


LANES = 384
BASE = 150000.0
MIB = 1 << 20


def shape_of(shape, dtype=jnp.bfloat16):
    return jax.ShapeDtypeStruct(shape, dtype)


def vmem():
    return pl.BlockSpec(memory_space=pltpu.VMEM)


def smem():
    return pl.BlockSpec(memory_space=pltpu.SMEM)


def outside():
    return pl.BlockSpec(memory_space=pltpu.HBM)


def dot_last(left, right):
    return lax.dot_general(left, right, (((1,), (1,)), ((), ())), preferred_element_type=jnp.float32)


def swap(value, axes, mask):
    size = lax.axis_size(axes)
    return lax.ppermute(value, axes, [(i, i ^ mask) for i in range(size)])


def lane_of(by_group):
    tp = lax.axis_index("tp")
    number = lax.axis_index("sec") ^ (tp & 1) ^ (tp >> 1)
    return number ^ (lax.axis_index("grp") & 1) if by_group else number


def lane_swap(value, mask, shard_masks_by_lane, by_group):
    groups, tps = lax.axis_size("grp"), lax.axis_size("tp")

    def parity(group, shard):
        return (shard & 1) ^ (shard >> 1) ^ (group & 1 if by_group else 0)

    pairs = []
    for core in range(2):
        for group in range(groups):
            for shard in range(tps):
                number = core ^ parity(group, shard)
                to_group, to_shard = group ^ mask, shard ^ shard_masks_by_lane[number]
                to_core = number ^ parity(to_group, to_shard)
                pairs.append(((core * groups + group) * tps + shard, (to_core * groups + to_group) * tps + to_shard))
    return lax.ppermute(value, ("sec", "grp", "tp"), pairs)


def shard_swaps(parts, by_group):
    return [lane_swap(part, 0, masks, by_group) for part, masks in zip(parts, ((3, 3), (1, 2), (2, 1)))]


def shard_masks(by_group):
    number = lane_of(by_group)
    return 3, 1 + number, 2 - number


def split_width(width):
    cuts = list(range(0, width, 768)) + [width]
    return list(zip(cuts[:-1], cuts[1:]))


def attention_kernel(lengths_hbm, sinks_hbm, routes_hbm, weights_hbm, gain_hbm, x_hbm, wq_hbm, wkv_hbm, cache_hbm, wo_hbm,
                     other_ref, own_x_ref, mix_ref, wo_ref,
                     lengths_ref, sinks_ref, routes_ref, weights_ref, gain_ref, x_ref, wq_ref, wkv_ref, cache_ref,
                     xs_ref, turned_ref, mixed_ref, sems):
    total_rows, width = x_ref.shape
    rows, slots, pair = cache_ref.shape
    steps = total_rows // rows
    heads = wq_ref.shape[1] // HEAD_SIZE
    per_row = heads * steps
    tps = other_ref.shape[0]
    cuts = split_width(width)
    small = [(lengths_hbm, lengths_ref), (x_hbm, x_ref), (gain_hbm, gain_ref), (routes_hbm, routes_ref), (weights_hbm, weights_ref),
             (sinks_hbm, sinks_ref)]
    small = [pltpu.make_async_copy(source, target, sems.at[n]) for n, (source, target) in enumerate(small)]
    copies = [pltpu.make_async_copy(wkv_hbm, wkv_ref, sems.at[6])]
    for n, (low, high) in enumerate(cuts):
        part = pl.ds(low, high - low)
        copies.append(pltpu.make_async_copy(wq_hbm.at[part], wq_ref.at[part], sems.at[9 + n]))
    copies.append(pltpu.make_async_copy(cache_hbm, cache_ref, sems.at[7]))
    for copy in small + copies:
        copy.start()
    middle = tps * LANES
    halves = [pltpu.make_async_copy(wo_hbm.at[part], wo_ref.at[part], sems.at[sem])
              for part, sem in ((pl.ds(0, middle), 8), (pl.ds(middle, width - middle), 9 + len(cuts)))]
    for at in range(2):
        @pl.when(lane_of(True) == at)
        def _(at=at):
            halves[1 - at].start()
            halves[at].start()

    small[1].wait()
    small[2].wait()
    x = x_ref[...].astype(jnp.float32)
    scale = lax.rsqrt(jnp.mean(x * x, axis=-1, keepdims=True) + 1e-05)
    normed = (x * scale * gain_ref[...].reshape(1, width)).astype(jnp.bfloat16)
    copies[0].wait()
    pairs = jnp.dot(normed, wkv_ref[...], preferred_element_type=jnp.float32)
    query = jnp.zeros((total_rows, wq_ref.shape[1]), jnp.float32)
    for n, (low, high) in enumerate(cuts[:-1]):
        copies[1 + n].wait()
        query = query + jnp.dot(normed[:, low:high], wq_ref[low:high, :], preferred_element_type=jnp.float32)
    for copy in (small[0], *small[3:], copies[len(cuts)]):
        copy.wait()
    query = query + jnp.dot(normed[:, cuts[-1][0]:], wq_ref[cuts[-1][0]:, :], preferred_element_type=jnp.float32)

    lane = lax.broadcasted_iota(jnp.int32, (total_rows, pair), 1)
    line = lax.broadcasted_iota(jnp.int32, (total_rows, pair), 0)
    position = jnp.zeros((total_rows, pair), jnp.int32)
    for r in range(rows):
        for s in range(steps):
            position = jnp.where(line == s * rows + r, lengths_ref[r] + s, position)
    half = HEAD_SIZE // 2
    counter = jnp.bitwise_and(lane, half - 1).astype(jnp.float32)
    frequency = jnp.exp(counter * jnp.float32(-2.0 / HEAD_SIZE * np.log(BASE)))
    angle = position.astype(jnp.float32) * frequency
    cosine, sine = jnp.cos(angle), jnp.sin(angle)
    low_half = jnp.bitwise_and(lane, HEAD_SIZE - 1) < half
    sine = jnp.where(low_half, -sine, sine)

    def turn(two):
        return two * cosine + jnp.where(low_half, pltpu.roll(two, pair - half, 1), pltpu.roll(two, half, 1)) * sine

    spare = xs_ref.shape[1] - width
    spare_at = lax.broadcasted_iota(jnp.int32, (rows, spare), 1)
    corner = lax.broadcasted_iota(jnp.int32, (rows, rows), 0) == lax.broadcasted_iota(jnp.int32, (rows, rows), 1)
    tables = []
    for s in range(steps):
        table = jnp.zeros((rows, spare), jnp.float32)
        for e in range(TOP):
            across = jnp.sum(jnp.where(routes_ref[s] == e, weights_ref[s], 0.0), axis=0, keepdims=True)
            column = jnp.sum(jnp.where(corner, across, 0.0), axis=1, keepdims=True)
            high_part = column.astype(jnp.bfloat16).astype(jnp.float32)
            table = jnp.where(spare_at == 2 * e, high_part, jnp.where(spare_at == 2 * e + 1, column - high_part, table))
        tables.append(table)
    xs_ref[...] = jnp.concatenate([x, jnp.concatenate(tables, axis=0)], axis=1)
    own = (lane_of(True) * tps + lax.axis_index("tp")) * LANES
    own_x_ref[...] = xs_ref[:, pl.ds(pl.multiple_of(own, LANES), LANES)]
    is_key = lane < HEAD_SIZE
    fresh = jnp.where(is_key, turn(pairs), pairs).astype(jnp.bfloat16)
    for m in range(heads // 2):
        two = turn(query[:, m * pair:(m + 1) * pair])
        for odd in range(2):
            one = two if odd == 0 else pltpu.roll(two, HEAD_SIZE, 1)
            one = jnp.where(is_key, one, 0.0)
            for s in range(steps):
                slot = (2 * m + odd) * steps + s
                turned_ref[pl.ds(slot, rows, stride=per_row), :] = one[s * rows:(s + 1) * rows]
    turned = turned_ref[...].astype(jnp.bfloat16)

    copies[-1].wait()
    place = lax.broadcasted_iota(jnp.int32, (per_row, slots), 1)
    scores = []
    for r in range(rows):
        score = dot_last(turned[r * per_row:(r + 1) * per_row], cache_ref[r]) * 0.125
        scores.append(jnp.where(place < lengths_ref[r], score, -jnp.inf))
    cached = jnp.concatenate(scores, axis=0)
    row_at = lax.broadcasted_iota(jnp.int32, (rows * per_row, total_rows), 0)
    fresh_at = lax.broadcasted_iota(jnp.int32, (rows * per_row, total_rows), 1)
    seen = (row_at // per_row == fresh_at % rows) & (fresh_at // rows <= row_at % steps)
    new = jnp.where(seen, dot_last(turned, fresh) * 0.125, -jnp.inf)
    head_at = lax.broadcasted_iota(jnp.int32, (rows * per_row, 1), 0) % per_row // steps
    sink = jnp.zeros((rows * per_row, 1), jnp.float32)
    for h in range(heads):
        sink = jnp.where(head_at == h, sinks_ref[h], sink)
    largest = jnp.maximum(jnp.maximum(jnp.max(cached, axis=-1, keepdims=True), jnp.max(new, axis=-1, keepdims=True)), sink)
    cached = jnp.exp(cached - largest)
    new = jnp.exp(new - largest)
    total = jnp.sum(cached, axis=-1, keepdims=True) + jnp.sum(new, axis=-1, keepdims=True) + jnp.exp(sink - largest)
    share = 1.0 / total
    cached = (cached * share).astype(jnp.bfloat16)
    new = (new * share).astype(jnp.bfloat16)
    mixed = []
    for r in range(rows):
        mixed.append(jnp.dot(cached[r * per_row:(r + 1) * per_row], cache_ref[r], preferred_element_type=jnp.float32))
    mixed_ref[...] = jnp.concatenate(mixed, axis=0) + jnp.dot(new, fresh, preferred_element_type=jnp.float32)

    def head(h):
        return jnp.concatenate([mixed_ref[pl.ds(h * steps + s, rows, stride=per_row), :] for s in range(steps)], axis=0)

    mix_ref[...] = jnp.concatenate(
        [jnp.where(is_key, pltpu.roll(head(2 * m), HEAD_SIZE, 1), head(2 * m + 1)) for m in range(heads // 2)], axis=1
    ).astype(jnp.bfloat16)
    project(mix_ref, wo_ref, other_ref, 1 - lane_of(True), halves)
    for at in range(2):
        @pl.when(lane_of(True) == at)
        def _(at=at):
            halves[at].wait()


def project(mix_ref, wo_ref, out_ref, side, halves=None):
    width, (tps, total_rows, _) = wo_ref.shape[0], out_ref.shape
    for at in range(2):
        start, stop = at * tps * LANES, min((at + 1) * tps * LANES, width)

        @pl.when(side == at)
        def _(at=at, start=start, stop=stop):
            if halves is not None:
                halves[at].wait()
            partial = dot_last(mix_ref[...], wo_ref[start:stop, :])
            for t in range(tps):
                low, high = t * LANES, min((t + 1) * LANES, stop - start)
                piece = partial[:, low:high]
                if high - low < LANES:
                    piece = jnp.concatenate([piece, jnp.zeros((total_rows, LANES - (high - low)), jnp.float32)], axis=1)
                out_ref[t] = piece.astype(out_ref.dtype)


def own_projection_kernel(mix_ref, wo_ref, mine_ref):
    project(mix_ref, wo_ref, mine_ref, lane_of(True))


def attention_partial(flat, gain, w_query, key_value, sinks, w_output, cache, lengths, routes, weights, secs, tps):
    total_rows, width = flat.shape
    rows, slots, pair = cache.shape
    per_row = w_query.shape[1] // HEAD_SIZE * (total_rows // rows)
    shards = secs * tps
    operands = (lengths, sinks, routes, weights, gain, flat, w_query, key_value, cache, w_output.swapaxes(0, 1))
    return pl.pallas_call(
        attention_kernel,
        name="attention",
        out_shape=[shape_of((tps, total_rows, LANES)), shape_of((total_rows, LANES), jnp.float32),
                   shape_of((total_rows, w_output.shape[0])), shape_of((width, w_output.shape[0]))],
        in_specs=[outside()] * len(operands),
        out_specs=[vmem()] * 4,
        scratch_shapes=[
            pltpu.SMEM(lengths.shape, jnp.int32),
            pltpu.SMEM(sinks.shape, jnp.float32),
            pltpu.VMEM(routes.shape, jnp.int32),
            pltpu.VMEM(weights.shape, jnp.float32),
            pltpu.VMEM(gain.shape, jnp.float32),
            pltpu.VMEM((total_rows, width), jnp.bfloat16),
            pltpu.VMEM(w_query.shape, jnp.bfloat16),
            pltpu.VMEM(key_value.shape, jnp.bfloat16),
            pltpu.VMEM(cache.shape, jnp.bfloat16),
            pltpu.VMEM((total_rows, shards * LANES), jnp.float32),
            pltpu.VMEM((rows * per_row, pair), jnp.float32),
            pltpu.VMEM((rows * per_row, pair), jnp.float32),
            pltpu.SemaphoreType.DMA((10 + len(split_width(width)),)),
        ],
        compiler_params=pltpu.CompilerParams(vmem_limit_bytes=24 * MIB),
    )(*[pltpu.with_memory_space_constraint(operand, pltpu.HBM) for operand in operands])


def call(kernel, name, outs, *operands, limit=4, flops=0):
    single = not isinstance(outs, list)
    held = [*operands, *([outs] if single else outs)]
    return pl.pallas_call(
        kernel,
        name=name,
        out_shape=outs,
        in_specs=[vmem()] * len(operands),
        out_specs=vmem() if single else [vmem()] * len(outs),
        compiler_params=pltpu.CompilerParams(vmem_limit_bytes=limit * MIB),
        cost_estimate=pl.CostEstimate(flops=flops, transcendentals=0,
                                      bytes_accessed=sum(math.prod(a.shape) * a.dtype.itemsize for a in held)),
    )(*operands)


def after_core_kernel(mine_ref, come_ref, own_ref, *send_refs):
    tp = lax.axis_index("tp")
    own_ref[...] = mine_ref[tp] + come_ref[tp].astype(jnp.float32)
    for mask, ref in zip(shard_masks(True), send_refs):
        to = jnp.bitwise_xor(tp, mask)
        ref[...] = (mine_ref[to] + come_ref[to].astype(jnp.float32)).astype(jnp.bfloat16)


def after_core_halves_kernel(mine_ref, come_ref, own_ref, *send_refs):
    tp, half = lax.axis_index("tp"), mine_ref.shape[1] // 2
    own_ref[...] = mine_ref[tp] + come_ref[tp].astype(jnp.float32)
    for mask, second, first in zip(shard_masks(False), send_refs[:3], send_refs[3:]):
        to = jnp.bitwise_xor(tp, mask)
        part = (mine_ref[to] + come_ref[to].astype(jnp.float32)).astype(jnp.bfloat16)
        second[...] = part[half:]
        first[...] = part[:half]


def add_all(*refs):
    total = refs[0][...]
    for ref in refs[1:]:
        total = total + ref[...].astype(jnp.float32)
    return total


def sum_kernel(*refs):
    refs[-1][...] = add_all(*refs[:-1]).astype(jnp.bfloat16).reshape(refs[-1].shape)


def sum_rows_kernel(own_ref, *refs, line):
    come, outs = refs[:3], refs[3:]
    lines = outs[0].shape[0]
    total = own_ref[line:line + len(outs) * lines]
    for ref in come:
        total = total + ref[...].astype(jnp.float32)
    for n, out in enumerate(outs):
        out[...] = total[n * lines:(n + 1) * lines].astype(out.dtype)


def scatter_shards(mine, come):
    tps, lines, part = mine.shape
    own, *parts = call(after_core_kernel, "after_core", [shape_of((lines, part), jnp.float32)] + [shape_of((lines, part))] * (tps - 1),
                       mine, come)
    return [own] + shard_swaps(parts, True)


def first_products(pieces, masks, side, x_ref, gain_ref, gate_ref, up_ref, gate_out, up_out, square_out):
    width, lines = gate_ref.shape[1], x_ref.shape[0]
    tp = lax.axis_index("tp")
    for mask, piece in zip(masks, pieces):
        at = pl.multiple_of(jnp.bitwise_xor(tp, mask) * LANES, LANES)
        x_ref[:, pl.ds(at, LANES)] = piece[...].reshape(lines, LANES)
    for at in range(2):
        start, stop = at * x_ref.shape[1], min((at + 1) * x_ref.shape[1], width)

        @pl.when(side == at)
        def _(start=start, stop=stop):
            x = x_ref[:, :stop - start].astype(jnp.float32)
            square_out[...] = jnp.broadcast_to(jnp.sum(x * x, axis=-1, keepdims=True), square_out.shape)
            scaled = (x * gain_ref[:, start:stop]).astype(jnp.bfloat16)
            gate_out[...] = dot_last(scaled, gate_ref[:, start:stop])
            up_out[...] = dot_last(scaled, up_ref[:, start:stop])


def near_kernel(gain_ref, gate_ref, up_ref, *refs):
    pieces, (x_ref, gate_out, up_out, square_out) = refs[:-4], refs[-4:]
    first_products(pieces, (0, *shard_masks(True)), lane_of(True), x_ref, gain_ref, gate_ref, up_ref, gate_out, up_out,
                   square_out)


def second_product(act_ref, down_ref, out_ref, number):
    tps, _, part = out_ref.shape

    for at in range(2):
        starts = [((at ^ (t & 1) ^ (t >> 1)) * tps + t) * part for t in range(tps)]

        @pl.when(number == at)
        def _(starts=starts):
            for first, last in ((0, 0), (1, 2), (3, 3)):
                shift = starts[first] % 128
                out = jnp.dot(act_ref[...], down_ref[:, starts[first] - shift:starts[last] + part],
                              preferred_element_type=jnp.float32)
                for n, t in enumerate(range(first, last + 1)):
                    out_ref[t] = out[:, shift + n * part:shift + (n + 1) * part].astype(out_ref.dtype)


def far_kernel(gain_ref, gate_ref, up_ref, down_ref, near_x_ref, near_gate_ref, near_up_ref, near_square_ref, *refs):
    pieces, (other_ref, act_ref, far_x_ref, gate_out, up_out, square_out) = refs[:-6], refs[-6:]
    side, grp = lane_of(True), lax.axis_index("grp")
    masks = shard_masks(True)
    first_products(pieces, (0, masks[0], masks[2], masks[1]), 1 - side, far_x_ref, gain_ref, gate_ref, up_ref, gate_out, up_out,
                   square_out)
    width, half = gate_ref.shape[1], near_x_ref.shape[1]
    spare = jnp.where(side == 1, near_x_ref[:, width - half:], far_x_ref[:, width - half:]).astype(jnp.float32)
    spare_at = lax.broadcasted_iota(jnp.int32, spare.shape, 1)
    weight = jnp.sum(jnp.where((spare_at == 2 * grp) | (spare_at == 2 * grp + 1), spare, 0.0), axis=1, keepdims=True)
    square = (near_square_ref[...] + square_out[...])[:, :1]
    scale = lax.rsqrt(square / width + 1e-05)
    gate_h = (near_gate_ref[...] + gate_out[...]) * scale
    up_h = (near_up_ref[...] + up_out[...]) * scale
    act_ref[...] = ((up_h + 1.0) * gate_h * jax.nn.sigmoid(1.702 * gate_h) * weight).astype(jnp.bfloat16)
    second_product(act_ref, down_ref, other_ref, 1 - lane_of(False))


def last_kernel(act_ref, down_ref, near_x_ref, far_x_ref, mine_ref, middle_ref, row_ref):
    sec, tp = lax.axis_index("sec"), lax.axis_index("tp")
    second_product(act_ref, down_ref, mine_ref, lane_of(False))
    total_rows, part = middle_ref.shape
    near, far = near_x_ref[:total_rows].astype(jnp.float32), far_x_ref[:total_rows].astype(jnp.float32)
    first = lane_of(True) == 0
    x = jnp.concatenate([jnp.where(first, near, far), jnp.where(first, far, near)], axis=1)
    for c in range(row_ref.shape[0]):
        row_ref[c] = x[:, c * part:(c + 1) * part]
    middle_ref[...] = row_ref[sec * mine_ref.shape[0] + tp]


def experts(gain, w_gate, w_up, w_down, pieces, part):
    gain, w_gate, w_up = gain.reshape(1, -1), w_gate.swapaxes(0, 1), w_up.swapaxes(0, 1)
    (hidden, width), tps, (groups, total_rows, _) = w_gate.shape, len(pieces), pieces[0].shape
    lines = groups * total_rows
    far_pieces = [swap(piece, "sec", 1) for piece in pieces]
    halves = [shape_of((lines, tps * LANES)), shape_of((lines, hidden), jnp.float32), shape_of((lines, hidden), jnp.float32),
              shape_of((lines, 128), jnp.float32)]
    near = call(near_kernel, "near_columns", halves, gain, w_gate, w_up, *pieces, limit=12, flops=2 * lines * width * hidden)
    other, act, far_x = pl.pallas_call(
        far_kernel,
        name="far_columns",
        out_shape=[shape_of((tps, lines, part)), shape_of((lines, hidden)), halves[0]],
        in_specs=[vmem()] * (8 + len(far_pieces)),
        out_specs=[vmem()] * 3,
        scratch_shapes=[pltpu.VMEM(half.shape, half.dtype) for half in halves[1:]],
        compiler_params=pltpu.CompilerParams(vmem_limit_bytes=16 * MIB),
    )(gain, w_gate, w_up, w_down, *near, *far_pieces)
    come = swap(other, "sec", 1)
    mine, middle = pl.pallas_call(
        last_kernel,
        name="own_columns",
        out_shape=[shape_of((tps, lines, part), jnp.float32), shape_of((total_rows, part), jnp.float32)],
        in_specs=[vmem()] * 4,
        out_specs=[vmem()] * 2,
        scratch_shapes=[pltpu.VMEM((2 * tps, total_rows, part), jnp.float32)],
        compiler_params=pltpu.CompilerParams(vmem_limit_bytes=12 * MIB),
        cost_estimate=pl.CostEstimate(flops=lines * width * hidden, transcendentals=0, bytes_accessed=2 * lines * width),
    )(act, w_down, near[0], far_x)
    return mine, come, middle


def every_expert_body(inputs, attention_gain, w_query, key_value_weight, head_sink_logits, w_output, cache_pairs, lengths,
                      expert_gain, w_gate, w_up, w_down, routes, gate_weights):
    secs, tps, groups = lax.axis_size("sec"), lax.axis_size("tp"), lax.axis_size("grp")
    steps, rows, width = inputs.shape
    flat = inputs.reshape(steps * rows, width)
    other, own_x, mix, held = attention_partial(
        flat, attention_gain, w_query, key_value_weight[:, 0], head_sink_logits, w_output, cache_pairs[:, :, 0], lengths,
        routes.swapaxes(1, 2), gate_weights.swapaxes(1, 2), secs, tps)
    w_gate, w_up, w_down, other = lax.optimization_barrier((w_gate, w_up, w_down, other))
    come = swap(other, "sec", 1)
    mine = call(own_projection_kernel, "own_projection", shape_of(other.shape, jnp.float32), mix, held, limit=12,
                flops=mix.size * width)
    middle = call(sum_kernel, "sum", shape_of((steps * rows, LANES)), *scatter_shards(mine, come), own_x)
    stacked = jnp.stack([middle] + [lane_swap(middle, m, (0, 0), True) for m in range(1, groups)])
    pieces = [stacked] + shard_swaps([stacked] * (tps - 1), True)
    part = width // (secs * tps)
    mine, come, own_middle = experts(expert_gain, w_gate[0], w_up[0], w_down[0], pieces, part)
    lines = steps * rows
    own, *parts = call(after_core_halves_kernel, "after_core_halves",
                       [shape_of((groups * lines, part), jnp.float32)] + [shape_of((groups // 2 * lines, part))] * 6, mine, come)
    second_come, first_come = shard_swaps(parts[:3], False), shard_swaps(parts[3:], False)
    second, third = call(functools.partial(sum_rows_kernel, line=2 * lines), "sum_far_rows", [shape_of((lines, part))] * 2,
                         own, *second_come)
    third, second = swap(third, "grp", 3), swap(second, "grp", 2)
    own, nearest = call(functools.partial(sum_rows_kernel, line=0), "sum_near_rows",
                        [shape_of((lines, part), jnp.float32), shape_of((lines, part))], own, *first_come)
    return call(sum_kernel, "combine", shape_of((steps, rows, part)), own, third, second, swap(nearest, "grp", 1), own_middle)


def body(*args):
    sizes = lax.axis_size("sec"), lax.axis_size("tp"), lax.axis_size("grp"), args[9].shape[0]
    if sizes == (2, 4, TOP, 1):
        return every_expert_body(*args)
    return general_body(*args)


def solution(mesh):
    placed = (
        P(None, "grp", None),
        P(),
        P(None, ("sec", "tp")),
        P(None, ("sec", "tp"), None),
        P(("sec", "tp")),
        P(("sec", "tp"), None),
        P("grp", None, ("sec", "tp"), None),
        P("grp"),
        P(),
        P("grp", None, ("sec", "tp")),
        P("grp", None, ("sec", "tp")),
        P("grp", ("sec", "tp"), None),
        P(None, "grp", None),
        P(None, "grp", None),
    )
    return jax.shard_map(
        body, mesh=mesh, in_specs=placed, out_specs=P(None, "grp", ("sec", "tp")), check_vma=False
    )
```

```python
import functools
import math

import jax
import jax.numpy as jnp
import numpy as np
from jax import lax
from jax.experimental import pallas as pl
from jax.experimental.pallas import tpu as pltpu
from jax.sharding import PartitionSpec as P

HEAD_SIZE = 64
TOP = 4


def rms_norm(values, scale_row):
    widened = values.astype(jnp.float32)
    scale_factor = lax.rsqrt(jnp.mean(widened * widened, axis=-1, keepdims=True) + 1e-05)
    return (widened * scale_factor * scale_row).astype(jnp.bfloat16)


def rotate(vectors, position):
    half_size = vectors.shape[-1] // 2
    counter = jnp.arange(half_size).astype(jnp.float32)
    frequency = jnp.power(jnp.float32(150000.0), counter * (-2.0 / vectors.shape[-1]))
    angle_table = position * frequency
    cosine = jnp.cos(angle_table)
    sine_table = jnp.sin(angle_table)
    first_half = vectors[..., :half_size]
    second_half = vectors[..., half_size:]
    return jnp.concatenate(
        [
            first_half * cosine - second_half * sine_table,
            first_half * sine_table + second_half * cosine,
        ],
        axis=-1,
    )


def attend(
    normalized_input,
    w_query,
    key_value_weight,
    head_sink_logits,
    w_output,
    cache_pairs,
    lengths,
    step_index,
    fresh_keys,
    fresh_values,
):
    row_count = normalized_input.shape[0]
    kv_heads = key_value_weight.shape[1]
    query = jnp.dot(normalized_input, w_query, preferred_element_type=jnp.float32).reshape(
        row_count, -1, HEAD_SIZE
    )
    cache_entry_pairs = jnp.dot(
        normalized_input,
        key_value_weight.reshape(key_value_weight.shape[0], -1),
        preferred_element_type=jnp.float32,
    ).reshape(row_count, kv_heads, 2 * HEAD_SIZE)
    position = (lengths + step_index).astype(jnp.float32)[:, None, None]
    rotated_rows = rotate(query, position).astype(jnp.bfloat16)
    fresh_keys = fresh_keys + [
        rotate(cache_entry_pairs[..., :HEAD_SIZE], position).astype(jnp.bfloat16)
    ]
    fresh_values = fresh_values + [cache_entry_pairs[..., HEAD_SIZE:].astype(jnp.bfloat16)]
    grouped_queries = rotated_rows.reshape(row_count, kv_heads, -1, HEAD_SIZE)
    new_keys = jnp.stack(fresh_keys, 1)
    new_values = jnp.stack(fresh_values, 1)
    cached = (
        jnp.einsum(
            "rkgd,rjkd->rkgj",
            grouped_queries,
            cache_pairs[..., :HEAD_SIZE],
            preferred_element_type=jnp.float32,
        )
        * 0.125
    )
    valid = (jnp.arange(cache_pairs.shape[1])[None, :] < lengths[:, None])[:, None, None, :]
    cached = jnp.where(valid, cached, -jnp.inf)
    fresh = (
        jnp.einsum("rkgd,rikd->rkgi", grouped_queries, new_keys, preferred_element_type=jnp.float32)
        * 0.125
    )
    sink_row = head_sink_logits.reshape(kv_heads, -1)[None]
    largest = jnp.maximum(jnp.maximum(jnp.max(cached, axis=-1), jnp.max(fresh, axis=-1)), sink_row)
    cached_exp = jnp.exp(cached - largest[..., None])
    fresh_exp = jnp.exp(fresh - largest[..., None])
    denominator = (
        jnp.sum(cached_exp, axis=-1) + jnp.sum(fresh_exp, axis=-1) + jnp.exp(sink_row - largest)
    )
    cached_probs = (cached_exp / denominator[..., None]).astype(jnp.bfloat16)
    fresh_probs = (fresh_exp / denominator[..., None]).astype(jnp.bfloat16)
    mixed = jnp.einsum(
        "rkgj,rjkd->rkgd",
        cached_probs,
        cache_pairs[..., HEAD_SIZE:],
        preferred_element_type=jnp.float32,
    )
    mixed = mixed + jnp.einsum(
        "rkgi,rikd->rkgd", fresh_probs, new_values, preferred_element_type=jnp.float32
    )
    attention_mix = mixed.reshape(row_count, -1).astype(jnp.bfloat16)
    partial_sum = jnp.dot(attention_mix, w_output, preferred_element_type=jnp.float32)
    return (partial_sum, fresh_keys, fresh_values)


def general_body(
    inputs,
    attention_gain,
    w_query,
    key_value_weight,
    head_sink_logits,
    w_output,
    cache_pairs,
    lengths,
    expert_gain,
    w_gate,
    w_up,
    w_down,
    routes,
    gate_weights,
):
    shards = lax.axis_size(("sec", "tp"))
    shard_index = lax.axis_index(("sec", "tp"))
    experts = lax.axis_size("grp") * w_gate.shape[0]
    group_rows = inputs.shape[1]
    width = inputs.shape[2]
    part_width = width // shards
    chosen = max(TOP, experts // 2)
    capacity = group_rows * TOP // chosen
    slot_total = experts * capacity
    gate_matrix = w_gate[0]
    up_matrix = w_up[0]
    down_matrix = w_down[0]
    fresh_keys = []
    fresh_values = []
    results = []
    for step_index in range(inputs.shape[0]):
        normalized_input = rms_norm(inputs[step_index], attention_gain)
        partial_sum, fresh_keys, fresh_values = attend(
            normalized_input,
            w_query,
            key_value_weight,
            head_sink_logits,
            w_output,
            cache_pairs,
            lengths,
            step_index,
            fresh_keys,
            fresh_values,
        )
        summed = lax.psum(partial_sum[None], ("sec", "tp"))
        middle = (inputs[step_index][None].astype(jnp.float32) + summed).astype(jnp.bfloat16)
        route_rows = routes[step_index][None]
        step_count = middle.shape[0]
        expert_in = rms_norm(middle, expert_gain)
        flat_routes = route_rows.reshape(step_count, group_rows * TOP)
        onehot = (flat_routes[..., None] == jnp.arange(experts)[None, None, :]).astype(jnp.int32)
        earlier = jnp.cumsum(onehot, axis=1) - onehot
        slot_index = jnp.sum(earlier * onehot, axis=-1).reshape(step_count, group_rows, TOP)
        target = route_rows * capacity + slot_index
        placed = target[..., None] == jnp.arange(slot_total)[None, None, None, :]
        dispatch_table = jnp.sum(placed.astype(jnp.int32), axis=2).astype(jnp.bfloat16)
        combine_table = jnp.sum(
            jnp.where(placed, gate_weights[step_index][None][..., None], 0.0), axis=2
        )
        outgoing = jnp.einsum(
            "crm,crd->cmd", dispatch_table, expert_in, preferred_element_type=jnp.float32
        )
        outgoing = outgoing.astype(jnp.bfloat16).reshape(step_count, experts, capacity, width)
        arrived = lax.all_to_all(outgoing, "grp", split_axis=1, concat_axis=1, tiled=True)
        gate_h = jnp.einsum(
            "snpd,dh->snph", arrived, gate_matrix, preferred_element_type=jnp.float32
        )
        up_h = jnp.einsum("snpd,dh->snph", arrived, up_matrix, preferred_element_type=jnp.float32)
        act = ((up_h + 1.0) * gate_h * jax.nn.sigmoid(1.702 * gate_h)).astype(jnp.bfloat16)
        partial_out = jnp.einsum(
            "snph,hd->snpd", act, down_matrix, preferred_element_type=jnp.float32
        )
        reduced = lax.psum_scatter(
            partial_out, ("sec", "tp"), scatter_dimension=3, tiled=True
        ).astype(jnp.bfloat16)
        returned = lax.all_to_all(reduced, "grp", split_axis=1, concat_axis=1, tiled=True)
        returned_rows = returned.reshape(step_count, slot_total, part_width).astype(jnp.float32)
        weighted = jnp.einsum(
            "srm,smd->srd", combine_table, returned_rows, precision=lax.Precision.HIGHEST
        )
        own_middle = lax.dynamic_slice_in_dim(
            middle, shard_index * part_width, part_width, 2
        ).astype(jnp.float32)
        results.append((own_middle + weighted).astype(jnp.bfloat16)[0])
    return jnp.stack(results, 0)


LANES = 384
BASE = 150000.0
MIB = 1 << 20


def shape_of(shape, dtype=jnp.bfloat16):
    return jax.ShapeDtypeStruct(shape, dtype)


def vmem():
    return pl.BlockSpec(memory_space=pltpu.VMEM)


def smem():
    return pl.BlockSpec(memory_space=pltpu.SMEM)


def outside():
    return pl.BlockSpec(memory_space=pltpu.HBM)


def dot_last(left, right):
    return lax.dot_general(left, right, (((1,), (1,)), ((), ())), preferred_element_type=jnp.float32)


def swap(value, axes, mask):
    size = lax.axis_size(axes)
    return lax.ppermute(value, axes, [(i, i ^ mask) for i in range(size)])


def lane_of(by_group):
    tp = lax.axis_index("tp")
    number = lax.axis_index("sec") ^ (tp & 1) ^ (tp >> 1)
    return number ^ (lax.axis_index("grp") & 1) if by_group else number


def lane_swap(value, mask, shard_masks_by_lane, by_group):
    groups, tps = lax.axis_size("grp"), lax.axis_size("tp")

    def parity(group, shard):
        return (shard & 1) ^ (shard >> 1) ^ (group & 1 if by_group else 0)

    pairs = []
    for core in range(2):
        for group in range(groups):
            for shard in range(tps):
                number = core ^ parity(group, shard)
                to_group, to_shard = group ^ mask, shard ^ shard_masks_by_lane[number]
                to_core = number ^ parity(to_group, to_shard)
                pairs.append(((core * groups + group) * tps + shard, (to_core * groups + to_group) * tps + to_shard))
    return lax.ppermute(value, ("sec", "grp", "tp"), pairs)


def shard_swaps(parts, by_group):
    return [lane_swap(part, 0, masks, by_group) for part, masks in zip(parts, ((3, 3), (1, 2), (2, 1)))]


def shard_masks(by_group):
    number = lane_of(by_group)
    return 3, 1 + number, 2 - number


def split_width(width):
    cuts = list(range(0, width, 768)) + [width]
    return list(zip(cuts[:-1], cuts[1:]))


def attention_kernel(lengths_hbm, sinks_hbm, routes_hbm, weights_hbm, gain_hbm, x_hbm, wq_hbm, wkv_hbm, cache_hbm, wo_hbm,
                     other_ref, own_x_ref, mix_ref, wo_ref,
                     lengths_ref, sinks_ref, routes_ref, weights_ref, gain_ref, x_ref, wq_ref, wkv_ref, cache_ref,
                     xs_ref, turned_ref, mixed_ref, sems):
    total_rows, width = x_ref.shape
    rows, slots, pair = cache_ref.shape
    steps = total_rows // rows
    heads = wq_ref.shape[1] // HEAD_SIZE
    per_row = heads * steps
    tps = other_ref.shape[0]
    cuts = split_width(width)
    small = [(lengths_hbm, lengths_ref), (x_hbm, x_ref), (gain_hbm, gain_ref), (routes_hbm, routes_ref), (weights_hbm, weights_ref),
             (sinks_hbm, sinks_ref)]
    small = [pltpu.make_async_copy(source, target, sems.at[n]) for n, (source, target) in enumerate(small)]
    copies = [pltpu.make_async_copy(wkv_hbm, wkv_ref, sems.at[6])]
    for n, (low, high) in enumerate(cuts):
        part = pl.ds(low, high - low)
        copies.append(pltpu.make_async_copy(wq_hbm.at[part], wq_ref.at[part], sems.at[9 + n]))
    copies.append(pltpu.make_async_copy(cache_hbm, cache_ref, sems.at[7]))
    copies.append(pltpu.make_async_copy(wo_hbm, wo_ref, sems.at[8]))
    for copy in small + copies:
        copy.start()
    small[1].wait()
    small[2].wait()
    x = x_ref[...].astype(jnp.float32)
    scale = lax.rsqrt(jnp.mean(x * x, axis=-1, keepdims=True) + 1e-05)
    normed = (x * scale * gain_ref[...].reshape(1, width)).astype(jnp.bfloat16)
    copies[0].wait()
    pairs = jnp.dot(normed, wkv_ref[...], preferred_element_type=jnp.float32)
    query = jnp.zeros((total_rows, wq_ref.shape[1]), jnp.float32)
    for n, (low, high) in enumerate(cuts[:-1]):
        copies[1 + n].wait()
        query = query + jnp.dot(normed[:, low:high], wq_ref[low:high, :], preferred_element_type=jnp.float32)
    for copy in (small[0], *small[3:], copies[len(cuts)]):
        copy.wait()
    query = query + jnp.dot(normed[:, cuts[-1][0]:], wq_ref[cuts[-1][0]:, :], preferred_element_type=jnp.float32)

    lane = lax.broadcasted_iota(jnp.int32, (total_rows, pair), 1)
    line = lax.broadcasted_iota(jnp.int32, (total_rows, pair), 0)
    position = jnp.zeros((total_rows, pair), jnp.int32)
    for r in range(rows):
        for s in range(steps):
            position = jnp.where(line == s * rows + r, lengths_ref[r] + s, position)
    half = HEAD_SIZE // 2
    counter = jnp.bitwise_and(lane, half - 1).astype(jnp.float32)
    frequency = jnp.exp(counter * jnp.float32(-2.0 / HEAD_SIZE * np.log(BASE)))
    angle = position.astype(jnp.float32) * frequency
    cosine, sine = jnp.cos(angle), jnp.sin(angle)
    low_half = jnp.bitwise_and(lane, HEAD_SIZE - 1) < half
    sine = jnp.where(low_half, -sine, sine)

    def turn(two):
        return two * cosine + jnp.where(low_half, pltpu.roll(two, pair - half, 1), pltpu.roll(two, half, 1)) * sine

    spare = xs_ref.shape[1] - width
    spare_at = lax.broadcasted_iota(jnp.int32, (rows, spare), 1)
    corner = lax.broadcasted_iota(jnp.int32, (rows, rows), 0) == lax.broadcasted_iota(jnp.int32, (rows, rows), 1)
    tables = []
    for s in range(steps):
        table = jnp.zeros((rows, spare), jnp.float32)
        for e in range(TOP):
            across = jnp.sum(jnp.where(routes_ref[s] == e, weights_ref[s], 0.0), axis=0, keepdims=True)
            column = jnp.sum(jnp.where(corner, across, 0.0), axis=1, keepdims=True)
            high_part = column.astype(jnp.bfloat16).astype(jnp.float32)
            table = jnp.where(spare_at == 2 * e, high_part, jnp.where(spare_at == 2 * e + 1, column - high_part, table))
        tables.append(table)
    xs_ref[...] = jnp.concatenate([x, jnp.concatenate(tables, axis=0)], axis=1)
    own = (lane_of(True) * tps + lax.axis_index("tp")) * LANES
    own_x_ref[...] = xs_ref[:, pl.ds(pl.multiple_of(own, LANES), LANES)]
    is_key = lane < HEAD_SIZE
    fresh = jnp.where(is_key, turn(pairs), pairs).astype(jnp.bfloat16)
    for m in range(heads // 2):
        two = turn(query[:, m * pair:(m + 1) * pair])
        for odd in range(2):
            one = two if odd == 0 else pltpu.roll(two, HEAD_SIZE, 1)
            one = jnp.where(is_key, one, 0.0)
            for s in range(steps):
                slot = (2 * m + odd) * steps + s
                turned_ref[pl.ds(slot, rows, stride=per_row), :] = one[s * rows:(s + 1) * rows]
    turned = turned_ref[...].astype(jnp.bfloat16)

    copies[-2].wait()
    place = lax.broadcasted_iota(jnp.int32, (per_row, slots), 1)
    scores = []
    for r in range(rows):
        score = dot_last(turned[r * per_row:(r + 1) * per_row], cache_ref[r]) * 0.125
        scores.append(jnp.where(place < lengths_ref[r], score, -jnp.inf))
    cached = jnp.concatenate(scores, axis=0)
    row_at = lax.broadcasted_iota(jnp.int32, (rows * per_row, total_rows), 0)
    fresh_at = lax.broadcasted_iota(jnp.int32, (rows * per_row, total_rows), 1)
    seen = (row_at // per_row == fresh_at % rows) & (fresh_at // rows <= row_at % steps)
    new = jnp.where(seen, dot_last(turned, fresh) * 0.125, -jnp.inf)
    head_at = lax.broadcasted_iota(jnp.int32, (rows * per_row, 1), 0) % per_row // steps
    sink = jnp.zeros((rows * per_row, 1), jnp.float32)
    for h in range(heads):
        sink = jnp.where(head_at == h, sinks_ref[h], sink)
    largest = jnp.maximum(jnp.maximum(jnp.max(cached, axis=-1, keepdims=True), jnp.max(new, axis=-1, keepdims=True)), sink)
    cached = jnp.exp(cached - largest)
    new = jnp.exp(new - largest)
    total = jnp.sum(cached, axis=-1, keepdims=True) + jnp.sum(new, axis=-1, keepdims=True) + jnp.exp(sink - largest)
    share = 1.0 / total
    cached = (cached * share).astype(jnp.bfloat16)
    new = (new * share).astype(jnp.bfloat16)
    mixed = []
    for r in range(rows):
        mixed.append(jnp.dot(cached[r * per_row:(r + 1) * per_row], cache_ref[r], preferred_element_type=jnp.float32))
    mixed_ref[...] = jnp.concatenate(mixed, axis=0) + jnp.dot(new, fresh, preferred_element_type=jnp.float32)

    def head(h):
        return jnp.concatenate([mixed_ref[pl.ds(h * steps + s, rows, stride=per_row), :] for s in range(steps)], axis=0)

    mix_ref[...] = jnp.concatenate(
        [jnp.where(is_key, pltpu.roll(head(2 * m), HEAD_SIZE, 1), head(2 * m + 1)) for m in range(heads // 2)], axis=1
    ).astype(jnp.bfloat16)
    copies[-1].wait()
    project(mix_ref, wo_ref, other_ref, 1 - lane_of(True))


def project(mix_ref, wo_ref, out_ref, side):
    width, (tps, total_rows, _) = wo_ref.shape[0], out_ref.shape
    for at in range(2):
        start, stop = at * tps * LANES, min((at + 1) * tps * LANES, width)

        @pl.when(side == at)
        def _(start=start, stop=stop):
            partial = dot_last(mix_ref[...], wo_ref[start:stop, :])
            for t in range(tps):
                low, high = t * LANES, min((t + 1) * LANES, stop - start)
                piece = partial[:, low:high]
                if high - low < LANES:
                    piece = jnp.concatenate([piece, jnp.zeros((total_rows, LANES - (high - low)), jnp.float32)], axis=1)
                out_ref[t] = piece.astype(out_ref.dtype)


def own_projection_kernel(mix_ref, wo_ref, mine_ref):
    project(mix_ref, wo_ref, mine_ref, lane_of(True))


def attention_partial(flat, gain, w_query, key_value, sinks, w_output, cache, lengths, routes, weights, secs, tps):
    total_rows, width = flat.shape
    rows, slots, pair = cache.shape
    per_row = w_query.shape[1] // HEAD_SIZE * (total_rows // rows)
    shards = secs * tps
    operands = (lengths, sinks, routes, weights, gain, flat, w_query, key_value, cache, w_output.swapaxes(0, 1))
    return pl.pallas_call(
        attention_kernel,
        name="attention",
        out_shape=[shape_of((tps, total_rows, LANES)), shape_of((total_rows, LANES), jnp.float32),
                   shape_of((total_rows, w_output.shape[0])), shape_of((width, w_output.shape[0]))],
        in_specs=[outside()] * len(operands),
        out_specs=[vmem()] * 4,
        scratch_shapes=[
            pltpu.SMEM(lengths.shape, jnp.int32),
            pltpu.SMEM(sinks.shape, jnp.float32),
            pltpu.VMEM(routes.shape, jnp.int32),
            pltpu.VMEM(weights.shape, jnp.float32),
            pltpu.VMEM(gain.shape, jnp.float32),
            pltpu.VMEM((total_rows, width), jnp.bfloat16),
            pltpu.VMEM(w_query.shape, jnp.bfloat16),
            pltpu.VMEM(key_value.shape, jnp.bfloat16),
            pltpu.VMEM(cache.shape, jnp.bfloat16),
            pltpu.VMEM((total_rows, shards * LANES), jnp.float32),
            pltpu.VMEM((rows * per_row, pair), jnp.float32),
            pltpu.VMEM((rows * per_row, pair), jnp.float32),
            pltpu.SemaphoreType.DMA((9 + len(split_width(width)),)),
        ],
        compiler_params=pltpu.CompilerParams(vmem_limit_bytes=24 * MIB),
    )(*[pltpu.with_memory_space_constraint(operand, pltpu.HBM) for operand in operands])


def call(kernel, name, outs, *operands, limit=4, flops=0):
    single = not isinstance(outs, list)
    held = [*operands, *([outs] if single else outs)]
    return pl.pallas_call(
        kernel,
        name=name,
        out_shape=outs,
        in_specs=[vmem()] * len(operands),
        out_specs=vmem() if single else [vmem()] * len(outs),
        compiler_params=pltpu.CompilerParams(vmem_limit_bytes=limit * MIB),
        cost_estimate=pl.CostEstimate(flops=flops, transcendentals=0,
                                      bytes_accessed=sum(math.prod(a.shape) * a.dtype.itemsize for a in held)),
    )(*operands)


def after_core_kernel(mine_ref, come_ref, own_ref, *send_refs):
    tp = lax.axis_index("tp")
    own_ref[...] = mine_ref[tp] + come_ref[tp].astype(jnp.float32)
    for mask, ref in zip(shard_masks(True), send_refs):
        to = jnp.bitwise_xor(tp, mask)
        ref[...] = (mine_ref[to] + come_ref[to].astype(jnp.float32)).astype(jnp.bfloat16)


def after_core_halves_kernel(mine_ref, come_ref, own_ref, *send_refs):
    tp, half = lax.axis_index("tp"), mine_ref.shape[1] // 2
    own_ref[...] = mine_ref[tp] + come_ref[tp].astype(jnp.float32)
    for mask, first, second in zip(shard_masks(False), send_refs[:3], send_refs[3:]):
        to = jnp.bitwise_xor(tp, mask)
        part = (mine_ref[to] + come_ref[to].astype(jnp.float32)).astype(jnp.bfloat16)
        first[...] = part[:half]
        second[...] = part[half:]


def add_all(*refs):
    total = refs[0][...]
    for ref in refs[1:]:
        total = total + ref[...].astype(jnp.float32)
    return total


def sum_kernel(*refs):
    refs[-1][...] = add_all(*refs[:-1]).astype(jnp.bfloat16).reshape(refs[-1].shape)


def sum_rows_kernel(own_ref, *refs, line):
    come, outs = refs[:3], refs[3:]
    lines = outs[0].shape[0]
    total = own_ref[line:line + len(outs) * lines]
    for ref in come:
        total = total + ref[...].astype(jnp.float32)
    for n, out in enumerate(outs):
        out[...] = total[n * lines:(n + 1) * lines].astype(out.dtype)


def scatter_shards(mine, come):
    tps, lines, part = mine.shape
    own, *parts = call(after_core_kernel, "after_core", [shape_of((lines, part), jnp.float32)] + [shape_of((lines, part))] * (tps - 1),
                       mine, come)
    return [own] + shard_swaps(parts, True)


def first_products(pieces, masks, side, x_ref, gain_ref, gate_ref, up_ref, gate_out, up_out, square_out):
    width, lines = gate_ref.shape[1], x_ref.shape[0]
    tp = lax.axis_index("tp")
    for mask, piece in zip(masks, pieces):
        at = pl.multiple_of(jnp.bitwise_xor(tp, mask) * LANES, LANES)
        x_ref[:, pl.ds(at, LANES)] = piece[...].reshape(lines, LANES)
    for at in range(2):
        start, stop = at * x_ref.shape[1], min((at + 1) * x_ref.shape[1], width)

        @pl.when(side == at)
        def _(start=start, stop=stop):
            x = x_ref[:, :stop - start].astype(jnp.float32)
            square_out[...] = jnp.broadcast_to(jnp.sum(x * x, axis=-1, keepdims=True), square_out.shape)
            scaled = (x * gain_ref[:, start:stop]).astype(jnp.bfloat16)
            gate_out[...] = dot_last(scaled, gate_ref[:, start:stop])
            up_out[...] = dot_last(scaled, up_ref[:, start:stop])


def near_kernel(gain_ref, gate_ref, up_ref, *refs):
    pieces, (x_ref, gate_out, up_out, square_out) = refs[:-4], refs[-4:]
    first_products(pieces, (0, *shard_masks(True)), lane_of(True), x_ref, gain_ref, gate_ref, up_ref, gate_out, up_out,
                   square_out)


def second_product(act_ref, down_ref, out_ref, number):
    tps, _, part = out_ref.shape

    for at in range(2):
        starts = [((at ^ (t & 1) ^ (t >> 1)) * tps + t) * part for t in range(tps)]

        @pl.when(number == at)
        def _(starts=starts):
            for first, last in ((0, 0), (1, 2), (3, 3)):
                shift = starts[first] % 128
                out = jnp.dot(act_ref[...], down_ref[:, starts[first] - shift:starts[last] + part],
                              preferred_element_type=jnp.float32)
                for n, t in enumerate(range(first, last + 1)):
                    out_ref[t] = out[:, shift + n * part:shift + (n + 1) * part].astype(out_ref.dtype)


def far_kernel(gain_ref, gate_ref, up_ref, down_ref, near_x_ref, near_gate_ref, near_up_ref, near_square_ref, *refs):
    pieces, (other_ref, act_ref, far_x_ref, gate_out, up_out, square_out) = refs[:-6], refs[-6:]
    side, grp = lane_of(True), lax.axis_index("grp")
    masks = shard_masks(True)
    first_products(pieces, (0, masks[0], masks[2], masks[1]), 1 - side, far_x_ref, gain_ref, gate_ref, up_ref, gate_out, up_out,
                   square_out)
    width, half = gate_ref.shape[1], near_x_ref.shape[1]
    spare = jnp.where(side == 1, near_x_ref[:, width - half:], far_x_ref[:, width - half:]).astype(jnp.float32)
    spare_at = lax.broadcasted_iota(jnp.int32, spare.shape, 1)
    weight = jnp.sum(jnp.where((spare_at == 2 * grp) | (spare_at == 2 * grp + 1), spare, 0.0), axis=1, keepdims=True)
    square = (near_square_ref[...] + square_out[...])[:, :1]
    scale = lax.rsqrt(square / width + 1e-05)
    gate_h = (near_gate_ref[...] + gate_out[...]) * scale
    up_h = (near_up_ref[...] + up_out[...]) * scale
    act_ref[...] = ((up_h + 1.0) * gate_h * jax.nn.sigmoid(1.702 * gate_h) * weight).astype(jnp.bfloat16)
    second_product(act_ref, down_ref, other_ref, 1 - lane_of(False))


def last_kernel(act_ref, down_ref, near_x_ref, far_x_ref, mine_ref, middle_ref, row_ref):
    sec, tp = lax.axis_index("sec"), lax.axis_index("tp")
    second_product(act_ref, down_ref, mine_ref, lane_of(False))
    total_rows, part = middle_ref.shape
    near, far = near_x_ref[-total_rows:].astype(jnp.float32), far_x_ref[-total_rows:].astype(jnp.float32)
    first = lane_of(True) == 0
    x = jnp.concatenate([jnp.where(first, near, far), jnp.where(first, far, near)], axis=1)
    for c in range(row_ref.shape[0]):
        row_ref[c] = x[:, c * part:(c + 1) * part]
    middle_ref[...] = row_ref[sec * mine_ref.shape[0] + tp]


def experts(gain, w_gate, w_up, w_down, pieces, part):
    gain, w_gate, w_up = gain.reshape(1, -1), w_gate.swapaxes(0, 1), w_up.swapaxes(0, 1)
    (hidden, width), tps, (groups, total_rows, _) = w_gate.shape, len(pieces), pieces[0].shape
    lines = groups * total_rows
    far_pieces = [swap(piece, "sec", 1) for piece in pieces]
    halves = [shape_of((lines, tps * LANES)), shape_of((lines, hidden), jnp.float32), shape_of((lines, hidden), jnp.float32),
              shape_of((lines, 128), jnp.float32)]
    near = call(near_kernel, "near_columns", halves, gain, w_gate, w_up, *pieces, limit=12, flops=2 * lines * width * hidden)
    other, act, far_x = pl.pallas_call(
        far_kernel,
        name="far_columns",
        out_shape=[shape_of((tps, lines, part)), shape_of((lines, hidden)), halves[0]],
        in_specs=[vmem()] * (8 + len(far_pieces)),
        out_specs=[vmem()] * 3,
        scratch_shapes=[pltpu.VMEM(half.shape, half.dtype) for half in halves[1:]],
        compiler_params=pltpu.CompilerParams(vmem_limit_bytes=16 * MIB),
    )(gain, w_gate, w_up, w_down, *near, *far_pieces)
    come = swap(other, "sec", 1)
    mine, middle = pl.pallas_call(
        last_kernel,
        name="own_columns",
        out_shape=[shape_of((tps, lines, part), jnp.float32), shape_of((total_rows, part), jnp.float32)],
        in_specs=[vmem()] * 4,
        out_specs=[vmem()] * 2,
        scratch_shapes=[pltpu.VMEM((2 * tps, total_rows, part), jnp.float32)],
        compiler_params=pltpu.CompilerParams(vmem_limit_bytes=12 * MIB),
        cost_estimate=pl.CostEstimate(flops=lines * width * hidden, transcendentals=0, bytes_accessed=2 * lines * width),
    )(act, w_down, near[0], far_x)
    return mine, come, middle


def every_expert_body(inputs, attention_gain, w_query, key_value_weight, head_sink_logits, w_output, cache_pairs, lengths,
                      expert_gain, w_gate, w_up, w_down, routes, gate_weights):
    secs, tps, groups = lax.axis_size("sec"), lax.axis_size("tp"), lax.axis_size("grp")
    steps, rows, width = inputs.shape
    flat = inputs.reshape(steps * rows, width)
    other, own_x, mix, held = attention_partial(
        flat, attention_gain, w_query, key_value_weight[:, 0], head_sink_logits, w_output, cache_pairs[:, :, 0], lengths,
        routes.swapaxes(1, 2), gate_weights.swapaxes(1, 2), secs, tps)
    come = swap(other, "sec", 1)
    mine = call(own_projection_kernel, "own_projection", shape_of(other.shape, jnp.float32), mix, held, limit=12,
                flops=mix.size * width)
    middle = call(sum_kernel, "sum", shape_of((steps * rows, LANES)), *scatter_shards(mine, come), own_x)
    stacked = jnp.stack([lane_swap(middle, m, (0, 0), True) for m in reversed(range(1, groups))] + [middle])
    pieces = [stacked] + shard_swaps([stacked] * (tps - 1), True)
    part = width // (secs * tps)
    mine, come, own_middle = experts(expert_gain, w_gate[0], w_up[0], w_down[0], pieces, part)
    lines = steps * rows
    own, *parts = call(after_core_halves_kernel, "after_core_halves",
                       [shape_of((groups * lines, part), jnp.float32)] + [shape_of((groups // 2 * lines, part))] * 6, mine, come)
    far_come, near_come = shard_swaps(parts[:3], False), shard_swaps(parts[3:], False)
    third, second = call(functools.partial(sum_rows_kernel, line=0), "sum_far_rows", [shape_of((lines, part))] * 2,
                         own, *far_come)
    third, second = swap(third, "grp", 3), swap(second, "grp", 2)
    nearest, own = call(functools.partial(sum_rows_kernel, line=2 * lines), "sum_near_rows",
                        [shape_of((lines, part)), shape_of((lines, part), jnp.float32)], own, *near_come)
    return call(sum_kernel, "combine", shape_of((steps, rows, part)), own, third, second, swap(nearest, "grp", 1), own_middle)


def body(*args):
    sizes = lax.axis_size("sec"), lax.axis_size("tp"), lax.axis_size("grp"), args[9].shape[0]
    if sizes == (2, 4, TOP, 1):
        return every_expert_body(*args)
    return general_body(*args)


def solution(mesh):
    placed = (
        P(None, "grp", None),
        P(),
        P(None, ("sec", "tp")),
        P(None, ("sec", "tp"), None),
        P(("sec", "tp")),
        P(("sec", "tp"), None),
        P("grp", None, ("sec", "tp"), None),
        P("grp"),
        P(),
        P("grp", None, ("sec", "tp")),
        P("grp", None, ("sec", "tp")),
        P("grp", ("sec", "tp"), None),
        P(None, "grp", None),
        P(None, "grp", None),
    )
    return jax.shard_map(
        body, mesh=mesh, in_specs=placed, out_specs=P(None, "grp", ("sec", "tp")), check_vma=False
    )
```

```python
import functools
import math

import jax
import jax.numpy as jnp
import numpy as np
from jax import lax
from jax.experimental import pallas as pl
from jax.experimental.pallas import tpu as pltpu
from jax.sharding import PartitionSpec as P

HEAD_SIZE = 64
TOP = 4


def rms_norm(values, scale_row):
    widened = values.astype(jnp.float32)
    scale_factor = lax.rsqrt(jnp.mean(widened * widened, axis=-1, keepdims=True) + 1e-05)
    return (widened * scale_factor * scale_row).astype(jnp.bfloat16)


def rotate(vectors, position):
    half_size = vectors.shape[-1] // 2
    counter = jnp.arange(half_size).astype(jnp.float32)
    frequency = jnp.power(jnp.float32(150000.0), counter * (-2.0 / vectors.shape[-1]))
    angle_table = position * frequency
    cosine = jnp.cos(angle_table)
    sine_table = jnp.sin(angle_table)
    first_half = vectors[..., :half_size]
    second_half = vectors[..., half_size:]
    return jnp.concatenate(
        [
            first_half * cosine - second_half * sine_table,
            first_half * sine_table + second_half * cosine,
        ],
        axis=-1,
    )


def attend(
    normalized_input,
    w_query,
    key_value_weight,
    head_sink_logits,
    w_output,
    cache_pairs,
    lengths,
    step_index,
    fresh_keys,
    fresh_values,
):
    row_count = normalized_input.shape[0]
    kv_heads = key_value_weight.shape[1]
    query = jnp.dot(normalized_input, w_query, preferred_element_type=jnp.float32).reshape(
        row_count, -1, HEAD_SIZE
    )
    cache_entry_pairs = jnp.dot(
        normalized_input,
        key_value_weight.reshape(key_value_weight.shape[0], -1),
        preferred_element_type=jnp.float32,
    ).reshape(row_count, kv_heads, 2 * HEAD_SIZE)
    position = (lengths + step_index).astype(jnp.float32)[:, None, None]
    rotated_rows = rotate(query, position).astype(jnp.bfloat16)
    fresh_keys = fresh_keys + [
        rotate(cache_entry_pairs[..., :HEAD_SIZE], position).astype(jnp.bfloat16)
    ]
    fresh_values = fresh_values + [cache_entry_pairs[..., HEAD_SIZE:].astype(jnp.bfloat16)]
    grouped_queries = rotated_rows.reshape(row_count, kv_heads, -1, HEAD_SIZE)
    new_keys = jnp.stack(fresh_keys, 1)
    new_values = jnp.stack(fresh_values, 1)
    cached = (
        jnp.einsum(
            "rkgd,rjkd->rkgj",
            grouped_queries,
            cache_pairs[..., :HEAD_SIZE],
            preferred_element_type=jnp.float32,
        )
        * 0.125
    )
    valid = (jnp.arange(cache_pairs.shape[1])[None, :] < lengths[:, None])[:, None, None, :]
    cached = jnp.where(valid, cached, -jnp.inf)
    fresh = (
        jnp.einsum("rkgd,rikd->rkgi", grouped_queries, new_keys, preferred_element_type=jnp.float32)
        * 0.125
    )
    sink_row = head_sink_logits.reshape(kv_heads, -1)[None]
    largest = jnp.maximum(jnp.maximum(jnp.max(cached, axis=-1), jnp.max(fresh, axis=-1)), sink_row)
    cached_exp = jnp.exp(cached - largest[..., None])
    fresh_exp = jnp.exp(fresh - largest[..., None])
    denominator = (
        jnp.sum(cached_exp, axis=-1) + jnp.sum(fresh_exp, axis=-1) + jnp.exp(sink_row - largest)
    )
    cached_probs = (cached_exp / denominator[..., None]).astype(jnp.bfloat16)
    fresh_probs = (fresh_exp / denominator[..., None]).astype(jnp.bfloat16)
    mixed = jnp.einsum(
        "rkgj,rjkd->rkgd",
        cached_probs,
        cache_pairs[..., HEAD_SIZE:],
        preferred_element_type=jnp.float32,
    )
    mixed = mixed + jnp.einsum(
        "rkgi,rikd->rkgd", fresh_probs, new_values, preferred_element_type=jnp.float32
    )
    attention_mix = mixed.reshape(row_count, -1).astype(jnp.bfloat16)
    partial_sum = jnp.dot(attention_mix, w_output, preferred_element_type=jnp.float32)
    return (partial_sum, fresh_keys, fresh_values)


def general_body(
    inputs,
    attention_gain,
    w_query,
    key_value_weight,
    head_sink_logits,
    w_output,
    cache_pairs,
    lengths,
    expert_gain,
    w_gate,
    w_up,
    w_down,
    routes,
    gate_weights,
):
    shards = lax.axis_size(("sec", "tp"))
    shard_index = lax.axis_index(("sec", "tp"))
    experts = lax.axis_size("grp") * w_gate.shape[0]
    group_rows = inputs.shape[1]
    width = inputs.shape[2]
    part_width = width // shards
    chosen = max(TOP, experts // 2)
    capacity = group_rows * TOP // chosen
    slot_total = experts * capacity
    gate_matrix = w_gate[0]
    up_matrix = w_up[0]
    down_matrix = w_down[0]
    fresh_keys = []
    fresh_values = []
    results = []
    for step_index in range(inputs.shape[0]):
        normalized_input = rms_norm(inputs[step_index], attention_gain)
        partial_sum, fresh_keys, fresh_values = attend(
            normalized_input,
            w_query,
            key_value_weight,
            head_sink_logits,
            w_output,
            cache_pairs,
            lengths,
            step_index,
            fresh_keys,
            fresh_values,
        )
        summed = lax.psum(partial_sum[None], ("sec", "tp"))
        middle = (inputs[step_index][None].astype(jnp.float32) + summed).astype(jnp.bfloat16)
        route_rows = routes[step_index][None]
        step_count = middle.shape[0]
        expert_in = rms_norm(middle, expert_gain)
        flat_routes = route_rows.reshape(step_count, group_rows * TOP)
        onehot = (flat_routes[..., None] == jnp.arange(experts)[None, None, :]).astype(jnp.int32)
        earlier = jnp.cumsum(onehot, axis=1) - onehot
        slot_index = jnp.sum(earlier * onehot, axis=-1).reshape(step_count, group_rows, TOP)
        target = route_rows * capacity + slot_index
        placed = target[..., None] == jnp.arange(slot_total)[None, None, None, :]
        dispatch_table = jnp.sum(placed.astype(jnp.int32), axis=2).astype(jnp.bfloat16)
        combine_table = jnp.sum(
            jnp.where(placed, gate_weights[step_index][None][..., None], 0.0), axis=2
        )
        outgoing = jnp.einsum(
            "crm,crd->cmd", dispatch_table, expert_in, preferred_element_type=jnp.float32
        )
        outgoing = outgoing.astype(jnp.bfloat16).reshape(step_count, experts, capacity, width)
        arrived = lax.all_to_all(outgoing, "grp", split_axis=1, concat_axis=1, tiled=True)
        gate_h = jnp.einsum(
            "snpd,dh->snph", arrived, gate_matrix, preferred_element_type=jnp.float32
        )
        up_h = jnp.einsum("snpd,dh->snph", arrived, up_matrix, preferred_element_type=jnp.float32)
        act = ((up_h + 1.0) * gate_h * jax.nn.sigmoid(1.702 * gate_h)).astype(jnp.bfloat16)
        partial_out = jnp.einsum(
            "snph,hd->snpd", act, down_matrix, preferred_element_type=jnp.float32
        )
        reduced = lax.psum_scatter(
            partial_out, ("sec", "tp"), scatter_dimension=3, tiled=True
        ).astype(jnp.bfloat16)
        returned = lax.all_to_all(reduced, "grp", split_axis=1, concat_axis=1, tiled=True)
        returned_rows = returned.reshape(step_count, slot_total, part_width).astype(jnp.float32)
        weighted = jnp.einsum(
            "srm,smd->srd", combine_table, returned_rows, precision=lax.Precision.HIGHEST
        )
        own_middle = lax.dynamic_slice_in_dim(
            middle, shard_index * part_width, part_width, 2
        ).astype(jnp.float32)
        results.append((own_middle + weighted).astype(jnp.bfloat16)[0])
    return jnp.stack(results, 0)


LANES = 384
BASE = 150000.0
MIB = 1 << 20


def shape_of(shape, dtype=jnp.bfloat16):
    return jax.ShapeDtypeStruct(shape, dtype)


def vmem():
    return pl.BlockSpec(memory_space=pltpu.VMEM)


def smem():
    return pl.BlockSpec(memory_space=pltpu.SMEM)


def outside():
    return pl.BlockSpec(memory_space=pltpu.HBM)


def dot_last(left, right):
    return lax.dot_general(left, right, (((1,), (1,)), ((), ())), preferred_element_type=jnp.float32)


def swap(value, axes, mask):
    size = lax.axis_size(axes)
    return lax.ppermute(value, axes, [(i, i ^ mask) for i in range(size)])


def lane_of(by_group):
    tp = lax.axis_index("tp")
    number = lax.axis_index("sec") ^ (tp & 1) ^ (tp >> 1)
    return number ^ (lax.axis_index("grp") & 1) if by_group else number


def lane_swap(value, mask, shard_masks_by_lane, by_group):
    groups, tps = lax.axis_size("grp"), lax.axis_size("tp")

    def parity(group, shard):
        return (shard & 1) ^ (shard >> 1) ^ (group & 1 if by_group else 0)

    pairs = []
    for core in range(2):
        for group in range(groups):
            for shard in range(tps):
                number = core ^ parity(group, shard)
                to_group, to_shard = group ^ mask, shard ^ shard_masks_by_lane[number]
                to_core = number ^ parity(to_group, to_shard)
                pairs.append(((core * groups + group) * tps + shard, (to_core * groups + to_group) * tps + to_shard))
    return lax.ppermute(value, ("sec", "grp", "tp"), pairs)


def shard_swaps(parts, by_group):
    return [lane_swap(part, 0, masks, by_group) for part, masks in zip(parts, ((3, 3), (1, 2), (2, 1)))]


def shard_masks(by_group):
    number = lane_of(by_group)
    return 3, 1 + number, 2 - number


def split_width(width):
    cuts = list(range(0, width, 768)) + [width]
    return list(zip(cuts[:-1], cuts[1:]))


def attention_kernel(lengths_hbm, sinks_hbm, routes_hbm, weights_hbm, gain_hbm, x_hbm, wq_hbm, wkv_hbm, cache_hbm, wo_hbm,
                     other_ref, own_x_ref, mix_ref, wo_ref,
                     lengths_ref, sinks_ref, routes_ref, weights_ref, gain_ref, x_ref, wq_ref, wkv_ref, cache_ref,
                     xs_ref, turned_ref, mixed_ref, sems):
    total_rows, width = x_ref.shape
    rows, slots, pair = cache_ref.shape
    steps = total_rows // rows
    heads = wq_ref.shape[1] // HEAD_SIZE
    per_row = heads * steps
    tps = other_ref.shape[0]
    cuts = split_width(width)
    small = [(lengths_hbm, lengths_ref), (x_hbm, x_ref), (gain_hbm, gain_ref), (routes_hbm, routes_ref), (weights_hbm, weights_ref),
             (sinks_hbm, sinks_ref)]
    small = [pltpu.make_async_copy(source, target, sems.at[n]) for n, (source, target) in enumerate(small)]
    copies = [pltpu.make_async_copy(wkv_hbm, wkv_ref, sems.at[6])]
    for n, (low, high) in enumerate(cuts):
        part = pl.ds(low, high - low)
        copies.append(pltpu.make_async_copy(wq_hbm.at[part], wq_ref.at[part], sems.at[9 + n]))
    copies.append(pltpu.make_async_copy(cache_hbm, cache_ref, sems.at[7]))
    copies.append(pltpu.make_async_copy(wo_hbm, wo_ref, sems.at[8]))
    for copy in small + copies:
        copy.start()
    small[1].wait()
    small[2].wait()
    x = x_ref[...].astype(jnp.float32)
    scale = lax.rsqrt(jnp.mean(x * x, axis=-1, keepdims=True) + 1e-05)
    normed = (x * scale * gain_ref[...].reshape(1, width)).astype(jnp.bfloat16)
    copies[0].wait()
    pairs = jnp.dot(normed, wkv_ref[...], preferred_element_type=jnp.float32)
    query = jnp.zeros((total_rows, wq_ref.shape[1]), jnp.float32)
    for n, (low, high) in enumerate(cuts[:-1]):
        copies[1 + n].wait()
        query = query + jnp.dot(normed[:, low:high], wq_ref[low:high, :], preferred_element_type=jnp.float32)
    for copy in (small[0], *small[3:], copies[len(cuts)]):
        copy.wait()
    query = query + jnp.dot(normed[:, cuts[-1][0]:], wq_ref[cuts[-1][0]:, :], preferred_element_type=jnp.float32)

    lane = lax.broadcasted_iota(jnp.int32, (total_rows, pair), 1)
    line = lax.broadcasted_iota(jnp.int32, (total_rows, pair), 0)
    position = jnp.zeros((total_rows, pair), jnp.int32)
    for r in range(rows):
        for s in range(steps):
            position = jnp.where(line == s * rows + r, lengths_ref[r] + s, position)
    half = HEAD_SIZE // 2
    counter = jnp.bitwise_and(lane, half - 1).astype(jnp.float32)
    frequency = jnp.exp(counter * jnp.float32(-2.0 / HEAD_SIZE * np.log(BASE)))
    angle = position.astype(jnp.float32) * frequency
    cosine, sine = jnp.cos(angle), jnp.sin(angle)
    low_half = jnp.bitwise_and(lane, HEAD_SIZE - 1) < half
    sine = jnp.where(low_half, -sine, sine)

    def turn(two):
        return two * cosine + jnp.where(low_half, pltpu.roll(two, pair - half, 1), pltpu.roll(two, half, 1)) * sine

    spare = xs_ref.shape[1] - width
    spare_at = lax.broadcasted_iota(jnp.int32, (rows, spare), 1)
    corner = lax.broadcasted_iota(jnp.int32, (rows, rows), 0) == lax.broadcasted_iota(jnp.int32, (rows, rows), 1)
    tables = []
    for s in range(steps):
        table = jnp.zeros((rows, spare), jnp.float32)
        for e in range(TOP):
            across = jnp.sum(jnp.where(routes_ref[s] == e, weights_ref[s], 0.0), axis=0, keepdims=True)
            column = jnp.sum(jnp.where(corner, across, 0.0), axis=1, keepdims=True)
            high_part = column.astype(jnp.bfloat16).astype(jnp.float32)
            table = jnp.where(spare_at == 2 * e, high_part, jnp.where(spare_at == 2 * e + 1, column - high_part, table))
        tables.append(table)
    xs_ref[...] = jnp.concatenate([x, jnp.concatenate(tables, axis=0)], axis=1)
    own = (lane_of(True) * tps + lax.axis_index("tp")) * LANES
    own_x_ref[...] = xs_ref[:, pl.ds(pl.multiple_of(own, LANES), LANES)]
    is_key = lane < HEAD_SIZE
    fresh = jnp.where(is_key, turn(pairs), pairs).astype(jnp.bfloat16)
    for m in range(heads // 2):
        two = turn(query[:, m * pair:(m + 1) * pair])
        for odd in range(2):
            one = two if odd == 0 else pltpu.roll(two, HEAD_SIZE, 1)
            one = jnp.where(is_key, one, 0.0)
            for s in range(steps):
                slot = (2 * m + odd) * steps + s
                turned_ref[pl.ds(slot, rows, stride=per_row), :] = one[s * rows:(s + 1) * rows]
    turned = turned_ref[...].astype(jnp.bfloat16)

    copies[-2].wait()
    place = lax.broadcasted_iota(jnp.int32, (per_row, slots), 1)
    scores = []
    for r in range(rows):
        score = dot_last(turned[r * per_row:(r + 1) * per_row], cache_ref[r]) * 0.125
        scores.append(jnp.where(place < lengths_ref[r], score, -jnp.inf))
    cached = jnp.concatenate(scores, axis=0)
    row_at = lax.broadcasted_iota(jnp.int32, (rows * per_row, total_rows), 0)
    fresh_at = lax.broadcasted_iota(jnp.int32, (rows * per_row, total_rows), 1)
    seen = (row_at // per_row == fresh_at % rows) & (fresh_at // rows <= row_at % steps)
    new = jnp.where(seen, dot_last(turned, fresh) * 0.125, -jnp.inf)
    head_at = lax.broadcasted_iota(jnp.int32, (rows * per_row, 1), 0) % per_row // steps
    sink = jnp.zeros((rows * per_row, 1), jnp.float32)
    for h in range(heads):
        sink = jnp.where(head_at == h, sinks_ref[h], sink)
    largest = jnp.maximum(jnp.maximum(jnp.max(cached, axis=-1, keepdims=True), jnp.max(new, axis=-1, keepdims=True)), sink)
    cached = jnp.exp(cached - largest)
    new = jnp.exp(new - largest)
    total = jnp.sum(cached, axis=-1, keepdims=True) + jnp.sum(new, axis=-1, keepdims=True) + jnp.exp(sink - largest)
    share = 1.0 / total
    cached = (cached * share).astype(jnp.bfloat16)
    new = (new * share).astype(jnp.bfloat16)
    mixed = []
    for r in range(rows):
        mixed.append(jnp.dot(cached[r * per_row:(r + 1) * per_row], cache_ref[r], preferred_element_type=jnp.float32))
    mixed_ref[...] = jnp.concatenate(mixed, axis=0) + jnp.dot(new, fresh, preferred_element_type=jnp.float32)

    def head(h):
        return jnp.concatenate([mixed_ref[pl.ds(h * steps + s, rows, stride=per_row), :] for s in range(steps)], axis=0)

    mix_ref[...] = jnp.concatenate(
        [jnp.where(is_key, pltpu.roll(head(2 * m), HEAD_SIZE, 1), head(2 * m + 1)) for m in range(heads // 2)], axis=1
    ).astype(jnp.bfloat16)
    copies[-1].wait()
    project(mix_ref, wo_ref, other_ref, 1 - lane_of(True))


def project(mix_ref, wo_ref, out_ref, side):
    width, (tps, total_rows, _) = wo_ref.shape[0], out_ref.shape
    for at in range(2):
        start, stop = at * tps * LANES, min((at + 1) * tps * LANES, width)

        @pl.when(side == at)
        def _(start=start, stop=stop):
            partial = dot_last(mix_ref[...], wo_ref[start:stop, :])
            for t in range(tps):
                low, high = t * LANES, min((t + 1) * LANES, stop - start)
                piece = partial[:, low:high]
                if high - low < LANES:
                    piece = jnp.concatenate([piece, jnp.zeros((total_rows, LANES - (high - low)), jnp.float32)], axis=1)
                out_ref[t] = piece.astype(out_ref.dtype)


def own_projection_kernel(mix_ref, wo_ref, mine_ref):
    project(mix_ref, wo_ref, mine_ref, lane_of(True))


def attention_partial(flat, gain, w_query, key_value, sinks, w_output, cache, lengths, routes, weights, secs, tps):
    total_rows, width = flat.shape
    rows, slots, pair = cache.shape
    per_row = w_query.shape[1] // HEAD_SIZE * (total_rows // rows)
    shards = secs * tps
    operands = (lengths, sinks, routes, weights, gain, flat, w_query, key_value, cache, w_output.swapaxes(0, 1))
    return pl.pallas_call(
        attention_kernel,
        name="attention",
        out_shape=[shape_of((tps, total_rows, LANES)), shape_of((total_rows, LANES), jnp.float32),
                   shape_of((total_rows, w_output.shape[0])), shape_of((width, w_output.shape[0]))],
        in_specs=[outside()] * len(operands),
        out_specs=[vmem()] * 4,
        scratch_shapes=[
            pltpu.SMEM(lengths.shape, jnp.int32),
            pltpu.SMEM(sinks.shape, jnp.float32),
            pltpu.VMEM(routes.shape, jnp.int32),
            pltpu.VMEM(weights.shape, jnp.float32),
            pltpu.VMEM(gain.shape, jnp.float32),
            pltpu.VMEM((total_rows, width), jnp.bfloat16),
            pltpu.VMEM(w_query.shape, jnp.bfloat16),
            pltpu.VMEM(key_value.shape, jnp.bfloat16),
            pltpu.VMEM(cache.shape, jnp.bfloat16),
            pltpu.VMEM((total_rows, shards * LANES), jnp.float32),
            pltpu.VMEM((rows * per_row, pair), jnp.float32),
            pltpu.VMEM((rows * per_row, pair), jnp.float32),
            pltpu.SemaphoreType.DMA((9 + len(split_width(width)),)),
        ],
        compiler_params=pltpu.CompilerParams(vmem_limit_bytes=24 * MIB),
    )(*[pltpu.with_memory_space_constraint(operand, pltpu.HBM) for operand in operands])


def call(kernel, name, outs, *operands, limit=4, flops=0):
    single = not isinstance(outs, list)
    held = [*operands, *([outs] if single else outs)]
    return pl.pallas_call(
        kernel,
        name=name,
        out_shape=outs,
        in_specs=[vmem()] * len(operands),
        out_specs=vmem() if single else [vmem()] * len(outs),
        compiler_params=pltpu.CompilerParams(vmem_limit_bytes=limit * MIB),
        cost_estimate=pl.CostEstimate(flops=flops, transcendentals=0,
                                      bytes_accessed=sum(math.prod(a.shape) * a.dtype.itemsize for a in held)),
    )(*operands)


def after_core_kernel(mine_ref, come_ref, own_ref, *send_refs):
    tp = lax.axis_index("tp")
    own_ref[...] = mine_ref[tp] + come_ref[tp].astype(jnp.float32)
    for mask, ref in zip(shard_masks(True), send_refs):
        to = jnp.bitwise_xor(tp, mask)
        ref[...] = (mine_ref[to] + come_ref[to].astype(jnp.float32)).astype(jnp.bfloat16)


def after_core_halves_kernel(mine_ref, come_ref, own_ref, *send_refs):
    tp, half = lax.axis_index("tp"), mine_ref.shape[1] // 2
    own_ref[...] = mine_ref[tp] + come_ref[tp].astype(jnp.float32)
    for mask, first, second in zip(shard_masks(False), send_refs[:3], send_refs[3:]):
        to = jnp.bitwise_xor(tp, mask)
        part = (mine_ref[to] + come_ref[to].astype(jnp.float32)).astype(jnp.bfloat16)
        first[...] = part[:half]
        second[...] = part[half:]


def add_all(*refs):
    total = refs[0][...]
    for ref in refs[1:]:
        total = total + ref[...].astype(jnp.float32)
    return total


def sum_kernel(*refs):
    refs[-1][...] = add_all(*refs[:-1]).astype(jnp.bfloat16).reshape(refs[-1].shape)


def sum_rows_kernel(own_ref, *refs, line):
    come, outs = refs[:3], refs[3:]
    lines = outs[0].shape[0]
    total = own_ref[line:line + len(outs) * lines]
    for ref in come:
        total = total + ref[...].astype(jnp.float32)
    for n, out in enumerate(outs):
        out[...] = total[n * lines:(n + 1) * lines].astype(out.dtype)


def scatter_shards(mine, come):
    tps, lines, part = mine.shape
    own, *parts = call(after_core_kernel, "after_core", [shape_of((lines, part), jnp.float32)] + [shape_of((lines, part))] * (tps - 1),
                       mine, come)
    return [own] + shard_swaps(parts, True)


def first_products(pieces, masks, side, x_ref, gain_ref, gate_ref, up_ref, gate_out, up_out, square_out):
    width, lines = gate_ref.shape[1], x_ref.shape[0]
    tp = lax.axis_index("tp")
    for mask, piece in zip(masks, pieces):
        at = pl.multiple_of(jnp.bitwise_xor(tp, mask) * LANES, LANES)
        x_ref[:, pl.ds(at, LANES)] = piece[...].reshape(lines, LANES)
    for at in range(2):
        start, stop = at * x_ref.shape[1], min((at + 1) * x_ref.shape[1], width)

        @pl.when(side == at)
        def _(start=start, stop=stop):
            x = x_ref[:, :stop - start].astype(jnp.float32)
            square_out[...] = jnp.broadcast_to(jnp.sum(x * x, axis=-1, keepdims=True), square_out.shape)
            scaled = (x * gain_ref[:, start:stop]).astype(jnp.bfloat16)
            gate_out[...] = dot_last(scaled, gate_ref[:, start:stop])
            up_out[...] = dot_last(scaled, up_ref[:, start:stop])


def near_kernel(gain_ref, gate_ref, up_ref, *refs):
    pieces, (x_ref, gate_out, up_out, square_out) = refs[:-4], refs[-4:]
    first_products(pieces, (0, *shard_masks(True)), lane_of(True), x_ref, gain_ref, gate_ref, up_ref, gate_out, up_out,
                   square_out)


def second_product(act_ref, down_ref, out_ref, number):
    tps, _, part = out_ref.shape

    for at in range(2):
        starts = [((at ^ (t & 1) ^ (t >> 1)) * tps + t) * part for t in range(tps)]

        @pl.when(number == at)
        def _(starts=starts):
            for first, last in ((0, 0), (1, 2), (3, 3)):
                shift = starts[first] % 128
                out = jnp.dot(act_ref[...], down_ref[:, starts[first] - shift:starts[last] + part],
                              preferred_element_type=jnp.float32)
                for n, t in enumerate(range(first, last + 1)):
                    out_ref[t] = out[:, shift + n * part:shift + (n + 1) * part].astype(out_ref.dtype)


def far_kernel(gain_ref, gate_ref, up_ref, down_ref, near_x_ref, near_gate_ref, near_up_ref, near_square_ref, *refs):
    pieces, (other_ref, act_ref, far_x_ref, gate_out, up_out, square_out) = refs[:-6], refs[-6:]
    side, grp = lane_of(True), lax.axis_index("grp")
    masks = shard_masks(True)
    first_products(pieces, (0, masks[0], masks[2], masks[1]), 1 - side, far_x_ref, gain_ref, gate_ref, up_ref, gate_out, up_out,
                   square_out)
    width, half = gate_ref.shape[1], near_x_ref.shape[1]
    spare = jnp.where(side == 1, near_x_ref[:, width - half:], far_x_ref[:, width - half:]).astype(jnp.float32)
    spare_at = lax.broadcasted_iota(jnp.int32, spare.shape, 1)
    weight = jnp.sum(jnp.where((spare_at == 2 * grp) | (spare_at == 2 * grp + 1), spare, 0.0), axis=1, keepdims=True)
    square = (near_square_ref[...] + square_out[...])[:, :1]
    scale = lax.rsqrt(square / width + 1e-05)
    gate_h = (near_gate_ref[...] + gate_out[...]) * scale
    up_h = (near_up_ref[...] + up_out[...]) * scale
    act_ref[...] = ((up_h + 1.0) * gate_h * jax.nn.sigmoid(1.702 * gate_h) * weight).astype(jnp.bfloat16)
    second_product(act_ref, down_ref, other_ref, 1 - lane_of(False))


def last_kernel(act_ref, down_ref, near_x_ref, far_x_ref, mine_ref, middle_ref, row_ref):
    sec, tp = lax.axis_index("sec"), lax.axis_index("tp")
    second_product(act_ref, down_ref, mine_ref, lane_of(False))
    total_rows, part = middle_ref.shape
    near, far = near_x_ref[-total_rows:].astype(jnp.float32), far_x_ref[-total_rows:].astype(jnp.float32)
    first = lane_of(True) == 0
    x = jnp.concatenate([jnp.where(first, near, far), jnp.where(first, far, near)], axis=1)
    for c in range(row_ref.shape[0]):
        row_ref[c] = x[:, c * part:(c + 1) * part]
    middle_ref[...] = row_ref[sec * mine_ref.shape[0] + tp]


def experts(gain, w_gate, w_up, w_down, pieces, part):
    gain, w_gate, w_up = gain.reshape(1, -1), w_gate.swapaxes(0, 1), w_up.swapaxes(0, 1)
    (hidden, width), tps, (groups, total_rows, _) = w_gate.shape, len(pieces), pieces[0].shape
    lines = groups * total_rows
    far_pieces = [swap(piece, "sec", 1) for piece in pieces]
    halves = [shape_of((lines, tps * LANES)), shape_of((lines, hidden), jnp.float32), shape_of((lines, hidden), jnp.float32),
              shape_of((lines, 128), jnp.float32)]
    near = call(near_kernel, "near_columns", halves, gain, w_gate, w_up, *pieces, limit=12, flops=2 * lines * width * hidden)
    other, act, far_x = pl.pallas_call(
        far_kernel,
        name="far_columns",
        out_shape=[shape_of((tps, lines, part)), shape_of((lines, hidden)), halves[0]],
        in_specs=[vmem()] * (8 + len(far_pieces)),
        out_specs=[vmem()] * 3,
        scratch_shapes=[pltpu.VMEM(half.shape, half.dtype) for half in halves[1:]],
        compiler_params=pltpu.CompilerParams(vmem_limit_bytes=16 * MIB),
    )(gain, w_gate, w_up, w_down, *near, *far_pieces)
    come = swap(other, "sec", 1)
    mine, middle = pl.pallas_call(
        last_kernel,
        name="own_columns",
        out_shape=[shape_of((tps, lines, part), jnp.float32), shape_of((total_rows, part), jnp.float32)],
        in_specs=[vmem()] * 4,
        out_specs=[vmem()] * 2,
        scratch_shapes=[pltpu.VMEM((2 * tps, total_rows, part), jnp.float32)],
        compiler_params=pltpu.CompilerParams(vmem_limit_bytes=12 * MIB),
        cost_estimate=pl.CostEstimate(flops=lines * width * hidden, transcendentals=0, bytes_accessed=2 * lines * width),
    )(act, w_down, near[0], far_x)
    return mine, come, middle


def every_expert_body(inputs, attention_gain, w_query, key_value_weight, head_sink_logits, w_output, cache_pairs, lengths,
                      expert_gain, w_gate, w_up, w_down, routes, gate_weights):
    secs, tps, groups = lax.axis_size("sec"), lax.axis_size("tp"), lax.axis_size("grp")
    steps, rows, width = inputs.shape
    flat = inputs.reshape(steps * rows, width)
    other, own_x, mix, held = attention_partial(
        flat, attention_gain, w_query, key_value_weight[:, 0], head_sink_logits, w_output, cache_pairs[:, :, 0], lengths,
        routes.swapaxes(1, 2), gate_weights.swapaxes(1, 2), secs, tps)
    come = swap(other, "sec", 1)
    mine = call(own_projection_kernel, "own_projection", shape_of(other.shape, jnp.float32), mix, held, limit=12,
                flops=mix.size * width)
    middle = call(sum_kernel, "sum", shape_of((steps * rows, LANES)), *scatter_shards(mine, come), own_x)
    stacked = jnp.stack([lane_swap(middle, m, (0, 0), True) for m in (2, 3, 1)] + [middle])
    pieces = [stacked] + shard_swaps([stacked] * (tps - 1), True)
    part = width // (secs * tps)
    mine, come, own_middle = experts(expert_gain, w_gate[0], w_up[0], w_down[0], pieces, part)
    lines = steps * rows
    own, *parts = call(after_core_halves_kernel, "after_core_halves",
                       [shape_of((groups * lines, part), jnp.float32)] + [shape_of((groups // 2 * lines, part))] * 6, mine, come)
    far_come, near_come = shard_swaps(parts[:3], False), shard_swaps(parts[3:], False)
    second, third = call(functools.partial(sum_rows_kernel, line=0), "sum_far_rows", [shape_of((lines, part))] * 2,
                         own, *far_come)
    third, second = swap(third, "grp", 3), swap(second, "grp", 2)
    nearest, own = call(functools.partial(sum_rows_kernel, line=2 * lines), "sum_near_rows",
                        [shape_of((lines, part)), shape_of((lines, part), jnp.float32)], own, *near_come)
    return call(sum_kernel, "combine", shape_of((steps, rows, part)), own, third, second, swap(nearest, "grp", 1), own_middle)


def body(*args):
    sizes = lax.axis_size("sec"), lax.axis_size("tp"), lax.axis_size("grp"), args[9].shape[0]
    if sizes == (2, 4, TOP, 1):
        return every_expert_body(*args)
    return general_body(*args)


def solution(mesh):
    placed = (
        P(None, "grp", None),
        P(),
        P(None, ("sec", "tp")),
        P(None, ("sec", "tp"), None),
        P(("sec", "tp")),
        P(("sec", "tp"), None),
        P("grp", None, ("sec", "tp"), None),
        P("grp"),
        P(),
        P("grp", None, ("sec", "tp")),
        P("grp", None, ("sec", "tp")),
        P("grp", ("sec", "tp"), None),
        P(None, "grp", None),
        P(None, "grp", None),
    )
    return jax.shard_map(
        body, mesh=mesh, in_specs=placed, out_specs=P(None, "grp", ("sec", "tp")), check_vma=False
    )
```

```python
import functools
import math

import jax
import jax.numpy as jnp
import numpy as np
from jax import lax
from jax.experimental import pallas as pl
from jax.experimental.pallas import tpu as pltpu
from jax.sharding import PartitionSpec as P

HEAD_SIZE = 64
TOP = 4


def rms_norm(values, scale_row):
    widened = values.astype(jnp.float32)
    scale_factor = lax.rsqrt(jnp.mean(widened * widened, axis=-1, keepdims=True) + 1e-05)
    return (widened * scale_factor * scale_row).astype(jnp.bfloat16)


def rotate(vectors, position):
    half_size = vectors.shape[-1] // 2
    counter = jnp.arange(half_size).astype(jnp.float32)
    frequency = jnp.power(jnp.float32(150000.0), counter * (-2.0 / vectors.shape[-1]))
    angle_table = position * frequency
    cosine = jnp.cos(angle_table)
    sine_table = jnp.sin(angle_table)
    first_half = vectors[..., :half_size]
    second_half = vectors[..., half_size:]
    return jnp.concatenate(
        [
            first_half * cosine - second_half * sine_table,
            first_half * sine_table + second_half * cosine,
        ],
        axis=-1,
    )


def attend(
    normalized_input,
    w_query,
    key_value_weight,
    head_sink_logits,
    w_output,
    cache_pairs,
    lengths,
    step_index,
    fresh_keys,
    fresh_values,
):
    row_count = normalized_input.shape[0]
    kv_heads = key_value_weight.shape[1]
    query = jnp.dot(normalized_input, w_query, preferred_element_type=jnp.float32).reshape(
        row_count, -1, HEAD_SIZE
    )
    cache_entry_pairs = jnp.dot(
        normalized_input,
        key_value_weight.reshape(key_value_weight.shape[0], -1),
        preferred_element_type=jnp.float32,
    ).reshape(row_count, kv_heads, 2 * HEAD_SIZE)
    position = (lengths + step_index).astype(jnp.float32)[:, None, None]
    rotated_rows = rotate(query, position).astype(jnp.bfloat16)
    fresh_keys = fresh_keys + [
        rotate(cache_entry_pairs[..., :HEAD_SIZE], position).astype(jnp.bfloat16)
    ]
    fresh_values = fresh_values + [cache_entry_pairs[..., HEAD_SIZE:].astype(jnp.bfloat16)]
    grouped_queries = rotated_rows.reshape(row_count, kv_heads, -1, HEAD_SIZE)
    new_keys = jnp.stack(fresh_keys, 1)
    new_values = jnp.stack(fresh_values, 1)
    cached = (
        jnp.einsum(
            "rkgd,rjkd->rkgj",
            grouped_queries,
            cache_pairs[..., :HEAD_SIZE],
            preferred_element_type=jnp.float32,
        )
        * 0.125
    )
    valid = (jnp.arange(cache_pairs.shape[1])[None, :] < lengths[:, None])[:, None, None, :]
    cached = jnp.where(valid, cached, -jnp.inf)
    fresh = (
        jnp.einsum("rkgd,rikd->rkgi", grouped_queries, new_keys, preferred_element_type=jnp.float32)
        * 0.125
    )
    sink_row = head_sink_logits.reshape(kv_heads, -1)[None]
    largest = jnp.maximum(jnp.maximum(jnp.max(cached, axis=-1), jnp.max(fresh, axis=-1)), sink_row)
    cached_exp = jnp.exp(cached - largest[..., None])
    fresh_exp = jnp.exp(fresh - largest[..., None])
    denominator = (
        jnp.sum(cached_exp, axis=-1) + jnp.sum(fresh_exp, axis=-1) + jnp.exp(sink_row - largest)
    )
    cached_probs = (cached_exp / denominator[..., None]).astype(jnp.bfloat16)
    fresh_probs = (fresh_exp / denominator[..., None]).astype(jnp.bfloat16)
    mixed = jnp.einsum(
        "rkgj,rjkd->rkgd",
        cached_probs,
        cache_pairs[..., HEAD_SIZE:],
        preferred_element_type=jnp.float32,
    )
    mixed = mixed + jnp.einsum(
        "rkgi,rikd->rkgd", fresh_probs, new_values, preferred_element_type=jnp.float32
    )
    attention_mix = mixed.reshape(row_count, -1).astype(jnp.bfloat16)
    partial_sum = jnp.dot(attention_mix, w_output, preferred_element_type=jnp.float32)
    return (partial_sum, fresh_keys, fresh_values)


def general_body(
    inputs,
    attention_gain,
    w_query,
    key_value_weight,
    head_sink_logits,
    w_output,
    cache_pairs,
    lengths,
    expert_gain,
    w_gate,
    w_up,
    w_down,
    routes,
    gate_weights,
):
    shards = lax.axis_size(("sec", "tp"))
    shard_index = lax.axis_index(("sec", "tp"))
    experts = lax.axis_size("grp") * w_gate.shape[0]
    group_rows = inputs.shape[1]
    width = inputs.shape[2]
    part_width = width // shards
    chosen = max(TOP, experts // 2)
    capacity = group_rows * TOP // chosen
    slot_total = experts * capacity
    gate_matrix = w_gate[0]
    up_matrix = w_up[0]
    down_matrix = w_down[0]
    fresh_keys = []
    fresh_values = []
    results = []
    for step_index in range(inputs.shape[0]):
        normalized_input = rms_norm(inputs[step_index], attention_gain)
        partial_sum, fresh_keys, fresh_values = attend(
            normalized_input,
            w_query,
            key_value_weight,
            head_sink_logits,
            w_output,
            cache_pairs,
            lengths,
            step_index,
            fresh_keys,
            fresh_values,
        )
        summed = lax.psum(partial_sum[None], ("sec", "tp"))
        middle = (inputs[step_index][None].astype(jnp.float32) + summed).astype(jnp.bfloat16)
        route_rows = routes[step_index][None]
        step_count = middle.shape[0]
        expert_in = rms_norm(middle, expert_gain)
        flat_routes = route_rows.reshape(step_count, group_rows * TOP)
        onehot = (flat_routes[..., None] == jnp.arange(experts)[None, None, :]).astype(jnp.int32)
        earlier = jnp.cumsum(onehot, axis=1) - onehot
        slot_index = jnp.sum(earlier * onehot, axis=-1).reshape(step_count, group_rows, TOP)
        target = route_rows * capacity + slot_index
        placed = target[..., None] == jnp.arange(slot_total)[None, None, None, :]
        dispatch_table = jnp.sum(placed.astype(jnp.int32), axis=2).astype(jnp.bfloat16)
        combine_table = jnp.sum(
            jnp.where(placed, gate_weights[step_index][None][..., None], 0.0), axis=2
        )
        outgoing = jnp.einsum(
            "crm,crd->cmd", dispatch_table, expert_in, preferred_element_type=jnp.float32
        )
        outgoing = outgoing.astype(jnp.bfloat16).reshape(step_count, experts, capacity, width)
        arrived = lax.all_to_all(outgoing, "grp", split_axis=1, concat_axis=1, tiled=True)
        gate_h = jnp.einsum(
            "snpd,dh->snph", arrived, gate_matrix, preferred_element_type=jnp.float32
        )
        up_h = jnp.einsum("snpd,dh->snph", arrived, up_matrix, preferred_element_type=jnp.float32)
        act = ((up_h + 1.0) * gate_h * jax.nn.sigmoid(1.702 * gate_h)).astype(jnp.bfloat16)
        partial_out = jnp.einsum(
            "snph,hd->snpd", act, down_matrix, preferred_element_type=jnp.float32
        )
        reduced = lax.psum_scatter(
            partial_out, ("sec", "tp"), scatter_dimension=3, tiled=True
        ).astype(jnp.bfloat16)
        returned = lax.all_to_all(reduced, "grp", split_axis=1, concat_axis=1, tiled=True)
        returned_rows = returned.reshape(step_count, slot_total, part_width).astype(jnp.float32)
        weighted = jnp.einsum(
            "srm,smd->srd", combine_table, returned_rows, precision=lax.Precision.HIGHEST
        )
        own_middle = lax.dynamic_slice_in_dim(
            middle, shard_index * part_width, part_width, 2
        ).astype(jnp.float32)
        results.append((own_middle + weighted).astype(jnp.bfloat16)[0])
    return jnp.stack(results, 0)


LANES = 384
BASE = 150000.0
MIB = 1 << 20


def shape_of(shape, dtype=jnp.bfloat16):
    return jax.ShapeDtypeStruct(shape, dtype)


def vmem():
    return pl.BlockSpec(memory_space=pltpu.VMEM)


def smem():
    return pl.BlockSpec(memory_space=pltpu.SMEM)


def outside():
    return pl.BlockSpec(memory_space=pltpu.HBM)


def dot_last(left, right):
    return lax.dot_general(left, right, (((1,), (1,)), ((), ())), preferred_element_type=jnp.float32)


def swap(value, axes, mask):
    size = lax.axis_size(axes)
    return lax.ppermute(value, axes, [(i, i ^ mask) for i in range(size)])


def lane_of(by_group):
    tp = lax.axis_index("tp")
    number = lax.axis_index("sec") ^ (tp & 1) ^ (tp >> 1)
    return number ^ (lax.axis_index("grp") & 1) if by_group else number


def lane_swap(value, mask, shard_masks_by_lane, by_group):
    groups, tps = lax.axis_size("grp"), lax.axis_size("tp")

    def parity(group, shard):
        return (shard & 1) ^ (shard >> 1) ^ (group & 1 if by_group else 0)

    pairs = []
    for core in range(2):
        for group in range(groups):
            for shard in range(tps):
                number = core ^ parity(group, shard)
                to_group, to_shard = group ^ mask, shard ^ shard_masks_by_lane[number]
                to_core = number ^ parity(to_group, to_shard)
                pairs.append(((core * groups + group) * tps + shard, (to_core * groups + to_group) * tps + to_shard))
    return lax.ppermute(value, ("sec", "grp", "tp"), pairs)


def shard_swaps(parts, by_group):
    return [lane_swap(part, 0, masks, by_group) for part, masks in zip(parts, ((1, 2), (3, 3), (2, 1)))]


def shard_masks(by_group):
    number = lane_of(by_group)
    return 1 + number, 3, 2 - number


def split_width(width):
    cuts = list(range(0, width, 768)) + [width]
    return list(zip(cuts[:-1], cuts[1:]))


def attention_kernel(lengths_hbm, sinks_hbm, routes_hbm, weights_hbm, gain_hbm, x_hbm, wq_hbm, wkv_hbm, cache_hbm, wo_hbm,
                     other_ref, own_x_ref, mix_ref, wo_ref,
                     lengths_ref, sinks_ref, routes_ref, weights_ref, gain_ref, x_ref, wq_ref, wkv_ref, cache_ref,
                     xs_ref, turned_ref, mixed_ref, sems):
    total_rows, width = x_ref.shape
    rows, slots, pair = cache_ref.shape
    steps = total_rows // rows
    heads = wq_ref.shape[1] // HEAD_SIZE
    per_row = heads * steps
    tps = other_ref.shape[0]
    cuts = split_width(width)
    small = [(lengths_hbm, lengths_ref), (x_hbm, x_ref), (gain_hbm, gain_ref), (routes_hbm, routes_ref), (weights_hbm, weights_ref),
             (sinks_hbm, sinks_ref)]
    small = [pltpu.make_async_copy(source, target, sems.at[n]) for n, (source, target) in enumerate(small)]
    copies = [pltpu.make_async_copy(wkv_hbm, wkv_ref, sems.at[6])]
    for n, (low, high) in enumerate(cuts):
        part = pl.ds(low, high - low)
        copies.append(pltpu.make_async_copy(wq_hbm.at[part], wq_ref.at[part], sems.at[9 + n]))
    copies.append(pltpu.make_async_copy(cache_hbm, cache_ref, sems.at[7]))
    copies.append(pltpu.make_async_copy(wo_hbm, wo_ref, sems.at[8]))
    for copy in small + copies:
        copy.start()
    small[1].wait()
    small[2].wait()
    x = x_ref[...].astype(jnp.float32)
    scale = lax.rsqrt(jnp.mean(x * x, axis=-1, keepdims=True) + 1e-05)
    normed = (x * scale * gain_ref[...].reshape(1, width)).astype(jnp.bfloat16)
    copies[0].wait()
    pairs = jnp.dot(normed, wkv_ref[...], preferred_element_type=jnp.float32)
    query = jnp.zeros((total_rows, wq_ref.shape[1]), jnp.float32)
    for n, (low, high) in enumerate(cuts[:-1]):
        copies[1 + n].wait()
        query = query + jnp.dot(normed[:, low:high], wq_ref[low:high, :], preferred_element_type=jnp.float32)
    for copy in (small[0], *small[3:], copies[len(cuts)]):
        copy.wait()
    query = query + jnp.dot(normed[:, cuts[-1][0]:], wq_ref[cuts[-1][0]:, :], preferred_element_type=jnp.float32)

    lane = lax.broadcasted_iota(jnp.int32, (total_rows, pair), 1)
    line = lax.broadcasted_iota(jnp.int32, (total_rows, pair), 0)
    position = jnp.zeros((total_rows, pair), jnp.int32)
    for r in range(rows):
        for s in range(steps):
            position = jnp.where(line == s * rows + r, lengths_ref[r] + s, position)
    half = HEAD_SIZE // 2
    counter = jnp.bitwise_and(lane, half - 1).astype(jnp.float32)
    frequency = jnp.exp(counter * jnp.float32(-2.0 / HEAD_SIZE * np.log(BASE)))
    angle = position.astype(jnp.float32) * frequency
    cosine, sine = jnp.cos(angle), jnp.sin(angle)
    low_half = jnp.bitwise_and(lane, HEAD_SIZE - 1) < half
    sine = jnp.where(low_half, -sine, sine)

    def turn(two):
        return two * cosine + jnp.where(low_half, pltpu.roll(two, pair - half, 1), pltpu.roll(two, half, 1)) * sine

    spare = xs_ref.shape[1] - width
    spare_at = lax.broadcasted_iota(jnp.int32, (rows, spare), 1)
    corner = lax.broadcasted_iota(jnp.int32, (rows, rows), 0) == lax.broadcasted_iota(jnp.int32, (rows, rows), 1)
    tables = []
    for s in range(steps):
        table = jnp.zeros((rows, spare), jnp.float32)
        for e in range(TOP):
            across = jnp.sum(jnp.where(routes_ref[s] == e, weights_ref[s], 0.0), axis=0, keepdims=True)
            column = jnp.sum(jnp.where(corner, across, 0.0), axis=1, keepdims=True)
            high_part = column.astype(jnp.bfloat16).astype(jnp.float32)
            table = jnp.where(spare_at == 2 * e, high_part, jnp.where(spare_at == 2 * e + 1, column - high_part, table))
        tables.append(table)
    xs_ref[...] = jnp.concatenate([x, jnp.concatenate(tables, axis=0)], axis=1)
    own = (lane_of(True) * tps + lax.axis_index("tp")) * LANES
    own_x_ref[...] = xs_ref[:, pl.ds(pl.multiple_of(own, LANES), LANES)]
    is_key = lane < HEAD_SIZE
    fresh = jnp.where(is_key, turn(pairs), pairs).astype(jnp.bfloat16)
    for m in range(heads // 2):
        two = turn(query[:, m * pair:(m + 1) * pair])
        for odd in range(2):
            one = two if odd == 0 else pltpu.roll(two, HEAD_SIZE, 1)
            one = jnp.where(is_key, one, 0.0)
            for s in range(steps):
                slot = (2 * m + odd) * steps + s
                turned_ref[pl.ds(slot, rows, stride=per_row), :] = one[s * rows:(s + 1) * rows]
    turned = turned_ref[...].astype(jnp.bfloat16)

    copies[-2].wait()
    place = lax.broadcasted_iota(jnp.int32, (per_row, slots), 1)
    scores = []
    for r in range(rows):
        score = dot_last(turned[r * per_row:(r + 1) * per_row], cache_ref[r]) * 0.125
        scores.append(jnp.where(place < lengths_ref[r], score, -jnp.inf))
    cached = jnp.concatenate(scores, axis=0)
    row_at = lax.broadcasted_iota(jnp.int32, (rows * per_row, total_rows), 0)
    fresh_at = lax.broadcasted_iota(jnp.int32, (rows * per_row, total_rows), 1)
    seen = (row_at // per_row == fresh_at % rows) & (fresh_at // rows <= row_at % steps)
    new = jnp.where(seen, dot_last(turned, fresh) * 0.125, -jnp.inf)
    head_at = lax.broadcasted_iota(jnp.int32, (rows * per_row, 1), 0) % per_row // steps
    sink = jnp.zeros((rows * per_row, 1), jnp.float32)
    for h in range(heads):
        sink = jnp.where(head_at == h, sinks_ref[h], sink)
    largest = jnp.maximum(jnp.maximum(jnp.max(cached, axis=-1, keepdims=True), jnp.max(new, axis=-1, keepdims=True)), sink)
    cached = jnp.exp(cached - largest)
    new = jnp.exp(new - largest)
    total = jnp.sum(cached, axis=-1, keepdims=True) + jnp.sum(new, axis=-1, keepdims=True) + jnp.exp(sink - largest)
    share = 1.0 / total
    cached = (cached * share).astype(jnp.bfloat16)
    new = (new * share).astype(jnp.bfloat16)
    mixed = []
    for r in range(rows):
        mixed.append(jnp.dot(cached[r * per_row:(r + 1) * per_row], cache_ref[r], preferred_element_type=jnp.float32))
    mixed_ref[...] = jnp.concatenate(mixed, axis=0) + jnp.dot(new, fresh, preferred_element_type=jnp.float32)

    def head(h):
        return jnp.concatenate([mixed_ref[pl.ds(h * steps + s, rows, stride=per_row), :] for s in range(steps)], axis=0)

    mix_ref[...] = jnp.concatenate(
        [jnp.where(is_key, pltpu.roll(head(2 * m), HEAD_SIZE, 1), head(2 * m + 1)) for m in range(heads // 2)], axis=1
    ).astype(jnp.bfloat16)
    copies[-1].wait()
    project(mix_ref, wo_ref, other_ref, 1 - lane_of(True))


def project(mix_ref, wo_ref, out_ref, side):
    width, (tps, total_rows, _) = wo_ref.shape[0], out_ref.shape
    for at in range(2):
        start, stop = at * tps * LANES, min((at + 1) * tps * LANES, width)

        @pl.when(side == at)
        def _(start=start, stop=stop):
            partial = dot_last(mix_ref[...], wo_ref[start:stop, :])
            for t in range(tps):
                low, high = t * LANES, min((t + 1) * LANES, stop - start)
                piece = partial[:, low:high]
                if high - low < LANES:
                    piece = jnp.concatenate([piece, jnp.zeros((total_rows, LANES - (high - low)), jnp.float32)], axis=1)
                out_ref[t] = piece.astype(out_ref.dtype)


def own_projection_kernel(mix_ref, wo_ref, mine_ref):
    project(mix_ref, wo_ref, mine_ref, lane_of(True))


def attention_partial(flat, gain, w_query, key_value, sinks, w_output, cache, lengths, routes, weights, secs, tps):
    total_rows, width = flat.shape
    rows, slots, pair = cache.shape
    per_row = w_query.shape[1] // HEAD_SIZE * (total_rows // rows)
    shards = secs * tps
    operands = (lengths, sinks, routes, weights, gain, flat, w_query, key_value, cache, w_output.swapaxes(0, 1))
    return pl.pallas_call(
        attention_kernel,
        name="attention",
        out_shape=[shape_of((tps, total_rows, LANES)), shape_of((total_rows, LANES), jnp.float32),
                   shape_of((total_rows, w_output.shape[0])), shape_of((width, w_output.shape[0]))],
        in_specs=[outside()] * len(operands),
        out_specs=[vmem()] * 4,
        scratch_shapes=[
            pltpu.SMEM(lengths.shape, jnp.int32),
            pltpu.SMEM(sinks.shape, jnp.float32),
            pltpu.VMEM(routes.shape, jnp.int32),
            pltpu.VMEM(weights.shape, jnp.float32),
            pltpu.VMEM(gain.shape, jnp.float32),
            pltpu.VMEM((total_rows, width), jnp.bfloat16),
            pltpu.VMEM(w_query.shape, jnp.bfloat16),
            pltpu.VMEM(key_value.shape, jnp.bfloat16),
            pltpu.VMEM(cache.shape, jnp.bfloat16),
            pltpu.VMEM((total_rows, shards * LANES), jnp.float32),
            pltpu.VMEM((rows * per_row, pair), jnp.float32),
            pltpu.VMEM((rows * per_row, pair), jnp.float32),
            pltpu.SemaphoreType.DMA((9 + len(split_width(width)),)),
        ],
        compiler_params=pltpu.CompilerParams(vmem_limit_bytes=24 * MIB),
    )(*[pltpu.with_memory_space_constraint(operand, pltpu.HBM) for operand in operands])


def call(kernel, name, outs, *operands, limit=4, flops=0):
    single = not isinstance(outs, list)
    held = [*operands, *([outs] if single else outs)]
    return pl.pallas_call(
        kernel,
        name=name,
        out_shape=outs,
        in_specs=[vmem()] * len(operands),
        out_specs=vmem() if single else [vmem()] * len(outs),
        compiler_params=pltpu.CompilerParams(vmem_limit_bytes=limit * MIB),
        cost_estimate=pl.CostEstimate(flops=flops, transcendentals=0,
                                      bytes_accessed=sum(math.prod(a.shape) * a.dtype.itemsize for a in held)),
    )(*operands)


def after_core_kernel(mine_ref, come_ref, own_ref, *send_refs):
    tp = lax.axis_index("tp")
    own_ref[...] = mine_ref[tp] + come_ref[tp].astype(jnp.float32)
    for mask, ref in zip(shard_masks(True), send_refs):
        to = jnp.bitwise_xor(tp, mask)
        ref[...] = (mine_ref[to] + come_ref[to].astype(jnp.float32)).astype(jnp.bfloat16)


def after_core_halves_kernel(mine_ref, come_ref, own_ref, *send_refs):
    tp, half = lax.axis_index("tp"), mine_ref.shape[1] // 2
    own_ref[...] = mine_ref[tp] + come_ref[tp].astype(jnp.float32)
    for mask, first, second in zip(shard_masks(False), send_refs[:3], send_refs[3:]):
        to = jnp.bitwise_xor(tp, mask)
        part = (mine_ref[to] + come_ref[to].astype(jnp.float32)).astype(jnp.bfloat16)
        first[...] = part[:half]
        second[...] = part[half:]


def add_all(*refs):
    total = refs[0][...]
    for ref in refs[1:]:
        total = total + ref[...].astype(jnp.float32)
    return total


def sum_kernel(*refs):
    refs[-1][...] = add_all(*refs[:-1]).astype(jnp.bfloat16).reshape(refs[-1].shape)


def sum_rows_kernel(own_ref, *refs, line):
    come, outs = refs[:3], refs[3:]
    lines = outs[0].shape[0]
    total = own_ref[line:line + len(outs) * lines]
    for ref in come:
        total = total + ref[...].astype(jnp.float32)
    for n, out in enumerate(outs):
        out[...] = total[n * lines:(n + 1) * lines].astype(out.dtype)


def scatter_shards(mine, come):
    tps, lines, part = mine.shape
    own, *parts = call(after_core_kernel, "after_core", [shape_of((lines, part), jnp.float32)] + [shape_of((lines, part))] * (tps - 1),
                       mine, come)
    return [own] + shard_swaps(parts, True)


def first_products(pieces, masks, side, x_ref, gain_ref, gate_ref, up_ref, gate_out, up_out, square_out):
    width, lines = gate_ref.shape[1], x_ref.shape[0]
    tp = lax.axis_index("tp")
    for mask, piece in zip(masks, pieces):
        at = pl.multiple_of(jnp.bitwise_xor(tp, mask) * LANES, LANES)
        x_ref[:, pl.ds(at, LANES)] = piece[...].reshape(lines, LANES)
    for at in range(2):
        start, stop = at * x_ref.shape[1], min((at + 1) * x_ref.shape[1], width)

        @pl.when(side == at)
        def _(start=start, stop=stop):
            x = x_ref[:, :stop - start].astype(jnp.float32)
            square_out[...] = jnp.broadcast_to(jnp.sum(x * x, axis=-1, keepdims=True), square_out.shape)
            scaled = (x * gain_ref[:, start:stop]).astype(jnp.bfloat16)
            gate_out[...] = dot_last(scaled, gate_ref[:, start:stop])
            up_out[...] = dot_last(scaled, up_ref[:, start:stop])


def near_kernel(gain_ref, gate_ref, up_ref, *refs):
    pieces, (x_ref, gate_out, up_out, square_out) = refs[:-4], refs[-4:]
    first_products(pieces, (0, *shard_masks(True)), lane_of(True), x_ref, gain_ref, gate_ref, up_ref, gate_out, up_out,
                   square_out)


def second_product(act_ref, down_ref, out_ref, number):
    tps, _, part = out_ref.shape

    for at in range(2):
        starts = [((at ^ (t & 1) ^ (t >> 1)) * tps + t) * part for t in range(tps)]

        @pl.when(number == at)
        def _(starts=starts):
            for first, last in ((0, 0), (1, 2), (3, 3)):
                shift = starts[first] % 128
                out = jnp.dot(act_ref[...], down_ref[:, starts[first] - shift:starts[last] + part],
                              preferred_element_type=jnp.float32)
                for n, t in enumerate(range(first, last + 1)):
                    out_ref[t] = out[:, shift + n * part:shift + (n + 1) * part].astype(out_ref.dtype)


def far_kernel(gain_ref, gate_ref, up_ref, down_ref, near_x_ref, near_gate_ref, near_up_ref, near_square_ref, *refs):
    pieces, (other_ref, act_ref, far_x_ref, gate_out, up_out, square_out) = refs[:-6], refs[-6:]
    side, grp = lane_of(True), lax.axis_index("grp")
    masks = shard_masks(True)
    first_products(pieces, (0, masks[2], masks[1], masks[0]), 1 - side, far_x_ref, gain_ref, gate_ref, up_ref, gate_out, up_out,
                   square_out)
    width, half = gate_ref.shape[1], near_x_ref.shape[1]
    spare = jnp.where(side == 1, near_x_ref[:, width - half:], far_x_ref[:, width - half:]).astype(jnp.float32)
    spare_at = lax.broadcasted_iota(jnp.int32, spare.shape, 1)
    weight = jnp.sum(jnp.where((spare_at == 2 * grp) | (spare_at == 2 * grp + 1), spare, 0.0), axis=1, keepdims=True)
    square = (near_square_ref[...] + square_out[...])[:, :1]
    scale = lax.rsqrt(square / width + 1e-05)
    gate_h = (near_gate_ref[...] + gate_out[...]) * scale
    up_h = (near_up_ref[...] + up_out[...]) * scale
    act_ref[...] = ((up_h + 1.0) * gate_h * jax.nn.sigmoid(1.702 * gate_h) * weight).astype(jnp.bfloat16)
    second_product(act_ref, down_ref, other_ref, 1 - lane_of(False))


def last_kernel(act_ref, down_ref, near_x_ref, far_x_ref, mine_ref, middle_ref, row_ref):
    sec, tp = lax.axis_index("sec"), lax.axis_index("tp")
    second_product(act_ref, down_ref, mine_ref, lane_of(False))
    total_rows, part = middle_ref.shape
    near, far = near_x_ref[-total_rows:].astype(jnp.float32), far_x_ref[-total_rows:].astype(jnp.float32)
    first = lane_of(True) == 0
    x = jnp.concatenate([jnp.where(first, near, far), jnp.where(first, far, near)], axis=1)
    for c in range(row_ref.shape[0]):
        row_ref[c] = x[:, c * part:(c + 1) * part]
    middle_ref[...] = row_ref[sec * mine_ref.shape[0] + tp]


def experts(gain, w_gate, w_up, w_down, pieces, part):
    gain, w_gate, w_up = gain.reshape(1, -1), w_gate.swapaxes(0, 1), w_up.swapaxes(0, 1)
    (hidden, width), tps, (groups, total_rows, _) = w_gate.shape, len(pieces), pieces[0].shape
    lines = groups * total_rows
    far_pieces = [swap(piece, "sec", 1) for piece in pieces]
    halves = [shape_of((lines, tps * LANES)), shape_of((lines, hidden), jnp.float32), shape_of((lines, hidden), jnp.float32),
              shape_of((lines, 128), jnp.float32)]
    near = call(near_kernel, "near_columns", halves, gain, w_gate, w_up, *pieces, limit=12, flops=2 * lines * width * hidden)
    other, act, far_x = pl.pallas_call(
        far_kernel,
        name="far_columns",
        out_shape=[shape_of((tps, lines, part)), shape_of((lines, hidden)), halves[0]],
        in_specs=[vmem()] * (8 + len(far_pieces)),
        out_specs=[vmem()] * 3,
        scratch_shapes=[pltpu.VMEM(half.shape, half.dtype) for half in halves[1:]],
        compiler_params=pltpu.CompilerParams(vmem_limit_bytes=16 * MIB),
    )(gain, w_gate, w_up, w_down, *near, *far_pieces)
    come = swap(other, "sec", 1)
    mine, middle = pl.pallas_call(
        last_kernel,
        name="own_columns",
        out_shape=[shape_of((tps, lines, part), jnp.float32), shape_of((total_rows, part), jnp.float32)],
        in_specs=[vmem()] * 4,
        out_specs=[vmem()] * 2,
        scratch_shapes=[pltpu.VMEM((2 * tps, total_rows, part), jnp.float32)],
        compiler_params=pltpu.CompilerParams(vmem_limit_bytes=12 * MIB),
        cost_estimate=pl.CostEstimate(flops=lines * width * hidden, transcendentals=0, bytes_accessed=2 * lines * width),
    )(act, w_down, near[0], far_x)
    return mine, come, middle


def every_expert_body(inputs, attention_gain, w_query, key_value_weight, head_sink_logits, w_output, cache_pairs, lengths,
                      expert_gain, w_gate, w_up, w_down, routes, gate_weights):
    secs, tps, groups = lax.axis_size("sec"), lax.axis_size("tp"), lax.axis_size("grp")
    steps, rows, width = inputs.shape
    flat = inputs.reshape(steps * rows, width)
    other, own_x, mix, held = attention_partial(
        flat, attention_gain, w_query, key_value_weight[:, 0], head_sink_logits, w_output, cache_pairs[:, :, 0], lengths,
        routes.swapaxes(1, 2), gate_weights.swapaxes(1, 2), secs, tps)
    come = swap(other, "sec", 1)
    mine = call(own_projection_kernel, "own_projection", shape_of(other.shape, jnp.float32), mix, held, limit=12,
                flops=mix.size * width)
    middle = call(sum_kernel, "sum", shape_of((steps * rows, LANES)), *scatter_shards(mine, come), own_x)
    stacked = jnp.stack([lane_swap(middle, m, (0, 0), True) for m in reversed(range(1, groups))] + [middle])
    pieces = [stacked] + shard_swaps([stacked] * (tps - 1), True)
    part = width // (secs * tps)
    mine, come, own_middle = experts(expert_gain, w_gate[0], w_up[0], w_down[0], pieces, part)
    lines = steps * rows
    own, *parts = call(after_core_halves_kernel, "after_core_halves",
                       [shape_of((groups * lines, part), jnp.float32)] + [shape_of((groups // 2 * lines, part))] * 6, mine, come)
    far_come, near_come = shard_swaps(parts[:3], False), shard_swaps(parts[3:], False)
    third, second = call(functools.partial(sum_rows_kernel, line=0), "sum_far_rows", [shape_of((lines, part))] * 2,
                         own, *far_come)
    third, second = swap(third, "grp", 3), swap(second, "grp", 2)
    nearest, own = call(functools.partial(sum_rows_kernel, line=2 * lines), "sum_near_rows",
                        [shape_of((lines, part)), shape_of((lines, part), jnp.float32)], own, *near_come)
    return call(sum_kernel, "combine", shape_of((steps, rows, part)), own, third, second, swap(nearest, "grp", 1), own_middle)


def body(*args):
    sizes = lax.axis_size("sec"), lax.axis_size("tp"), lax.axis_size("grp"), args[9].shape[0]
    if sizes == (2, 4, TOP, 1):
        return every_expert_body(*args)
    return general_body(*args)


def solution(mesh):
    placed = (
        P(None, "grp", None),
        P(),
        P(None, ("sec", "tp")),
        P(None, ("sec", "tp"), None),
        P(("sec", "tp")),
        P(("sec", "tp"), None),
        P("grp", None, ("sec", "tp"), None),
        P("grp"),
        P(),
        P("grp", None, ("sec", "tp")),
        P("grp", None, ("sec", "tp")),
        P("grp", ("sec", "tp"), None),
        P(None, "grp", None),
        P(None, "grp", None),
    )
    return jax.shard_map(
        body, mesh=mesh, in_specs=placed, out_specs=P(None, "grp", ("sec", "tp")), check_vma=False
    )
```

```python
import functools
import math

import jax
import jax.numpy as jnp
import numpy as np
from jax import lax
from jax.experimental import pallas as pl
from jax.experimental.pallas import tpu as pltpu
from jax.sharding import PartitionSpec as P

HEAD_SIZE = 64
TOP = 4


def rms_norm(values, scale_row):
    widened = values.astype(jnp.float32)
    scale_factor = lax.rsqrt(jnp.mean(widened * widened, axis=-1, keepdims=True) + 1e-05)
    return (widened * scale_factor * scale_row).astype(jnp.bfloat16)


def rotate(vectors, position):
    half_size = vectors.shape[-1] // 2
    counter = jnp.arange(half_size).astype(jnp.float32)
    frequency = jnp.power(jnp.float32(150000.0), counter * (-2.0 / vectors.shape[-1]))
    angle_table = position * frequency
    cosine = jnp.cos(angle_table)
    sine_table = jnp.sin(angle_table)
    first_half = vectors[..., :half_size]
    second_half = vectors[..., half_size:]
    return jnp.concatenate(
        [
            first_half * cosine - second_half * sine_table,
            first_half * sine_table + second_half * cosine,
        ],
        axis=-1,
    )


def attend(
    normalized_input,
    w_query,
    key_value_weight,
    head_sink_logits,
    w_output,
    cache_pairs,
    lengths,
    step_index,
    fresh_keys,
    fresh_values,
):
    row_count = normalized_input.shape[0]
    kv_heads = key_value_weight.shape[1]
    query = jnp.dot(normalized_input, w_query, preferred_element_type=jnp.float32).reshape(
        row_count, -1, HEAD_SIZE
    )
    cache_entry_pairs = jnp.dot(
        normalized_input,
        key_value_weight.reshape(key_value_weight.shape[0], -1),
        preferred_element_type=jnp.float32,
    ).reshape(row_count, kv_heads, 2 * HEAD_SIZE)
    position = (lengths + step_index).astype(jnp.float32)[:, None, None]
    rotated_rows = rotate(query, position).astype(jnp.bfloat16)
    fresh_keys = fresh_keys + [
        rotate(cache_entry_pairs[..., :HEAD_SIZE], position).astype(jnp.bfloat16)
    ]
    fresh_values = fresh_values + [cache_entry_pairs[..., HEAD_SIZE:].astype(jnp.bfloat16)]
    grouped_queries = rotated_rows.reshape(row_count, kv_heads, -1, HEAD_SIZE)
    new_keys = jnp.stack(fresh_keys, 1)
    new_values = jnp.stack(fresh_values, 1)
    cached = (
        jnp.einsum(
            "rkgd,rjkd->rkgj",
            grouped_queries,
            cache_pairs[..., :HEAD_SIZE],
            preferred_element_type=jnp.float32,
        )
        * 0.125
    )
    valid = (jnp.arange(cache_pairs.shape[1])[None, :] < lengths[:, None])[:, None, None, :]
    cached = jnp.where(valid, cached, -jnp.inf)
    fresh = (
        jnp.einsum("rkgd,rikd->rkgi", grouped_queries, new_keys, preferred_element_type=jnp.float32)
        * 0.125
    )
    sink_row = head_sink_logits.reshape(kv_heads, -1)[None]
    largest = jnp.maximum(jnp.maximum(jnp.max(cached, axis=-1), jnp.max(fresh, axis=-1)), sink_row)
    cached_exp = jnp.exp(cached - largest[..., None])
    fresh_exp = jnp.exp(fresh - largest[..., None])
    denominator = (
        jnp.sum(cached_exp, axis=-1) + jnp.sum(fresh_exp, axis=-1) + jnp.exp(sink_row - largest)
    )
    cached_probs = (cached_exp / denominator[..., None]).astype(jnp.bfloat16)
    fresh_probs = (fresh_exp / denominator[..., None]).astype(jnp.bfloat16)
    mixed = jnp.einsum(
        "rkgj,rjkd->rkgd",
        cached_probs,
        cache_pairs[..., HEAD_SIZE:],
        preferred_element_type=jnp.float32,
    )
    mixed = mixed + jnp.einsum(
        "rkgi,rikd->rkgd", fresh_probs, new_values, preferred_element_type=jnp.float32
    )
    attention_mix = mixed.reshape(row_count, -1).astype(jnp.bfloat16)
    partial_sum = jnp.dot(attention_mix, w_output, preferred_element_type=jnp.float32)
    return (partial_sum, fresh_keys, fresh_values)


def general_body(
    inputs,
    attention_gain,
    w_query,
    key_value_weight,
    head_sink_logits,
    w_output,
    cache_pairs,
    lengths,
    expert_gain,
    w_gate,
    w_up,
    w_down,
    routes,
    gate_weights,
):
    shards = lax.axis_size(("sec", "tp"))
    shard_index = lax.axis_index(("sec", "tp"))
    experts = lax.axis_size("grp") * w_gate.shape[0]
    group_rows = inputs.shape[1]
    width = inputs.shape[2]
    part_width = width // shards
    chosen = max(TOP, experts // 2)
    capacity = group_rows * TOP // chosen
    slot_total = experts * capacity
    gate_matrix = w_gate[0]
    up_matrix = w_up[0]
    down_matrix = w_down[0]
    fresh_keys = []
    fresh_values = []
    results = []
    for step_index in range(inputs.shape[0]):
        normalized_input = rms_norm(inputs[step_index], attention_gain)
        partial_sum, fresh_keys, fresh_values = attend(
            normalized_input,
            w_query,
            key_value_weight,
            head_sink_logits,
            w_output,
            cache_pairs,
            lengths,
            step_index,
            fresh_keys,
            fresh_values,
        )
        summed = lax.psum(partial_sum[None], ("sec", "tp"))
        middle = (inputs[step_index][None].astype(jnp.float32) + summed).astype(jnp.bfloat16)
        route_rows = routes[step_index][None]
        step_count = middle.shape[0]
        expert_in = rms_norm(middle, expert_gain)
        flat_routes = route_rows.reshape(step_count, group_rows * TOP)
        onehot = (flat_routes[..., None] == jnp.arange(experts)[None, None, :]).astype(jnp.int32)
        earlier = jnp.cumsum(onehot, axis=1) - onehot
        slot_index = jnp.sum(earlier * onehot, axis=-1).reshape(step_count, group_rows, TOP)
        target = route_rows * capacity + slot_index
        placed = target[..., None] == jnp.arange(slot_total)[None, None, None, :]
        dispatch_table = jnp.sum(placed.astype(jnp.int32), axis=2).astype(jnp.bfloat16)
        combine_table = jnp.sum(
            jnp.where(placed, gate_weights[step_index][None][..., None], 0.0), axis=2
        )
        outgoing = jnp.einsum(
            "crm,crd->cmd", dispatch_table, expert_in, preferred_element_type=jnp.float32
        )
        outgoing = outgoing.astype(jnp.bfloat16).reshape(step_count, experts, capacity, width)
        arrived = lax.all_to_all(outgoing, "grp", split_axis=1, concat_axis=1, tiled=True)
        gate_h = jnp.einsum(
            "snpd,dh->snph", arrived, gate_matrix, preferred_element_type=jnp.float32
        )
        up_h = jnp.einsum("snpd,dh->snph", arrived, up_matrix, preferred_element_type=jnp.float32)
        act = ((up_h + 1.0) * gate_h * jax.nn.sigmoid(1.702 * gate_h)).astype(jnp.bfloat16)
        partial_out = jnp.einsum(
            "snph,hd->snpd", act, down_matrix, preferred_element_type=jnp.float32
        )
        reduced = lax.psum_scatter(
            partial_out, ("sec", "tp"), scatter_dimension=3, tiled=True
        ).astype(jnp.bfloat16)
        returned = lax.all_to_all(reduced, "grp", split_axis=1, concat_axis=1, tiled=True)
        returned_rows = returned.reshape(step_count, slot_total, part_width).astype(jnp.float32)
        weighted = jnp.einsum(
            "srm,smd->srd", combine_table, returned_rows, precision=lax.Precision.HIGHEST
        )
        own_middle = lax.dynamic_slice_in_dim(
            middle, shard_index * part_width, part_width, 2
        ).astype(jnp.float32)
        results.append((own_middle + weighted).astype(jnp.bfloat16)[0])
    return jnp.stack(results, 0)


LANES = 384
BASE = 150000.0
MIB = 1 << 20


def shape_of(shape, dtype=jnp.bfloat16):
    return jax.ShapeDtypeStruct(shape, dtype)


def vmem():
    return pl.BlockSpec(memory_space=pltpu.VMEM)


def smem():
    return pl.BlockSpec(memory_space=pltpu.SMEM)


def outside():
    return pl.BlockSpec(memory_space=pltpu.HBM)


def dot_last(left, right):
    return lax.dot_general(left, right, (((1,), (1,)), ((), ())), preferred_element_type=jnp.float32)


def swap(value, axes, mask):
    size = lax.axis_size(axes)
    return lax.ppermute(value, axes, [(i, i ^ mask) for i in range(size)])


def lane_of(by_group):
    tp = lax.axis_index("tp")
    number = lax.axis_index("sec") ^ (tp & 1) ^ (tp >> 1)
    return number ^ (lax.axis_index("grp") & 1) if by_group else number


def lane_swap(value, mask, shard_masks_by_lane, by_group):
    groups, tps = lax.axis_size("grp"), lax.axis_size("tp")

    def parity(group, shard):
        return (shard & 1) ^ (shard >> 1) ^ (group & 1 if by_group else 0)

    pairs = []
    for core in range(2):
        for group in range(groups):
            for shard in range(tps):
                number = core ^ parity(group, shard)
                to_group, to_shard = group ^ mask, shard ^ shard_masks_by_lane[number]
                to_core = number ^ parity(to_group, to_shard)
                pairs.append(((core * groups + group) * tps + shard, (to_core * groups + to_group) * tps + to_shard))
    return lax.ppermute(value, ("sec", "grp", "tp"), pairs)


def shard_swaps(parts, by_group):
    return [lane_swap(part, 0, masks, by_group) for part, masks in zip(parts, ((3, 3), (1, 2), (2, 1)))]


def shard_masks(by_group):
    number = lane_of(by_group)
    return 3, 1 + number, 2 - number


def split_width(width):
    cuts = list(range(0, width, 768)) + [width]
    return list(zip(cuts[:-1], cuts[1:]))


def attention_kernel(lengths_hbm, sinks_hbm, routes_hbm, weights_hbm, gain_hbm, x_hbm, wq_hbm, wkv_hbm, cache_hbm, wo_hbm,
                     other_ref, own_x_ref, mix_ref, wo_ref,
                     lengths_ref, sinks_ref, routes_ref, weights_ref, gain_ref, x_ref, wq_ref, wkv_ref, cache_ref,
                     xs_ref, turned_ref, mixed_ref, sems):
    total_rows, width = x_ref.shape
    rows, slots, pair = cache_ref.shape
    steps = total_rows // rows
    heads = wq_ref.shape[1] // HEAD_SIZE
    per_row = heads * steps
    tps = other_ref.shape[0]
    cuts = split_width(width)
    small = [(lengths_hbm, lengths_ref), (x_hbm, x_ref), (gain_hbm, gain_ref), (routes_hbm, routes_ref), (weights_hbm, weights_ref),
             (sinks_hbm, sinks_ref)]
    small = [pltpu.make_async_copy(source, target, sems.at[n]) for n, (source, target) in enumerate(small)]
    copies = [pltpu.make_async_copy(wkv_hbm, wkv_ref, sems.at[6])]
    for n, (low, high) in enumerate(cuts):
        part = pl.ds(low, high - low)
        copies.append(pltpu.make_async_copy(wq_hbm.at[part], wq_ref.at[part], sems.at[9 + n]))
    copies.append(pltpu.make_async_copy(cache_hbm, cache_ref, sems.at[7]))
    copies.append(pltpu.make_async_copy(wo_hbm, wo_ref, sems.at[8]))
    for copy in small + copies:
        copy.start()
    small[1].wait()
    small[2].wait()
    x = x_ref[...].astype(jnp.float32)
    scale = lax.rsqrt(jnp.mean(x * x, axis=-1, keepdims=True) + 1e-05)
    normed = (x * scale * gain_ref[...].reshape(1, width)).astype(jnp.bfloat16)
    copies[0].wait()
    pairs = jnp.dot(normed, wkv_ref[...], preferred_element_type=jnp.float32)
    query = jnp.zeros((total_rows, wq_ref.shape[1]), jnp.float32)
    for n, (low, high) in enumerate(cuts[:-1]):
        copies[1 + n].wait()
        query = query + jnp.dot(normed[:, low:high], wq_ref[low:high, :], preferred_element_type=jnp.float32)
    for copy in (small[0], *small[3:], copies[len(cuts)]):
        copy.wait()
    query = query + jnp.dot(normed[:, cuts[-1][0]:], wq_ref[cuts[-1][0]:, :], preferred_element_type=jnp.float32)

    lane = lax.broadcasted_iota(jnp.int32, (total_rows, pair), 1)
    line = lax.broadcasted_iota(jnp.int32, (total_rows, pair), 0)
    position = jnp.zeros((total_rows, pair), jnp.int32)
    for r in range(rows):
        for s in range(steps):
            position = jnp.where(line == s * rows + r, lengths_ref[r] + s, position)
    half = HEAD_SIZE // 2
    counter = jnp.bitwise_and(lane, half - 1).astype(jnp.float32)
    frequency = jnp.exp(counter * jnp.float32(-2.0 / HEAD_SIZE * np.log(BASE)))
    angle = position.astype(jnp.float32) * frequency
    cosine, sine = jnp.cos(angle), jnp.sin(angle)
    low_half = jnp.bitwise_and(lane, HEAD_SIZE - 1) < half
    sine = jnp.where(low_half, -sine, sine)

    def turn(two):
        return two * cosine + jnp.where(low_half, pltpu.roll(two, pair - half, 1), pltpu.roll(two, half, 1)) * sine

    spare = xs_ref.shape[1] - width
    spare_at = lax.broadcasted_iota(jnp.int32, (rows, spare), 1)
    corner = lax.broadcasted_iota(jnp.int32, (rows, rows), 0) == lax.broadcasted_iota(jnp.int32, (rows, rows), 1)
    tables = []
    for s in range(steps):
        table = jnp.zeros((rows, spare), jnp.float32)
        for e in range(TOP):
            across = jnp.sum(jnp.where(routes_ref[s] == e, weights_ref[s], 0.0), axis=0, keepdims=True)
            column = jnp.sum(jnp.where(corner, across, 0.0), axis=1, keepdims=True)
            high_part = column.astype(jnp.bfloat16).astype(jnp.float32)
            table = jnp.where(spare_at == 2 * e, high_part, jnp.where(spare_at == 2 * e + 1, column - high_part, table))
        tables.append(table)
    xs_ref[...] = jnp.concatenate([x, jnp.concatenate(tables, axis=0)], axis=1)
    own = (lane_of(True) * tps + lax.axis_index("tp")) * LANES
    own_x_ref[...] = xs_ref[:, pl.ds(pl.multiple_of(own, LANES), LANES)]
    is_key = lane < HEAD_SIZE
    fresh = jnp.where(is_key, turn(pairs), pairs).astype(jnp.bfloat16)
    for m in range(heads // 2):
        two = turn(query[:, m * pair:(m + 1) * pair])
        for odd in range(2):
            one = two if odd == 0 else pltpu.roll(two, HEAD_SIZE, 1)
            one = jnp.where(is_key, one, 0.0)
            for s in range(steps):
                slot = (2 * m + odd) * steps + s
                turned_ref[pl.ds(slot, rows, stride=per_row), :] = one[s * rows:(s + 1) * rows]
    turned = turned_ref[...].astype(jnp.bfloat16)

    copies[-2].wait()
    place = lax.broadcasted_iota(jnp.int32, (per_row, slots), 1)
    scores = []
    for r in range(rows):
        score = dot_last(turned[r * per_row:(r + 1) * per_row], cache_ref[r]) * 0.125
        scores.append(jnp.where(place < lengths_ref[r], score, -jnp.inf))
    cached = jnp.concatenate(scores, axis=0)
    row_at = lax.broadcasted_iota(jnp.int32, (rows * per_row, total_rows), 0)
    fresh_at = lax.broadcasted_iota(jnp.int32, (rows * per_row, total_rows), 1)
    seen = (row_at // per_row == fresh_at % rows) & (fresh_at // rows <= row_at % steps)
    new = jnp.where(seen, dot_last(turned, fresh) * 0.125, -jnp.inf)
    head_at = lax.broadcasted_iota(jnp.int32, (rows * per_row, 1), 0) % per_row // steps
    sink = jnp.zeros((rows * per_row, 1), jnp.float32)
    for h in range(heads):
        sink = jnp.where(head_at == h, sinks_ref[h], sink)
    largest = jnp.maximum(jnp.maximum(jnp.max(cached, axis=-1, keepdims=True), jnp.max(new, axis=-1, keepdims=True)), sink)
    cached = jnp.exp(cached - largest)
    new = jnp.exp(new - largest)
    total = jnp.sum(cached, axis=-1, keepdims=True) + jnp.sum(new, axis=-1, keepdims=True) + jnp.exp(sink - largest)
    share = 1.0 / total
    cached = (cached * share).astype(jnp.bfloat16)
    new = (new * share).astype(jnp.bfloat16)
    mixed = []
    for r in range(rows):
        mixed.append(jnp.dot(cached[r * per_row:(r + 1) * per_row], cache_ref[r], preferred_element_type=jnp.float32))
    mixed_ref[...] = jnp.concatenate(mixed, axis=0) + jnp.dot(new, fresh, preferred_element_type=jnp.float32)

    def head(h):
        return jnp.concatenate([mixed_ref[pl.ds(h * steps + s, rows, stride=per_row), :] for s in range(steps)], axis=0)

    mix_ref[...] = jnp.concatenate(
        [jnp.where(is_key, pltpu.roll(head(2 * m), HEAD_SIZE, 1), head(2 * m + 1)) for m in range(heads // 2)], axis=1
    ).astype(jnp.bfloat16)
    copies[-1].wait()
    project(mix_ref, wo_ref, other_ref, 1 - lane_of(True))


def project(mix_ref, wo_ref, out_ref, side):
    width, (tps, total_rows, _) = wo_ref.shape[0], out_ref.shape
    for at in range(2):
        start, stop = at * tps * LANES, min((at + 1) * tps * LANES, width)

        @pl.when(side == at)
        def _(start=start, stop=stop):
            partial = dot_last(mix_ref[...], wo_ref[start:stop, :])
            for t in range(tps):
                low, high = t * LANES, min((t + 1) * LANES, stop - start)
                piece = partial[:, low:high]
                if high - low < LANES:
                    piece = jnp.concatenate([piece, jnp.zeros((total_rows, LANES - (high - low)), jnp.float32)], axis=1)
                out_ref[t] = piece.astype(out_ref.dtype)


def own_projection_kernel(mix_ref, wo_ref, mine_ref):
    project(mix_ref, wo_ref, mine_ref, lane_of(True))


def attention_partial(flat, gain, w_query, key_value, sinks, w_output, cache, lengths, routes, weights, secs, tps):
    total_rows, width = flat.shape
    rows, slots, pair = cache.shape
    per_row = w_query.shape[1] // HEAD_SIZE * (total_rows // rows)
    shards = secs * tps
    operands = (lengths, sinks, routes, weights, gain, flat, w_query, key_value, cache, w_output.swapaxes(0, 1))
    return pl.pallas_call(
        attention_kernel,
        name="attention",
        out_shape=[shape_of((tps, total_rows, LANES)), shape_of((total_rows, LANES), jnp.float32),
                   shape_of((total_rows, w_output.shape[0])), shape_of((width, w_output.shape[0]))],
        in_specs=[outside()] * len(operands),
        out_specs=[vmem()] * 4,
        scratch_shapes=[
            pltpu.SMEM(lengths.shape, jnp.int32),
            pltpu.SMEM(sinks.shape, jnp.float32),
            pltpu.VMEM(routes.shape, jnp.int32),
            pltpu.VMEM(weights.shape, jnp.float32),
            pltpu.VMEM(gain.shape, jnp.float32),
            pltpu.VMEM((total_rows, width), jnp.bfloat16),
            pltpu.VMEM(w_query.shape, jnp.bfloat16),
            pltpu.VMEM(key_value.shape, jnp.bfloat16),
            pltpu.VMEM(cache.shape, jnp.bfloat16),
            pltpu.VMEM((total_rows, shards * LANES), jnp.float32),
            pltpu.VMEM((rows * per_row, pair), jnp.float32),
            pltpu.VMEM((rows * per_row, pair), jnp.float32),
            pltpu.SemaphoreType.DMA((9 + len(split_width(width)),)),
        ],
        compiler_params=pltpu.CompilerParams(vmem_limit_bytes=24 * MIB),
    )(*[pltpu.with_memory_space_constraint(operand, pltpu.HBM) for operand in operands])


def call(kernel, name, outs, *operands, limit=4, flops=0):
    single = not isinstance(outs, list)
    held = [*operands, *([outs] if single else outs)]
    return pl.pallas_call(
        kernel,
        name=name,
        out_shape=outs,
        in_specs=[vmem()] * len(operands),
        out_specs=vmem() if single else [vmem()] * len(outs),
        compiler_params=pltpu.CompilerParams(vmem_limit_bytes=limit * MIB),
        cost_estimate=pl.CostEstimate(flops=flops, transcendentals=0,
                                      bytes_accessed=sum(math.prod(a.shape) * a.dtype.itemsize for a in held)),
    )(*operands)


def after_core_kernel(mine_ref, come_ref, own_ref, *send_refs):
    tp = lax.axis_index("tp")
    own_ref[...] = mine_ref[tp] + come_ref[tp].astype(jnp.float32)
    for mask, ref in zip(shard_masks(True), send_refs):
        to = jnp.bitwise_xor(tp, mask)
        ref[...] = (mine_ref[to] + come_ref[to].astype(jnp.float32)).astype(jnp.bfloat16)


def after_core_halves_kernel(mine_ref, come_ref, own_ref, *send_refs):
    tp, half = lax.axis_index("tp"), mine_ref.shape[1] // 2
    own_ref[...] = mine_ref[tp] + come_ref[tp].astype(jnp.float32)
    for mask, first, second in zip(shard_masks(False), send_refs[:3], send_refs[3:]):
        to = jnp.bitwise_xor(tp, mask)
        part = (mine_ref[to] + come_ref[to].astype(jnp.float32)).astype(jnp.bfloat16)
        first[...] = part[:half]
        second[...] = part[half:]


def add_all(*refs):
    total = refs[0][...]
    for ref in refs[1:]:
        total = total + ref[...].astype(jnp.float32)
    return total


def sum_kernel(*refs):
    refs[-1][...] = add_all(*refs[:-1]).astype(jnp.bfloat16).reshape(refs[-1].shape)


def sum_rows_kernel(own_ref, *refs, line):
    come, outs = refs[:3], refs[3:]
    lines = outs[0].shape[0]
    total = own_ref[line:line + len(outs) * lines]
    for ref in come:
        total = total + ref[...].astype(jnp.float32)
    for n, out in enumerate(outs):
        out[...] = total[n * lines:(n + 1) * lines].astype(out.dtype)


def scatter_shards(mine, come):
    tps, lines, part = mine.shape
    own, *parts = call(after_core_kernel, "after_core", [shape_of((lines, part), jnp.float32)] + [shape_of((lines, part))] * (tps - 1),
                       mine, come)
    return [own] + shard_swaps(parts, True)


def first_products(pieces, masks, side, x_ref, gain_ref, gate_ref, up_ref, gate_out, up_out, square_out):
    width, lines = gate_ref.shape[1], x_ref.shape[0]
    tp = lax.axis_index("tp")
    for mask, piece in zip(masks, pieces):
        at = pl.multiple_of(jnp.bitwise_xor(tp, mask) * LANES, LANES)
        x_ref[:, pl.ds(at, LANES)] = piece[...].reshape(lines, LANES)
    for at in range(2):
        start, stop = at * x_ref.shape[1], min((at + 1) * x_ref.shape[1], width)

        @pl.when(side == at)
        def _(start=start, stop=stop):
            x = x_ref[:, :stop - start].astype(jnp.float32)
            square_out[...] = jnp.broadcast_to(jnp.sum(x * x, axis=-1, keepdims=True), square_out.shape)
            scaled = (x * gain_ref[:, start:stop]).astype(jnp.bfloat16)
            gate_out[...] = dot_last(scaled, gate_ref[:, start:stop])
            up_out[...] = dot_last(scaled, up_ref[:, start:stop])


def near_kernel(gain_ref, gate_ref, up_ref, *refs):
    pieces, (x_ref, gate_out, up_out, square_out) = refs[:-4], refs[-4:]
    first_products(pieces, (0, *shard_masks(True)), lane_of(True), x_ref, gain_ref, gate_ref, up_ref, gate_out, up_out,
                   square_out)


def second_product(act_ref, down_ref, out_ref, number):
    tps, _, part = out_ref.shape

    for at in range(2):
        starts = [((at ^ (t & 1) ^ (t >> 1)) * tps + t) * part for t in range(tps)]

        @pl.when(number == at)
        def _(starts=starts):
            for first, last in ((0, 0), (1, 2), (3, 3)):
                shift = starts[first] % 128
                out = jnp.dot(act_ref[...], down_ref[:, starts[first] - shift:starts[last] + part],
                              preferred_element_type=jnp.float32)
                for n, t in enumerate(range(first, last + 1)):
                    out_ref[t] = out[:, shift + n * part:shift + (n + 1) * part].astype(out_ref.dtype)


def far_kernel(gain_ref, gate_ref, up_ref, down_ref, near_x_ref, near_gate_ref, near_up_ref, near_square_ref, *refs):
    pieces, (other_ref, act_ref, far_x_ref, gate_out, up_out, square_out) = refs[:-6], refs[-6:]
    side, grp = lane_of(True), lax.axis_index("grp")
    masks = shard_masks(True)
    first_products(pieces, (0, masks[0], masks[2], masks[1]), 1 - side, far_x_ref, gain_ref, gate_ref, up_ref, gate_out, up_out,
                   square_out)
    width, half = gate_ref.shape[1], near_x_ref.shape[1]
    spare = jnp.where(side == 1, near_x_ref[:, width - half:], far_x_ref[:, width - half:]).astype(jnp.float32)
    spare_at = lax.broadcasted_iota(jnp.int32, spare.shape, 1)
    weight = jnp.sum(jnp.where((spare_at == 2 * grp) | (spare_at == 2 * grp + 1), spare, 0.0), axis=1, keepdims=True)
    square = (near_square_ref[...] + square_out[...])[:, :1]
    scale = lax.rsqrt(square / width + 1e-05)
    gate_h = (near_gate_ref[...] + gate_out[...]) * scale
    up_h = (near_up_ref[...] + up_out[...]) * scale
    act_ref[...] = ((up_h + 1.0) * gate_h * jax.nn.sigmoid(1.702 * gate_h) * weight).astype(jnp.bfloat16)
    second_product(act_ref, down_ref, other_ref, 1 - lane_of(False))


def last_kernel(act_ref, down_ref, near_x_ref, far_x_ref, mine_ref, middle_ref, row_ref):
    sec, tp = lax.axis_index("sec"), lax.axis_index("tp")
    second_product(act_ref, down_ref, mine_ref, lane_of(False))
    total_rows, part = middle_ref.shape
    near, far = near_x_ref[-total_rows:].astype(jnp.float32), far_x_ref[-total_rows:].astype(jnp.float32)
    first = lane_of(True) == 0
    x = jnp.concatenate([jnp.where(first, near, far), jnp.where(first, far, near)], axis=1)
    for c in range(row_ref.shape[0]):
        row_ref[c] = x[:, c * part:(c + 1) * part]
    middle_ref[...] = row_ref[sec * mine_ref.shape[0] + tp]


def experts(gain, w_gate, w_up, w_down, pieces, part):
    gain, w_gate, w_up = gain.reshape(1, -1), w_gate.swapaxes(0, 1), w_up.swapaxes(0, 1)
    (hidden, width), tps, (groups, total_rows, _) = w_gate.shape, len(pieces), pieces[0].shape
    lines = groups * total_rows
    far_pieces = [swap(piece, "sec", 1) for piece in pieces]
    halves = [shape_of((lines, tps * LANES)), shape_of((lines, hidden), jnp.float32), shape_of((lines, hidden), jnp.float32),
              shape_of((lines, 128), jnp.float32)]
    near = call(near_kernel, "near_columns", halves, gain, w_gate, w_up, *pieces, limit=12, flops=2 * lines * width * hidden)
    other, act, far_x = pl.pallas_call(
        far_kernel,
        name="far_columns",
        out_shape=[shape_of((tps, lines, part)), shape_of((lines, hidden)), halves[0]],
        in_specs=[vmem()] * (8 + len(far_pieces)),
        out_specs=[vmem()] * 3,
        scratch_shapes=[pltpu.VMEM(half.shape, half.dtype) for half in halves[1:]],
        compiler_params=pltpu.CompilerParams(vmem_limit_bytes=16 * MIB),
    )(gain, w_gate, w_up, w_down, *near, *far_pieces)
    come = swap(other, "sec", 1)
    mine, middle = pl.pallas_call(
        last_kernel,
        name="own_columns",
        out_shape=[shape_of((tps, lines, part), jnp.float32), shape_of((total_rows, part), jnp.float32)],
        in_specs=[vmem()] * 4,
        out_specs=[vmem()] * 2,
        scratch_shapes=[pltpu.VMEM((2 * tps, total_rows, part), jnp.float32)],
        compiler_params=pltpu.CompilerParams(vmem_limit_bytes=12 * MIB),
        cost_estimate=pl.CostEstimate(flops=lines * width * hidden, transcendentals=0, bytes_accessed=2 * lines * width),
    )(act, w_down, near[0], far_x)
    return mine, come, middle


def every_expert_body(inputs, attention_gain, w_query, key_value_weight, head_sink_logits, w_output, cache_pairs, lengths,
                      expert_gain, w_gate, w_up, w_down, routes, gate_weights):
    secs, tps, groups = lax.axis_size("sec"), lax.axis_size("tp"), lax.axis_size("grp")
    steps, rows, width = inputs.shape
    flat = inputs.reshape(steps * rows, width)
    other, own_x, mix, held = attention_partial(
        flat, attention_gain, w_query, key_value_weight[:, 0], head_sink_logits, w_output, cache_pairs[:, :, 0], lengths,
        routes.swapaxes(1, 2), gate_weights.swapaxes(1, 2), secs, tps)
    come = swap(other, "sec", 1)
    mine = call(own_projection_kernel, "own_projection", shape_of(other.shape, jnp.float32), mix, held, limit=12,
                flops=mix.size * width)
    middle = call(sum_kernel, "sum", shape_of((steps * rows, LANES)), *scatter_shards(mine, come), own_x)
    stacked = jnp.stack([lane_swap(middle, m, (0, 0), True) for m in reversed(range(1, groups))] + [middle])
    pieces = [stacked] + shard_swaps([stacked] * (tps - 1), True)
    part = width // (secs * tps)
    mine, come, own_middle = experts(expert_gain, w_gate[0], w_up[0], w_down[0], pieces, part)
    lines = steps * rows
    own, *parts = call(after_core_halves_kernel, "after_core_halves",
                       [shape_of((groups * lines, part), jnp.float32)] + [shape_of((groups // 2 * lines, part))] * 6, mine, come)
    far_come, near_come = shard_swaps(parts[:3], False), shard_swaps(parts[3:], False)
    third, second = call(functools.partial(sum_rows_kernel, line=0), "sum_far_rows", [shape_of((lines, part))] * 2,
                         own, *far_come)
    second, third = swap(second, "grp", 2), swap(third, "grp", 3)
    nearest, own = call(functools.partial(sum_rows_kernel, line=2 * lines), "sum_near_rows",
                        [shape_of((lines, part)), shape_of((lines, part), jnp.float32)], own, *near_come)
    return call(sum_kernel, "combine", shape_of((steps, rows, part)), own, second, third, swap(nearest, "grp", 1), own_middle)


def body(*args):
    sizes = lax.axis_size("sec"), lax.axis_size("tp"), lax.axis_size("grp"), args[9].shape[0]
    if sizes == (2, 4, TOP, 1):
        return every_expert_body(*args)
    return general_body(*args)


def solution(mesh):
    placed = (
        P(None, "grp", None),
        P(),
        P(None, ("sec", "tp")),
        P(None, ("sec", "tp"), None),
        P(("sec", "tp")),
        P(("sec", "tp"), None),
        P("grp", None, ("sec", "tp"), None),
        P("grp"),
        P(),
        P("grp", None, ("sec", "tp")),
        P("grp", None, ("sec", "tp")),
        P("grp", ("sec", "tp"), None),
        P(None, "grp", None),
        P(None, "grp", None),
    )
    return jax.shard_map(
        body, mesh=mesh, in_specs=placed, out_specs=P(None, "grp", ("sec", "tp")), check_vma=False
    )
```
